32 devices in a mesh: wide: 8 (over y, x, core), narrow: 4 (over z).
Axes of the slice: x: 2, y: 2, z: 4, core: 2. Of those that a mesh axis runs over, the one named last changes fastest.
Arguments:
- tracers: float32 [4, 221, 65536], P(None, None, ('wide', 'narrow')), may hold values from -6 to 6
- column_rate: float32 [65536], P(('wide', 'narrow')), may hold values from 0.25 to 2
- loss_rate: float32 [221], replicated, may hold values from 0.05 to 3
- coupling: bfloat16 [221, 221], replicated, may hold values from -0.375 to 0.375
- phys_index: int32 [65536], P(('wide', 'narrow')), may hold values from 0 to 65535, as said below
- iter_count: int32 [65536], P(('wide', 'narrow')), may hold values from 2 to 12, as said below
Outputs:
- updated: float32 [4, 221, 65536], P(None, None, ('wide', 'narrow'))
The draws below stay inside these ranges and needn't reach their ends.
Inputs may be any that keep to these rules, and one draw needn't show every extreme that they name: A permutation of the columns: column c goes to the device phys_index[c] // 2048 (devices in wide-major order) at slot phys_index[c] % 2048. A device at wide index w sends columns only to devices at wide indices w - 1 to w + 2, with wrap. For each wide step and narrow step (with wrap) every device sends the same number of columns to the device that many steps further on; at most 256, and exactly 256 for some pair of steps. The columns from one device to one device fill a contiguous range of slots. `iter_count`: columns whose physics device lies in 4 consecutive wide indices (with wrap) take 12 // 2 to 12 substeps, the others 2 to 3.
All inputs are finite; a program needn't handle non-finite values.
Results may differ from the reference program's by a relative error of at most 0.00072.
Values sent between devices are 32-bit elements; how exact they have to be, the bound alone decides.
No kernel may reach another device: no remote copies, remote signals or barrier semaphores. Data moves between devices by JAX's collectives and lax.ppermute only.
A program may use at most 128 MiB of HBM per device.

```python
import math
import jax
import jax.numpy as jnp
from jax import lax

S = 221
LEV = 4
MAXIT = 12
WIN = 4
COL_DEV = 2048
COLUMNS = 65536
N_WIDE = 8
N_NARROW = 4
DEVICES = 32


def column_layout(key):
    pair_count = WIN * N_NARROW
    mean_count = COL_DEV // pair_count
    count_key, order_key, perm_key = jax.random.split(jax.random.fold_in(key, 17), 3)
    swing = jax.random.randint(count_key, (pair_count // 2,), -mean_count, mean_count + 1)
    swing = swing.at[0].set(mean_count)
    per_pair = jnp.stack([mean_count + swing, mean_count - swing], 1).reshape(pair_count)
    per_pair = per_pair[jax.random.permutation(perm_key, pair_count)]
    bounds = jnp.cumsum(per_pair)
    perm_keys = jax.random.split(order_key, DEVICES)
    column_rank = jax.vmap(lambda subkey: jax.random.permutation(subkey, COL_DEV))(perm_keys).astype(jnp.int32)
    pair_of = jnp.searchsorted(bounds, column_rank, side='right').astype(jnp.int32)
    wide_step = pair_of // N_NARROW
    narrow_step = pair_of % N_NARROW
    source_dev = jnp.arange(DEVICES, dtype=jnp.int32)[:, None]
    target_dev = (source_dev // N_NARROW + wide_step - 1) % N_WIDE * N_NARROW + (source_dev % N_NARROW + narrow_step) % N_NARROW
    return (target_dev * COL_DEV + column_rank).reshape(COLUMNS).astype(jnp.int32)


def draw_phys_index(key, part):
    return column_layout(key)


def draw_iter_count(key, part):
    position = column_layout(key)
    key = jax.random.fold_in(key, 5)
    noon_key, day_key, night_key = jax.random.split(key, 3)
    noon_wide = jax.random.randint(noon_key, (), 0, N_WIDE)
    span_wide = position // COL_DEV // N_NARROW
    daylit = (span_wide - noon_wide) % N_WIDE < N_WIDE // 2
    day_iters = jax.random.randint(day_key, (COLUMNS,), MAXIT // 2, MAXIT + 1)
    night_iters = jax.random.randint(night_key, (COLUMNS,), 2, MAXIT // 4 + 1)
    iters = jnp.where(daylit, day_iters, night_iters)
    iters = jnp.where(position == noon_wide * N_NARROW * COL_DEV, MAXIT, iters)
    return iters.astype(jnp.int32)


def block_scale(own_key, extent, cuts, low, largest):
    loudness = 1.0
    for dim, shards_of in cuts:
        draws = jax.random.uniform(jax.random.fold_in(jax.random.fold_in(own_key, 6), dim), (shards_of,), jnp.float32, low / len(cuts), largest / len(cuts))
        loudness = loudness * jnp.repeat(jnp.exp(draws), extent[dim] // shards_of).reshape((-1,) + (1,) * (len(extent) - 1 - dim))
    return loudness


def centred(rng, shape, spread, bound, cuts=(), kind=jnp.bfloat16):
    array = spread * jax.random.normal(rng, shape, jnp.float32)
    if cuts:
        array = array * block_scale(rng, shape, cuts, -0.22, 0.18)
    return jnp.clip(array, -bound, bound).astype(kind)


def setup_inputs(seed: int = 0) -> dict:
    seeds = jax.random.split(jax.random.key(seed), 7)
    return {
        "tracers": centred(seeds[0], (LEV, S, COLUMNS), 1.0, 6.0, ((2, 32),), jnp.float32),
        "column_rate": jnp.clip(jnp.exp(math.log(2.0) - 2.0794415 * jax.random.uniform(seeds[1], (COLUMNS,), jnp.float32) ** block_scale(seeds[1], (COLUMNS,), ((0, 32),), -0.2, 0.2)), 0.25, 2.0),
        "loss_rate": jnp.clip(jnp.exp(jax.random.uniform(seeds[2], (S,), jnp.float32, math.log(0.05), math.log(3.0))), 0.05, 3.0),
        "coupling": centred(seeds[3], (S, S), S ** -0.5, 0.375),
        "phys_index": draw_phys_index(jax.random.fold_in(seeds[6], 71), 0),
        "iter_count": draw_iter_count(jax.random.fold_in(seeds[6], 71), 0),
    }


def reference(tracers, column_rate, loss_rate, coupling, phys_index, iter_count):
    states = tracers.reshape(LEV, S, DEVICES, COL_DEV).transpose(2, 0, 1, 3)
    rates = column_rate.reshape(DEVICES, COL_DEV)
    counts = iter_count.reshape(DEVICES, COL_DEV)
    weight = coupling.astype(jnp.float32)

    def chemistry(block_item):
        initial, rate, count = block_item
        step_len = rate / count.astype(jnp.float32)
        divisor = 1.0 + step_len[None, None, :] * loss_rate[None, :, None]

        def advance(k, y):
            squashed = lax.optimization_barrier(jnp.tanh(y).astype(jnp.bfloat16)).astype(jnp.float32)
            produced = jnp.einsum("st,ltc->lsc", weight, squashed)
            nxt = (y + step_len[None, None, :] * produced) / divisor
            return jnp.where(k < count[None, None, :], nxt, y)

        return lax.fori_loop(0, MAXIT, advance, initial)

    finished = lax.map(chemistry, (states, rates, counts))
    flat_result = finished.transpose(1, 2, 0, 3).reshape(LEV, S, COLUMNS)
    return jnp.zeros((LEV, S, COLUMNS), jnp.float32).at[:, :, phys_index].set(flat_result)
```

```python
import functools

import jax
import jax.numpy as jnp
from jax import lax
from jax.experimental import pallas as pl
from jax.experimental.pallas import tpu as pltpu
from jax.sharding import PartitionSpec as P

WIN = 4
LANES = 128
SORT_ROWS = 512
INT_ROWS = 256
SEND_ROWS = 32
VMEM = 60 * 1024 * 1024


def from_behind(value, axis, steps):
    count = lax.axis_size(axis)
    pairs = [(source, (source + steps) % count) for source in range(count)]
    return lax.ppermute(value, axis, pairs)


def log2(value):
    bits = value.bit_length() - 1
    assert 1 << bits == value
    return bits


def sort_kernel(sizes, me_ref, phys_ref, rate_ref, count_ref, tracers_ref, rows_ref, table_ref,
                pos_ref, tail_ref, high_ref, low_ref, onehot_ref, total_ref):
    levels, species, columns, pad, tiles, wide_count, narrow_count, pair_total = sizes
    step = pl.program_id(0)

    @pl.when(step == 0)
    def _():
        phys = phys_ref[...]
        target = lax.shift_right_logical(phys, log2(columns))
        slot = phys & (columns - 1)
        wide_step = (lax.shift_right_logical(target, log2(narrow_count)) - me_ref[0] + 1) & (
            wide_count - 1
        )
        narrow_step = ((target & (narrow_count - 1)) - me_ref[1]) & (narrow_count - 1)
        pair = narrow_step * WIN + wide_step
        member = pair == lax.broadcasted_iota(jnp.int32, (pair_total, columns), 0)
        counts = jnp.sum(jnp.where(member, 1.0, 0.0), axis=1, keepdims=True)
        slot_f = slot.astype(jnp.float32)
        starts = jnp.min(jnp.where(member, slot_f, float(columns)), axis=1, keepdims=True)
        rounded = ((counts.astype(jnp.int32) + 7) & -8).astype(jnp.float32)
        lane = lax.broadcasted_iota(jnp.int32, (pair_total, LANES), 1)
        row = lax.broadcasted_iota(jnp.int32, (pair_total, LANES), 0)
        rounded_t = jnp.sum(jnp.where(lane == row, rounded, 0.0), axis=0, keepdims=True)
        counts_t = jnp.sum(jnp.where(lane == row, counts, 0.0), axis=0, keepdims=True)
        base = jnp.sum(jnp.where(lane < row, rounded_t, 0.0), axis=1, keepdims=True)
        base_t = jnp.sum(jnp.where(lane == row, base, 0.0), axis=0, keepdims=True)
        pos = slot_f + jnp.sum(jnp.where(member, base - starts, 0.0), axis=0, keepdims=True)
        pos_ref[...] = pos.astype(jnp.int32)
        total_ref[0] = jnp.max(base + rounded).astype(jnp.int32)
        table_ref[0:1, :] = counts_t.astype(jnp.int32)
        table_ref[1:2, :] = base_t.astype(jnp.int32)

        def split(value, begin, size):
            high = value.astype(jnp.bfloat16)
            high_ref[pl.ds(begin, size), :] = high
            low_ref[pl.ds(begin, size), :] = (value - high.astype(jnp.float32)).astype(jnp.bfloat16)

        body = species // 16 * 16
        rest = species - body

        def one_level(level, carry):
            begin = pl.multiple_of(level * pad, 16)

            def one_part(part, inner):
                at = pl.multiple_of(part * 16, 16)
                split(tracers_ref[level, pl.ds(at, 16), :], pl.multiple_of(begin + at, 16), 16)
                return inner

            lax.fori_loop(0, body // 16, one_part, 0)
            tail_ref[...] = jnp.zeros_like(tail_ref)
            tail_ref[0:rest, :] = tracers_ref[level, body:species, :]

            @pl.when(level == 0)
            def _():
                tail_ref[pad - body - 3:pad - body - 2, :] = slot_f
                tail_ref[pad - body - 2:pad - body - 1, :] = rate_ref[...]
                tail_ref[pad - body - 1:pad - body, :] = count_ref[...].astype(jnp.float32)

            split(tail_ref[...], pl.multiple_of(begin + body, 16), 16)
            return carry

        lax.fori_loop(0, levels, one_level, 0)

    @pl.when(step * SORT_ROWS < total_ref[0])
    def _():
        wanted = step * SORT_ROWS + lax.broadcasted_iota(jnp.int32, (SORT_ROWS, LANES), 0)

        def one_hot(part, carry):
            at = pl.ds(pl.multiple_of(part * LANES, LANES), LANES)
            onehot_ref[:, at] = jnp.where(wanted == pos_ref[:, at], 1.0, 0.0).astype(jnp.bfloat16)
            return carry

        lax.fori_loop(0, columns // LANES, one_hot, 0)
        over_both = (((1,), (1,)), ((), ()))
        for first in range(0, tiles, 2):
            count = min(2, tiles - first)
            span = slice(first * LANES, (first + count) * LANES)
            out = lax.dot_general(
                onehot_ref[...], high_ref[span, :], over_both, preferred_element_type=jnp.float32
            ) + lax.dot_general(
                onehot_ref[...], low_ref[span, :], over_both, preferred_element_type=jnp.float32
            )
            for extra in range(count):
                rows_ref[:, first + extra] = out[:, extra * LANES:(extra + 1) * LANES].reshape(
                    SORT_ROWS // 8, 8, LANES
                )


def integrate_kernel(sizes, total_ref, rows_ref, loss_ref, coupling_ref, out_ref,
                     y_ref, inverse_ref):
    levels, species, pad, tiles = sizes
    per = LANES // 8
    halves = INT_ROWS // LANES

    @pl.when(pl.program_id(0) * INT_ROWS < total_ref[0])
    def _():
        for tile in range(tiles):
            for half in range(halves):
                block = rows_ref[half * per:(half + 1) * per, tile].reshape(LANES, LANES)
                y_ref[tile * LANES:(tile + 1) * LANES, half * LANES:(half + 1) * LANES] = block.T
        rate = y_ref[pad - 2:pad - 1, :]
        count = y_ref[pad - 1:pad, :]
        step_len = rate / jnp.maximum(count, 1.0)
        inverse_ref[...] = 1.0 / (1.0 + step_len * loss_ref[...])
        last = jnp.max(count).astype(jnp.int32)

        def advance(k, carry):
            active = k.astype(jnp.float32) < count
            for level in range(levels):
                span = slice(level * pad, (level + 1) * pad)
                y = y_ref[span, :]
                squashed = jnp.tanh(y).astype(jnp.bfloat16)
                produced = jnp.dot(
                    coupling_ref[...], squashed, preferred_element_type=jnp.float32
                )
                y_ref[span, :] = jnp.where(
                    active, (y + step_len * produced) * inverse_ref[...], y
                )
            return carry

        lax.fori_loop(0, last, advance, 0)
        for tile in range(tiles):
            for half in range(halves):
                block = y_ref[tile * LANES:(tile + 1) * LANES, half * LANES:(half + 1) * LANES]
                out_ref[half * per:(half + 1) * per, tile] = block.T.reshape(per, 8, LANES)


def finish_kernel(sizes, sources, offset_ref, count_ref, *refs):
    levels, species, columns, pad, tiles, room = sizes
    groups = room // 8
    buffers = refs[:-4]
    out_ref, piece_ref, placed_ref, sem_ref = refs[-4:]
    copies = []
    for pair, source in enumerate(sources):
        copy = pltpu.make_async_copy(
            buffers[source].at[pl.ds(offset_ref[pair], groups)], piece_ref.at[pair], sem_ref.at[pair]
        )
        copy.start()
        copies.append(copy)
    slot_tile, slot_lane = divmod(pad - 3, LANES)
    lane = lax.broadcasted_iota(jnp.int32, (1, LANES), 1)
    in_group = lax.broadcasted_iota(jnp.int32, (8, LANES), 0)
    for pair in range(len(sources)):
        copies[pair].wait()
        count = count_ref[pair]
        first = piece_ref[pair, 0, slot_tile][0:1, :]
        start = jnp.max(jnp.where(lane == slot_lane, first, 0.0)).astype(jnp.int32)
        start = jnp.clip(start, 0, columns - 1)
        whole = lax.shift_right_logical(count, 3)

        def move(group, carry):
            for tile in range(tiles):
                placed_ref[tile, pl.ds(start + group * 8, 8), :] = piece_ref[pair, group, tile]
            return carry

        lax.fori_loop(0, whole, move, 0)

        @pl.when((count & 7) > 0)
        def _():
            for tile in range(tiles):
                at = pl.ds(start + whole * 8, 8)
                placed_ref[tile, at, :] = jnp.where(
                    in_group < (count & 7), piece_ref[pair, whole, tile], placed_ref[tile, at, :]
                )

    def turn(part, carry):
        at = pl.ds(pl.multiple_of(part * LANES, LANES), LANES)
        for tile in range(tiles):
            block = placed_ref[tile, at, :].T
            done = 0
            while done < LANES:
                level, begin = divmod(tile * LANES + done, pad)
                size = min(LANES - done, pad - begin)
                keep = min(size, species - begin)
                out_ref[level, begin:begin + keep, at] = block[done:done + keep, :]
                done += size
        return carry

    lax.fori_loop(0, columns // LANES, turn, 0)


def local(tracers, column_rate, loss_rate, coupling, phys_index, iter_count):
    levels, species, columns = tracers.shape
    wide_count = lax.axis_size("wide")
    narrow_count = lax.axis_size("narrow")
    pair_total = WIN * narrow_count
    room = 2 * columns // pair_total
    piece = room // 8
    pad = -(-(species + 3) // 16) * 16
    while levels * pad % LANES:
        pad += 16
    tiles = levels * pad // LANES
    most = columns + 7 * pair_total + room + SEND_ROWS
    rows_room = -(-most // SORT_ROWS) * SORT_ROWS
    full = pl.BlockSpec(memory_space=pltpu.VMEM)
    smem = pl.BlockSpec(memory_space=pltpu.SMEM)
    row_shape = (tiles, 8, LANES)

    def row_block(rows):
        return pl.BlockSpec((rows // 8,) + row_shape, lambda at: (at, 0, 0, 0))

    me = jnp.stack([lax.axis_index("wide"), lax.axis_index("narrow")]).astype(jnp.int32)
    rows, table = pl.pallas_call(
        functools.partial(
            sort_kernel,
            (levels, species, columns, pad, tiles, wide_count, narrow_count, pair_total),
        ),
        grid=(rows_room // SORT_ROWS,),
        in_specs=[smem, full, full, full, full],
        out_specs=[row_block(SORT_ROWS), full],
        out_shape=[
            jax.ShapeDtypeStruct((rows_room // 8,) + row_shape, jnp.float32),
            jax.ShapeDtypeStruct((8, LANES), jnp.int32),
        ],
        scratch_shapes=[
            pltpu.VMEM((1, columns), jnp.int32),
            pltpu.VMEM((16, columns), jnp.float32),
            pltpu.VMEM((levels * pad, columns), jnp.bfloat16),
            pltpu.VMEM((levels * pad, columns), jnp.bfloat16),
            pltpu.VMEM((SORT_ROWS, columns), jnp.bfloat16),
            pltpu.SMEM((1,), jnp.int32),
        ],
        compiler_params=pltpu.CompilerParams(vmem_limit_bytes=VMEM),
        name="sort_columns",
    )(
        me,
        phys_index.reshape(1, columns),
        column_rate.reshape(1, columns),
        iter_count.reshape(1, columns),
        tracers,
    )
    counts = table[0, :pair_total].reshape(narrow_count, WIN)
    base = table[1, :pair_total].reshape(narrow_count, WIN) // 8
    groups = (counts + 7) // 8
    total = (base[-1, -1] + groups[-1, -1]) * 8
    inner = base - base[:, :1]
    sections = -(-jnp.sum(groups, 1) * 8 // SEND_ROWS)

    loss_pad = jnp.pad(loss_rate, (0, pad - species)).reshape(pad, 1)
    coupling_pad = jnp.pad(coupling, ((0, pad - species), (0, pad - species)))
    rows = pl.pallas_call(
        functools.partial(integrate_kernel, (levels, species, pad, tiles)),
        grid=(rows_room // INT_ROWS,),
        in_specs=[smem, row_block(INT_ROWS), full, full],
        out_specs=row_block(INT_ROWS),
        out_shape=jax.ShapeDtypeStruct((rows_room // 8,) + row_shape, jnp.float32),
        scratch_shapes=[
            pltpu.VMEM((levels * pad, INT_ROWS), jnp.float32),
            pltpu.VMEM((pad, INT_ROWS), jnp.float32),
        ],
        compiler_params=pltpu.CompilerParams(vmem_limit_bytes=VMEM),
        name="integrate_columns",
    )(total.reshape(1), rows, loss_pad, coupling_pad)

    arrival_room = (WIN + 1) * piece
    send_groups = SEND_ROWS // 8
    most_sections = WIN * room // SEND_ROWS

    def sections_by(step, source, begin, wide_moves):
        operands = [source, begin] + [value for move in wide_moves for value in move[:2]]

        def branch(count, source, begin, *moves):
            got = []
            for at, move in enumerate(wide_moves):
                part = lax.dynamic_slice_in_dim(moves[2 * at], moves[2 * at + 1], piece, 0)
                got.append(from_behind(part, "wide", move[2]))
            if count == 0:
                arrived = jnp.zeros((arrival_room,) + row_shape, jnp.float32)
            else:
                part = lax.dynamic_slice_in_dim(source, begin, count * send_groups, 0)
                arrived = from_behind(part, "narrow", step)
                spare = arrival_room - count * send_groups
                arrived = jnp.pad(arrived, ((0, spare), (0, 0), (0, 0), (0, 0)))
            return arrived, got

        return lax.switch(
            sections[step],
            [functools.partial(branch, count) for count in range(most_sections + 1)],
            *operands,
        )

    moving = [at for at in range(WIN) if at != 1]
    last = narrow_count - 1
    order = [narrow_count // 2]
    order += [step for step in range(1, last) if step not in order]
    held = {(1, 0): (rows, base[0, 1])}
    zero = jnp.zeros((), jnp.int32)

    wide_moves = [(rows, base[0, at], at - 1) for at in moving]
    wide_moves += [(rows, base[last, at], at - 1) for at in moving]
    previous = None
    for step in order:
        if previous is not None:
            wide_moves = [(arrived, inner[previous, at], at - 1) for at in moving]
        arrived, got = sections_by(step, rows, base[step, 0], wide_moves)
        held[1, step] = (arrived, inner[step, 1])
        if previous is None:
            for index, at in enumerate(moving):
                held[at, 0] = (got[index], zero)
            early = dict(zip(moving, got[len(moving):]))
            early[1] = lax.dynamic_slice_in_dim(rows, base[last, 1], piece, 0)
            merged = jnp.zeros((arrival_room,) + row_shape, jnp.float32)
            for at in range(WIN):
                merged = lax.dynamic_update_slice_in_dim(merged, early[at], inner[last, at], 0)
        else:
            for index, at in enumerate(moving):
                held[at, previous] = (got[index], zero)
        previous = step
    wide_moves = [(arrived, inner[previous, at], at - 1) for at in moving]
    arrived, got = sections_by(last, merged, zero, wide_moves)
    for index, at in enumerate(moving):
        held[at, previous] = (got[index], zero)
    for at in range(WIN):
        held[at, last] = (arrived, inner[last, at])

    buffers, sources, offsets = [], [], []
    for step in range(narrow_count):
        for at in range(WIN):
            value, offset = held[at, step]
            known = [index for index, other in enumerate(buffers) if other is value]
            if not known:
                buffers.append(value)
                known = [len(buffers) - 1]
            sources.append(known[0])
            offsets.append(offset)
    return pl.pallas_call(
        functools.partial(
            finish_kernel, (levels, species, columns, pad, tiles, room), tuple(sources)
        ),
        in_specs=[smem, smem] + [pl.BlockSpec(memory_space=pl.ANY)] * len(buffers),
        out_specs=full,
        out_shape=jax.ShapeDtypeStruct((levels, species, columns), jnp.float32),
        scratch_shapes=[
            pltpu.VMEM((pair_total, piece) + row_shape, jnp.float32),
            pltpu.VMEM((tiles, columns + 8, LANES), jnp.float32),
            pltpu.SemaphoreType.DMA((pair_total,)),
        ],
        compiler_params=pltpu.CompilerParams(vmem_limit_bytes=VMEM),
        name="place_columns",
    )(jnp.stack(offsets).astype(jnp.int32), counts.reshape(-1), *buffers)


def solution(mesh):
    placed = (
        P(None, None, ("wide", "narrow")),
        P(("wide", "narrow")),
        P(),
        P(),
        P(("wide", "narrow")),
        P(("wide", "narrow")),
    )
    return jax.shard_map(
        local,
        mesh=mesh,
        in_specs=placed,
        out_specs=P(None, None, ("wide", "narrow")),
        check_vma=False,
    )
```

```python
import functools

import jax
import jax.numpy as jnp
from jax import lax
from jax.experimental import pallas as pl
from jax.experimental.pallas import tpu as pltpu
from jax.sharding import PartitionSpec as P

WIN = 4
LANES = 128
SORT_COLUMNS = 256
INT_ROWS = 256
SEND_ROWS = 32
VMEM = 60 * 1024 * 1024


def from_behind(value, axis, steps):
    count = lax.axis_size(axis)
    pairs = [(source, (source + steps) % count) for source in range(count)]
    return lax.ppermute(value, axis, pairs)


def log2(value):
    bits = value.bit_length() - 1
    assert 1 << bits == value
    return bits


def sort_kernel(sizes, me_ref, phys_ref, rate_ref, count_ref, tracers_ref, rows_ref, table_ref,
                pos_ref, turn_ref, wide_ref, sorted_ref, out_ref, at_ref, total_ref, sem_ref,
                out_sem):
    species, levels, columns, tiles, wide_count, narrow_count, pair_total = sizes
    step = pl.program_id(0)
    lanes = tiles * LANES
    real = species * levels

    @pl.when(step == 0)
    def _():
        phys = phys_ref[...]
        target = lax.shift_right_logical(phys, log2(columns))
        slot = phys & (columns - 1)
        wide_step = (lax.shift_right_logical(target, log2(narrow_count)) - me_ref[0] + 1) & (
            wide_count - 1
        )
        narrow_step = ((target & (narrow_count - 1)) - me_ref[1]) & (narrow_count - 1)
        pair = narrow_step * WIN + wide_step
        member = pair == lax.broadcasted_iota(jnp.int32, (pair_total, columns), 0)
        counts = jnp.sum(jnp.where(member, 1.0, 0.0), axis=1, keepdims=True)
        slot_f = slot.astype(jnp.float32)
        starts = jnp.min(jnp.where(member, slot_f, float(columns)), axis=1, keepdims=True)
        groups = lax.shift_right_logical(counts.astype(jnp.int32) + 7, 3).astype(jnp.float32)
        lane = lax.broadcasted_iota(jnp.int32, (pair_total, LANES), 1)
        row = lax.broadcasted_iota(jnp.int32, (pair_total, LANES), 0)

        def across(value):
            return jnp.sum(jnp.where(lane == row, value, 0.0), axis=0, keepdims=True)

        groups_t = across(groups)
        base = jnp.sum(jnp.where(lane < row, groups_t, 0.0), axis=1, keepdims=True)
        section = row & -WIN
        inner = base - jnp.sum(jnp.where(lane < section, groups_t, 0.0), axis=1, keepdims=True)
        same = (lane & -WIN) == section
        in_step = jnp.sum(jnp.where(same, groups_t, 0.0), axis=1, keepdims=True)
        per = SEND_ROWS // 8
        sections = lax.shift_right_logical(in_step.astype(jnp.int32) + per - 1, log2(per))
        pos = slot_f + jnp.sum(jnp.where(member, base * 8.0 - starts, 0.0), axis=0, keepdims=True)
        pos_ref[...] = pos.astype(jnp.int32)
        copy = pltpu.make_async_copy(pos_ref, at_ref, sem_ref)
        copy.start()
        total_ref[0] = jnp.max(base + groups).astype(jnp.int32)
        for at, value in enumerate((counts, base, inner, sections.astype(jnp.float32))):
            table_ref[at:at + 1, :] = across(value).astype(jnp.int32)
        copy.wait()

    block = tracers_ref.shape[2]
    begin = step * block
    in_group = lax.broadcasted_iota(jnp.int32, (8, LANES), 0)
    for half in range(block // LANES):
        span = slice(half * LANES, (half + 1) * LANES)
        at = pl.ds(pl.multiple_of(begin + half * LANES, LANES), LANES)
        turn_ref[lanes - 16:lanes, :] = jnp.zeros((16, LANES), jnp.float32)
        turn_ref[0:real, :] = tracers_ref[:, :, span].reshape(real, LANES)
        extra = jnp.where(in_group == 5, (phys_ref[:, at] & (columns - 1)).astype(jnp.float32), 0.0)
        extra = jnp.where(in_group == 6, rate_ref[:, at], extra)
        extra = jnp.where(in_group == 7, count_ref[:, at].astype(jnp.float32), extra)
        turn_ref[lanes - 8:lanes, :] = extra
        for tile in range(tiles):
            wide_ref[pl.ds(tile, LANES, stride=8), :] = turn_ref[
                tile * LANES:(tile + 1) * LANES, :
            ].T

        def move(part, carry):
            for extra_row in range(16):
                column = part * 16 + extra_row
                to = pl.multiple_of(at_ref[0, begin + half * LANES + column] * 8, 8)
                sorted_ref[pl.ds(to, 8), :] = wide_ref[pl.ds(pl.multiple_of(column * 8, 8), 8), :]
            return carry

        lax.fori_loop(0, LANES // 16, move, 0)

    @pl.when(step == pl.num_programs(0) - 1)
    def _():
        chunk = 32
        chunks = out_ref.shape[0] // chunk
        for part in range(chunks):
            @pl.when(part * chunk < total_ref[0])
            def _():
                def gather(group, carry):
                    for tile in range(tiles):
                        out_ref[group, tile] = sorted_ref[pl.ds(group * 64 + tile, 8, stride=8), :]
                    return carry

                lax.fori_loop(part * chunk, (part + 1) * chunk, gather, 0)
                here = pl.ds(part * chunk, chunk)
                pltpu.make_async_copy(out_ref.at[here], rows_ref.at[here], out_sem.at[part]).start()
        for part in range(chunks):
            @pl.when(part * chunk < total_ref[0])
            def _():
                here = pl.ds(part * chunk, chunk)
                pltpu.make_async_copy(out_ref.at[here], rows_ref.at[here], out_sem.at[part]).wait()


def integrate_kernel(sizes, total_ref, rows_ref, loss_ref, coupling_ref, out_ref,
                     turn_ref, y_ref, inverse_ref):
    levels, pad, tiles = sizes
    per = LANES // 8
    halves = INT_ROWS // LANES
    lanes = tiles * LANES

    @pl.when(pl.program_id(0) * INT_ROWS < total_ref[0])
    def _():
        for half in range(halves):
            for tile in range(tiles):
                block = rows_ref[half * per:(half + 1) * per, tile].reshape(LANES, LANES)
                turn_ref[half, tile * LANES:(tile + 1) * LANES, :] = block.T
            for level in range(levels):
                y_ref[level * pad:(level + 1) * pad, half * LANES:(half + 1) * LANES] = turn_ref[
                    half, pl.ds(level, pad, stride=levels), :
                ]
        rate = jnp.concatenate(
            [turn_ref[half, lanes - 2:lanes - 1, :] for half in range(halves)], axis=1
        )
        count = jnp.concatenate(
            [turn_ref[half, lanes - 1:lanes, :] for half in range(halves)], axis=1
        )
        step_len = rate / jnp.maximum(count, 1.0)
        inverse_ref[...] = 1.0 / (1.0 + step_len * loss_ref[...])
        last = jnp.max(count).astype(jnp.int32)

        def advance(k, carry):
            active = k.astype(jnp.float32) < count
            for level in range(levels):
                span = slice(level * pad, (level + 1) * pad)
                y = y_ref[span, :]
                squashed = jnp.tanh(y).astype(jnp.bfloat16)
                produced = jnp.dot(
                    coupling_ref[...], squashed, preferred_element_type=jnp.float32
                )
                y_ref[span, :] = jnp.where(
                    active, (y + step_len * produced) * inverse_ref[...], y
                )
            return carry

        lax.fori_loop(0, last, advance, 0)
        for half in range(halves):
            for level in range(levels):
                turn_ref[half, pl.ds(level, pad, stride=levels), :] = y_ref[
                    level * pad:(level + 1) * pad, half * LANES:(half + 1) * LANES
                ]
            for tile in range(tiles):
                block = turn_ref[half, tile * LANES:(tile + 1) * LANES, :]
                out_ref[half * per:(half + 1) * per, tile] = block.T.reshape(per, 8, LANES)


def finish_kernel(sizes, sources, table_ref, *refs):
    species, levels, columns, tiles, room = sizes
    groups = room // 8
    buffers = refs[:-6]
    out_ref, piece_ref, placed_ref, whole_ref, sem_ref, out_sem = refs[-6:]
    copies = []
    for pair, (source, row) in enumerate(sources):
        begin = 0 if row is None else table_ref[row, pair]
        copy = pltpu.make_async_copy(
            buffers[source].at[pl.ds(begin, groups)], piece_ref.at[pair], sem_ref.at[pair]
        )
        copy.start()
        copies.append(copy)
    lane = lax.broadcasted_iota(jnp.int32, (1, LANES), 1)
    in_group = lax.broadcasted_iota(jnp.int32, (8, LANES), 0)
    for pair in range(len(sources)):
        copies[pair].wait()
        count = table_ref[0, pair]
        first = piece_ref[pair, 0, tiles - 1][0:1, :]
        start = jnp.max(jnp.where(lane == LANES - 3, first, 0.0)).astype(jnp.int32)
        start = jnp.clip(start, 0, columns - 1)
        full = lax.shift_right_logical(count, 3)

        def move(group, carry):
            for tile in range(tiles):
                placed_ref[tile, pl.ds(start + group * 8, 8), :] = piece_ref[pair, group, tile]
            return carry

        lax.fori_loop(0, full, move, 0)

        @pl.when((count & 7) > 0)
        def _():
            for tile in range(tiles):
                at = pl.ds(start + full * 8, 8)
                placed_ref[tile, at, :] = jnp.where(
                    in_group < (count & 7), piece_ref[pair, full, tile], placed_ref[tile, at, :]
                )

    per_tile = LANES // levels
    for part in range(columns // LANES):
        at = slice(part * LANES, (part + 1) * LANES)
        for tile in range(tiles):
            block = placed_ref[tile, at, :].T.reshape(per_tile, levels, LANES)
            keep = min(per_tile, species - tile * per_tile)
            whole_ref[tile * per_tile:tile * per_tile + keep, :, at] = block[:keep]
        pltpu.make_async_copy(whole_ref.at[:, :, at], out_ref.at[:, :, at], out_sem.at[part]).start()
    for part in range(columns // LANES):
        at = slice(part * LANES, (part + 1) * LANES)
        pltpu.make_async_copy(whole_ref.at[:, :, at], out_ref.at[:, :, at], out_sem.at[part]).wait()


def tree(index, leaves, *operands):
    def build(low, high):
        if high - low == 1:
            return leaves[low]
        middle = (low + high) // 2
        return lambda at, *rest: lax.cond(
            at < middle, build(low, middle), build(middle, high), at, *rest
        )

    return build(0, len(leaves))(index, *operands)


def local(tracers, column_rate, loss_rate, coupling, phys_index, iter_count):
    levels, species, columns = tracers.shape
    wide_count = lax.axis_size("wide")
    narrow_count = lax.axis_size("narrow")
    pair_total = WIN * narrow_count
    room = 2 * columns // pair_total
    piece = room // 8
    pad = -(-species // 8) * 8
    while levels * pad % LANES or levels * (pad - species) < 8:
        pad += 8
    tiles = levels * pad // LANES
    most = columns + 7 * pair_total + room + SEND_ROWS
    rows_room = -(-most // INT_ROWS) * INT_ROWS
    full = pl.BlockSpec(memory_space=pltpu.VMEM)
    smem = pl.BlockSpec(memory_space=pltpu.SMEM)
    hbm = pl.BlockSpec(memory_space=pl.ANY)
    row_shape = (tiles, 8, LANES)
    rows_type = jax.ShapeDtypeStruct((rows_room // 8,) + row_shape, jnp.float32)

    me = jnp.stack([lax.axis_index("wide"), lax.axis_index("narrow")]).astype(jnp.int32)
    rows, table = pl.pallas_call(
        functools.partial(
            sort_kernel,
            (species, levels, columns, tiles, wide_count, narrow_count, pair_total),
        ),
        grid=(columns // SORT_COLUMNS,),
        in_specs=[smem, full, full, full,
                  pl.BlockSpec((species, levels, SORT_COLUMNS), lambda at: (0, 0, at))],
        out_specs=[hbm, full],
        out_shape=[rows_type, jax.ShapeDtypeStruct((8, LANES), jnp.int32)],
        scratch_shapes=[
            pltpu.VMEM((1, columns), jnp.int32),
            pltpu.VMEM((tiles * LANES, LANES), jnp.float32),
            pltpu.VMEM((LANES * 8, LANES), jnp.float32),
            pltpu.VMEM((rows_room * 8, LANES), jnp.float32),
            pltpu.VMEM((rows_room // 8,) + row_shape, jnp.float32),
            pltpu.SMEM((1, columns), jnp.int32),
            pltpu.SMEM((1,), jnp.int32),
            pltpu.SemaphoreType.DMA(()),
            pltpu.SemaphoreType.DMA((rows_room // INT_ROWS,)),
        ],
        compiler_params=pltpu.CompilerParams(vmem_limit_bytes=VMEM),
        name="sort_columns",
    )(
        me,
        phys_index.reshape(1, columns),
        column_rate.reshape(1, columns),
        iter_count.reshape(1, columns),
        tracers.transpose(1, 0, 2),
    )
    last = narrow_count - 1

    def base(step, at=0):
        return table[1, step * WIN + at]

    def inner(step, at):
        return table[2, step * WIN + at]

    loss_pad = jnp.pad(loss_rate, (0, pad - species)).reshape(pad, 1)
    coupling_pad = jnp.pad(coupling, ((0, pad - species), (0, pad - species)))
    total = (base(last, WIN - 1) * 8 + table[0, pair_total - 1]).reshape(1)
    row_block = pl.BlockSpec((INT_ROWS // 8,) + row_shape, lambda at: (at, 0, 0, 0))
    rows = pl.pallas_call(
        functools.partial(integrate_kernel, (levels, pad, tiles)),
        grid=(rows_room // INT_ROWS,),
        in_specs=[smem, row_block, full, full],
        out_specs=row_block,
        out_shape=rows_type,
        scratch_shapes=[
            pltpu.VMEM((INT_ROWS // LANES, tiles * LANES, LANES), jnp.float32),
            pltpu.VMEM((levels * pad, INT_ROWS), jnp.float32),
            pltpu.VMEM((pad, INT_ROWS), jnp.float32),
        ],
        compiler_params=pltpu.CompilerParams(vmem_limit_bytes=VMEM),
        name="integrate_columns",
    )(total, rows, loss_pad, coupling_pad)

    arrival_room = (WIN + 1) * piece
    send_groups = SEND_ROWS // 8
    most_sections = WIN * room // SEND_ROWS

    def sections_by(step, source, begin, wide_moves):
        operands = [source, begin] + [value for move in wide_moves for value in move[:2]]

        def branch(count, index, source, begin, *moves):
            got = []
            for at, move in enumerate(wide_moves):
                part = lax.dynamic_slice_in_dim(moves[2 * at], moves[2 * at + 1], piece, 0)
                got.append(from_behind(part, "wide", move[2]))
            if count == 0:
                arrived = jnp.zeros((arrival_room,) + row_shape, jnp.float32)
            else:
                part = lax.dynamic_slice_in_dim(source, begin, count * send_groups, 0)
                arrived = from_behind(part, "narrow", step)
                spare = arrival_room - count * send_groups
                arrived = jnp.pad(arrived, ((0, spare), (0, 0), (0, 0), (0, 0)))
            return arrived, got

        leaves = [functools.partial(branch, count) for count in range(most_sections + 1)]
        return tree(table[3, step * WIN], leaves, *operands)

    moving = [at for at in range(WIN) if at != 1]
    order = [narrow_count // 2]
    order += [step for step in range(1, last) if step not in order]
    held = {(1, 0): (rows, 1)}
    zero = jnp.zeros((), jnp.int32)

    wide_moves = [(rows, base(0, at), at - 1) for at in moving]
    wide_moves += [(rows, base(last, at), at - 1) for at in moving]
    previous = None
    for step in order:
        if previous is not None:
            wide_moves = [(arrived, inner(previous, at), at - 1) for at in moving]
        arrived, got = sections_by(step, rows, base(step), wide_moves)
        held[1, step] = (arrived, 2)
        if previous is None:
            for index, at in enumerate(moving):
                held[at, 0] = (got[index], None)
            early = dict(zip(moving, got[len(moving):]))
            early[1] = lax.dynamic_slice_in_dim(rows, base(last, 1), piece, 0)
            merged = jnp.zeros((arrival_room,) + row_shape, jnp.float32)
            for at in range(WIN):
                merged = lax.dynamic_update_slice_in_dim(merged, early[at], inner(last, at), 0)
        else:
            for index, at in enumerate(moving):
                held[at, previous] = (got[index], None)
        previous = step
    wide_moves = [(arrived, inner(previous, at), at - 1) for at in moving]
    arrived, got = sections_by(last, merged, zero, wide_moves)
    for index, at in enumerate(moving):
        held[at, previous] = (got[index], None)
    for at in range(WIN):
        held[at, last] = (arrived, 2)

    buffers, sources = [], []
    for step in range(narrow_count):
        for at in range(WIN):
            value, row = held[at, step]
            known = [index for index, other in enumerate(buffers) if other is value]
            if not known:
                buffers.append(value)
                known = [len(buffers) - 1]
            sources.append((known[0], row))
    updated = pl.pallas_call(
        functools.partial(finish_kernel, (species, levels, columns, tiles, room), tuple(sources)),
        in_specs=[smem] + [hbm] * len(buffers),
        out_specs=hbm,
        out_shape=jax.ShapeDtypeStruct((species, levels, columns), jnp.float32),
        scratch_shapes=[
            pltpu.VMEM((pair_total, piece) + row_shape, jnp.float32),
            pltpu.VMEM((tiles, columns + 8, LANES), jnp.float32),
            pltpu.VMEM((species, levels, columns), jnp.float32),
            pltpu.SemaphoreType.DMA((pair_total,)),
            pltpu.SemaphoreType.DMA((columns // LANES,)),
        ],
        compiler_params=pltpu.CompilerParams(vmem_limit_bytes=VMEM),
        name="place_columns",
    )(table, *buffers)
    return updated.transpose(1, 0, 2)


def solution(mesh):
    placed = (
        P(None, None, ("wide", "narrow")),
        P(("wide", "narrow")),
        P(),
        P(),
        P(("wide", "narrow")),
        P(("wide", "narrow")),
    )
    return jax.shard_map(
        local,
        mesh=mesh,
        in_specs=placed,
        out_specs=P(None, None, ("wide", "narrow")),
        check_vma=False,
    )
```

```python
import functools

import jax
import jax.numpy as jnp
from jax import lax
from jax.experimental import pallas as pl
from jax.experimental.pallas import tpu as pltpu
from jax.sharding import PartitionSpec as P

WIN = 4
MAXIT = 12
LANES = 128
SORT_COLUMNS = 256
INT_ROWS = 256
UNIT = 4
VMEM = 60 * 1024 * 1024


def from_behind(value, axis, steps):
    count = lax.axis_size(axis)
    pairs = [(source, (source + steps) % count) for source in range(count)]
    return lax.ppermute(value, axis, pairs)


def log2(value):
    bits = value.bit_length() - 1
    assert 1 << bits == value
    return bits


def sort_kernel(sizes, me_ref, phys_ref, rate_ref, count_ref, tracers_ref, rows_ref, table_ref,
                *rest):
    species, levels, columns, tiles, wide_count, narrow_count, pair_total = sizes[:7]
    cuts = sizes[7]
    cut_refs, scratch = rest[:len(cuts)], rest[len(cuts):]
    (pos_ref, turn_ref, wide_ref, sorted_ref, out_ref, at_ref, table_smem, sem_ref,
     out_sem) = scratch
    step = pl.program_id(0)
    lanes = tiles * LANES
    real = species * levels

    @pl.when(step == 0)
    def _():
        phys = phys_ref[...]
        target = lax.shift_right_logical(phys, log2(columns))
        slot = phys & (columns - 1)
        wide_step = (lax.shift_right_logical(target, log2(narrow_count)) - me_ref[0] + 1) & (
            wide_count - 1
        )
        narrow_step = ((target & (narrow_count - 1)) - me_ref[1]) & (narrow_count - 1)
        pair = narrow_step * WIN + wide_step
        member = pair == lax.broadcasted_iota(jnp.int32, (pair_total, columns), 0)
        counts = jnp.sum(jnp.where(member, 1.0, 0.0), axis=1, keepdims=True)
        slot_f = slot.astype(jnp.float32)
        starts = jnp.min(jnp.where(member, slot_f, float(columns)), axis=1, keepdims=True)
        groups = lax.shift_right_logical(counts.astype(jnp.int32) + 7, 3).astype(jnp.float32)
        lane = lax.broadcasted_iota(jnp.int32, (pair_total, LANES), 1)
        row = lax.broadcasted_iota(jnp.int32, (pair_total, LANES), 0)

        def across(value):
            return jnp.sum(jnp.where(lane == row, value, 0.0), axis=0, keepdims=True)

        groups_t = across(groups)
        base = jnp.sum(jnp.where(lane < row, groups_t, 0.0), axis=1, keepdims=True)
        section = row & -WIN
        inner = base - jnp.sum(jnp.where(lane < section, groups_t, 0.0), axis=1, keepdims=True)
        same = (lane & -WIN) == section
        in_step = jnp.sum(jnp.where(same, groups_t, 0.0), axis=1, keepdims=True)
        pos = slot_f + jnp.sum(jnp.where(member, base * 8.0 - starts, 0.0), axis=0, keepdims=True)
        pos_ref[...] = pos.astype(jnp.int32)
        copy = pltpu.make_async_copy(pos_ref, at_ref, sem_ref)
        copy.start()
        table_ref[...] = jnp.zeros_like(table_ref)
        for at, value in enumerate((counts, base, inner, in_step)):
            table_ref[at:at + 1, :] = across(value).astype(jnp.int32)
        copy.wait()
        copy = pltpu.make_async_copy(table_ref, table_smem, sem_ref)
        copy.start()
        copy.wait()

    block = tracers_ref.shape[2]
    begin = step * block
    in_group = lax.broadcasted_iota(jnp.int32, (8, LANES), 0)
    for half in range(block // LANES):
        span = slice(half * LANES, (half + 1) * LANES)
        at = pl.ds(pl.multiple_of(begin + half * LANES, LANES), LANES)
        turn_ref[lanes - 16:lanes, :] = jnp.zeros((16, LANES), jnp.float32)
        turn_ref[0:real, :] = tracers_ref[:, :, span].reshape(real, LANES)
        extra = jnp.where(in_group == 5, (phys_ref[:, at] & (columns - 1)).astype(jnp.float32), 0.0)
        extra = jnp.where(in_group == 6, rate_ref[:, at], extra)
        extra = jnp.where(in_group == 7, count_ref[:, at].astype(jnp.float32), extra)
        turn_ref[lanes - 8:lanes, :] = extra
        for tile in range(tiles):
            wide_ref[pl.ds(tile, LANES, stride=8), :] = turn_ref[
                tile * LANES:(tile + 1) * LANES, :
            ].T

        def move(part, carry):
            for extra_row in range(16):
                column = part * 16 + extra_row
                to = pl.multiple_of(at_ref[0, begin + half * LANES + column] * 8, 8)
                sorted_ref[pl.ds(to, 8), :] = wide_ref[pl.ds(pl.multiple_of(column * 8, 8), 8), :]
            return carry

        lax.fori_loop(0, LANES // 16, move, 0)

    @pl.when(step == pl.num_programs(0) - 1)
    def _():
        chunk = 32
        chunks = out_ref.shape[0] // chunk
        total = table_smem[1, pair_total - 1] + table_smem[0, pair_total - 1]
        for part in range(chunks):
            @pl.when(part * chunk < total)
            def _():
                def gather(group, carry):
                    for tile in range(tiles):
                        out_ref[group, tile] = sorted_ref[pl.ds(group * 64 + tile, 8, stride=8), :]
                    return carry

                lax.fori_loop(part * chunk, (part + 1) * chunk, gather, 0)

        copies = [pltpu.make_async_copy(out_ref, rows_ref.at[pl.ds(0, out_ref.shape[0])],
                                        out_sem.at[len(cuts)])]
        for index, (begin, size) in enumerate(cuts):
            begin = jnp.minimum(begin(table_smem), out_ref.shape[0] - size)
            copies.append(pltpu.make_async_copy(
                out_ref.at[pl.ds(begin, size)], cut_refs[index], out_sem.at[index]
            ))
        for copy in copies:
            copy.start()
        for copy in copies:
            copy.wait()


def chunk_sizes(static):
    units = static // UNIT
    return [UNIT] + [UNIT << bit for bit in reversed(range(log2(units)))]


def units_over(in_step, static):
    return lax.shift_right_logical(jnp.maximum(in_step - static, 0) + UNIT - 1, log2(UNIT))


def chunk_places(in_step, static):
    units = units_over(in_step, static)
    rest = jnp.maximum(units - 1, 0)
    places = [(units > 0, jnp.int32(static))]
    begin = static + UNIT
    for size in chunk_sizes(static)[1:]:
        digit = lax.shift_right_logical(rest, log2(size // UNIT)) & 1
        places.append((digit > 0, begin))
        begin = begin + digit * size
    return places


def start_arrival(refs, sems, room_ref, in_step, static, first):
    copy = pltpu.make_async_copy(refs[0], room_ref.at[pl.ds(first, static)], sems(0))
    copy.start()
    waits = [(None, copy)]
    places = chunk_places(in_step, static)
    for index, (wanted, begin) in enumerate(places):
        size = chunk_sizes(static)[index]
        copy = pltpu.make_async_copy(
            refs[1 + index], room_ref.at[pl.ds(first + begin, size)], sems(1 + index)
        )
        pl.when(wanted)(copy.start)
        waits.append((wanted, copy))
    return waits


def wait_all(waits):
    for wanted, copy in waits:
        if wanted is None:
            copy.wait()
        else:
            pl.when(wanted)(copy.wait)


def integrate_block(sizes, room_ref, first, valid, loss_ref, coupling_ref,
                    turn_ref, y_ref, inverse_ref):
    levels, pad, tiles = sizes
    per = LANES // 8
    halves = INT_ROWS // LANES
    lanes = tiles * LANES
    for half in range(halves):
        begin = first + half * per
        for tile in range(tiles):
            block = room_ref[pl.ds(begin, per), tile].reshape(LANES, LANES)
            turn_ref[half, tile * LANES:(tile + 1) * LANES, :] = block.T
        for level in range(levels):
            y_ref[level, :, half * LANES:(half + 1) * LANES] = turn_ref[
                half, pl.ds(level, pad, stride=levels), :
            ]
    rate = jnp.concatenate(
        [turn_ref[half, lanes - 2:lanes - 1, :] for half in range(halves)], axis=1
    )
    count = jnp.concatenate(
        [turn_ref[half, lanes - 1:lanes, :] for half in range(halves)], axis=1
    )
    lane = lax.broadcasted_iota(jnp.int32, (1, INT_ROWS), 1)
    count = jnp.where((lane < valid) & (count <= MAXIT), count, 0.0)
    step_len = rate / jnp.maximum(count, 1.0)
    inverse_ref[...] = 1.0 / (1.0 + step_len * loss_ref[...])
    last = jnp.max(count).astype(jnp.int32)

    def advance(k, carry):
        active = k.astype(jnp.float32) < count

        def one_level(level, inner):
            y = y_ref[level]
            squashed = jnp.tanh(y).astype(jnp.bfloat16)
            produced = jnp.dot(coupling_ref[...], squashed, preferred_element_type=jnp.float32)
            y_ref[level] = jnp.where(active, (y + step_len * produced) * inverse_ref[...], y)
            return inner

        for level in range(levels):
            one_level(level, 0)
        return carry

    lax.fori_loop(0, last, advance, 0)
    for half in range(halves):
        begin = first + half * per
        for level in range(levels):
            turn_ref[half, pl.ds(level, pad, stride=levels), :] = y_ref[
                level, :, half * LANES:(half + 1) * LANES
            ]
        for tile in range(tiles):
            block = turn_ref[half, tile * LANES:(tile + 1) * LANES, :]
            room_ref[pl.ds(begin, per), tile] = block.T.reshape(per, 8, LANES)


def integrate_kernel(sizes, plan, table_ref, loss_ref, coupling_ref, *refs):
    loads, merges, blocks, stores, operands = plan
    sources = refs[:operands]
    results = refs[operands:operands + len(stores)]
    room_ref, turn_ref, y_ref, inverse_ref, rows_ref, sem_ref, out_sem = refs[
        operands + len(stores):
    ]
    copies = []
    for index, (source, begin, groups, to) in enumerate(loads):
        ref = sources[source]
        if begin is not None:
            ref = ref.at[pl.ds(begin(table_ref), groups)]
        copies.append(
            pltpu.make_async_copy(ref, room_ref.at[pl.ds(to, groups)], sem_ref.at[index])
        )
    for copy in copies:
        copy.start()
    for copy in copies:
        copy.wait()
    for begin, groups, to in merges:
        to = to(table_ref)

        def move(group, carry):
            room_ref[to + group] = room_ref[begin + group]
            return carry

        lax.fori_loop(0, groups(table_ref), move, 0)
    for index, (begin, rows) in enumerate(blocks):
        rows_ref[0, index] = jnp.int32(begin)
        rows_ref[1, index] = rows(table_ref)

    def one_block(index, carry):
        valid = rows_ref[1, index]

        @pl.when(valid > 0)
        def _():
            integrate_block(sizes, room_ref, rows_ref[0, index], valid, loss_ref, coupling_ref,
                            turn_ref, y_ref, inverse_ref)

        return carry

    lax.fori_loop(0, len(blocks), one_block, 0)
    copies = []
    for index, (begin, groups) in enumerate(stores):
        copies.append(pltpu.make_async_copy(
            room_ref.at[pl.ds(begin(table_ref), groups)], results[index], out_sem.at[index]
        ))
    for copy in copies:
        copy.start()
    for copy in copies:
        copy.wait()


def cut_kernel(static, step, table_ref, *refs):
    arrived = len(chunk_sizes(static)) + 1
    pieces = refs[arrived:arrived + WIN]
    room_ref, sem_ref, out_sem = refs[arrived + WIN:]
    wait_all(start_arrival(refs[:arrived], lambda at: sem_ref.at[at], room_ref,
                           table_ref[3, step * WIN], static, 0))
    copies = []
    for at in range(WIN):
        begin = table_ref[2, step * WIN + at]
        copies.append(pltpu.make_async_copy(
            room_ref.at[pl.ds(begin, pieces[at].shape[0])], pieces[at], out_sem.at[at]
        ))
    for copy in copies:
        copy.start()
    for copy in copies:
        copy.wait()


def finish_kernel(sizes, table_ref, *refs):
    species, levels, columns, tiles, static, narrow_count = sizes
    arrived = len(chunk_sizes(static)) + 1
    pair_total = narrow_count * WIN
    whole_pieces = pair_total - WIN
    out_ref, piece_ref, room_ref, placed_ref, whole_ref, sem_ref, out_sem = refs[-7:]
    copies = []
    for pair in range(whole_pieces):
        copies.append(pltpu.make_async_copy(refs[pair], piece_ref.at[pair], sem_ref.at[pair]))
        copies[-1].start()
    waits = start_arrival(refs[whole_pieces:whole_pieces + arrived],
                          lambda at: sem_ref.at[whole_pieces + at], room_ref,
                          table_ref[3, whole_pieces], static, 0)
    lane = lax.broadcasted_iota(jnp.int32, (1, LANES), 1)
    in_group = lax.broadcasted_iota(jnp.int32, (8, LANES), 0)
    for pair in range(pair_total):
        if pair < whole_pieces:
            copies[pair].wait()
            piece = piece_ref.at[pair]
            begin = 0
        else:
            if pair == whole_pieces:
                wait_all(waits)
            piece = room_ref
            begin = table_ref[2, pair]
        count = table_ref[0, pair]
        first = piece[begin, tiles - 1][0:1, :]
        start = jnp.max(jnp.where(lane == LANES - 3, first, 0.0)).astype(jnp.int32)
        start = jnp.clip(start, 0, columns - 1)
        full = lax.shift_right_logical(count, 3)

        def move(group, carry):
            for tile in range(tiles):
                placed_ref[tile, pl.ds(start + group * 8, 8), :] = piece[begin + group, tile]
            return carry

        lax.fori_loop(0, full, move, 0)

        @pl.when((count & 7) > 0)
        def _():
            for tile in range(tiles):
                at = pl.ds(start + full * 8, 8)
                placed_ref[tile, at, :] = jnp.where(
                    in_group < (count & 7), piece[begin + full, tile], placed_ref[tile, at, :]
                )

    per_tile = LANES // levels
    for part in range(columns // LANES):
        at = slice(part * LANES, (part + 1) * LANES)
        for tile in range(tiles):
            block = placed_ref[tile, at, :].T.reshape(per_tile, levels, LANES)
            keep = min(per_tile, species - tile * per_tile)
            whole_ref[tile * per_tile:tile * per_tile + keep, :, at] = block[:keep]
        pltpu.make_async_copy(whole_ref.at[:, :, at], out_ref.at[:, :, at], out_sem.at[part]).start()
    for part in range(columns // LANES):
        at = slice(part * LANES, (part + 1) * LANES)
        pltpu.make_async_copy(whole_ref.at[:, :, at], out_ref.at[:, :, at], out_sem.at[part]).wait()


def local(tracers, column_rate, loss_rate, coupling, phys_index, iter_count):
    levels, species, columns = tracers.shape
    wide_count = lax.axis_size("wide")
    narrow_count = lax.axis_size("narrow")
    pair_total = WIN * narrow_count
    room = 2 * columns // pair_total
    piece = room // 8
    pad = -(-species // 8) * 8
    while levels * pad % LANES or levels * (pad - species) < 8:
        pad += 8
    tiles = levels * pad // LANES
    static = columns // narrow_count // 8
    sizes = chunk_sizes(static)
    most = columns + 7 * pair_total + UNIT * 8
    sort_room = -(-max(most, columns + 7 * pair_total + room) // INT_ROWS) * INT_ROWS
    rows_room = sort_room // 8 + 2 * static
    full = pl.BlockSpec(memory_space=pltpu.VMEM)
    smem = pl.BlockSpec(memory_space=pltpu.SMEM)
    hbm = pl.BlockSpec(memory_space=pl.ANY)
    row_shape = (tiles, 8, LANES)
    last = narrow_count - 1
    moving = [at for at in range(WIN) if at != 1]
    order = [narrow_count // 2]
    order += [step for step in range(1, last) if step not in order] + [last]
    params = pltpu.CompilerParams(vmem_limit_bytes=VMEM)

    def rows_type(groups):
        return jax.ShapeDtypeStruct((groups,) + row_shape, jnp.float32)

    def entry(row, step, at=0):
        return lambda table: table[row, step * WIN + at]

    def group_cuts(begin, in_step):
        cuts = [(begin, static)]
        for index, size in enumerate(sizes):
            cuts.append((
                lambda table, index=index: begin(table)
                + chunk_places(in_step(table), static)[index][1],
                size,
            ))
        return cuts

    cuts = group_cuts(entry(1, order[0]), entry(3, order[0]))
    cuts += [(entry(1, 0, at), piece) for at in moving]
    cuts += [(entry(1, last, at), piece) for at in moving]
    me = jnp.stack([lax.axis_index("wide"), lax.axis_index("narrow")]).astype(jnp.int32)
    rows, table, *first = pl.pallas_call(
        functools.partial(
            sort_kernel,
            (species, levels, columns, tiles, wide_count, narrow_count, pair_total, cuts),
        ),
        grid=(columns // SORT_COLUMNS,),
        in_specs=[smem, full, full, full,
                  pl.BlockSpec((species, levels, SORT_COLUMNS), lambda at: (0, 0, at))],
        out_specs=[hbm, full] + [hbm] * len(cuts),
        out_shape=[rows_type(rows_room), jax.ShapeDtypeStruct((8, LANES), jnp.int32)]
        + [rows_type(size) for _, size in cuts],
        scratch_shapes=[
            pltpu.VMEM((1, columns), jnp.int32),
            pltpu.VMEM((tiles * LANES, LANES), jnp.float32),
            pltpu.VMEM((LANES * 8, LANES), jnp.float32),
            pltpu.VMEM((sort_room * 8, LANES), jnp.float32),
            pltpu.VMEM((sort_room // 8,) + row_shape, jnp.float32),
            pltpu.SMEM((1, columns), jnp.int32),
            pltpu.SMEM((8, LANES), jnp.int32),
            pltpu.SemaphoreType.DMA(()),
            pltpu.SemaphoreType.DMA((len(cuts) + 1,)),
        ],
        compiler_params=params,
        name="sort_columns",
    )(
        me,
        phys_index.reshape(1, columns),
        column_rate.reshape(1, columns),
        iter_count.reshape(1, columns),
        tracers.transpose(1, 0, 2),
    )
    loss_pad = jnp.pad(loss_rate, (0, pad - species)).reshape(pad, 1)
    coupling_pad = jnp.pad(coupling, ((0, pad - species), (0, pad - species)))
    block = INT_ROWS // 8

    def integrate(operands, loads, merges, blocks, stores):
        groups = max([to + size for _, _, size, to in loads] + [begin + block for begin, _ in blocks])
        groups += static
        flops = 2 * levels * pad * pad * 6 * INT_ROWS * len(blocks)
        return pl.pallas_call(
            functools.partial(
                integrate_kernel, (levels, pad, tiles),
                (loads, merges, blocks, stores, len(operands)),
            ),
            in_specs=[smem, full, full] + [hbm] * len(operands),
            out_specs=[hbm] * len(stores),
            out_shape=[rows_type(size) for _, size in stores],
            scratch_shapes=[
                pltpu.VMEM((groups,) + row_shape, jnp.float32),
                pltpu.VMEM((INT_ROWS // LANES, tiles * LANES, LANES), jnp.float32),
                pltpu.VMEM((levels, pad, INT_ROWS), jnp.float32),
                pltpu.VMEM((pad, INT_ROWS), jnp.float32),
                pltpu.SMEM((2, LANES), jnp.int32),
                pltpu.SemaphoreType.DMA((len(loads),)),
                pltpu.SemaphoreType.DMA((len(stores),)),
            ],
            compiler_params=params,
            cost_estimate=pl.CostEstimate(
                flops=flops, bytes_accessed=8 * groups * 8 * tiles * LANES,
                transcendentals=flops // (2 * pad),
            ),
            name="integrate_columns",
        )(table, loss_pad, coupling_pad, *operands)

    def rows_of(step, at=0):
        return entry(0, step, at)

    def group_blocks(begin, step):
        return [
            (begin + part * block,
             lambda table, part=part: table[3, step * WIN] * 8 - part * INT_ROWS)
            for part in range(2 * static // block)
        ]

    def here(begin):
        return lambda table: jnp.int32(begin)

    def step_over(step, parts):
        def leaf(units, *parts):
            taken = [units > 0]
            taken += [(units - 1) // (size // UNIT) % 2 == 1 and units > 0 for size in sizes[1:]]
            return [
                from_behind(part, "narrow", step) if sent else jnp.zeros_like(part)
                for part, sent in zip(parts, taken)
            ]

        leaves = [functools.partial(leaf, units) for units in range(static // UNIT + 1)]
        return lax.switch(units_over(table[3, step * WIN], static), leaves, *parts)

    pieces = {}
    outgoing = first[:len(sizes) + 1]
    wide_now = list(first[len(sizes) + 1:])
    keys_now = [(at, 0) for at in moving] + [(at, last) for at in moving]
    for phase, step in enumerate(order):
        static_part = from_behind(outgoing[0], "narrow", step)
        wide_got = [
            from_behind(value, "wide", key[0] - 1) for value, key in zip(wide_now, keys_now)
        ]
        operands, loads, merges, blocks, stores, named = [], [], [], [], [], []
        used = 0
        if phase + 1 < len(order):
            coming = order[phase + 1]
            if coming == last:
                operands += [pieces[at, last] for at in moving] + [rows]
                for index, at in enumerate(moving):
                    loads.append((index, None, piece, 2 * static + at * piece))
                loads.append((len(moving), entry(1, last, 1), piece, 2 * static + piece))
                for at in range(WIN):
                    merges.append((2 * static + at * piece, lambda table, at=at: (
                        lax.shift_right_logical(table[0, last * WIN + at] + 7, 3)
                    ), entry(2, last, at)))
                used = 2 * static + WIN * piece
            else:
                operands.append(rows)
                loads.append((0, entry(1, coming), 2 * static, 0))
                used = 2 * static
            blocks += group_blocks(0, coming)
            stores += group_cuts(here(0), entry(3, coming))
        extra = []
        if phase == 0:
            extra.append(((1, 0), None))
        if phase == 1:
            extra += [((at, 0), pieces[at, 0]) for at in moving]
        if phase == 2:
            extra += [((at, order[0]), pieces[at, order[0]]) for at in range(WIN)]
        used = -(-used // block) * block
        for key, value in extra:
            if value is None:
                loads.append((operands.index(rows), entry(1, key[1], key[0]), piece, used))
            else:
                operands.append(value)
                loads.append((len(operands) - 1, None, piece, used))
            blocks.append((used, rows_of(key[1], key[0])))
            stores.append((here(used), piece))
            named.append(key)
            used += block
        if stores:
            results = integrate(operands, loads, merges, blocks, stores)
            done = dict(zip(named, results[len(results) - len(named):]))
        over = step_over(step, outgoing[1:])
        pieces.update(zip(keys_now, wide_got))
        if stores:
            pieces.update(done)
            outgoing = results[:len(results) - len(named)]
        arrived = [static_part] + list(over)
        if step != last:
            cut = pl.pallas_call(
                functools.partial(cut_kernel, static, step),
                in_specs=[smem] + [hbm] * len(arrived),
                out_specs=[hbm] * WIN,
                out_shape=[rows_type(piece)] * WIN,
                scratch_shapes=[
                    pltpu.VMEM((3 * static,) + row_shape, jnp.float32),
                    pltpu.SemaphoreType.DMA((len(arrived),)),
                    pltpu.SemaphoreType.DMA((WIN,)),
                ],
                compiler_params=params,
                name="cut_pieces",
            )(table, *arrived)
            pieces[1, step] = cut[1]
            wide_now = [cut[at] for at in moving]
            keys_now = [(at, step) for at in moving]

    buffers = [pieces[at, step] for step in range(last) for at in range(WIN)] + arrived
    updated = pl.pallas_call(
        functools.partial(
            finish_kernel, (species, levels, columns, tiles, static, narrow_count)
        ),
        in_specs=[smem] + [hbm] * len(buffers),
        out_specs=hbm,
        out_shape=jax.ShapeDtypeStruct((species, levels, columns), jnp.float32),
        scratch_shapes=[
            pltpu.VMEM((pair_total - WIN, piece) + row_shape, jnp.float32),
            pltpu.VMEM((3 * static,) + row_shape, jnp.float32),
            pltpu.VMEM((tiles, columns + 8, LANES), jnp.float32),
            pltpu.VMEM((species, levels, columns), jnp.float32),
            pltpu.SemaphoreType.DMA((len(buffers),)),
            pltpu.SemaphoreType.DMA((columns // LANES,)),
        ],
        compiler_params=params,
        name="place_columns",
    )(table, *buffers)
    return updated.transpose(1, 0, 2)


def solution(mesh):
    placed = (
        P(None, None, ("wide", "narrow")),
        P(("wide", "narrow")),
        P(),
        P(),
        P(("wide", "narrow")),
        P(("wide", "narrow")),
    )
    return jax.shard_map(
        local,
        mesh=mesh,
        in_specs=placed,
        out_specs=P(None, None, ("wide", "narrow")),
        check_vma=False,
    )
```

```python
import functools

import jax
import jax.numpy as jnp
from jax import lax
from jax.experimental import pallas as pl
from jax.experimental.pallas import tpu as pltpu
from jax.sharding import PartitionSpec as P

WIN = 4
MAXIT = 12
LANES = 128
SORT_COLUMNS = 256
INT_ROWS = 256
UNIT = 4
VMEM = 60 * 1024 * 1024


def from_behind(value, axis, steps):
    count = lax.axis_size(axis)
    pairs = [(source, (source + steps) % count) for source in range(count)]
    return lax.ppermute(value, axis, pairs)


def log2(value):
    bits = value.bit_length() - 1
    assert 1 << bits == value
    return bits


def sort_kernel(sizes, me_ref, phys_ref, rate_ref, count_ref, tracers_ref, rows_ref, table_ref,
                *rest):
    species, levels, columns, tiles, wide_count, narrow_count, pair_total = sizes[:7]
    cuts, targets = sizes[7:]
    cut_refs, scratch = rest[:targets], rest[targets:]
    (pos_ref, turn_ref, wide_ref, sorted_ref, out_ref, at_ref, table_smem, sem_ref,
     out_sem) = scratch
    step = pl.program_id(0)
    lanes = tiles * LANES
    real = species * levels

    @pl.when(step == 0)
    def _():
        phys = phys_ref[...]
        target = lax.shift_right_logical(phys, log2(columns))
        slot = phys & (columns - 1)
        wide_step = (lax.shift_right_logical(target, log2(narrow_count)) - me_ref[0] + 1) & (
            wide_count - 1
        )
        narrow_step = ((target & (narrow_count - 1)) - me_ref[1]) & (narrow_count - 1)
        pair = narrow_step * WIN + wide_step
        member = pair == lax.broadcasted_iota(jnp.int32, (pair_total, columns), 0)
        counts = jnp.sum(jnp.where(member, 1.0, 0.0), axis=1, keepdims=True)
        slot_f = slot.astype(jnp.float32)
        starts = jnp.min(jnp.where(member, slot_f, float(columns)), axis=1, keepdims=True)
        groups = lax.shift_right_logical(counts.astype(jnp.int32) + 7, 3).astype(jnp.float32)
        lane = lax.broadcasted_iota(jnp.int32, (pair_total, LANES), 1)
        row = lax.broadcasted_iota(jnp.int32, (pair_total, LANES), 0)

        def across(value):
            return jnp.sum(jnp.where(lane == row, value, 0.0), axis=0, keepdims=True)

        groups_t = across(groups)
        base = jnp.sum(jnp.where(lane < row, groups_t, 0.0), axis=1, keepdims=True)
        section = row & -WIN
        inner = base - jnp.sum(jnp.where(lane < section, groups_t, 0.0), axis=1, keepdims=True)
        same = (lane & -WIN) == section
        in_step = jnp.sum(jnp.where(same, groups_t, 0.0), axis=1, keepdims=True)
        pos = slot_f + jnp.sum(jnp.where(member, base * 8.0 - starts, 0.0), axis=0, keepdims=True)
        pos_ref[...] = pos.astype(jnp.int32)
        copy = pltpu.make_async_copy(pos_ref, at_ref, sem_ref)
        copy.start()
        table_ref[...] = jnp.zeros_like(table_ref)
        for at, value in enumerate((counts, base, inner, in_step)):
            table_ref[at:at + 1, :] = across(value).astype(jnp.int32)
        copy.wait()
        copy = pltpu.make_async_copy(table_ref, table_smem, sem_ref)
        copy.start()
        copy.wait()

    block = tracers_ref.shape[2]
    begin = step * block
    in_group = lax.broadcasted_iota(jnp.int32, (8, LANES), 0)
    for half in range(block // LANES):
        span = slice(half * LANES, (half + 1) * LANES)
        at = pl.ds(pl.multiple_of(begin + half * LANES, LANES), LANES)
        turn_ref[lanes - 16:lanes, :] = jnp.zeros((16, LANES), jnp.float32)
        turn_ref[0:real, :] = tracers_ref[:, :, span].reshape(real, LANES)
        extra = jnp.where(in_group == 5, (phys_ref[:, at] & (columns - 1)).astype(jnp.float32), 0.0)
        extra = jnp.where(in_group == 6, rate_ref[:, at], extra)
        extra = jnp.where(in_group == 7, count_ref[:, at].astype(jnp.float32), extra)
        turn_ref[lanes - 8:lanes, :] = extra
        for tile in range(tiles):
            wide_ref[pl.ds(tile, LANES, stride=8), :] = turn_ref[
                tile * LANES:(tile + 1) * LANES, :
            ].T

        def move(part, carry):
            for extra_row in range(16):
                column = part * 16 + extra_row
                to = pl.multiple_of(at_ref[0, begin + half * LANES + column] * 8, 8)
                sorted_ref[pl.ds(to, 8), :] = wide_ref[pl.ds(pl.multiple_of(column * 8, 8), 8), :]
            return carry

        lax.fori_loop(0, LANES // 16, move, 0)

    @pl.when(step == pl.num_programs(0) - 1)
    def _():
        chunk = 32
        chunks = out_ref.shape[0] // chunk
        total = table_smem[1, pair_total - 1] + table_smem[0, pair_total - 1]
        for part in range(chunks):
            @pl.when(part * chunk < total)
            def _():
                def gather(group, carry):
                    for tile in range(tiles):
                        out_ref[group, tile] = sorted_ref[pl.ds(group * 64 + tile, 8, stride=8), :]
                    return carry

                lax.fori_loop(part * chunk, (part + 1) * chunk, gather, 0)

        copies = [pltpu.make_async_copy(out_ref, rows_ref.at[pl.ds(0, out_ref.shape[0])],
                                        out_sem.at[len(cuts)])]
        for index, (target, to, begin, size) in enumerate(cuts):
            begin = jnp.minimum(begin(table_smem), out_ref.shape[0] - size)
            copies.append(pltpu.make_async_copy(
                out_ref.at[pl.ds(begin, size)], cut_refs[target].at[pl.ds(to, size)],
                out_sem.at[index],
            ))
        for copy in copies:
            copy.start()
        for copy in copies:
            copy.wait()


def chunk_sizes(static):
    units = static // UNIT
    return [UNIT] + [UNIT << bit for bit in reversed(range(log2(units)))]


def units_over(in_step, static):
    return lax.shift_right_logical(jnp.maximum(in_step - static, 0) + UNIT - 1, log2(UNIT))


def chunk_places(in_step, static):
    units = units_over(in_step, static)
    rest = jnp.maximum(units - 1, 0)
    places = [(units > 0, jnp.int32(static))]
    begin = static + UNIT
    for size in chunk_sizes(static)[1:]:
        digit = lax.shift_right_logical(rest, log2(size // UNIT)) & 1
        places.append((digit > 0, begin))
        begin = begin + digit * size
    return places


def start_arrival(refs, sems, room_ref, in_step, static, first):
    copy = pltpu.make_async_copy(refs[0], room_ref.at[pl.ds(first, static)], sems(0))
    copy.start()
    waits = [(None, copy)]
    places = chunk_places(in_step, static)
    for index, (wanted, begin) in enumerate(places):
        size = chunk_sizes(static)[index]
        copy = pltpu.make_async_copy(
            refs[1 + index], room_ref.at[pl.ds(first + begin, size)], sems(1 + index)
        )
        pl.when(wanted)(copy.start)
        waits.append((wanted, copy))
    return waits


def wait_all(waits):
    for wanted, copy in waits:
        if wanted is None:
            copy.wait()
        else:
            pl.when(wanted)(copy.wait)


def integrate_block(sizes, room_ref, first, valid, loss_ref, coupling_ref,
                    turn_ref, y_ref, inverse_ref):
    levels, pad, tiles = sizes
    per = LANES // 8
    halves = INT_ROWS // LANES
    lanes = tiles * LANES
    for half in range(halves):
        begin = first + half * per
        for tile in range(tiles):
            block = room_ref[pl.ds(begin, per), tile].reshape(LANES, LANES)
            turn_ref[half, tile * LANES:(tile + 1) * LANES, :] = block.T
        for level in range(levels):
            y_ref[level, :, half * LANES:(half + 1) * LANES] = turn_ref[
                half, pl.ds(level, pad, stride=levels), :
            ]
    rate = jnp.concatenate(
        [turn_ref[half, lanes - 2:lanes - 1, :] for half in range(halves)], axis=1
    )
    count = jnp.concatenate(
        [turn_ref[half, lanes - 1:lanes, :] for half in range(halves)], axis=1
    )
    lane = lax.broadcasted_iota(jnp.int32, (1, INT_ROWS), 1)
    count = jnp.where((lane < valid) & (count <= MAXIT), count, 0.0)
    step_len = rate / jnp.maximum(count, 1.0)
    inverse_ref[...] = 1.0 / (1.0 + step_len * loss_ref[...])
    last = jnp.max(count).astype(jnp.int32)

    def advance(k, carry):
        active = k.astype(jnp.float32) < count

        def one_level(level, inner):
            y = y_ref[level]
            squashed = jnp.tanh(y).astype(jnp.bfloat16)
            produced = jnp.dot(coupling_ref[...], squashed, preferred_element_type=jnp.float32)
            y_ref[level] = jnp.where(active, (y + step_len * produced) * inverse_ref[...], y)
            return inner

        for level in range(levels):
            one_level(level, 0)
        return carry

    lax.fori_loop(0, last, advance, 0)
    for half in range(halves):
        begin = first + half * per
        for level in range(levels):
            turn_ref[half, pl.ds(level, pad, stride=levels), :] = y_ref[
                level, :, half * LANES:(half + 1) * LANES
            ]
        for tile in range(tiles):
            block = turn_ref[half, tile * LANES:(tile + 1) * LANES, :]
            room_ref[pl.ds(begin, per), tile] = block.T.reshape(per, 8, LANES)


def integrate_kernel(sizes, plan, table_ref, loss_ref, coupling_ref, *refs):
    loads, merges, blocks, stores, operands = plan
    sources = refs[:operands]
    results = refs[operands:operands + len(stores)]
    room_ref, turn_ref, y_ref, inverse_ref, rows_ref, sem_ref, out_sem = refs[
        operands + len(stores):
    ]
    copies = []
    for index, (source, begin, groups, to) in enumerate(loads):
        ref = sources[source]
        if begin is not None:
            ref = ref.at[pl.ds(begin(table_ref), groups)]
        copies.append(
            pltpu.make_async_copy(ref, room_ref.at[pl.ds(to, groups)], sem_ref.at[index])
        )
    for copy in copies:
        copy.start()
    for copy in copies:
        copy.wait()
    for begin, groups, to in merges:
        to = to(table_ref)

        def move(group, carry):
            room_ref[to + group] = room_ref[begin + group]
            return carry

        lax.fori_loop(0, groups(table_ref), move, 0)
    for index, (begin, rows) in enumerate(blocks):
        rows_ref[0, index] = jnp.int32(begin)
        rows_ref[1, index] = rows(table_ref)

    def one_block(index, carry):
        valid = rows_ref[1, index]

        @pl.when(valid > 0)
        def _():
            integrate_block(sizes, room_ref, rows_ref[0, index], valid, loss_ref, coupling_ref,
                            turn_ref, y_ref, inverse_ref)

        return carry

    lax.fori_loop(0, len(blocks), one_block, 0)
    copies = []
    for index, (begin, groups) in enumerate(stores):
        copies.append(pltpu.make_async_copy(
            room_ref.at[pl.ds(begin(table_ref), groups)], results[index], out_sem.at[index]
        ))
    for copy in copies:
        copy.start()
    for copy in copies:
        copy.wait()


def cut_kernel(static, step, table_ref, *refs):
    arrived = len(chunk_sizes(static)) + 1
    pieces = refs[arrived:arrived + WIN]
    room_ref, sem_ref, out_sem = refs[arrived + WIN:]
    wait_all(start_arrival(refs[:arrived], lambda at: sem_ref.at[at], room_ref,
                           table_ref[3, step * WIN], static, 0))
    copies = []
    for at in range(WIN):
        begin = table_ref[2, step * WIN + at]
        copies.append(pltpu.make_async_copy(
            room_ref.at[pl.ds(begin, pieces[at].shape[0])], pieces[at], out_sem.at[at]
        ))
    for copy in copies:
        copy.start()
    for copy in copies:
        copy.wait()


def finish_kernel(sizes, table_ref, *refs):
    species, levels, columns, tiles, static, narrow_count, begins = sizes
    arrived = len(chunk_sizes(static)) + 1
    pair_total = narrow_count * WIN
    whole_pieces = pair_total - WIN
    out_ref, piece_ref, room_ref, placed_ref, whole_ref, sem_ref, out_sem = refs[-7:]
    copies = []
    for pair in range(whole_pieces):
        source = refs[pair].at[pl.ds(begins[pair], piece_ref.shape[1])]
        copies.append(pltpu.make_async_copy(source, piece_ref.at[pair], sem_ref.at[pair]))
        copies[-1].start()
    waits = start_arrival(refs[whole_pieces:whole_pieces + arrived],
                          lambda at: sem_ref.at[whole_pieces + at], room_ref,
                          table_ref[3, whole_pieces], static, 0)
    lane = lax.broadcasted_iota(jnp.int32, (1, LANES), 1)
    in_group = lax.broadcasted_iota(jnp.int32, (8, LANES), 0)
    for pair in range(pair_total):
        if pair < whole_pieces:
            copies[pair].wait()
            piece = piece_ref.at[pair]
            begin = 0
        else:
            if pair == whole_pieces:
                wait_all(waits)
            piece = room_ref
            begin = table_ref[2, pair]
        count = table_ref[0, pair]
        first = piece[begin, tiles - 1][0:1, :]
        start = jnp.max(jnp.where(lane == LANES - 3, first, 0.0)).astype(jnp.int32)
        start = jnp.clip(start, 0, columns - 1)
        full = lax.shift_right_logical(count, 3)

        def move(group, carry):
            for tile in range(tiles):
                placed_ref[tile, pl.ds(start + group * 8, 8), :] = piece[begin + group, tile]
            return carry

        lax.fori_loop(0, full, move, 0)

        @pl.when((count & 7) > 0)
        def _():
            for tile in range(tiles):
                at = pl.ds(start + full * 8, 8)
                placed_ref[tile, at, :] = jnp.where(
                    in_group < (count & 7), piece[begin + full, tile], placed_ref[tile, at, :]
                )

    per_tile = LANES // levels
    for part in range(columns // LANES):
        at = slice(part * LANES, (part + 1) * LANES)
        for tile in range(tiles):
            block = placed_ref[tile, at, :].T.reshape(per_tile, levels, LANES)
            keep = min(per_tile, species - tile * per_tile)
            whole_ref[tile * per_tile:tile * per_tile + keep, :, at] = block[:keep]
        pltpu.make_async_copy(whole_ref.at[:, :, at], out_ref.at[:, :, at], out_sem.at[part]).start()
    for part in range(columns // LANES):
        at = slice(part * LANES, (part + 1) * LANES)
        pltpu.make_async_copy(whole_ref.at[:, :, at], out_ref.at[:, :, at], out_sem.at[part]).wait()


def local(tracers, column_rate, loss_rate, coupling, phys_index, iter_count):
    levels, species, columns = tracers.shape
    wide_count = lax.axis_size("wide")
    narrow_count = lax.axis_size("narrow")
    pair_total = WIN * narrow_count
    room = 2 * columns // pair_total
    piece = room // 8
    pad = -(-species // 8) * 8
    while levels * pad % LANES or levels * (pad - species) < 8:
        pad += 8
    tiles = levels * pad // LANES
    static = columns // narrow_count // 8
    sizes = chunk_sizes(static)
    most = columns + 7 * pair_total + UNIT * 8
    sort_room = -(-max(most, columns + 7 * pair_total + room) // INT_ROWS) * INT_ROWS
    rows_room = sort_room // 8 + 2 * static
    full = pl.BlockSpec(memory_space=pltpu.VMEM)
    smem = pl.BlockSpec(memory_space=pltpu.SMEM)
    hbm = pl.BlockSpec(memory_space=pltpu.HBM)
    row_shape = (tiles, 8, LANES)
    last = narrow_count - 1
    moving = [at for at in range(WIN) if at != 1]
    order = [narrow_count // 2]
    order += [step for step in range(1, last) if step not in order] + [last]
    params = pltpu.CompilerParams(vmem_limit_bytes=VMEM)

    def rows_type(groups):
        return jax.ShapeDtypeStruct((groups,) + row_shape, jnp.float32)

    def entry(row, step, at=0):
        return lambda table: table[row, step * WIN + at]

    def group_cuts(begin, in_step):
        cuts = [(begin, static)]
        for index, size in enumerate(sizes):
            cuts.append((
                lambda table, index=index: begin(table)
                + chunk_places(in_step(table), static)[index][1],
                size,
            ))
        return cuts

    cuts = [
        (index, 0, begin, size)
        for index, (begin, size) in enumerate(group_cuts(entry(1, order[0]), entry(3, order[0])))
    ]
    target_sizes = [cut[3] for cut in cuts] + [2 * piece] * len(moving)
    for index, at in enumerate(moving):
        cuts.append((len(sizes) + 1 + index, 0, entry(1, 0, at), piece))
        cuts.append((len(sizes) + 1 + index, piece, entry(1, last, at), piece))
    me = jnp.stack([lax.axis_index("wide"), lax.axis_index("narrow")]).astype(jnp.int32)
    rows, table, *first = pl.pallas_call(
        functools.partial(
            sort_kernel,
            (species, levels, columns, tiles, wide_count, narrow_count, pair_total, cuts,
             len(target_sizes)),
        ),
        grid=(columns // SORT_COLUMNS,),
        in_specs=[smem, full, full, full,
                  pl.BlockSpec((species, levels, SORT_COLUMNS), lambda at: (0, 0, at))],
        out_specs=[hbm, full] + [hbm] * len(target_sizes),
        out_shape=[rows_type(rows_room), jax.ShapeDtypeStruct((8, LANES), jnp.int32)]
        + [rows_type(size) for size in target_sizes],
        scratch_shapes=[
            pltpu.VMEM((1, columns), jnp.int32),
            pltpu.VMEM((tiles * LANES, LANES), jnp.float32),
            pltpu.VMEM((LANES * 8, LANES), jnp.float32),
            pltpu.VMEM((sort_room * 8, LANES), jnp.float32),
            pltpu.VMEM((sort_room // 8,) + row_shape, jnp.float32),
            pltpu.SMEM((1, columns), jnp.int32),
            pltpu.SMEM((8, LANES), jnp.int32),
            pltpu.SemaphoreType.DMA(()),
            pltpu.SemaphoreType.DMA((len(cuts) + 1,)),
        ],
        compiler_params=params,
        name="sort_columns",
    )(
        me,
        phys_index.reshape(1, columns),
        column_rate.reshape(1, columns),
        iter_count.reshape(1, columns),
        tracers.transpose(1, 0, 2),
    )
    loss_pad = jnp.pad(loss_rate, (0, pad - species)).reshape(pad, 1)
    coupling_pad = jnp.pad(coupling, ((0, pad - species), (0, pad - species)))
    block = INT_ROWS // 8

    def integrate(operands, loads, merges, blocks, stores):
        groups = max([to + size for _, _, size, to in loads] + [begin + block for begin, _ in blocks])
        groups += static
        flops = 2 * levels * pad * pad * 6 * INT_ROWS * len(blocks)
        return pl.pallas_call(
            functools.partial(
                integrate_kernel, (levels, pad, tiles),
                (loads, merges, blocks, stores, len(operands)),
            ),
            in_specs=[smem, full, full] + [hbm] * len(operands),
            out_specs=[hbm] * len(stores),
            out_shape=[rows_type(size) for _, size in stores],
            scratch_shapes=[
                pltpu.VMEM((groups,) + row_shape, jnp.float32),
                pltpu.VMEM((INT_ROWS // LANES, tiles * LANES, LANES), jnp.float32),
                pltpu.VMEM((levels, pad, INT_ROWS), jnp.float32),
                pltpu.VMEM((pad, INT_ROWS), jnp.float32),
                pltpu.SMEM((2, LANES), jnp.int32),
                pltpu.SemaphoreType.DMA((len(loads),)),
                pltpu.SemaphoreType.DMA((len(stores),)),
            ],
            compiler_params=params,
            cost_estimate=pl.CostEstimate(
                flops=flops, bytes_accessed=8 * groups * 8 * tiles * LANES,
                transcendentals=flops // (2 * pad),
            ),
            name="integrate_columns",
        )(table, loss_pad, coupling_pad, *operands)

    def rows_of(step, at=0):
        return entry(0, step, at)

    def group_blocks(begin, step):
        return [
            (begin + part * block,
             lambda table, part=part: table[3, step * WIN] * 8 - part * INT_ROWS)
            for part in range(2 * static // block)
        ]

    def here(begin):
        return lambda table: jnp.int32(begin)

    def step_over(step, parts):
        def leaf(units, *parts):
            taken = [units > 0]
            taken += [(units - 1) // (size // UNIT) % 2 == 1 and units > 0 for size in sizes[1:]]
            return [
                from_behind(part, "narrow", step) if sent else jnp.zeros_like(part)
                for part, sent in zip(parts, taken)
            ]

        leaves = [functools.partial(leaf, units) for units in range(static // UNIT + 1)]
        return lax.switch(units_over(table[3, step * WIN], static), leaves, *parts)

    pieces = {}
    outgoing = first[:len(sizes) + 1]
    wide_now = list(first[len(sizes) + 1:])
    keys_now = [[(at, 0), (at, last)] for at in moving]
    for phase, step in enumerate(order):
        static_part = from_behind(outgoing[0], "narrow", step)
        wide_got = [
            from_behind(value, "wide", keys[0][0] - 1) for value, keys in zip(wide_now, keys_now)
        ]
        operands, loads, merges, blocks, stores, named = [], [], [], [], [], []
        used = 0
        if phase + 1 < len(order):
            coming = order[phase + 1]
            if coming == last:
                operands += [pieces[at, last][0] for at in moving] + [rows]
                for index, at in enumerate(moving):
                    loads.append((index, here(pieces[at, last][1]), piece, 2 * static + at * piece))
                loads.append((len(moving), entry(1, last, 1), piece, 2 * static + piece))
                for at in range(WIN):
                    merges.append((2 * static + at * piece, lambda table, at=at: (
                        lax.shift_right_logical(table[0, last * WIN + at] + 7, 3)
                    ), entry(2, last, at)))
                used = 2 * static + WIN * piece
            else:
                operands.append(rows)
                loads.append((0, entry(1, coming), 2 * static, 0))
                used = 2 * static
            blocks += group_blocks(0, coming)
            stores += group_cuts(here(0), entry(3, coming))
        extra = []
        if phase == 0:
            extra.append(((1, 0), None))
        if phase == 1:
            extra += [((at, 0), pieces[at, 0]) for at in moving]
        if phase == 2:
            extra += [((at, order[0]), pieces[at, order[0]]) for at in range(WIN)]
        used = -(-used // block) * block
        for key, value in extra:
            if value is None:
                loads.append((operands.index(rows), entry(1, key[1], key[0]), piece, used))
            else:
                operands.append(value[0])
                loads.append((len(operands) - 1, here(value[1]), piece, used))
            blocks.append((used, rows_of(key[1], key[0])))
            stores.append((here(used), piece))
            named.append(key)
            used += block
        if stores:
            results = integrate(operands, loads, merges, blocks, stores)
        else:
            results = []
        static_part, wide_got, results, over = lax.optimization_barrier(
            (static_part, wide_got, results, outgoing[1:])
        )
        done = {key: (value, 0) for key, value in zip(named, results[len(results) - len(named):])}
        over = step_over(step, over)
        for keys, value in zip(keys_now, wide_got):
            pieces.update({key: (value, part * piece) for part, key in enumerate(keys)})
        pieces.update(done)
        outgoing = results[:len(results) - len(named)]
        arrived = [static_part] + list(over)
        if step != last:
            cut = pl.pallas_call(
                functools.partial(cut_kernel, static, step),
                in_specs=[smem] + [hbm] * len(arrived),
                out_specs=[hbm] * WIN,
                out_shape=[rows_type(piece)] * WIN,
                scratch_shapes=[
                    pltpu.VMEM((3 * static,) + row_shape, jnp.float32),
                    pltpu.SemaphoreType.DMA((len(arrived),)),
                    pltpu.SemaphoreType.DMA((WIN,)),
                ],
                compiler_params=params,
                name="cut_pieces",
            )(table, *arrived)
            pieces[1, step] = (cut[1], 0)
            wide_now = [cut[at] for at in moving]
            keys_now = [[(at, step)] for at in moving]

    held = [pieces[at, step] for step in range(last) for at in range(WIN)]
    buffers = [value for value, _ in held] + arrived
    updated = pl.pallas_call(
        functools.partial(
            finish_kernel,
            (species, levels, columns, tiles, static, narrow_count, [begin for _, begin in held]),
        ),
        in_specs=[smem] + [hbm] * len(buffers),
        out_specs=hbm,
        out_shape=jax.ShapeDtypeStruct((species, levels, columns), jnp.float32),
        scratch_shapes=[
            pltpu.VMEM((pair_total - WIN, piece) + row_shape, jnp.float32),
            pltpu.VMEM((3 * static,) + row_shape, jnp.float32),
            pltpu.VMEM((tiles, columns + 8, LANES), jnp.float32),
            pltpu.VMEM((species, levels, columns), jnp.float32),
            pltpu.SemaphoreType.DMA((len(buffers),)),
            pltpu.SemaphoreType.DMA((columns // LANES,)),
        ],
        compiler_params=params,
        name="place_columns",
    )(table, *buffers)
    return updated.transpose(1, 0, 2)


def solution(mesh):
    placed = (
        P(None, None, ("wide", "narrow")),
        P(("wide", "narrow")),
        P(),
        P(),
        P(("wide", "narrow")),
        P(("wide", "narrow")),
    )
    return jax.shard_map(
        local,
        mesh=mesh,
        in_specs=placed,
        out_specs=P(None, None, ("wide", "narrow")),
        check_vma=False,
    )
```

```python
import functools

import jax
import jax.numpy as jnp
from jax import lax
from jax.experimental import pallas as pl
from jax.experimental.pallas import tpu as pltpu
from jax.sharding import PartitionSpec as P

WIN = 4
MAXIT = 12
LANES = 128
SORT_COLUMNS = 256
INT_ROWS = 256
UNIT = 8
VMEM = 60 * 1024 * 1024


def from_behind(value, axis, steps):
    count = lax.axis_size(axis)
    pairs = [(source, (source + steps) % count) for source in range(count)]
    return lax.ppermute(value, axis, pairs)


def log2(value):
    bits = value.bit_length() - 1
    assert 1 << bits == value
    return bits


def sort_kernel(sizes, me_ref, phys_ref, rate_ref, count_ref, tracers_ref, rows_ref, table_ref,
                *rest):
    species, levels, columns, tiles, wide_count, narrow_count, pair_total = sizes[:7]
    cuts, targets = sizes[7:]
    cut_refs, scratch = rest[:targets], rest[targets:]
    (pos_ref, turn_ref, wide_ref, sorted_ref, out_ref, at_ref, table_smem, sem_ref,
     out_sem) = scratch
    step = pl.program_id(0)
    lanes = tiles * LANES
    real = species * levels

    @pl.when(step == 0)
    def _():
        phys = phys_ref[...]
        target = lax.shift_right_logical(phys, log2(columns))
        slot = phys & (columns - 1)
        wide_step = (lax.shift_right_logical(target, log2(narrow_count)) - me_ref[0] + 1) & (
            wide_count - 1
        )
        narrow_step = ((target & (narrow_count - 1)) - me_ref[1]) & (narrow_count - 1)
        pair = narrow_step * WIN + wide_step
        member = pair == lax.broadcasted_iota(jnp.int32, (pair_total, columns), 0)
        counts = jnp.sum(jnp.where(member, 1.0, 0.0), axis=1, keepdims=True)
        slot_f = slot.astype(jnp.float32)
        starts = jnp.min(jnp.where(member, slot_f, float(columns)), axis=1, keepdims=True)
        groups = lax.shift_right_logical(counts.astype(jnp.int32) + 7, 3).astype(jnp.float32)
        lane = lax.broadcasted_iota(jnp.int32, (pair_total, LANES), 1)
        row = lax.broadcasted_iota(jnp.int32, (pair_total, LANES), 0)

        def across(value):
            return jnp.sum(jnp.where(lane == row, value, 0.0), axis=0, keepdims=True)

        groups_t = across(groups)
        base = jnp.sum(jnp.where(lane < row, groups_t, 0.0), axis=1, keepdims=True)
        section = row & -WIN
        inner = base - jnp.sum(jnp.where(lane < section, groups_t, 0.0), axis=1, keepdims=True)
        same = (lane & -WIN) == section
        in_step = jnp.sum(jnp.where(same, groups_t, 0.0), axis=1, keepdims=True)
        pos = slot_f + jnp.sum(jnp.where(member, base * 8.0 - starts, 0.0), axis=0, keepdims=True)
        pos_ref[...] = pos.astype(jnp.int32)
        copy = pltpu.make_async_copy(pos_ref, at_ref, sem_ref)
        copy.start()
        table_ref[...] = jnp.zeros_like(table_ref)
        for at, value in enumerate((counts, base, inner, in_step)):
            table_ref[at:at + 1, :] = across(value).astype(jnp.int32)
        copy.wait()
        copy = pltpu.make_async_copy(table_ref, table_smem, sem_ref)
        copy.start()
        copy.wait()

    block = tracers_ref.shape[2]
    begin = step * block
    in_group = lax.broadcasted_iota(jnp.int32, (8, LANES), 0)
    for half in range(block // LANES):
        span = slice(half * LANES, (half + 1) * LANES)
        at = pl.ds(pl.multiple_of(begin + half * LANES, LANES), LANES)
        turn_ref[lanes - 16:lanes, :] = jnp.zeros((16, LANES), jnp.float32)
        turn_ref[0:real, :] = tracers_ref[:, :, span].reshape(real, LANES)
        extra = jnp.where(in_group == 5, (phys_ref[:, at] & (columns - 1)).astype(jnp.float32), 0.0)
        extra = jnp.where(in_group == 6, rate_ref[:, at], extra)
        extra = jnp.where(in_group == 7, count_ref[:, at].astype(jnp.float32), extra)
        turn_ref[lanes - 8:lanes, :] = extra
        for tile in range(tiles):
            wide_ref[pl.ds(tile, LANES, stride=8), :] = turn_ref[
                tile * LANES:(tile + 1) * LANES, :
            ].T

        def move(part, carry):
            for extra_row in range(16):
                column = part * 16 + extra_row
                to = pl.multiple_of(at_ref[0, begin + half * LANES + column] * 8, 8)
                sorted_ref[pl.ds(to, 8), :] = wide_ref[pl.ds(pl.multiple_of(column * 8, 8), 8), :]
            return carry

        lax.fori_loop(0, LANES // 16, move, 0)

    @pl.when(step == pl.num_programs(0) - 1)
    def _():
        chunk = 32
        held = sorted_ref.shape[0] // 64
        chunks = held // chunk
        total = table_smem[1, pair_total - 1] + table_smem[0, pair_total - 1]
        for part in range(chunks):
            @pl.when(part * chunk < total)
            def _():
                def gather(group, carry):
                    for tile in range(tiles):
                        out_ref[group, tile] = sorted_ref[pl.ds(group * 64 + tile, 8, stride=8), :]
                    return carry

                lax.fori_loop(part * chunk, (part + 1) * chunk, gather, 0)

        copies = [pltpu.make_async_copy(out_ref.at[pl.ds(0, held)], rows_ref.at[pl.ds(0, held)],
                                        out_sem.at[len(cuts)])]
        for index, (target, to, begin, size) in enumerate(cuts):
            copies.append(pltpu.make_async_copy(
                out_ref.at[pl.ds(begin(table_smem), size)], cut_refs[target].at[pl.ds(to, size)],
                out_sem.at[index],
            ))
        for copy in copies:
            copy.start()
        for copy in copies:
            copy.wait()


def start_arrival(refs, sems, room_ref, in_step, static):
    waits = []
    for index, wanted in enumerate((None, in_step > static)):
        copy = pltpu.make_async_copy(
            refs[index], room_ref.at[pl.ds(index * static, static)], sems(index)
        )
        if wanted is None:
            copy.start()
        else:
            pl.when(wanted)(copy.start)
        waits.append((wanted, copy))
    return waits


def wait_all(waits):
    for wanted, copy in waits:
        if wanted is None:
            copy.wait()
        else:
            pl.when(wanted)(copy.wait)


def integrate_block(sizes, room_ref, first, valid, loss_ref, coupling_ref,
                    turn_ref, y_ref, inverse_ref):
    levels, pad, tiles = sizes
    per = LANES // 8
    halves = INT_ROWS // LANES
    lanes = tiles * LANES
    for half in range(halves):
        begin = first + half * per
        for tile in range(tiles):
            block = room_ref[pl.ds(begin, per), tile].reshape(LANES, LANES)
            turn_ref[half, tile * LANES:(tile + 1) * LANES, :] = block.T
        for level in range(levels):
            y_ref[level, :, half * LANES:(half + 1) * LANES] = turn_ref[
                half, pl.ds(level, pad, stride=levels), :
            ]
    rate = jnp.concatenate(
        [turn_ref[half, lanes - 2:lanes - 1, :] for half in range(halves)], axis=1
    )
    count = jnp.concatenate(
        [turn_ref[half, lanes - 1:lanes, :] for half in range(halves)], axis=1
    )
    lane = lax.broadcasted_iota(jnp.int32, (1, INT_ROWS), 1)
    count = jnp.where((lane < valid) & (count <= MAXIT), count, 0.0)
    step_len = rate / jnp.maximum(count, 1.0)
    inverse_ref[...] = 1.0 / (1.0 + step_len * loss_ref[...])
    last = jnp.max(count).astype(jnp.int32)

    def advance(k, carry):
        active = k.astype(jnp.float32) < count

        def one_level(level, inner):
            y = y_ref[level]
            squashed = jnp.tanh(y).astype(jnp.bfloat16)
            produced = jnp.dot(coupling_ref[...], squashed, preferred_element_type=jnp.float32)
            y_ref[level] = jnp.where(active, (y + step_len * produced) * inverse_ref[...], y)
            return inner

        for level in range(levels):
            one_level(level, 0)
        return carry

    lax.fori_loop(0, last, advance, 0)
    for half in range(halves):
        begin = first + half * per
        for level in range(levels):
            turn_ref[half, pl.ds(level, pad, stride=levels), :] = y_ref[
                level, :, half * LANES:(half + 1) * LANES
            ]
        for tile in range(tiles):
            block = turn_ref[half, tile * LANES:(tile + 1) * LANES, :]
            room_ref[pl.ds(begin, per), tile] = block.T.reshape(per, 8, LANES)


def integrate_kernel(sizes, plan, table_ref, loss_ref, coupling_ref, *refs):
    loads, merges, blocks, stores, operands = plan
    sources = refs[:operands]
    results = refs[operands:operands + len(stores)]
    room_ref, turn_ref, y_ref, inverse_ref, rows_ref, sem_ref, out_sem = refs[
        operands + len(stores):
    ]
    copies = []
    for index, (source, begin, groups, to) in enumerate(loads):
        ref = sources[source]
        if begin is not None:
            ref = ref.at[pl.ds(begin(table_ref), groups)]
        copies.append(
            pltpu.make_async_copy(ref, room_ref.at[pl.ds(to, groups)], sem_ref.at[index])
        )
    for copy in copies:
        copy.start()
    for copy in copies:
        copy.wait()
    for begin, groups, to in merges:
        to = to(table_ref)

        def move(group, carry):
            room_ref[to + group] = room_ref[begin + group]
            return carry

        lax.fori_loop(0, groups(table_ref), move, 0)
    for index, (begin, rows) in enumerate(blocks):
        rows_ref[0, index] = jnp.int32(begin)
        rows_ref[1, index] = rows(table_ref)

    def one_block(index, carry):
        valid = rows_ref[1, index]

        @pl.when(valid > 0)
        def _():
            integrate_block(sizes, room_ref, rows_ref[0, index], valid, loss_ref, coupling_ref,
                            turn_ref, y_ref, inverse_ref)

        return carry

    lax.fori_loop(0, len(blocks), one_block, 0)
    copies = []
    for index, (begin, groups) in enumerate(stores):
        copies.append(pltpu.make_async_copy(
            room_ref.at[pl.ds(begin(table_ref), groups)], results[index], out_sem.at[index]
        ))
    for copy in copies:
        copy.start()
    for copy in copies:
        copy.wait()


def cut_kernel(static, step, table_ref, *refs):
    pieces = refs[2:2 + WIN]
    room_ref, sem_ref, out_sem = refs[2 + WIN:]
    wait_all(start_arrival(refs[:2], lambda at: sem_ref.at[at], room_ref,
                           table_ref[3, step * WIN], static))
    copies = []
    for at in range(WIN):
        begin = table_ref[2, step * WIN + at]
        copies.append(pltpu.make_async_copy(
            room_ref.at[pl.ds(begin, pieces[at].shape[0])], pieces[at], out_sem.at[at]
        ))
    for copy in copies:
        copy.start()
    for copy in copies:
        copy.wait()


def finish_kernel(sizes, table_ref, *refs):
    species, levels, columns, tiles, static, narrow_count, begins = sizes
    pair_total = narrow_count * WIN
    whole_pieces = pair_total - WIN
    out_ref, piece_ref, room_ref, placed_ref, whole_ref, sem_ref, out_sem = refs[-7:]
    copies = []
    for pair in range(whole_pieces):
        source = refs[pair].at[pl.ds(begins[pair], piece_ref.shape[1])]
        copies.append(pltpu.make_async_copy(source, piece_ref.at[pair], sem_ref.at[pair]))
        copies[-1].start()
    waits = start_arrival(refs[whole_pieces:whole_pieces + 2],
                          lambda at: sem_ref.at[whole_pieces + at], room_ref,
                          table_ref[3, whole_pieces], static)
    lane = lax.broadcasted_iota(jnp.int32, (1, LANES), 1)
    in_group = lax.broadcasted_iota(jnp.int32, (8, LANES), 0)
    for pair in range(pair_total):
        if pair < whole_pieces:
            copies[pair].wait()
            piece = piece_ref.at[pair]
            begin = 0
        else:
            if pair == whole_pieces:
                wait_all(waits)
            piece = room_ref
            begin = table_ref[2, pair]
        count = table_ref[0, pair]
        first = piece[begin, tiles - 1][0:1, :]
        start = jnp.max(jnp.where(lane == LANES - 3, first, 0.0)).astype(jnp.int32)
        start = jnp.clip(start, 0, columns - 1)
        full = lax.shift_right_logical(count, 3)

        def move(group, carry):
            for tile in range(tiles):
                placed_ref[tile, pl.ds(start + group * 8, 8), :] = piece[begin + group, tile]
            return carry

        lax.fori_loop(0, full, move, 0)

        @pl.when((count & 7) > 0)
        def _():
            for tile in range(tiles):
                at = pl.ds(start + full * 8, 8)
                placed_ref[tile, at, :] = jnp.where(
                    in_group < (count & 7), piece[begin + full, tile], placed_ref[tile, at, :]
                )

    per_tile = LANES // levels
    for part in range(columns // LANES):
        at = slice(part * LANES, (part + 1) * LANES)
        for tile in range(tiles):
            block = placed_ref[tile, at, :].T.reshape(per_tile, levels, LANES)
            keep = min(per_tile, species - tile * per_tile)
            whole_ref[tile * per_tile:tile * per_tile + keep, :, at] = block[:keep]
        pltpu.make_async_copy(whole_ref.at[:, :, at], out_ref.at[:, :, at], out_sem.at[part]).start()
    for part in range(columns // LANES):
        at = slice(part * LANES, (part + 1) * LANES)
        pltpu.make_async_copy(whole_ref.at[:, :, at], out_ref.at[:, :, at], out_sem.at[part]).wait()


def local(tracers, column_rate, loss_rate, coupling, phys_index, iter_count):
    levels, species, columns = tracers.shape
    wide_count = lax.axis_size("wide")
    narrow_count = lax.axis_size("narrow")
    pair_total = WIN * narrow_count
    room = 2 * columns // pair_total
    piece = room // 8
    pad = -(-species // 8) * 8
    while levels * pad % LANES or levels * (pad - species) < 8:
        pad += 8
    tiles = levels * pad // LANES
    static = columns // narrow_count // 8
    most = columns + 7 * pair_total + UNIT * 8
    sort_room = -(-max(most, columns + 7 * pair_total + room) // INT_ROWS) * INT_ROWS
    rows_room = sort_room // 8 + 2 * static
    full = pl.BlockSpec(memory_space=pltpu.VMEM)
    smem = pl.BlockSpec(memory_space=pltpu.SMEM)
    hbm = pl.BlockSpec(memory_space=pltpu.HBM)
    row_shape = (tiles, 8, LANES)
    last = narrow_count - 1
    moving = [at for at in range(WIN) if at != 1]
    order = [narrow_count // 2]
    order += [step for step in range(1, last) if step not in order] + [last]
    params = pltpu.CompilerParams(vmem_limit_bytes=VMEM)

    def rows_type(groups):
        return jax.ShapeDtypeStruct((groups,) + row_shape, jnp.float32)

    def entry(row, step, at=0):
        return lambda table: table[row, step * WIN + at]

    def over(begin):
        return lambda table: begin(table) + static

    cuts = [
        (0, 0, entry(1, order[0]), static),
        (1, 0, over(entry(1, order[0])), static),
    ]
    target_sizes = [cut[3] for cut in cuts] + [2 * piece] * len(moving)
    for index, at in enumerate(moving):
        cuts.append((2 + index, 0, entry(1, 0, at), piece))
        cuts.append((2 + index, piece, entry(1, last, at), piece))
    me = jnp.stack([lax.axis_index("wide"), lax.axis_index("narrow")]).astype(jnp.int32)
    rows, table, *first = pl.pallas_call(
        functools.partial(
            sort_kernel,
            (species, levels, columns, tiles, wide_count, narrow_count, pair_total, cuts,
             len(target_sizes)),
        ),
        grid=(columns // SORT_COLUMNS,),
        in_specs=[smem, full, full, full,
                  pl.BlockSpec((species, levels, SORT_COLUMNS), lambda at: (0, 0, at))],
        out_specs=[hbm, full] + [hbm] * len(target_sizes),
        out_shape=[rows_type(rows_room), jax.ShapeDtypeStruct((8, LANES), jnp.int32)]
        + [rows_type(size) for size in target_sizes],
        scratch_shapes=[
            pltpu.VMEM((1, columns), jnp.int32),
            pltpu.VMEM((tiles * LANES, LANES), jnp.float32),
            pltpu.VMEM((LANES * 8, LANES), jnp.float32),
            pltpu.VMEM((sort_room * 8, LANES), jnp.float32),
            pltpu.VMEM((rows_room,) + row_shape, jnp.float32),
            pltpu.SMEM((1, columns), jnp.int32),
            pltpu.SMEM((8, LANES), jnp.int32),
            pltpu.SemaphoreType.DMA(()),
            pltpu.SemaphoreType.DMA((len(cuts) + 1,)),
        ],
        compiler_params=params,
        name="sort_columns",
    )(
        me,
        phys_index.reshape(1, columns),
        column_rate.reshape(1, columns),
        iter_count.reshape(1, columns),
        tracers.transpose(1, 0, 2),
    )
    loss_pad = jnp.pad(loss_rate, (0, pad - species)).reshape(pad, 1)
    coupling_pad = jnp.pad(coupling, ((0, pad - species), (0, pad - species)))
    block = INT_ROWS // 8

    def integrate(operands, loads, merges, blocks, stores):
        groups = max([to + size for _, _, size, to in loads] + [begin + block for begin, _ in blocks])
        groups += static
        flops = 2 * levels * pad * pad * 6 * INT_ROWS * len(blocks)
        return pl.pallas_call(
            functools.partial(
                integrate_kernel, (levels, pad, tiles),
                (loads, merges, blocks, stores, len(operands)),
            ),
            in_specs=[smem, full, full] + [hbm] * len(operands),
            out_specs=[hbm] * len(stores),
            out_shape=[rows_type(size) for _, size in stores],
            scratch_shapes=[
                pltpu.VMEM((groups,) + row_shape, jnp.float32),
                pltpu.VMEM((INT_ROWS // LANES, tiles * LANES, LANES), jnp.float32),
                pltpu.VMEM((levels, pad, INT_ROWS), jnp.float32),
                pltpu.VMEM((pad, INT_ROWS), jnp.float32),
                pltpu.SMEM((2, LANES), jnp.int32),
                pltpu.SemaphoreType.DMA((len(loads),)),
                pltpu.SemaphoreType.DMA((len(stores),)),
            ],
            compiler_params=params,
            cost_estimate=pl.CostEstimate(
                flops=flops, bytes_accessed=8 * groups * 8 * tiles * LANES,
                transcendentals=flops // (2 * pad),
            ),
            name="integrate_columns",
        )(table, loss_pad, coupling_pad, *operands)

    def rows_of(step, at=0):
        return entry(0, step, at)

    def group_blocks(begin, step):
        return [
            (begin + part * block,
             lambda table, part=part: table[3, step * WIN] * 8 - part * INT_ROWS)
            for part in range(2 * static // block)
        ]

    def here(begin):
        return lambda table: jnp.int32(begin)

    def step_over(step, rest):
        def leaf(units, rest):
            if units == 0:
                return jnp.zeros_like(rest)
            got = from_behind(rest[:units * UNIT], "narrow", step)
            return jnp.pad(got, ((0, static - units * UNIT), (0, 0), (0, 0), (0, 0)))

        units = (jnp.maximum(table[3, step * WIN] - static, 0) + UNIT - 1) // UNIT
        leaves = [functools.partial(leaf, count) for count in range(static // UNIT + 1)]
        return lax.switch(units, leaves, rest)

    pieces = {}
    outgoing = first[:2]
    wide_now = list(first[2:])
    keys_now = [[(at, 0), (at, last)] for at in moving]
    static_part = from_behind(outgoing[0], "narrow", order[0])
    wide_got = [from_behind(value, "wide", at - 1) for value, at in zip(wide_now, moving)]
    for phase, step in enumerate(order):
        operands, loads, merges, blocks, stores, named = [], [], [], [], [], []
        used = 0
        if phase + 1 < len(order):
            coming = order[phase + 1]
            if coming == last:
                operands += [pieces[at, last][0] for at in moving] + [rows]
                for index, at in enumerate(moving):
                    loads.append((index, here(pieces[at, last][1]), piece, 2 * static + at * piece))
                loads.append((len(moving), entry(1, last, 1), piece, 2 * static + piece))
                for at in range(WIN):
                    merges.append((2 * static + at * piece, lambda table, at=at: (
                        lax.shift_right_logical(table[0, last * WIN + at] + 7, 3)
                    ), entry(2, last, at)))
                used = 2 * static + WIN * piece
            else:
                operands.append(rows)
                loads.append((0, entry(1, coming), 2 * static, 0))
                used = 2 * static
            blocks += group_blocks(0, coming)
            stores += [(here(0), static), (here(static), static)]
        extra = []
        if phase == 0:
            extra.append(((1, 0), None))
        if phase == 1:
            extra += [((at, 0), pieces[at, 0]) for at in moving]
        if phase == 2:
            extra += [((at, order[0]), pieces[at, order[0]]) for at in range(WIN)]
        used = -(-used // block) * block
        for key, value in extra:
            if value is None:
                loads.append((operands.index(rows), entry(1, key[1], key[0]), piece, used))
            else:
                operands.append(value[0])
                loads.append((len(operands) - 1, here(value[1]), piece, used))
            blocks.append((used, rows_of(key[1], key[0])))
            stores.append((here(used), piece))
            named.append(key)
            used += block
        if stores:
            results = integrate(operands, loads, merges, blocks, stores)
        else:
            results = []
        rest = outgoing[1]
        if phase == 0:
            static_part, results, rest, wide_got = lax.optimization_barrier(
                (static_part, results, rest, wide_got)
            )
        else:
            static_part, results, rest = lax.optimization_barrier((static_part, results, rest))
        done = {key: (value, 0) for key, value in zip(named, results[len(results) - len(named):])}
        outgoing = results[:len(results) - len(named)]
        arrived = [static_part]
        if step != last:
            static_part = from_behind(outgoing[0], "narrow", order[phase + 1])
        arrived.append(step_over(step, rest))
        if step != last:
            cut = pl.pallas_call(
                functools.partial(cut_kernel, static, step),
                in_specs=[smem] + [hbm] * len(arrived),
                out_specs=[hbm] * WIN,
                out_shape=[rows_type(piece)] * WIN,
                scratch_shapes=[
                    pltpu.VMEM((3 * static,) + row_shape, jnp.float32),
                    pltpu.SemaphoreType.DMA((len(arrived),)),
                    pltpu.SemaphoreType.DMA((WIN,)),
                ],
                compiler_params=params,
                name="cut_pieces",
            )(table, *arrived)
            if phase > 0:
                cut, wide_got = lax.optimization_barrier((cut, wide_got))
        for keys, value in zip(keys_now, wide_got):
            pieces.update({key: (value, part * piece) for part, key in enumerate(keys)})
        pieces.update(done)
        if step != last:
            pieces[1, step] = (cut[1], 0)
            keys_now = [[(at, step)] for at in moving]
            wide_got = [from_behind(cut[at], "wide", at - 1) for at in moving]

    held = [pieces[at, step] for step in range(last) for at in range(WIN)]
    buffers = [value for value, _ in held] + arrived
    updated = pl.pallas_call(
        functools.partial(
            finish_kernel,
            (species, levels, columns, tiles, static, narrow_count, [begin for _, begin in held]),
        ),
        in_specs=[smem] + [hbm] * len(buffers),
        out_specs=hbm,
        out_shape=jax.ShapeDtypeStruct((species, levels, columns), jnp.float32),
        scratch_shapes=[
            pltpu.VMEM((pair_total - WIN, piece) + row_shape, jnp.float32),
            pltpu.VMEM((3 * static,) + row_shape, jnp.float32),
            pltpu.VMEM((tiles, columns + 8, LANES), jnp.float32),
            pltpu.VMEM((species, levels, columns), jnp.float32),
            pltpu.SemaphoreType.DMA((len(buffers),)),
            pltpu.SemaphoreType.DMA((columns // LANES,)),
        ],
        compiler_params=params,
        name="place_columns",
    )(table, *buffers)
    return updated.transpose(1, 0, 2)


def solution(mesh):
    placed = (
        P(None, None, ("wide", "narrow")),
        P(("wide", "narrow")),
        P(),
        P(),
        P(("wide", "narrow")),
        P(("wide", "narrow")),
    )
    return jax.shard_map(
        local,
        mesh=mesh,
        in_specs=placed,
        out_specs=P(None, None, ("wide", "narrow")),
        check_vma=False,
    )
```

```python
import functools

import jax
import jax.numpy as jnp
from jax import lax
from jax.experimental import pallas as pl
from jax.experimental.pallas import tpu as pltpu
from jax.sharding import PartitionSpec as P

WIN = 4
MAXIT = 12
LANES = 128
SORT_COLUMNS = 256
INT_ROWS = 256
UNIT = 8
VMEM = 60 * 1024 * 1024


def from_behind(value, axis, steps):
    count = lax.axis_size(axis)
    pairs = [(source, (source + steps) % count) for source in range(count)]
    return lax.ppermute(value, axis, pairs)


def log2(value):
    bits = value.bit_length() - 1
    assert 1 << bits == value
    return bits


def sort_kernel(sizes, phys_ref, rate_ref, count_ref, tracers_ref, table_ref, *rest):
    species, levels, columns, tiles, wide_count, narrow_count, pair_total = sizes[:7]
    cuts, targets = sizes[7:]
    cut_refs, scratch = rest[:targets], rest[targets:]
    (pos_ref, turn_ref, wide_ref, sorted_ref, out_ref, at_ref, table_smem, sem_ref,
     out_sem) = scratch
    step = pl.program_id(0)
    lanes = tiles * LANES
    real = species * levels

    @pl.when(step == 0)
    def _():
        phys = phys_ref[...]
        target = lax.shift_right_logical(phys, log2(columns))
        slot = phys & (columns - 1)
        wide_step = lax.shift_right_logical(target, log2(narrow_count)) - lax.axis_index("wide")
        wide_step = (wide_step + 1) & (wide_count - 1)
        narrow_step = ((target & (narrow_count - 1)) - lax.axis_index("narrow")) & (narrow_count - 1)
        pair = narrow_step * WIN + wide_step
        member = pair == lax.broadcasted_iota(jnp.int32, (pair_total, columns), 0)
        counts = jnp.sum(jnp.where(member, 1.0, 0.0), axis=1, keepdims=True)
        slot_f = slot.astype(jnp.float32)
        starts = jnp.min(jnp.where(member, slot_f, float(columns)), axis=1, keepdims=True)
        groups = lax.shift_right_logical(counts.astype(jnp.int32) + 7, 3).astype(jnp.float32)
        lane = lax.broadcasted_iota(jnp.int32, (pair_total, LANES), 1)
        row = lax.broadcasted_iota(jnp.int32, (pair_total, LANES), 0)

        def across(value):
            return jnp.sum(jnp.where(lane == row, value, 0.0), axis=0, keepdims=True)

        groups_t = across(groups)
        base = jnp.sum(jnp.where(lane < row, groups_t, 0.0), axis=1, keepdims=True)
        section = row & -WIN
        inner = base - jnp.sum(jnp.where(lane < section, groups_t, 0.0), axis=1, keepdims=True)
        same = (lane & -WIN) == section
        in_step = jnp.sum(jnp.where(same, groups_t, 0.0), axis=1, keepdims=True)
        pos = slot_f + jnp.sum(jnp.where(member, base * 8.0 - starts, 0.0), axis=0, keepdims=True)
        pos_ref[...] = pos.astype(jnp.int32)
        copy = pltpu.make_async_copy(pos_ref, at_ref, sem_ref)
        copy.start()
        table_ref[...] = jnp.zeros_like(table_ref)
        for at, value in enumerate((counts, base, inner, in_step)):
            table_ref[at:at + 1, :] = across(value).astype(jnp.int32)
        copy.wait()
        copy = pltpu.make_async_copy(table_ref, table_smem, sem_ref)
        copy.start()
        copy.wait()

    block = tracers_ref.shape[2]
    begin = step * block
    in_group = lax.broadcasted_iota(jnp.int32, (8, LANES), 0)
    for half in range(block // LANES):
        span = slice(half * LANES, (half + 1) * LANES)
        at = pl.ds(pl.multiple_of(begin + half * LANES, LANES), LANES)
        turn_ref[lanes - 16:lanes, :] = jnp.zeros((16, LANES), jnp.float32)
        turn_ref[0:real, :] = tracers_ref[:, :, span].reshape(real, LANES)
        extra = jnp.where(in_group == 5, (phys_ref[:, at] & (columns - 1)).astype(jnp.float32), 0.0)
        extra = jnp.where(in_group == 6, rate_ref[:, at], extra)
        extra = jnp.where(in_group == 7, count_ref[:, at].astype(jnp.float32), extra)
        turn_ref[lanes - 8:lanes, :] = extra
        for tile in range(tiles):
            wide_ref[pl.ds(tile, LANES, stride=8), :] = turn_ref[
                tile * LANES:(tile + 1) * LANES, :
            ].T

        def move(part, carry):
            for extra_row in range(16):
                column = part * 16 + extra_row
                to = pl.multiple_of(at_ref[0, begin + half * LANES + column] * 8, 8)
                sorted_ref[pl.ds(to, 8), :] = wide_ref[pl.ds(pl.multiple_of(column * 8, 8), 8), :]
            return carry

        lax.fori_loop(0, LANES // 16, move, 0)

    @pl.when(step == pl.num_programs(0) - 1)
    def _():
        copies = []
        filled = 0
        for index, (target, to, begin, size, valid) in enumerate(cuts):
            begin = begin(table_smem)
            valid = jnp.clip(valid(table_smem), 0, size)

            def gather(group, carry):
                for tile in range(tiles):
                    out_ref[filled + group, tile] = sorted_ref[
                        pl.ds((begin + group) * 64 + tile, 8, stride=8), :
                    ]
                return carry

            lax.fori_loop(0, valid, gather, 0)
            copy = pltpu.make_async_copy(
                out_ref.at[pl.ds(filled, size)], cut_refs[target].at[pl.ds(to, size)],
                out_sem.at[index],
            )
            pl.when(valid > 0)(copy.start)
            copies.append((valid > 0, copy))
            filled += size
        wait_all(copies)


def start_arrival(refs, sems, room_ref, in_step, static):
    waits = []
    for index, wanted in enumerate((None, in_step > static)):
        copy = pltpu.make_async_copy(
            refs[index], room_ref.at[pl.ds(index * static, static)], sems(index)
        )
        if wanted is None:
            copy.start()
        else:
            pl.when(wanted)(copy.start)
        waits.append((wanted, copy))
    return waits


def wait_all(waits):
    for wanted, copy in waits:
        if wanted is None:
            copy.wait()
        else:
            pl.when(wanted)(copy.wait)


def integrate_block(sizes, room_ref, first, valid, loss_ref, coupling_ref,
                    turn_ref, y_ref, inverse_ref):
    levels, pad, tiles = sizes
    per = LANES // 8
    halves = INT_ROWS // LANES
    lanes = tiles * LANES
    for half in range(halves):
        begin = first + half * per
        for tile in range(tiles):
            block = room_ref[pl.ds(begin, per), tile].reshape(LANES, LANES)
            turn_ref[half, tile * LANES:(tile + 1) * LANES, :] = block.T
        for level in range(levels):
            y_ref[level, :, half * LANES:(half + 1) * LANES] = turn_ref[
                half, pl.ds(level, pad, stride=levels), :
            ]
    rate = jnp.concatenate(
        [turn_ref[half, lanes - 2:lanes - 1, :] for half in range(halves)], axis=1
    )
    count = jnp.concatenate(
        [turn_ref[half, lanes - 1:lanes, :] for half in range(halves)], axis=1
    )
    lane = lax.broadcasted_iota(jnp.int32, (1, INT_ROWS), 1)
    count = jnp.where((lane < valid) & (count <= MAXIT), count, 0.0)
    step_len = rate / jnp.maximum(count, 1.0)
    inverse_ref[...] = 1.0 / (1.0 + step_len * loss_ref[...])
    last = jnp.max(count).astype(jnp.int32)

    def advance(k, carry):
        active = k.astype(jnp.float32) < count

        def one_level(level, inner):
            y = y_ref[level]
            squashed = jnp.tanh(y).astype(jnp.bfloat16)
            produced = jnp.dot(coupling_ref[...], squashed, preferred_element_type=jnp.float32)
            y_ref[level] = jnp.where(active, (y + step_len * produced) * inverse_ref[...], y)
            return inner

        for level in range(levels):
            one_level(level, 0)
        return carry

    lax.fori_loop(0, last, advance, 0)
    for half in range(halves):
        begin = first + half * per
        for level in range(levels):
            turn_ref[half, pl.ds(level, pad, stride=levels), :] = y_ref[
                level, :, half * LANES:(half + 1) * LANES
            ]
        for tile in range(tiles):
            block = turn_ref[half, tile * LANES:(tile + 1) * LANES, :]
            room_ref[pl.ds(begin, per), tile] = block.T.reshape(per, 8, LANES)


def integrate_kernel(sizes, plan, table_ref, loss_ref, coupling_ref, *refs):
    loads, merges, blocks, stores, operands = plan
    sources = refs[:operands]
    results = refs[operands:operands + len(stores)]
    room_ref, turn_ref, y_ref, inverse_ref, rows_ref, sem_ref, out_sem = refs[
        operands + len(stores):
    ]
    copies = []
    for index, (source, begin, groups, to) in enumerate(loads):
        ref = sources[source]
        if begin is not None:
            ref = ref.at[pl.ds(begin(table_ref), groups)]
        copies.append(
            pltpu.make_async_copy(ref, room_ref.at[pl.ds(to, groups)], sem_ref.at[index])
        )
    for copy in copies:
        copy.start()
    for copy in copies:
        copy.wait()
    for begin, groups, to in merges:
        to = to(table_ref)

        def move(group, carry):
            room_ref[to + group] = room_ref[begin + group]
            return carry

        lax.fori_loop(0, groups(table_ref), move, 0)
    for index, (begin, rows) in enumerate(blocks):
        rows_ref[0, index] = jnp.int32(begin)
        rows_ref[1, index] = rows(table_ref)

    def one_block(index, carry):
        valid = rows_ref[1, index]

        @pl.when(valid > 0)
        def _():
            integrate_block(sizes, room_ref, rows_ref[0, index], valid, loss_ref, coupling_ref,
                            turn_ref, y_ref, inverse_ref)

        return carry

    lax.fori_loop(0, len(blocks), one_block, 0)
    copies = []
    for index, (begin, groups) in enumerate(stores):
        copies.append(pltpu.make_async_copy(
            room_ref.at[pl.ds(begin(table_ref), groups)], results[index], out_sem.at[index]
        ))
    for copy in copies:
        copy.start()
    for copy in copies:
        copy.wait()


def cut_kernel(static, step, table_ref, *refs):
    pieces = refs[2:2 + WIN]
    room_ref, sem_ref, out_sem = refs[2 + WIN:]
    wait_all(start_arrival(refs[:2], lambda at: sem_ref.at[at], room_ref,
                           table_ref[3, step * WIN], static))
    copies = []
    for at in range(WIN):
        begin = table_ref[2, step * WIN + at]
        copies.append(pltpu.make_async_copy(
            room_ref.at[pl.ds(begin, pieces[at].shape[0])], pieces[at], out_sem.at[at]
        ))
    for copy in copies:
        copy.start()
    for copy in copies:
        copy.wait()


def finish_kernel(sizes, table_ref, *refs):
    species, levels, columns, tiles, static, narrow_count, begins = sizes
    pair_total = narrow_count * WIN
    whole_pieces = pair_total - WIN
    out_ref, piece_ref, room_ref, placed_ref, whole_ref, sem_ref, out_sem = refs[-7:]
    copies = []
    half = piece_ref.shape[1] // 2
    for pair in range(whole_pieces):
        both = []
        for part in range(2):
            source = refs[pair].at[pl.ds(begins[pair] + part * half, half)]
            copy = pltpu.make_async_copy(
                source, piece_ref.at[pair, pl.ds(part * half, half)], sem_ref.at[part, pair]
            )
            wanted = table_ref[0, pair] > part * half * 8
            pl.when(wanted)(copy.start)
            both.append((wanted, copy))
        copies.append(both)
    waits = start_arrival(refs[whole_pieces:whole_pieces + 2],
                          lambda at: sem_ref.at[at, whole_pieces], room_ref,
                          table_ref[3, whole_pieces], static)
    lane = lax.broadcasted_iota(jnp.int32, (1, LANES), 1)
    in_group = lax.broadcasted_iota(jnp.int32, (8, LANES), 0)
    for pair in range(pair_total):
        if pair < whole_pieces:
            wait_all(copies[pair])
            piece = piece_ref.at[pair]
            begin = 0
        else:
            if pair == whole_pieces:
                wait_all(waits)
            piece = room_ref
            begin = table_ref[2, pair]
        count = table_ref[0, pair]
        first = piece[begin, tiles - 1][0:1, :]
        start = jnp.max(jnp.where(lane == LANES - 3, first, 0.0)).astype(jnp.int32)
        start = jnp.clip(start, 0, columns - 1)
        full = lax.shift_right_logical(count, 3)

        def move(group, carry):
            for tile in range(tiles):
                placed_ref[tile, pl.ds(start + group * 8, 8), :] = piece[begin + group, tile]
            return carry

        lax.fori_loop(0, full, move, 0)

        @pl.when((count & 7) > 0)
        def _():
            for tile in range(tiles):
                at = pl.ds(start + full * 8, 8)
                placed_ref[tile, at, :] = jnp.where(
                    in_group < (count & 7), piece[begin + full, tile], placed_ref[tile, at, :]
                )

    per_tile = LANES // levels
    for part in range(columns // LANES):
        at = slice(part * LANES, (part + 1) * LANES)
        for tile in range(tiles):
            block = placed_ref[tile, at, :].T.reshape(per_tile, levels, LANES)
            keep = min(per_tile, species - tile * per_tile)
            whole_ref[tile * per_tile:tile * per_tile + keep, :, at] = block[:keep]
        pltpu.make_async_copy(whole_ref.at[:, :, at], out_ref.at[:, :, at], out_sem.at[part]).start()
    for part in range(columns // LANES):
        at = slice(part * LANES, (part + 1) * LANES)
        pltpu.make_async_copy(whole_ref.at[:, :, at], out_ref.at[:, :, at], out_sem.at[part]).wait()


def local(tracers, column_rate, loss_rate, coupling, phys_index, iter_count):
    levels, species, columns = tracers.shape
    wide_count = lax.axis_size("wide")
    narrow_count = lax.axis_size("narrow")
    pair_total = WIN * narrow_count
    room = 2 * columns // pair_total
    piece = room // 8
    pad = -(-species // 8) * 8
    while levels * pad % LANES or levels * (pad - species) < 8:
        pad += 8
    tiles = levels * pad // LANES
    static = columns // narrow_count // 8
    full = pl.BlockSpec(memory_space=pltpu.VMEM)
    smem = pl.BlockSpec(memory_space=pltpu.SMEM)
    hbm = pl.BlockSpec(memory_space=pltpu.HBM)
    row_shape = (tiles, 8, LANES)
    last = narrow_count - 1
    moving = [at for at in range(WIN) if at != 1]
    order = [narrow_count // 2]
    order += [step for step in range(1, last) if step not in order] + [last]
    params = pltpu.CompilerParams(vmem_limit_bytes=VMEM)

    def rows_type(groups):
        return jax.ShapeDtypeStruct((groups,) + row_shape, jnp.float32)

    def entry(row, step, at=0):
        return lambda table: table[row, step * WIN + at]

    def over(begin):
        return lambda table: begin(table) + static

    def groups_of(step, at):
        return lambda table: lax.shift_right_logical(table[0, step * WIN + at] + 7, 3)

    def groups_over(step):
        return lambda table: table[3, step * WIN] - static

    cuts = [
        (0, 0, entry(1, order[0]), static, entry(3, order[0])),
        (1, 0, over(entry(1, order[0])), static, groups_over(order[0])),
    ]
    target_sizes = [static, static]
    for at in moving + [1]:
        for part, step in enumerate((0, last)):
            cuts.append(
                (len(target_sizes), part * piece, entry(1, step, at), piece, groups_of(step, at))
            )
        target_sizes.append(2 * piece)
    for step in order[1:-1]:
        cuts.append((len(target_sizes), 0, entry(1, step), static, entry(3, step)))
        cuts.append(
            (len(target_sizes), static, over(entry(1, step)), static, groups_over(step))
        )
        target_sizes.append(2 * static)
    table, *first = pl.pallas_call(
        functools.partial(
            sort_kernel,
            (species, levels, columns, tiles, wide_count, narrow_count, pair_total, cuts,
             len(target_sizes)),
        ),
        grid=(columns // SORT_COLUMNS,),
        in_specs=[full, full, full,
                  pl.BlockSpec((species, levels, SORT_COLUMNS), lambda at: (0, 0, at))],
        out_specs=[full] + [hbm] * len(target_sizes),
        out_shape=[jax.ShapeDtypeStruct((8, LANES), jnp.int32)]
        + [rows_type(size) for size in target_sizes],
        scratch_shapes=[
            pltpu.VMEM((1, columns), jnp.int32),
            pltpu.VMEM((tiles * LANES, LANES), jnp.float32),
            pltpu.VMEM((LANES * 8, LANES), jnp.float32),
            pltpu.VMEM(((columns + 8 * pair_total) * 8, LANES), jnp.float32),
            pltpu.VMEM((sum(cut[3] for cut in cuts),) + row_shape, jnp.float32),
            pltpu.SMEM((1, columns), jnp.int32),
            pltpu.SMEM((8, LANES), jnp.int32),
            pltpu.SemaphoreType.DMA(()),
            pltpu.SemaphoreType.DMA((len(cuts),)),
        ],
        compiler_params=params,
        name="sort_columns",
    )(
        phys_index.reshape(1, columns),
        column_rate.reshape(1, columns),
        iter_count.reshape(1, columns),
        tracers.transpose(1, 0, 2),
    )
    local_rows = first[2 + len(moving)]
    raw_groups = dict(zip(order[1:-1], first[3 + len(moving):]))
    units = [
        (jnp.maximum(table[3, step * WIN] - static, 0) + UNIT - 1) // UNIT for step in order
    ]
    loss_pad = jnp.pad(loss_rate, (0, pad - species)).reshape(pad, 1)
    coupling_pad = jnp.pad(coupling, ((0, pad - species), (0, pad - species)))
    block = INT_ROWS // 8

    def integrate(operands, loads, merges, blocks, stores):
        groups = max([to + size for _, _, size, to in loads] + [begin + block for begin, _ in blocks])
        groups += static
        flops = 2 * levels * pad * pad * 6 * INT_ROWS * len(blocks)
        return pl.pallas_call(
            functools.partial(
                integrate_kernel, (levels, pad, tiles),
                (loads, merges, blocks, stores, len(operands)),
            ),
            in_specs=[smem, full, full] + [hbm] * len(operands),
            out_specs=[hbm] * len(stores),
            out_shape=[rows_type(size) for _, size in stores],
            scratch_shapes=[
                pltpu.VMEM((groups,) + row_shape, jnp.float32),
                pltpu.VMEM((INT_ROWS // LANES, tiles * LANES, LANES), jnp.float32),
                pltpu.VMEM((levels, pad, INT_ROWS), jnp.float32),
                pltpu.VMEM((pad, INT_ROWS), jnp.float32),
                pltpu.SMEM((2, LANES), jnp.int32),
                pltpu.SemaphoreType.DMA((len(loads),)),
                pltpu.SemaphoreType.DMA((len(stores),)),
            ],
            compiler_params=params,
            cost_estimate=pl.CostEstimate(
                flops=flops, bytes_accessed=8 * groups * 8 * tiles * LANES,
                transcendentals=flops // (2 * pad),
            ),
            name="integrate_columns",
        )(table, loss_pad, coupling_pad, *operands)

    def rows_of(step, at=0):
        return entry(0, step, at)

    def group_blocks(begin, step):
        return [
            (begin + part * block,
             lambda table, part=part: table[3, step * WIN] * 8 - part * INT_ROWS)
            for part in range(2 * static // block)
        ]

    def here(begin):
        return lambda table: jnp.int32(begin)

    def step_over(step, units, rest):
        def leaf(units, rest):
            if units == 0:
                return jnp.zeros_like(rest)
            got = from_behind(rest[:units * UNIT], "narrow", step)
            return jnp.pad(got, ((0, static - units * UNIT), (0, 0), (0, 0), (0, 0)))

        leaves = [functools.partial(leaf, count) for count in range(static // UNIT + 1)]
        return lax.switch(units, leaves, rest)

    pieces = {}
    outgoing = first[:2]
    wide_now = list(first[2:2 + len(moving)])
    keys_now = [[(at, 0), (at, last)] for at in moving]
    static_part = from_behind(outgoing[0], "narrow", order[0])
    wide_got = [from_behind(value, "wide", at - 1) for value, at in zip(wide_now, moving)]
    for phase, step in enumerate(order):
        operands, loads, merges, blocks, stores, named = [], [], [], [], [], []
        used = 0
        if phase + 1 < len(order):
            coming = order[phase + 1]
            if coming == last:
                operands += [pieces[at, last][0] for at in moving] + [local_rows]
                for index, at in enumerate(moving):
                    loads.append((index, here(pieces[at, last][1]), piece, 2 * static + at * piece))
                loads.append((len(moving), here(piece), piece, 2 * static + piece))
                for at in range(WIN):
                    merges.append(
                        (2 * static + at * piece, groups_of(last, at), entry(2, last, at))
                    )
                used = 2 * static + WIN * piece
            else:
                operands.append(raw_groups[coming])
                loads.append((0, None, 2 * static, 0))
                used = 2 * static
            blocks += group_blocks(0, coming)
            stores += [(here(0), static), (here(static), static)]
        extra = []
        if phase == 0:
            extra.append(((1, 0), (local_rows, 0)))
        if phase == 1:
            extra += [((at, 0), pieces[at, 0]) for at in moving]
        if phase == 2:
            extra += [((at, order[0]), pieces[at, order[0]]) for at in range(WIN)]
        used = -(-used // block) * block
        for key, value in extra:
            operands.append(value[0])
            loads.append((len(operands) - 1, here(value[1]), piece, used))
            blocks.append((used, rows_of(key[1], key[0])))
            stores.append((here(used), piece))
            named.append(key)
            used += block
        if stores:
            results = integrate(operands, loads, merges, blocks, stores)
        else:
            results = []
        rest = outgoing[1]
        if phase == 0:
            static_part, results, rest, wide_got, units = lax.optimization_barrier(
                (static_part, results, rest, wide_got, units)
            )
        else:
            static_part, results, rest = lax.optimization_barrier((static_part, results, rest))
        done = {key: (value, 0) for key, value in zip(named, results[len(results) - len(named):])}
        outgoing = results[:len(results) - len(named)]
        arrived = [static_part, step_over(step, units[phase], rest)]
        if step != last:
            arrived, outgoing = lax.optimization_barrier((arrived, outgoing))
            static_part = from_behind(outgoing[0], "narrow", order[phase + 1])
        if step != last:
            cut = pl.pallas_call(
                functools.partial(cut_kernel, static, step),
                in_specs=[smem] + [hbm] * len(arrived),
                out_specs=[hbm] * WIN,
                out_shape=[rows_type(piece)] * WIN,
                scratch_shapes=[
                    pltpu.VMEM((3 * static,) + row_shape, jnp.float32),
                    pltpu.SemaphoreType.DMA((len(arrived),)),
                    pltpu.SemaphoreType.DMA((WIN,)),
                ],
                compiler_params=params,
                name="cut_pieces",
            )(table, *arrived)
            if phase > 0:
                cut, wide_got = lax.optimization_barrier((cut, wide_got))
        for keys, value in zip(keys_now, wide_got):
            pieces.update({key: (value, part * piece) for part, key in enumerate(keys)})
        pieces.update(done)
        if step != last:
            pieces[1, step] = (cut[1], 0)
            keys_now = [[(at, step)] for at in moving]
            wide_got = [from_behind(cut[at], "wide", at - 1) for at in moving]

    held = [pieces[at, step] for step in range(last) for at in range(WIN)]
    buffers = [value for value, _ in held] + arrived
    updated = pl.pallas_call(
        functools.partial(
            finish_kernel,
            (species, levels, columns, tiles, static, narrow_count, [begin for _, begin in held]),
        ),
        in_specs=[smem] + [hbm] * len(buffers),
        out_specs=hbm,
        out_shape=jax.ShapeDtypeStruct((species, levels, columns), jnp.float32),
        scratch_shapes=[
            pltpu.VMEM((pair_total - WIN, piece) + row_shape, jnp.float32),
            pltpu.VMEM((3 * static,) + row_shape, jnp.float32),
            pltpu.VMEM((tiles, columns + 8, LANES), jnp.float32),
            pltpu.VMEM((species, levels, columns), jnp.float32),
            pltpu.SemaphoreType.DMA((2, pair_total)),
            pltpu.SemaphoreType.DMA((columns // LANES,)),
        ],
        compiler_params=params,
        name="place_columns",
    )(table, *buffers)
    return updated.transpose(1, 0, 2)


def solution(mesh):
    placed = (
        P(None, None, ("wide", "narrow")),
        P(("wide", "narrow")),
        P(),
        P(),
        P(("wide", "narrow")),
        P(("wide", "narrow")),
    )
    return jax.shard_map(
        local,
        mesh=mesh,
        in_specs=placed,
        out_specs=P(None, None, ("wide", "narrow")),
        check_vma=False,
    )
```

```python
import functools

import jax
import jax.numpy as jnp
from jax import lax
from jax.experimental import pallas as pl
from jax.experimental.pallas import tpu as pltpu
from jax.sharding import PartitionSpec as P

WIN = 4
MAXIT = 12
LANES = 128
SORT_COLUMNS = 256
INT_ROWS = 256
UNIT = 8
VMEM = 60 * 1024 * 1024


def from_behind(value, axis, steps):
    count = lax.axis_size(axis)
    pairs = [(source, (source + steps) % count) for source in range(count)]
    return lax.ppermute(value, axis, pairs)


def log2(value):
    bits = value.bit_length() - 1
    assert 1 << bits == value
    return bits


def span_of(group, groups, tiles):
    return pl.ds(pl.multiple_of(group * 8 * tiles, 8), groups * 8 * tiles)


def sort_kernel(sizes, phys_ref, rate_ref, count_ref, tracers_ref, table_ref, *rest):
    species, levels, columns, tiles, wide_count, narrow_count, pair_total = sizes[:7]
    cuts, targets = sizes[7:]
    cut_refs, scratch = rest[:targets], rest[targets:]
    pos_ref, turn_ref, wide_ref, sorted_ref, at_ref, table_smem, sem_ref, out_sem = scratch
    step = pl.program_id(0)
    lanes = tiles * LANES
    real = species * levels

    @pl.when(step == 0)
    def _():
        phys = phys_ref[...]
        target = lax.shift_right_logical(phys, log2(columns))
        slot = phys & (columns - 1)
        wide_step = lax.shift_right_logical(target, log2(narrow_count)) - lax.axis_index("wide")
        wide_step = (wide_step + 1) & (wide_count - 1)
        narrow_step = ((target & (narrow_count - 1)) - lax.axis_index("narrow")) & (narrow_count - 1)
        pair = narrow_step * WIN + wide_step
        member = pair == lax.broadcasted_iota(jnp.int32, (pair_total, columns), 0)
        counts = jnp.sum(jnp.where(member, 1.0, 0.0), axis=1, keepdims=True)
        slot_f = slot.astype(jnp.float32)
        starts = jnp.min(jnp.where(member, slot_f, float(columns)), axis=1, keepdims=True)
        groups = lax.shift_right_logical(counts.astype(jnp.int32) + 7, 3).astype(jnp.float32)
        lane = lax.broadcasted_iota(jnp.int32, (pair_total, LANES), 1)
        row = lax.broadcasted_iota(jnp.int32, (pair_total, LANES), 0)

        def across(value):
            return jnp.sum(jnp.where(lane == row, value, 0.0), axis=0, keepdims=True)

        groups_t = across(groups)
        base = jnp.sum(jnp.where(lane < row, groups_t, 0.0), axis=1, keepdims=True)
        section = row & -WIN
        inner = base - jnp.sum(jnp.where(lane < section, groups_t, 0.0), axis=1, keepdims=True)
        same = (lane & -WIN) == section
        in_step = jnp.sum(jnp.where(same, groups_t, 0.0), axis=1, keepdims=True)
        pos = slot_f + jnp.sum(jnp.where(member, base * 8.0 - starts, 0.0), axis=0, keepdims=True)
        pos_ref[...] = pos.astype(jnp.int32)
        copy = pltpu.make_async_copy(pos_ref, at_ref, sem_ref)
        copy.start()
        table_ref[...] = jnp.zeros_like(table_ref)
        for at, value in enumerate((counts, base, inner, in_step)):
            table_ref[at:at + 1, :] = across(value).astype(jnp.int32)
        copy.wait()
        copy = pltpu.make_async_copy(table_ref, table_smem, sem_ref)
        copy.start()
        copy.wait()

    block = tracers_ref.shape[2]
    begin = step * block
    in_group = lax.broadcasted_iota(jnp.int32, (8, LANES), 0)
    for half in range(block // LANES):
        span = slice(half * LANES, (half + 1) * LANES)
        at = pl.ds(pl.multiple_of(begin + half * LANES, LANES), LANES)
        turn_ref[lanes - 16:lanes, :] = jnp.zeros((16, LANES), jnp.float32)
        turn_ref[0:real, :] = tracers_ref[:, :, span].reshape(real, LANES)
        extra = jnp.where(in_group == 5, (phys_ref[:, at] & (columns - 1)).astype(jnp.float32), 0.0)
        extra = jnp.where(in_group == 6, rate_ref[:, at], extra)
        extra = jnp.where(in_group == 7, count_ref[:, at].astype(jnp.float32), extra)
        turn_ref[lanes - 8:lanes, :] = extra
        for tile in range(tiles):
            wide_ref[pl.ds(tile, LANES, stride=8), :] = turn_ref[
                tile * LANES:(tile + 1) * LANES, :
            ].T

        def move(part, carry):
            for extra_row in range(16):
                column = part * 16 + extra_row
                to = at_ref[0, begin + half * LANES + column] * tiles
                record = wide_ref[pl.ds(pl.multiple_of(column * 8, 8), 8), :]
                sorted_ref[pl.ds(to, tiles), :] = record[:tiles]
            return carry

        lax.fori_loop(0, LANES // 16, move, 0)

    @pl.when(step == pl.num_programs(0) - 1)
    def _():
        copies = []
        for index, (target, to, begin, size, valid) in enumerate(cuts):
            wanted = valid(table_smem) > 0
            copy = pltpu.make_async_copy(
                sorted_ref.at[span_of(begin(table_smem), size, tiles)],
                cut_refs[target].at[span_of(to, size, tiles)],
                out_sem.at[index],
            )
            pl.when(wanted)(copy.start)
            copies.append((wanted, copy))
        wait_all(copies)


def start_arrival(refs, sems, room_ref, in_step, static, tiles):
    waits = []
    for index, wanted in enumerate((None, in_step > static)):
        copy = pltpu.make_async_copy(
            refs[index], room_ref.at[span_of(index * static, static, tiles)], sems(index)
        )
        if wanted is None:
            copy.start()
        else:
            pl.when(wanted)(copy.start)
        waits.append((wanted, copy))
    return waits


def wait_all(waits):
    for wanted, copy in waits:
        if wanted is None:
            copy.wait()
        else:
            pl.when(wanted)(copy.wait)


def integrate_block(sizes, room_ref, first, valid, loss_ref, coupling_ref,
                    turn_ref, y_ref, inverse_ref):
    levels, pad, tiles = sizes
    halves = INT_ROWS // LANES
    lanes = tiles * LANES
    first = pl.multiple_of(first * 8 * tiles, 8)
    for half in range(halves):
        begin = first + half * LANES * tiles
        for tile in range(tiles):
            block = room_ref[pl.ds(begin + tile, LANES, stride=tiles), :]
            turn_ref[half, tile * LANES:(tile + 1) * LANES, :] = block.T
        for level in range(levels):
            y_ref[level, :, half * LANES:(half + 1) * LANES] = turn_ref[
                half, pl.ds(level, pad, stride=levels), :
            ]
    rate = jnp.concatenate(
        [turn_ref[half, lanes - 2:lanes - 1, :] for half in range(halves)], axis=1
    )
    count = jnp.concatenate(
        [turn_ref[half, lanes - 1:lanes, :] for half in range(halves)], axis=1
    )
    lane = lax.broadcasted_iota(jnp.int32, (1, INT_ROWS), 1)
    count = jnp.where((lane < valid) & (count <= MAXIT), count, 0.0)
    step_len = rate / jnp.maximum(count, 1.0)
    inverse_ref[...] = 1.0 / (1.0 + step_len * loss_ref[...])
    last = jnp.max(count).astype(jnp.int32)

    def advance(k, carry):
        active = k.astype(jnp.float32) < count

        def one_level(level, inner):
            y = y_ref[level]
            squashed = jnp.tanh(y).astype(jnp.bfloat16)
            produced = jnp.dot(coupling_ref[...], squashed, preferred_element_type=jnp.float32)
            y_ref[level] = jnp.where(active, (y + step_len * produced) * inverse_ref[...], y)
            return inner

        for level in range(levels):
            one_level(level, 0)
        return carry

    lax.fori_loop(0, last, advance, 0)
    for half in range(halves):
        begin = first + half * LANES * tiles
        for level in range(levels):
            turn_ref[half, pl.ds(level, pad, stride=levels), :] = y_ref[
                level, :, half * LANES:(half + 1) * LANES
            ]
        for tile in range(tiles):
            block = turn_ref[half, tile * LANES:(tile + 1) * LANES, :]
            room_ref[pl.ds(begin + tile, LANES, stride=tiles), :] = block.T


def integrate_kernel(sizes, plan, table_ref, loss_ref, coupling_ref, *refs):
    loads, merges, blocks, stores, operands = plan
    tiles = sizes[2]
    sources = refs[:operands]
    results = refs[operands:operands + len(stores)]
    room_ref, turn_ref, y_ref, inverse_ref, rows_ref, sem_ref, out_sem = refs[
        operands + len(stores):
    ]
    copies = []
    for index, (source, begin, groups, to) in enumerate(loads):
        ref = sources[source]
        if begin is not None:
            ref = ref.at[span_of(begin(table_ref), groups, tiles)]
        copies.append(pltpu.make_async_copy(
            ref, room_ref.at[span_of(to, groups, tiles)], sem_ref.at[index]
        ))
    for copy in copies:
        copy.start()
    for copy in copies:
        copy.wait()
    for begin, groups, to in merges:
        to = to(table_ref)

        def move(group, carry):
            room_ref[span_of(to + group, 1, tiles), :] = room_ref[
                span_of(begin + group, 1, tiles), :
            ]
            return carry

        lax.fori_loop(0, groups(table_ref), move, 0)
    for index, (begin, rows) in enumerate(blocks):
        rows_ref[0, index] = jnp.int32(begin)
        rows_ref[1, index] = rows(table_ref)

    def one_block(index, carry):
        valid = rows_ref[1, index]

        @pl.when(valid > 0)
        def _():
            integrate_block(sizes, room_ref, rows_ref[0, index], valid, loss_ref, coupling_ref,
                            turn_ref, y_ref, inverse_ref)

        return carry

    lax.fori_loop(0, len(blocks), one_block, 0)
    copies = []
    for index, (begin, groups) in enumerate(stores):
        copies.append(pltpu.make_async_copy(
            room_ref.at[span_of(begin(table_ref), groups, tiles)], results[index],
            out_sem.at[index],
        ))
    for copy in copies:
        copy.start()
    for copy in copies:
        copy.wait()


def cut_kernel(static, tiles, piece, step, table_ref, *refs):
    pieces = refs[2:2 + WIN]
    room_ref, sem_ref, out_sem = refs[2 + WIN:]
    wait_all(start_arrival(refs[:2], lambda at: sem_ref.at[at], room_ref,
                           table_ref[3, step * WIN], static, tiles))
    copies = []
    half = piece // 2
    for at in range(WIN):
        begin = table_ref[2, step * WIN + at]
        for part in range(2):
            wanted = table_ref[0, step * WIN + at] > part * half * 8
            copy = pltpu.make_async_copy(
                room_ref.at[span_of(begin + part * half, half, tiles)],
                pieces[at].at[span_of(part * half, half, tiles)], out_sem.at[part, at],
            )
            pl.when(wanted)(copy.start)
            copies.append((wanted, copy))
    wait_all(copies)


def finish_kernel(sizes, table_ref, *refs):
    species, levels, columns, tiles, static, piece, narrow_count, begins = sizes
    pair_total = narrow_count * WIN
    whole_pieces = pair_total - WIN
    (out_ref, head_ref, slot_ref, piece_ref, room_ref, placed_ref, whole_ref, start_ref, sem_ref,
     head_sem, out_sem) = refs[-11:]
    heads = []
    for pair in range(pair_total):
        to = head_ref.at[pl.ds(pair * 8, 8)]
        if pair < whole_pieces:
            source = refs[pair].at[pl.ds(begins[pair] * 8 * tiles, 8)]
            heads.append((None, pltpu.make_async_copy(source, to, head_sem.at[pair])))
            heads[-1][1].start()
        else:
            begin = table_ref[2, pair]
            for part in range(2):
                wanted = (begin < static) if part == 0 else (begin >= static)
                inside = jnp.clip(begin - part * static, 0, static - 1)
                source = refs[whole_pieces + part].at[
                    pl.ds(pl.multiple_of(inside * 8 * tiles, 8), 8)
                ]
                copy = pltpu.make_async_copy(source, to, head_sem.at[pair + part * WIN])
                pl.when(wanted)(copy.start)
                heads.append((wanted, copy))
    copies = []
    half = piece // 2
    for pair in range(whole_pieces):
        both = []
        for part in range(2):
            copy = pltpu.make_async_copy(
                refs[pair].at[span_of(begins[pair] + part * half, half, tiles)],
                piece_ref.at[pair, span_of(part * half, half, tiles)], sem_ref.at[part, pair],
            )
            wanted = table_ref[0, pair] > part * half * 8
            pl.when(wanted)(copy.start)
            both.append((wanted, copy))
        copies.append(both)
    waits = start_arrival(refs[whole_pieces:whole_pieces + 2],
                          lambda at: sem_ref.at[at, whole_pieces], room_ref,
                          table_ref[3, whole_pieces], static, tiles)
    wait_all(heads)
    first = head_ref[pl.ds(tiles - 1, pair_total, stride=8), :]
    lane = lax.broadcasted_iota(jnp.int32, first.shape, 1)
    first = jnp.max(jnp.where(lane == LANES - 3, first, 0.0), axis=1, keepdims=True)
    slot_ref[...] = jnp.broadcast_to(first, slot_ref.shape).astype(jnp.int32)
    copy = pltpu.make_async_copy(slot_ref, start_ref, head_sem.at[pair_total + WIN])
    copy.start()
    copy.wait()
    in_group = lax.broadcasted_iota(jnp.int32, (8, LANES), 0)
    for pair in range(pair_total):
        if pair < whole_pieces:
            wait_all(copies[pair])
            held = piece_ref.at[pair]
            begin = 0
        else:
            if pair == whole_pieces:
                wait_all(waits)
            held = room_ref
            begin = pl.multiple_of(table_ref[2, pair] * 8 * tiles, 8)
        count = table_ref[0, pair]
        start = jnp.clip(start_ref[pair, 0], 0, columns - 1) * tiles
        full = lax.shift_right_logical(count, 3)

        def move(group, carry):
            for row in range(0, 8 * tiles, 8):
                at = group * 8 * tiles + row
                placed_ref[pl.ds(start + at, 8), :] = held[pl.ds(pl.multiple_of(begin + at, 8), 8), :]
            return carry

        lax.fori_loop(0, full, move, 0)

        @pl.when((count & 7) > 0)
        def _():
            for row in range(0, 8 * tiles, 8):
                at = full * 8 * tiles + row
                to = pl.ds(start + at, 8)
                placed_ref[to, :] = jnp.where(
                    in_group + row < (count & 7) * tiles,
                    held[pl.ds(pl.multiple_of(begin + at, 8), 8), :], placed_ref[to, :],
                )

    per_tile = LANES // levels
    for part in range(columns // LANES):
        at = slice(part * LANES, (part + 1) * LANES)
        for tile in range(tiles):
            block = placed_ref[pl.ds(part * LANES * tiles + tile, LANES, stride=tiles), :]
            block = block.T.reshape(per_tile, levels, LANES)
            keep = min(per_tile, species - tile * per_tile)
            whole_ref[tile * per_tile:tile * per_tile + keep, :, at] = block[:keep]
        pltpu.make_async_copy(whole_ref.at[:, :, at], out_ref.at[:, :, at], out_sem.at[part]).start()
    for part in range(columns // LANES):
        at = slice(part * LANES, (part + 1) * LANES)
        pltpu.make_async_copy(whole_ref.at[:, :, at], out_ref.at[:, :, at], out_sem.at[part]).wait()


def local(tracers, column_rate, loss_rate, coupling, phys_index, iter_count):
    levels, species, columns = tracers.shape
    wide_count = lax.axis_size("wide")
    narrow_count = lax.axis_size("narrow")
    pair_total = WIN * narrow_count
    room = 2 * columns // pair_total
    piece = room // 8
    pad = -(-species // 8) * 8
    while levels * pad % LANES or levels * (pad - species) < 8:
        pad += 8
    tiles = levels * pad // LANES
    static = columns // narrow_count // 8
    full = pl.BlockSpec(memory_space=pltpu.VMEM)
    smem = pl.BlockSpec(memory_space=pltpu.SMEM)
    hbm = pl.BlockSpec(memory_space=pltpu.HBM)
    last = narrow_count - 1
    moving = [at for at in range(WIN) if at != 1]
    order = [narrow_count // 2]
    order += [step for step in range(1, last) if step not in order] + [last]
    params = pltpu.CompilerParams(vmem_limit_bytes=VMEM)

    def rows_type(groups):
        return jax.ShapeDtypeStruct((groups * 8 * tiles, LANES), jnp.float32)

    def room_type(groups):
        return pltpu.VMEM((groups * 8 * tiles, LANES), jnp.float32)

    def entry(row, step, at=0):
        return lambda table: table[row, step * WIN + at]

    def over(begin):
        return lambda table: begin(table) + static

    def groups_of(step, at):
        return lambda table: lax.shift_right_logical(table[0, step * WIN + at] + 7, 3)

    def groups_over(step):
        return lambda table: table[3, step * WIN] - static

    cuts = [
        (0, 0, entry(1, order[0]), static, entry(3, order[0])),
        (1, 0, over(entry(1, order[0])), static, groups_over(order[0])),
    ]
    target_sizes = [static, static]
    for at in moving + [1]:
        for part, step in enumerate((0, last)):
            for half in range(0, piece, piece // 2):
                cuts.append((
                    len(target_sizes), part * piece + half,
                    lambda table, step=step, at=at, half=half: entry(1, step, at)(table) + half,
                    piece // 2,
                    lambda table, step=step, at=at, half=half: groups_of(step, at)(table) - half,
                ))
        target_sizes.append(2 * piece)
    for step in order[1:-1]:
        cuts.append((len(target_sizes), 0, entry(1, step), static, entry(3, step)))
        cuts.append(
            (len(target_sizes), static, over(entry(1, step)), static, groups_over(step))
        )
        target_sizes.append(2 * static)
    table, *first = pl.pallas_call(
        functools.partial(
            sort_kernel,
            (species, levels, columns, tiles, wide_count, narrow_count, pair_total, cuts,
             len(target_sizes)),
        ),
        grid=(columns // SORT_COLUMNS,),
        in_specs=[full, full, full,
                  pl.BlockSpec((species, levels, SORT_COLUMNS), lambda at: (0, 0, at))],
        out_specs=[full] + [hbm] * len(target_sizes),
        out_shape=[jax.ShapeDtypeStruct((8, LANES), jnp.int32)]
        + [rows_type(size) for size in target_sizes],
        scratch_shapes=[
            pltpu.VMEM((1, columns), jnp.int32),
            pltpu.VMEM((tiles * LANES, LANES), jnp.float32),
            pltpu.VMEM((LANES * 8, LANES), jnp.float32),
            room_type(columns // 8 + pair_total + 2 * static),
            pltpu.SMEM((1, columns), jnp.int32),
            pltpu.SMEM((8, LANES), jnp.int32),
            pltpu.SemaphoreType.DMA(()),
            pltpu.SemaphoreType.DMA((len(cuts),)),
        ],
        compiler_params=params,
        name="sort_columns",
    )(
        phys_index.reshape(1, columns),
        column_rate.reshape(1, columns),
        iter_count.reshape(1, columns),
        tracers.transpose(1, 0, 2),
    )
    local_rows = first[2 + len(moving)]
    raw_groups = dict(zip(order[1:-1], first[3 + len(moving):]))
    units = [
        (jnp.maximum(table[3, step * WIN] - static, 0) + UNIT - 1) // UNIT for step in order
    ]
    loss_pad = jnp.pad(loss_rate, (0, pad - species)).reshape(pad, 1)
    coupling_pad = jnp.pad(coupling, ((0, pad - species), (0, pad - species)))
    block = INT_ROWS // 8

    def integrate(operands, loads, merges, blocks, stores):
        groups = max([to + size for _, _, size, to in loads] + [begin + block for begin, _ in blocks])
        groups += static
        flops = 2 * levels * pad * pad * 6 * INT_ROWS * len(blocks)
        return pl.pallas_call(
            functools.partial(
                integrate_kernel, (levels, pad, tiles),
                (loads, merges, blocks, stores, len(operands)),
            ),
            in_specs=[smem, full, full] + [hbm] * len(operands),
            out_specs=[hbm] * len(stores),
            out_shape=[rows_type(size) for _, size in stores],
            scratch_shapes=[
                room_type(groups),
                pltpu.VMEM((INT_ROWS // LANES, tiles * LANES, LANES), jnp.float32),
                pltpu.VMEM((levels, pad, INT_ROWS), jnp.float32),
                pltpu.VMEM((pad, INT_ROWS), jnp.float32),
                pltpu.SMEM((2, LANES), jnp.int32),
                pltpu.SemaphoreType.DMA((len(loads),)),
                pltpu.SemaphoreType.DMA((len(stores),)),
            ],
            compiler_params=params,
            cost_estimate=pl.CostEstimate(
                flops=flops, bytes_accessed=8 * groups * 8 * tiles * LANES,
                transcendentals=flops // (2 * pad),
            ),
            name="integrate_columns",
        )(table, loss_pad, coupling_pad, *operands)

    def rows_of(step, at=0):
        return entry(0, step, at)

    def group_blocks(begin, step):
        return [
            (begin + part * block,
             lambda table, part=part: table[3, step * WIN] * 8 - part * INT_ROWS)
            for part in range(2 * static // block)
        ]

    def here(begin):
        return lambda table: jnp.int32(begin)

    def step_over(step, units, rest):
        def leaf(units, rest):
            if units == 0:
                return jnp.zeros_like(rest)
            got = from_behind(rest[:units * UNIT * 8 * tiles], "narrow", step)
            return jnp.pad(got, ((0, rest.shape[0] - got.shape[0]), (0, 0)))

        leaves = [functools.partial(leaf, count) for count in range(static // UNIT + 1)]
        return lax.switch(units, leaves, rest)

    pieces = {}
    outgoing = first[:2]
    wide_now = list(first[2:2 + len(moving)])
    keys_now = [[(at, 0), (at, last)] for at in moving]
    static_part = from_behind(outgoing[0], "narrow", order[0])
    wide_got = [from_behind(value, "wide", at - 1) for value, at in zip(wide_now, moving)]
    for phase, step in enumerate(order):
        operands, loads, merges, blocks, stores, named = [], [], [], [], [], []
        used = 0
        if phase + 1 < len(order):
            coming = order[phase + 1]
            if coming == last:
                operands += [pieces[at, last][0] for at in moving] + [local_rows]
                for index, at in enumerate(moving):
                    loads.append((index, here(pieces[at, last][1]), piece, 2 * static + at * piece))
                loads.append((len(moving), here(piece), piece, 2 * static + piece))
                for at in range(WIN):
                    merges.append(
                        (2 * static + at * piece, groups_of(last, at), entry(2, last, at))
                    )
                used = 2 * static + WIN * piece
            else:
                operands.append(raw_groups[coming])
                loads.append((0, None, 2 * static, 0))
                used = 2 * static
            blocks += group_blocks(0, coming)
            stores += [(here(0), static), (here(static), static)]
        extra = []
        if phase == 0:
            extra.append(((1, 0), (local_rows, 0)))
        if phase == 1:
            extra += [((at, 0), pieces[at, 0]) for at in moving]
        if phase == 2:
            extra += [((at, order[0]), pieces[at, order[0]]) for at in range(WIN)]
        used = -(-used // block) * block
        for key, value in extra:
            operands.append(value[0])
            loads.append((len(operands) - 1, here(value[1]), piece, used))
            blocks.append((used, rows_of(key[1], key[0])))
            stores.append((here(used), piece))
            named.append(key)
            used += block
        if stores:
            results = integrate(operands, loads, merges, blocks, stores)
        else:
            results = []
        rest = outgoing[1]
        if phase == 0:
            static_part, results, rest, wide_got, units = lax.optimization_barrier(
                (static_part, results, rest, wide_got, units)
            )
        else:
            static_part, results, rest = lax.optimization_barrier((static_part, results, rest))
        done = {key: (value, 0) for key, value in zip(named, results[len(results) - len(named):])}
        outgoing = results[:len(results) - len(named)]
        arrived = [static_part, step_over(step, units[phase], rest)]
        if step != last:
            arrived, outgoing = lax.optimization_barrier((arrived, outgoing))
            static_part = from_behind(outgoing[0], "narrow", order[phase + 1])
        if step != last:
            cut = pl.pallas_call(
                functools.partial(cut_kernel, static, tiles, piece, step),
                in_specs=[smem] + [hbm] * len(arrived),
                out_specs=[hbm] * WIN,
                out_shape=[rows_type(piece)] * WIN,
                scratch_shapes=[
                    room_type(3 * static),
                    pltpu.SemaphoreType.DMA((len(arrived),)),
                    pltpu.SemaphoreType.DMA((2, WIN)),
                ],
                compiler_params=params,
                name="cut_pieces",
            )(table, *arrived)
            if phase > 0:
                cut, wide_got = lax.optimization_barrier((cut, wide_got))
        for keys, value in zip(keys_now, wide_got):
            pieces.update({key: (value, part * piece) for part, key in enumerate(keys)})
        pieces.update(done)
        if step != last:
            pieces[1, step] = (cut[1], 0)
            keys_now = [[(at, step)] for at in moving]
            wide_got = [from_behind(cut[at], "wide", at - 1) for at in moving]

    held = [pieces[at, step] for step in range(last) for at in range(WIN)]
    buffers = [value for value, _ in held] + arrived
    updated = pl.pallas_call(
        functools.partial(
            finish_kernel,
            (species, levels, columns, tiles, static, piece, narrow_count,
             [begin for _, begin in held]),
        ),
        in_specs=[smem] + [hbm] * len(buffers),
        out_specs=hbm,
        out_shape=jax.ShapeDtypeStruct((species, levels, columns), jnp.float32),
        scratch_shapes=[
            pltpu.VMEM((pair_total * 8, LANES), jnp.float32),
            pltpu.VMEM((pair_total, LANES), jnp.int32),
            pltpu.VMEM((pair_total - WIN, piece * 8 * tiles, LANES), jnp.float32),
            room_type(3 * static),
            room_type(columns // 8 + 1),
            pltpu.VMEM((species, levels, columns), jnp.float32),
            pltpu.SMEM((pair_total, LANES), jnp.int32),
            pltpu.SemaphoreType.DMA((2, pair_total)),
            pltpu.SemaphoreType.DMA((pair_total + WIN + 1,)),
            pltpu.SemaphoreType.DMA((columns // LANES,)),
        ],
        compiler_params=params,
        name="place_columns",
    )(table, *buffers)
    return updated.transpose(1, 0, 2)


def solution(mesh):
    placed = (
        P(None, None, ("wide", "narrow")),
        P(("wide", "narrow")),
        P(),
        P(),
        P(("wide", "narrow")),
        P(("wide", "narrow")),
    )
    return jax.shard_map(
        local,
        mesh=mesh,
        in_specs=placed,
        out_specs=P(None, None, ("wide", "narrow")),
        check_vma=False,
    )
```

```python
import functools

import jax
import jax.numpy as jnp
from jax import lax
from jax.experimental import pallas as pl
from jax.experimental.pallas import tpu as pltpu
from jax.sharding import PartitionSpec as P

WIN = 4
MAXIT = 12
LANES = 128
SORT_COLUMNS = 256
INT_ROWS = 256
UNIT = 8
SPARE = 4 * 1024 * 1024


def from_behind(value, axis, steps):
    count = lax.axis_size(axis)
    pairs = [(source, (source + steps) % count) for source in range(count)]
    return lax.ppermute(value, axis, pairs)


def log2(value):
    bits = value.bit_length() - 1
    assert 1 << bits == value
    return bits


def span_of(group, groups, tiles):
    return pl.ds(pl.multiple_of(group * 8 * tiles, 8), groups * 8 * tiles)


def sort_kernel(sizes, cuts, targets, early, *refs):
    species, levels, columns, tiles, wide_count, narrow_count, pair_total = sizes
    turn_ref, wide_ref, sorted_ref = refs[-4:-1]
    sem_ref = refs[-1]
    if early:
        phys_ref, rate_ref, count_ref, tracers_ref, table_ref, pos_ref = refs[:6]
        cut_refs = refs[6:6 + targets]
        at_ref, table_smem = refs[6 + targets:8 + targets]
    else:
        phys_ref, rate_ref, count_ref, tracers_ref, table_smem, at_ref = refs[:6]
        cut_refs = refs[6:6 + targets]
    step = pl.program_id(0)
    lanes = tiles * LANES
    real = species * levels

    def find_places():
        phys = phys_ref[...]
        target = lax.shift_right_logical(phys, log2(columns))
        slot = phys & (columns - 1)
        wide_step = lax.shift_right_logical(target, log2(narrow_count)) - lax.axis_index("wide")
        wide_step = (wide_step + 1) & (wide_count - 1)
        narrow_step = ((target & (narrow_count - 1)) - lax.axis_index("narrow")) & (narrow_count - 1)
        pair = narrow_step * WIN + wide_step
        member = pair == lax.broadcasted_iota(jnp.int32, (pair_total, columns), 0)
        counts = jnp.sum(jnp.where(member, 1.0, 0.0), axis=1, keepdims=True)
        slot_f = slot.astype(jnp.float32)
        starts = jnp.min(jnp.where(member, slot_f, float(columns)), axis=1, keepdims=True)
        groups = lax.shift_right_logical(counts.astype(jnp.int32) + 7, 3).astype(jnp.float32)
        lane = lax.broadcasted_iota(jnp.int32, (pair_total, LANES), 1)
        row = lax.broadcasted_iota(jnp.int32, (pair_total, LANES), 0)

        def across(value):
            return jnp.sum(jnp.where(lane == row, value, 0.0), axis=0, keepdims=True)

        groups_t = across(groups)
        base = jnp.sum(jnp.where(lane < row, groups_t, 0.0), axis=1, keepdims=True)
        section = row & -WIN
        inner = base - jnp.sum(jnp.where(lane < section, groups_t, 0.0), axis=1, keepdims=True)
        same = (lane & -WIN) == section
        in_step = jnp.sum(jnp.where(same, groups_t, 0.0), axis=1, keepdims=True)
        pos = slot_f + jnp.sum(jnp.where(member, base * 8.0 - starts, 0.0), axis=0, keepdims=True)
        pos_ref[...] = pos.astype(jnp.int32)
        copy = pltpu.make_async_copy(pos_ref, at_ref, sem_ref.at[0])
        copy.start()
        table_ref[...] = jnp.zeros_like(table_ref)
        for at, value in enumerate((counts, base, inner, in_step)):
            table_ref[at:at + 1, :] = across(value).astype(jnp.int32)
        copy.wait()
        copy = pltpu.make_async_copy(table_ref, table_smem, sem_ref.at[0])
        copy.start()
        copy.wait()

    if early:
        pl.when(step == 0)(find_places)
    block = tracers_ref.shape[2]
    begin = step * block
    in_group = lax.broadcasted_iota(jnp.int32, (8, LANES), 0)
    for half in range(block // LANES):
        span = slice(half * LANES, (half + 1) * LANES)
        at = pl.ds(pl.multiple_of(begin + half * LANES, LANES), LANES)
        turn_ref[lanes - 16:lanes, :] = jnp.zeros((16, LANES), jnp.float32)
        turn_ref[0:real, :] = tracers_ref[:, :, span].reshape(real, LANES)
        extra = jnp.where(in_group == 5, (phys_ref[:, at] & (columns - 1)).astype(jnp.float32), 0.0)
        extra = jnp.where(in_group == 6, rate_ref[:, at], extra)
        extra = jnp.where(in_group == 7, count_ref[:, at].astype(jnp.float32), extra)
        turn_ref[lanes - 8:lanes, :] = extra
        for tile in range(tiles):
            wide_ref[pl.ds(tile, LANES, stride=8), :] = turn_ref[
                tile * LANES:(tile + 1) * LANES, :
            ].T

        def move(part, carry):
            for extra_row in range(16):
                column = part * 16 + extra_row
                to = at_ref[0, begin + half * LANES + column] * tiles
                record = wide_ref[pl.ds(pl.multiple_of(column * 8, 8), 8), :]
                sorted_ref[pl.ds(to, tiles), :] = record[:tiles]
            return carry

        lax.fori_loop(0, LANES // 16, move, 0)

    @pl.when(step == pl.num_programs(0) - 1)
    def _():
        copies = []
        for index, (target, to, begin, size, valid) in enumerate(cuts):
            begin = begin(table_smem)
            valid = jnp.clip(valid(table_smem), 0, size)
            if early:
                def keep(group, carry):
                    cut_refs[target][span_of(to + group, 1, tiles), :] = sorted_ref[
                        span_of(begin + group, 1, tiles), :
                    ]
                    return carry

                lax.fori_loop(0, valid, keep, 0)
                continue
            copy = pltpu.make_async_copy(
                sorted_ref.at[span_of(begin, size, tiles)],
                cut_refs[target].at[span_of(to, size, tiles)], sem_ref.at[index],
            )
            pl.when(valid > 0)(copy.start)
            copies.append((valid > 0, copy))
        wait_all(copies)


def start_arrival(refs, sems, room_ref, in_step, static, tiles):
    waits = []
    for index, wanted in enumerate((None, in_step > static)):
        copy = pltpu.make_async_copy(
            refs[index], room_ref.at[pl.ds(index * static * 8 * tiles, refs[index].shape[0])],
            sems(index),
        )
        if wanted is None:
            copy.start()
        else:
            pl.when(wanted)(copy.start)
        waits.append((wanted, copy))
    return waits


def wait_all(waits):
    for wanted, copy in waits:
        if wanted is None:
            copy.wait()
        else:
            pl.when(wanted)(copy.wait)


def integrate_block(sizes, room_ref, first, valid, loss_ref, coupling_ref,
                    turn_ref, y_ref, inverse_ref):
    levels, pad, tiles = sizes
    halves = INT_ROWS // LANES
    lanes = tiles * LANES
    first = pl.multiple_of(first * 8 * tiles, 8)
    for half in range(halves):
        begin = first + half * LANES * tiles
        for tile in range(tiles):
            block = room_ref[pl.ds(begin + tile, LANES, stride=tiles), :]
            turn_ref[half, tile * LANES:(tile + 1) * LANES, :] = block.T
        for level in range(levels):
            y_ref[level, :, half * LANES:(half + 1) * LANES] = turn_ref[
                half, pl.ds(level, pad, stride=levels), :
            ]
    rate = jnp.concatenate(
        [turn_ref[half, lanes - 2:lanes - 1, :] for half in range(halves)], axis=1
    )
    count = jnp.concatenate(
        [turn_ref[half, lanes - 1:lanes, :] for half in range(halves)], axis=1
    )
    lane = lax.broadcasted_iota(jnp.int32, (1, INT_ROWS), 1)
    count = jnp.where((lane < valid) & (count <= MAXIT), count, 0.0)
    step_len = rate / jnp.maximum(count, 1.0)
    inverse_ref[...] = 1.0 / (1.0 + step_len * loss_ref[...])
    last = jnp.max(count).astype(jnp.int32)

    def advance(k, carry):
        active = k.astype(jnp.float32) < count

        def one_level(level, inner):
            y = y_ref[level]
            squashed = jnp.tanh(y).astype(jnp.bfloat16)
            produced = jnp.dot(coupling_ref[...], squashed, preferred_element_type=jnp.float32)
            y_ref[level] = jnp.where(active, (y + step_len * produced) * inverse_ref[...], y)
            return inner

        for level in range(levels):
            one_level(level, 0)
        return carry

    lax.fori_loop(0, last, advance, 0)
    for half in range(halves):
        begin = first + half * LANES * tiles
        for level in range(levels):
            turn_ref[half, pl.ds(level, pad, stride=levels), :] = y_ref[
                level, :, half * LANES:(half + 1) * LANES
            ]
        for tile in range(tiles):
            block = turn_ref[half, tile * LANES:(tile + 1) * LANES, :]
            room_ref[pl.ds(begin + tile, LANES, stride=tiles), :] = block.T


def integrate_kernel(sizes, plan, table_ref, loss_ref, coupling_ref, *refs):
    loads, merges, blocks, stores, operands = plan
    tiles = sizes[2]
    sources = refs[:operands]
    results = refs[operands:operands + len(stores)]
    room_ref, turn_ref, y_ref, inverse_ref, rows_ref, sem_ref, out_sem = refs[
        operands + len(stores):
    ]
    copies = []
    for index, (source, begin, groups, to) in enumerate(loads):
        ref = sources[source]
        if begin is not None:
            ref = ref.at[span_of(begin(table_ref), groups, tiles)]
        copies.append(pltpu.make_async_copy(
            ref, room_ref.at[span_of(to, groups, tiles)], sem_ref.at[index]
        ))
    for copy in copies:
        copy.start()
    for copy in copies:
        copy.wait()
    for begin, groups, to in merges:
        to = to(table_ref)

        def move(group, carry):
            room_ref[span_of(to + group, 1, tiles), :] = room_ref[
                span_of(begin + group, 1, tiles), :
            ]
            return carry

        lax.fori_loop(0, groups(table_ref), move, 0)
    for index, (begin, rows) in enumerate(blocks):
        rows_ref[0, index] = jnp.int32(begin)
        rows_ref[1, index] = rows(table_ref)

    def one_block(index, carry):
        valid = rows_ref[1, index]

        @pl.when(valid > 0)
        def _():
            integrate_block(sizes, room_ref, rows_ref[0, index], valid, loss_ref, coupling_ref,
                            turn_ref, y_ref, inverse_ref)

        return carry

    lax.fori_loop(0, len(blocks), one_block, 0)
    copies = []
    for index, (begin, groups) in enumerate(stores):
        copies.append(pltpu.make_async_copy(
            room_ref.at[span_of(begin(table_ref), groups, tiles)], results[index],
            out_sem.at[index],
        ))
    for copy in copies:
        copy.start()
    for copy in copies:
        copy.wait()


def cut_kernel(static, tiles, piece, step, table_ref, *refs):
    pieces = refs[2:2 + WIN]
    room_ref, sem_ref, out_sem = refs[2 + WIN:]
    wait_all(start_arrival(refs[:2], lambda at: sem_ref.at[at], room_ref,
                           table_ref[3, step * WIN], static, tiles))
    copies = []
    half = piece // 2
    for at in range(WIN):
        begin = table_ref[2, step * WIN + at]
        for part in range(2):
            wanted = table_ref[0, step * WIN + at] > part * half * 8
            copy = pltpu.make_async_copy(
                room_ref.at[span_of(begin + part * half, half, tiles)],
                pieces[at].at[span_of(part * half, half, tiles)], out_sem.at[part, at],
            )
            pl.when(wanted)(copy.start)
            copies.append((wanted, copy))
    wait_all(copies)


def finish_kernel(sizes, table_ref, *refs):
    species, levels, columns, tiles, static, piece, narrow_count, begins = sizes
    pair_total = narrow_count * WIN
    whole_pieces = pair_total - WIN
    (out_ref, head_ref, slot_ref, piece_ref, room_ref, placed_ref, whole_ref, start_ref, sem_ref,
     head_sem, out_sem) = refs[-11:]
    heads = []
    for pair in range(pair_total):
        to = head_ref.at[pl.ds(pair * 8, 8)]
        if pair < whole_pieces:
            source = refs[pair].at[pl.ds(begins[pair] * 8 * tiles, 8)]
            heads.append((None, pltpu.make_async_copy(source, to, head_sem.at[pair])))
            heads[-1][1].start()
        else:
            begin = table_ref[2, pair]
            for part in range(2):
                wanted = (begin < static) if part == 0 else (begin >= static)
                source = refs[whole_pieces + part]
                inside = jnp.clip(begin - part * static, 0, source.shape[0] // (8 * tiles) - 1)
                source = source.at[pl.ds(pl.multiple_of(inside * 8 * tiles, 8), 8)]
                copy = pltpu.make_async_copy(source, to, head_sem.at[pair + part * WIN])
                pl.when(wanted)(copy.start)
                heads.append((wanted, copy))
    copies = []
    half = piece // 2
    for pair in range(whole_pieces):
        both = []
        for part in range(2):
            copy = pltpu.make_async_copy(
                refs[pair].at[span_of(begins[pair] + part * half, half, tiles)],
                piece_ref.at[pair, span_of(part * half, half, tiles)], sem_ref.at[part, pair],
            )
            wanted = table_ref[0, pair] > part * half * 8
            pl.when(wanted)(copy.start)
            both.append((wanted, copy))
        copies.append(both)
    waits = start_arrival(refs[whole_pieces:whole_pieces + 2],
                          lambda at: sem_ref.at[at, whole_pieces], room_ref,
                          table_ref[3, whole_pieces], static, tiles)
    wait_all(heads)
    first = head_ref[pl.ds(tiles - 1, pair_total, stride=8), :]
    lane = lax.broadcasted_iota(jnp.int32, first.shape, 1)
    first = jnp.max(jnp.where(lane == LANES - 3, first, 0.0), axis=1, keepdims=True)
    slot_ref[...] = jnp.broadcast_to(first, slot_ref.shape).astype(jnp.int32)
    copy = pltpu.make_async_copy(slot_ref, start_ref, head_sem.at[pair_total + WIN])
    copy.start()
    copy.wait()
    in_group = lax.broadcasted_iota(jnp.int32, (8, LANES), 0)
    for pair in range(pair_total):
        if pair < whole_pieces:
            wait_all(copies[pair])
            held = piece_ref.at[pair]
            begin = 0
        else:
            if pair == whole_pieces:
                wait_all(waits)
            held = room_ref
            begin = pl.multiple_of(table_ref[2, pair] * 8 * tiles, 8)
        count = table_ref[0, pair]
        start = jnp.clip(start_ref[pair, 0], 0, columns - 1) * tiles
        full = lax.shift_right_logical(count, 3)

        def move(group, carry):
            for row in range(0, 8 * tiles, 8):
                at = group * 8 * tiles + row
                placed_ref[pl.ds(start + at, 8), :] = held[pl.ds(pl.multiple_of(begin + at, 8), 8), :]
            return carry

        lax.fori_loop(0, full, move, 0)

        @pl.when((count & 7) > 0)
        def _():
            for row in range(0, 8 * tiles, 8):
                at = full * 8 * tiles + row
                to = pl.ds(start + at, 8)
                placed_ref[to, :] = jnp.where(
                    in_group + row < (count & 7) * tiles,
                    held[pl.ds(pl.multiple_of(begin + at, 8), 8), :], placed_ref[to, :],
                )

    per_tile = LANES // levels
    for part in range(columns // LANES):
        at = slice(part * LANES, (part + 1) * LANES)
        for tile in range(tiles):
            block = placed_ref[pl.ds(part * LANES * tiles + tile, LANES, stride=tiles), :]
            block = block.T.reshape(per_tile, levels, LANES)
            keep = min(per_tile, species - tile * per_tile)
            whole_ref[tile * per_tile:tile * per_tile + keep, :, at] = block[:keep]
        pltpu.make_async_copy(whole_ref.at[:, :, at], out_ref.at[:, :, at], out_sem.at[part]).start()
    for part in range(columns // LANES):
        at = slice(part * LANES, (part + 1) * LANES)
        pltpu.make_async_copy(whole_ref.at[:, :, at], out_ref.at[:, :, at], out_sem.at[part]).wait()


def local(tracers, column_rate, loss_rate, coupling, phys_index, iter_count):
    levels, species, columns = tracers.shape
    wide_count = lax.axis_size("wide")
    narrow_count = lax.axis_size("narrow")
    pair_total = WIN * narrow_count
    room = 2 * columns // pair_total
    piece = room // 8
    pad = -(-species // 8) * 8
    while levels * pad % LANES or levels * (pad - species) < 8:
        pad += 8
    tiles = levels * pad // LANES
    mean = columns // narrow_count // 8
    full = pl.BlockSpec(memory_space=pltpu.VMEM)
    smem = pl.BlockSpec(memory_space=pltpu.SMEM)
    hbm = pl.BlockSpec(memory_space=pltpu.HBM)
    last = narrow_count - 1
    moving = [at for at in range(WIN) if at != 1]
    order = [narrow_count // 2]
    order += [step for step in range(1, last) if step not in order] + [last]
    statics = {step: mean if step == order[0] else mean + mean // 8 for step in order}
    most = WIN * piece

    def params(groups, extra=0):
        used = groups * 8 * tiles * LANES * 4 + extra
        return pltpu.CompilerParams(vmem_limit_bytes=used + SPARE)

    def rows_type(groups):
        return jax.ShapeDtypeStruct((groups * 8 * tiles, LANES), jnp.float32)

    def room_type(groups):
        return pltpu.VMEM((groups * 8 * tiles, LANES), jnp.float32)

    def entry(row, step, at=0):
        return lambda table: table[row, step * WIN + at]

    def over(step):
        return lambda table: entry(1, step)(table) + statics[step]

    def groups_of(step, at):
        return lambda table: lax.shift_right_logical(table[0, step * WIN + at] + 7, 3)

    def groups_over(step):
        return lambda table: table[3, step * WIN] - statics[step]

    def pair_cuts(target, at):
        return [
            (target, part * piece + half,
             lambda table, step=step, half=half: entry(1, step, at)(table) + half, piece // 2,
             lambda table, step=step, half=half: groups_of(step, at)(table) - half)
            for part, step in enumerate((0, last)) for half in range(0, piece, piece // 2)
        ]

    def sort(cuts, target_sizes, early, known):
        spec = full if early else hbm
        known_types = [
            jax.ShapeDtypeStruct((8, LANES), jnp.int32),
            jax.ShapeDtypeStruct((1, columns), jnp.int32),
        ]
        groups = columns // 8 + pair_total + most
        return pl.pallas_call(
            functools.partial(
                sort_kernel,
                (species, levels, columns, tiles, wide_count, narrow_count, pair_total),
                cuts, len(target_sizes), early,
            ),
            grid=(columns // SORT_COLUMNS,),
            in_specs=[full, full, full,
                      pl.BlockSpec((species, levels, SORT_COLUMNS), lambda at: (0, 0, at))]
            + [smem] * len(known),
            out_specs=([full, full] if early else []) + [spec] * len(target_sizes),
            out_shape=(known_types if early else []) + [rows_type(size) for size in target_sizes],
            scratch_shapes=([
                pltpu.SMEM((1, columns), jnp.int32), pltpu.SMEM((8, LANES), jnp.int32),
            ] if early else []) + [
                pltpu.VMEM((tiles * LANES, LANES), jnp.float32),
                pltpu.VMEM((LANES * 8, LANES), jnp.float32),
                room_type(groups),
                pltpu.SemaphoreType.DMA((len(cuts),)),
            ],
            compiler_params=params(
                groups + (sum(target_sizes) if early else 0),
                2 * species * levels * SORT_COLUMNS * 4,
            ),
            name="sort_columns" if early else "sort_later_columns",
        )(
            phys_index.reshape(1, columns),
            column_rate.reshape(1, columns),
            iter_count.reshape(1, columns),
            tracers.transpose(1, 0, 2),
            *known,
        )

    cuts = [(0, 0, entry(1, order[0]), mean, entry(3, order[0]))]
    for index, at in enumerate(moving):
        cuts += pair_cuts(1 + index, at)
    table, places, *first = sort(cuts, [mean] + [2 * piece] * len(moving), True, ())
    cuts = [(0, 0, over(order[0]), most - mean, groups_over(order[0]))] + pair_cuts(1, 1)
    for index, step in enumerate(order[1:-1]):
        rest = most - statics[step]
        cuts.append((2 + index, 0, entry(1, step), statics[step], entry(3, step)))
        cuts.append((2 + index, statics[step], over(step), rest, groups_over(step)))
    first_rest, local_rows, *raw = sort(
        cuts, [most - mean, 2 * piece] + [most] * (len(order) - 2), False, (table, places)
    )
    raw_groups = dict(zip(order[1:-1], raw))
    units = [
        (jnp.maximum(table[3, step * WIN] - statics[step], 0) + UNIT - 1) // UNIT
        for step in order
    ]
    loss_pad = jnp.pad(loss_rate, (0, pad - species)).reshape(pad, 1)
    coupling_pad = jnp.pad(coupling, ((0, pad - species), (0, pad - species)))
    block = INT_ROWS // 8

    def integrate(table, operands, loads, merges, blocks, stores):
        groups = max([to + size for _, _, size, to in loads] + [begin + block for begin, _ in blocks])
        groups += piece
        flops = 2 * levels * pad * pad * 6 * INT_ROWS * len(blocks)
        return pl.pallas_call(
            functools.partial(
                integrate_kernel, (levels, pad, tiles),
                (loads, merges, blocks, stores, len(operands)),
            ),
            in_specs=[smem, full, full] + [hbm] * len(operands),
            out_specs=[hbm] * len(stores),
            out_shape=[rows_type(size) for _, size in stores],
            scratch_shapes=[
                room_type(groups),
                pltpu.VMEM((INT_ROWS // LANES, tiles * LANES, LANES), jnp.float32),
                pltpu.VMEM((levels, pad, INT_ROWS), jnp.float32),
                pltpu.VMEM((pad, INT_ROWS), jnp.float32),
                pltpu.SMEM((2, LANES), jnp.int32),
                pltpu.SemaphoreType.DMA((len(loads),)),
                pltpu.SemaphoreType.DMA((len(stores),)),
            ],
            compiler_params=params(groups, 4 * levels * pad * INT_ROWS * 4),
            cost_estimate=pl.CostEstimate(
                flops=flops, bytes_accessed=8 * groups * 8 * tiles * LANES,
                transcendentals=flops // (2 * pad),
            ),
            name="integrate_columns",
        )(table, loss_pad, coupling_pad, *operands)

    def rows_of(step, at=0):
        return entry(0, step, at)

    def group_blocks(begin, step):
        return [
            (begin + part * block,
             lambda table, part=part: table[3, step * WIN] * 8 - part * INT_ROWS)
            for part in range(most // block)
        ]

    def here(begin):
        return lambda table: jnp.int32(begin)

    def step_over(step, units, rest):
        def leaf(units, rest):
            if units == 0:
                return jnp.zeros_like(rest)
            got = from_behind(rest[:units * UNIT * 8 * tiles], "narrow", step)
            return jnp.pad(got, ((0, rest.shape[0] - got.shape[0]), (0, 0)))

        leaves = [functools.partial(leaf, count) for count in range((most - statics[step]) // UNIT + 1)]
        return lax.switch(units, leaves, rest)

    pieces = {}
    outgoing = [first[0], first_rest]
    wide_now = first[1:]
    keys_now = [[(at, 0), (at, last)] for at in moving]
    static_part = from_behind(outgoing[0], "narrow", order[0])
    wide_got = [from_behind(value, "wide", at - 1) for value, at in zip(wide_now, moving)]
    table_then = table
    for phase, step in enumerate(order):
        static = statics[step]
        operands, loads, merges, blocks, stores, named = [], [], [], [], [], []
        used = 0
        if phase + 1 < len(order):
            coming = order[phase + 1]
            if coming == last:
                operands += [pieces[at, last][0] for at in moving] + [local_rows]
                for index, at in enumerate(moving):
                    loads.append((index, here(pieces[at, last][1]), piece, most + at * piece))
                loads.append((len(moving), here(piece), piece, most + piece))
                for at in range(WIN):
                    merges.append(
                        (most + at * piece, groups_of(last, at), entry(2, last, at))
                    )
                used = most + WIN * piece
            else:
                operands.append(raw_groups[coming])
                loads.append((0, None, most, 0))
                used = most
            blocks += group_blocks(0, coming)
            stores += [(here(0), statics[coming]), (here(statics[coming]), most - statics[coming])]
        extra = []
        if phase == 0:
            extra.append(((1, 0), (local_rows, 0)))
        if phase == 1:
            extra += [((at, 0), pieces[at, 0]) for at in moving]
        if phase == 2:
            extra += [((at, order[0]), pieces[at, order[0]]) for at in range(WIN)]
        used = -(-used // block) * block
        for key, value in extra:
            operands.append(value[0])
            loads.append((len(operands) - 1, here(value[1]), piece, used))
            blocks.append((used, rows_of(key[1], key[0])))
            stores.append((here(used), piece))
            named.append(key)
            used += block
        if stores:
            results = integrate(table_then, operands, loads, merges, blocks, stores)
        else:
            results = []
        rest = outgoing[1]
        if step != last:
            static_part, results, rest, wide_got, units = lax.optimization_barrier(
                (static_part, results, rest, wide_got, units)
            )
        else:
            static_part, results, rest = lax.optimization_barrier((static_part, results, rest))
        done = {key: (value, 0) for key, value in zip(named, results[len(results) - len(named):])}
        outgoing = results[:len(results) - len(named)]
        arrived = [static_part, step_over(step, units[phase], rest)]
        if step != last:
            arrived, outgoing = lax.optimization_barrier((arrived, outgoing))
            static_part = from_behind(outgoing[0], "narrow", order[phase + 1])
        if step != last:
            cut = pl.pallas_call(
                functools.partial(cut_kernel, static, tiles, piece, step),
                in_specs=[smem] + [hbm] * len(arrived),
                out_specs=[hbm] * WIN,
                out_shape=[rows_type(piece)] * WIN,
                scratch_shapes=[
                    room_type(most + piece),
                    pltpu.SemaphoreType.DMA((len(arrived),)),
                    pltpu.SemaphoreType.DMA((2, WIN)),
                ],
                compiler_params=params(most + piece),
                name="cut_pieces",
            )(table, *arrived)
            cut, table_then = lax.optimization_barrier((cut, table))
        for keys, value in zip(keys_now, wide_got):
            pieces.update({key: (value, part * piece) for part, key in enumerate(keys)})
        pieces.update(done)
        if step != last:
            pieces[1, step] = (cut[1], 0)
            keys_now = [[(at, step)] for at in moving]
            wide_got = [from_behind(cut[at], "wide", at - 1) for at in moving]

    held = [pieces[at, step] for step in range(last) for at in range(WIN)]
    buffers = [value for value, _ in held] + arrived
    updated = pl.pallas_call(
        functools.partial(
            finish_kernel,
            (species, levels, columns, tiles, static, piece, narrow_count,
             [begin for _, begin in held]),
        ),
        in_specs=[smem] + [hbm] * len(buffers),
        out_specs=hbm,
        out_shape=jax.ShapeDtypeStruct((species, levels, columns), jnp.float32),
        scratch_shapes=[
            pltpu.VMEM((pair_total * 8, LANES), jnp.float32),
            pltpu.VMEM((pair_total, LANES), jnp.int32),
            pltpu.VMEM((pair_total - WIN, piece * 8 * tiles, LANES), jnp.float32),
            room_type(most + piece),
            room_type(columns // 8 + 1),
            pltpu.VMEM((species, levels, columns), jnp.float32),
            pltpu.SMEM((pair_total, LANES), jnp.int32),
            pltpu.SemaphoreType.DMA((2, pair_total)),
            pltpu.SemaphoreType.DMA((pair_total + WIN + 1,)),
            pltpu.SemaphoreType.DMA((columns // LANES,)),
        ],
        compiler_params=params(
            pair_total * piece + most + columns // 8, species * levels * columns * 4
        ),
        name="place_columns",
    )(table, *buffers)
    return updated.transpose(1, 0, 2)


def solution(mesh):
    placed = (
        P(None, None, ("wide", "narrow")),
        P(("wide", "narrow")),
        P(),
        P(),
        P(("wide", "narrow")),
        P(("wide", "narrow")),
    )
    return jax.shard_map(
        local,
        mesh=mesh,
        in_specs=placed,
        out_specs=P(None, None, ("wide", "narrow")),
        check_vma=False,
    )
```

```python
import functools

import jax
import jax.numpy as jnp
from jax import lax
from jax.experimental import pallas as pl
from jax.experimental.pallas import tpu as pltpu
from jax.sharding import PartitionSpec as P

WIN = 4
MAXIT = 12
LANES = 128
SORT_COLUMNS = 256
INT_ROWS = 256
UNIT = 8
VMEM = 60 * 1024 * 1024


def from_behind(value, axis, steps):
    count = lax.axis_size(axis)
    pairs = [(source, (source + steps) % count) for source in range(count)]
    return lax.ppermute(value, axis, pairs)


def log2(value):
    bits = value.bit_length() - 1
    assert 1 << bits == value
    return bits


def span_of(group, groups, tiles):
    return pl.ds(pl.multiple_of(group * 8 * tiles, 8), groups * 8 * tiles)


def sort_kernel(sizes, cuts, targets, early, *refs):
    species, levels, columns, tiles, wide_count, narrow_count, pair_total = sizes
    turn_ref, wide_ref, sorted_ref = refs[-4:-1]
    sem_ref = refs[-1]
    if early:
        phys_ref, rate_ref, count_ref, tracers_ref, table_ref, pos_ref = refs[:6]
        cut_refs = refs[6:6 + targets]
        at_ref, table_smem, place_sem = refs[6 + targets:9 + targets]
    else:
        phys_ref, rate_ref, count_ref, tracers_ref, table_smem, at_ref = refs[:6]
        cut_refs = refs[6:6 + targets]
    step = pl.program_id(0)
    lanes = tiles * LANES
    real = species * levels

    def find_places():
        phys = phys_ref[...]
        target = lax.shift_right_logical(phys, log2(columns))
        slot = phys & (columns - 1)
        wide_step = lax.shift_right_logical(target, log2(narrow_count)) - lax.axis_index("wide")
        wide_step = (wide_step + 1) & (wide_count - 1)
        narrow_step = ((target & (narrow_count - 1)) - lax.axis_index("narrow")) & (narrow_count - 1)
        pair = narrow_step * WIN + wide_step
        member = pair == lax.broadcasted_iota(jnp.int32, (pair_total, columns), 0)
        counts = jnp.sum(jnp.where(member, 1.0, 0.0), axis=1, keepdims=True)
        slot_f = slot.astype(jnp.float32)
        starts = jnp.min(jnp.where(member, slot_f, float(columns)), axis=1, keepdims=True)
        groups = lax.shift_right_logical(counts.astype(jnp.int32) + 7, 3).astype(jnp.float32)
        lane = lax.broadcasted_iota(jnp.int32, (pair_total, LANES), 1)
        row = lax.broadcasted_iota(jnp.int32, (pair_total, LANES), 0)

        def across(value):
            return jnp.sum(jnp.where(lane == row, value, 0.0), axis=0, keepdims=True)

        groups_t = across(groups)
        base = jnp.sum(jnp.where(lane < row, groups_t, 0.0), axis=1, keepdims=True)
        section = row & -WIN
        inner = base - jnp.sum(jnp.where(lane < section, groups_t, 0.0), axis=1, keepdims=True)
        same = (lane & -WIN) == section
        in_step = jnp.sum(jnp.where(same, groups_t, 0.0), axis=1, keepdims=True)
        pos = slot_f + jnp.sum(jnp.where(member, base * 8.0 - starts, 0.0), axis=0, keepdims=True)
        pos_ref[...] = pos.astype(jnp.int32)
        pltpu.make_async_copy(pos_ref, at_ref, place_sem.at[0]).start()
        table_ref[...] = jnp.zeros_like(table_ref)
        for at, value in enumerate((counts, base, inner, in_step, starts)):
            table_ref[at:at + 1, :] = across(value).astype(jnp.int32)
        pltpu.make_async_copy(table_ref, table_smem, place_sem.at[1]).start()

    if early:
        pl.when(step == 0)(find_places)
    block = tracers_ref.shape[2]
    begin = step * block
    in_group = lax.broadcasted_iota(jnp.int32, (8, LANES), 0)
    for half in range(block // LANES):
        span = slice(half * LANES, (half + 1) * LANES)
        at = pl.ds(pl.multiple_of(begin + half * LANES, LANES), LANES)
        turn_ref[lanes - 16:lanes, :] = jnp.zeros((16, LANES), jnp.float32)
        turn_ref[0:real, :] = tracers_ref[:, :, span].reshape(real, LANES)
        extra = jnp.where(in_group == 5, (phys_ref[:, at] & (columns - 1)).astype(jnp.float32), 0.0)
        extra = jnp.where(in_group == 6, rate_ref[:, at], extra)
        extra = jnp.where(in_group == 7, count_ref[:, at].astype(jnp.float32), extra)
        turn_ref[lanes - 8:lanes, :] = extra
        for tile in range(tiles):
            wide_ref[pl.ds(tile, LANES, stride=8), :] = turn_ref[
                tile * LANES:(tile + 1) * LANES, :
            ].T

        if early and half == 0:
            @pl.when(step == 0)
            def _():
                pltpu.make_async_copy(pos_ref, at_ref, place_sem.at[0]).wait()
                pltpu.make_async_copy(table_ref, table_smem, place_sem.at[1]).wait()

        def move(part, carry):
            for extra_row in range(16):
                column = part * 16 + extra_row
                to = at_ref[0, begin + half * LANES + column] * tiles
                record = wide_ref[pl.ds(pl.multiple_of(column * 8, 8), 8), :]
                sorted_ref[pl.ds(to, tiles), :] = record[:tiles]
            return carry

        lax.fori_loop(0, LANES // 16, move, 0)

    @pl.when(step == pl.num_programs(0) - 1)
    def _():
        copies = []
        for index, (target, to, begin, size, valid) in enumerate(cuts):
            begin = begin(table_smem)
            valid = jnp.clip(valid(table_smem), 0, size)
            copy = pltpu.make_async_copy(
                sorted_ref.at[span_of(begin, size, tiles)],
                cut_refs[target].at[span_of(to, size, tiles)], sem_ref.at[index],
            )
            pl.when(valid > 0)(copy.start)
            copies.append((valid > 0, copy))
        wait_all(copies)


def start_arrival(refs, sems, room_ref, in_step, static, tiles):
    waits = []
    for index, wanted in enumerate((None, in_step > static)):
        copy = pltpu.make_async_copy(
            refs[index], room_ref.at[pl.ds(index * static * 8 * tiles, refs[index].shape[0])],
            sems(index),
        )
        if wanted is None:
            copy.start()
        else:
            pl.when(wanted)(copy.start)
        waits.append((wanted, copy))
    return waits


def wait_all(waits):
    for wanted, copy in waits:
        if wanted is None:
            copy.wait()
        else:
            pl.when(wanted)(copy.wait)


def integrate_block(sizes, room_ref, first, valid, loss_ref, coupling_ref,
                    turn_ref, y_ref, inverse_ref):
    levels, pad, tiles = sizes
    halves = INT_ROWS // LANES
    lanes = tiles * LANES
    first = pl.multiple_of(first * 8 * tiles, 8)
    for half in range(halves):
        begin = first + half * LANES * tiles
        for tile in range(tiles):
            block = room_ref[pl.ds(begin + tile, LANES, stride=tiles), :]
            turn_ref[half, tile * LANES:(tile + 1) * LANES, :] = block.T
        for level in range(levels):
            y_ref[level, :, half * LANES:(half + 1) * LANES] = turn_ref[
                half, pl.ds(level, pad, stride=levels), :
            ]
    rate = jnp.concatenate(
        [turn_ref[half, lanes - 2:lanes - 1, :] for half in range(halves)], axis=1
    )
    count = jnp.concatenate(
        [turn_ref[half, lanes - 1:lanes, :] for half in range(halves)], axis=1
    )
    lane = lax.broadcasted_iota(jnp.int32, (1, INT_ROWS), 1)
    count = jnp.where((lane < valid) & (count <= MAXIT), count, 0.0)
    step_len = rate / jnp.maximum(count, 1.0)
    inverse_ref[...] = 1.0 / (1.0 + step_len * loss_ref[...])
    last = jnp.max(count).astype(jnp.int32)

    def advance(k, carry):
        active = k.astype(jnp.float32) < count

        def one_level(level, inner):
            y = y_ref[level]
            squashed = jnp.tanh(y).astype(jnp.bfloat16)
            produced = jnp.dot(coupling_ref[...], squashed, preferred_element_type=jnp.float32)
            y_ref[level] = jnp.where(active, (y + step_len * produced) * inverse_ref[...], y)
            return inner

        for level in range(levels):
            one_level(level, 0)
        return carry

    lax.fori_loop(0, last, advance, 0)
    for half in range(halves):
        begin = first + half * LANES * tiles
        for level in range(levels):
            turn_ref[half, pl.ds(level, pad, stride=levels), :] = y_ref[
                level, :, half * LANES:(half + 1) * LANES
            ]
        for tile in range(tiles):
            block = turn_ref[half, tile * LANES:(tile + 1) * LANES, :]
            room_ref[pl.ds(begin + tile, LANES, stride=tiles), :] = block.T


def integrate_kernel(sizes, plan, table_ref, loss_ref, coupling_ref, *refs):
    loads, merges, blocks, stores, operands = plan
    tiles = sizes[2]
    sources = refs[:operands]
    results = refs[operands:operands + len(stores)]
    room_ref, turn_ref, y_ref, inverse_ref, rows_ref, sem_ref, out_sem = refs[
        operands + len(stores):
    ]
    copies = []
    for index, (source, begin, groups, to) in enumerate(loads):
        ref = sources[source]
        if begin is not None:
            ref = ref.at[span_of(begin(table_ref), groups, tiles)]
        copies.append(pltpu.make_async_copy(
            ref, room_ref.at[span_of(to, groups, tiles)], sem_ref.at[index]
        ))
    for copy in copies:
        copy.start()
    for copy in copies:
        copy.wait()
    for begin, groups, to in merges:
        to = to(table_ref)

        def move(group, carry):
            room_ref[span_of(to + group, 1, tiles), :] = room_ref[
                span_of(begin + group, 1, tiles), :
            ]
            return carry

        lax.fori_loop(0, groups(table_ref), move, 0)
    for index, (begin, rows) in enumerate(blocks):
        rows_ref[0, index] = jnp.int32(begin)
        rows_ref[1, index] = rows(table_ref)

    def one_block(index, carry):
        valid = rows_ref[1, index]

        @pl.when(valid > 0)
        def _():
            integrate_block(sizes, room_ref, rows_ref[0, index], valid, loss_ref, coupling_ref,
                            turn_ref, y_ref, inverse_ref)

        return carry

    lax.fori_loop(0, len(blocks), one_block, 0)
    copies = []
    for index, (begin, groups) in enumerate(stores):
        copies.append(pltpu.make_async_copy(
            room_ref.at[span_of(begin(table_ref), groups, tiles)], results[index],
            out_sem.at[index],
        ))
    for copy in copies:
        copy.start()
    for copy in copies:
        copy.wait()


def cut_kernel(static, tiles, piece, step, table_ref, *refs):
    pieces = refs[2:2 + WIN]
    room_ref, sem_ref, out_sem = refs[2 + WIN:]
    wait_all(start_arrival(refs[:2], lambda at: sem_ref.at[at], room_ref,
                           table_ref[3, step * WIN], static, tiles))
    copies = []
    half = piece // 2
    for at in range(WIN):
        begin = table_ref[2, step * WIN + at]
        for part in range(2):
            wanted = table_ref[0, step * WIN + at] > part * half * 8
            copy = pltpu.make_async_copy(
                room_ref.at[span_of(begin + part * half, half, tiles)],
                pieces[at].at[span_of(part * half, half, tiles)], out_sem.at[part, at],
            )
            pl.when(wanted)(copy.start)
            copies.append((wanted, copy))
    wait_all(copies)


def finish_kernel(sizes, table_ref, starts_ref, *refs):
    species, levels, columns, tiles, static, piece, wide_count, narrow_count, begins = sizes
    pair_total = narrow_count * WIN
    whole_pieces = pair_total - WIN
    out_ref, piece_ref, room_ref, placed_ref, whole_ref, sem_ref, out_sem = refs[-7:]
    copies = []
    half = piece // 2
    for pair in range(whole_pieces):
        both = []
        for part in range(2):
            copy = pltpu.make_async_copy(
                refs[pair].at[span_of(begins[pair] + part * half, half, tiles)],
                piece_ref.at[pair, span_of(part * half, half, tiles)], sem_ref.at[part, pair],
            )
            wanted = table_ref[0, pair] > part * half * 8
            pl.when(wanted)(copy.start)
            both.append((wanted, copy))
        copies.append(both)
    waits = start_arrival(refs[whole_pieces:whole_pieces + 2],
                          lambda at: sem_ref.at[at, whole_pieces], room_ref,
                          table_ref[3, whole_pieces], static, tiles)
    in_group = lax.broadcasted_iota(jnp.int32, (8, LANES), 0)
    for pair in range(pair_total):
        if pair < whole_pieces:
            wait_all(copies[pair])
            held = piece_ref.at[pair]
            begin = 0
        else:
            if pair == whole_pieces:
                wait_all(waits)
            held = room_ref
            begin = pl.multiple_of(table_ref[2, pair] * 8 * tiles, 8)
        count = table_ref[0, pair]
        step, at = divmod(pair, WIN)
        wide = (lax.axis_index("wide") + wide_count + 1 - at) & (wide_count - 1)
        narrow = (lax.axis_index("narrow") + narrow_count - step) & (narrow_count - 1)
        start = jnp.clip(starts_ref[wide * narrow_count + narrow, pair], 0, columns - 1) * tiles
        full = lax.shift_right_logical(count, 3)

        def move(group, carry):
            for row in range(0, 8 * tiles, 8):
                at = group * 8 * tiles + row
                placed_ref[pl.ds(start + at, 8), :] = held[pl.ds(pl.multiple_of(begin + at, 8), 8), :]
            return carry

        lax.fori_loop(0, full, move, 0)

        @pl.when((count & 7) > 0)
        def _():
            for row in range(0, 8 * tiles, 8):
                at = full * 8 * tiles + row
                to = pl.ds(start + at, 8)
                placed_ref[to, :] = jnp.where(
                    in_group + row < (count & 7) * tiles,
                    held[pl.ds(pl.multiple_of(begin + at, 8), 8), :], placed_ref[to, :],
                )

    per_tile = LANES // levels
    for part in range(columns // LANES):
        at = slice(part * LANES, (part + 1) * LANES)
        for tile in range(tiles):
            block = placed_ref[pl.ds(part * LANES * tiles + tile, LANES, stride=tiles), :]
            block = block.T.reshape(per_tile, levels, LANES)
            keep = min(per_tile, species - tile * per_tile)
            whole_ref[tile * per_tile:tile * per_tile + keep, :, at] = block[:keep]
        pltpu.make_async_copy(whole_ref.at[:, :, at], out_ref.at[:, :, at], out_sem.at[part]).start()
    for part in range(columns // LANES):
        at = slice(part * LANES, (part + 1) * LANES)
        pltpu.make_async_copy(whole_ref.at[:, :, at], out_ref.at[:, :, at], out_sem.at[part]).wait()


def local(tracers, column_rate, loss_rate, coupling, phys_index, iter_count):
    levels, species, columns = tracers.shape
    wide_count = lax.axis_size("wide")
    narrow_count = lax.axis_size("narrow")
    pair_total = WIN * narrow_count
    room = 2 * columns // pair_total
    piece = room // 8
    pad = -(-species // 8) * 8
    while levels * pad % LANES or levels * (pad - species) < 8:
        pad += 8
    tiles = levels * pad // LANES
    mean = columns // narrow_count // 8
    full = pl.BlockSpec(memory_space=pltpu.VMEM)
    smem = pl.BlockSpec(memory_space=pltpu.SMEM)
    hbm = pl.BlockSpec(memory_space=pltpu.HBM)
    last = narrow_count - 1
    moving = [at for at in range(WIN) if at != 1]
    order = [narrow_count // 2]
    order += [step for step in range(1, last) if step not in order] + [last]
    statics = {step: mean if step == order[0] else mean + mean // 8 for step in order}
    most = WIN * piece

    params = pltpu.CompilerParams(vmem_limit_bytes=VMEM)

    def rows_type(groups):
        return jax.ShapeDtypeStruct((groups * 8 * tiles, LANES), jnp.float32)

    def room_type(groups):
        return pltpu.VMEM((groups * 8 * tiles, LANES), jnp.float32)

    def entry(row, step, at=0):
        return lambda table: table[row, step * WIN + at]

    def over(step):
        return lambda table: entry(1, step)(table) + statics[step]

    def groups_of(step, at):
        return lambda table: lax.shift_right_logical(table[0, step * WIN + at] + 7, 3)

    def groups_over(step):
        return lambda table: table[3, step * WIN] - statics[step]

    def pair_cuts(target, at):
        return [
            (target, part * piece + half,
             lambda table, step=step, half=half: entry(1, step, at)(table) + half, piece // 2,
             lambda table, step=step, half=half: groups_of(step, at)(table) - half)
            for part, step in enumerate((0, last)) for half in range(0, piece, piece // 2)
        ]

    def sort(cuts, target_sizes, early, known):
        known_types = [
            jax.ShapeDtypeStruct((8, LANES), jnp.int32),
            jax.ShapeDtypeStruct((1, columns), jnp.int32),
        ]
        groups = columns // 8 + pair_total + most
        return pl.pallas_call(
            functools.partial(
                sort_kernel,
                (species, levels, columns, tiles, wide_count, narrow_count, pair_total),
                cuts, len(target_sizes), early,
            ),
            grid=(columns // SORT_COLUMNS,),
            in_specs=[full, full, full,
                      pl.BlockSpec((species, levels, SORT_COLUMNS), lambda at: (0, 0, at))]
            + [smem] * len(known),
            out_specs=([full, full] if early else []) + [hbm] * len(target_sizes),
            out_shape=(known_types if early else []) + [rows_type(size) for size in target_sizes],
            scratch_shapes=([
                pltpu.SMEM((1, columns), jnp.int32), pltpu.SMEM((8, LANES), jnp.int32),
                pltpu.SemaphoreType.DMA((2,)),
            ] if early else []) + [
                pltpu.VMEM((tiles * LANES, LANES), jnp.float32),
                pltpu.VMEM((LANES * 8, LANES), jnp.float32),
                room_type(groups),
                pltpu.SemaphoreType.DMA((len(cuts),)),
            ],
            compiler_params=params,
            name="sort_columns" if early else "sort_later_columns",
        )(
            phys_index.reshape(1, columns),
            column_rate.reshape(1, columns),
            iter_count.reshape(1, columns),
            tracers.transpose(1, 0, 2),
            *known,
        )

    cuts = [(0, 0, entry(1, order[0]), mean, entry(3, order[0]))]
    for index, at in enumerate(moving):
        cuts += pair_cuts(1 + index, at)
    table, places, *first = sort(cuts, [mean] + [2 * piece] * len(moving), True, ())
    cuts = [(0, 0, over(order[0]), most - mean, groups_over(order[0]))] + pair_cuts(1, 1)
    for index, step in enumerate(order[1:-1]):
        rest = most - statics[step]
        cuts.append((2 + index, 0, entry(1, step), statics[step], entry(3, step)))
        cuts.append((2 + index, statics[step], over(step), rest, groups_over(step)))
    first_rest, local_rows, *raw = sort(
        cuts, [most - mean, 2 * piece] + [most] * (len(order) - 2), False, (table, places)
    )
    raw_groups = dict(zip(order[1:-1], raw))
    starts = lax.all_gather(table[4], ("wide", "narrow"))
    units = [
        (jnp.maximum(table[3, step * WIN] - statics[step], 0) + UNIT - 1) // UNIT
        for step in order
    ]
    loss_pad = jnp.pad(loss_rate, (0, pad - species)).reshape(pad, 1)
    coupling_pad = jnp.pad(coupling, ((0, pad - species), (0, pad - species)))
    block = INT_ROWS // 8

    def integrate(table, operands, loads, merges, blocks, stores):
        groups = max([to + size for _, _, size, to in loads] + [begin + block for begin, _ in blocks])
        groups += piece
        flops = 2 * levels * pad * pad * 6 * INT_ROWS * len(blocks)
        return pl.pallas_call(
            functools.partial(
                integrate_kernel, (levels, pad, tiles),
                (loads, merges, blocks, stores, len(operands)),
            ),
            in_specs=[smem, full, full] + [hbm] * len(operands),
            out_specs=[hbm] * len(stores),
            out_shape=[rows_type(size) for _, size in stores],
            scratch_shapes=[
                room_type(groups),
                pltpu.VMEM((INT_ROWS // LANES, tiles * LANES, LANES), jnp.float32),
                pltpu.VMEM((levels, pad, INT_ROWS), jnp.float32),
                pltpu.VMEM((pad, INT_ROWS), jnp.float32),
                pltpu.SMEM((2, LANES), jnp.int32),
                pltpu.SemaphoreType.DMA((len(loads),)),
                pltpu.SemaphoreType.DMA((len(stores),)),
            ],
            compiler_params=params,
            cost_estimate=pl.CostEstimate(
                flops=flops, bytes_accessed=8 * groups * 8 * tiles * LANES,
                transcendentals=flops // (2 * pad),
            ),
            name="integrate_columns",
        )(table, loss_pad, coupling_pad, *operands)

    def rows_of(step, at=0):
        return entry(0, step, at)

    def group_blocks(begin, step):
        return [
            (begin + part * block,
             lambda table, part=part: table[3, step * WIN] * 8 - part * INT_ROWS)
            for part in range(most // block)
        ]

    def here(begin):
        return lambda table: jnp.int32(begin)

    def step_over(step, units, rest):
        def leaf(units, rest):
            if units == 0:
                return jnp.zeros_like(rest)
            got = from_behind(rest[:units * UNIT * 8 * tiles], "narrow", step)
            return jnp.pad(got, ((0, rest.shape[0] - got.shape[0]), (0, 0)))

        leaves = [functools.partial(leaf, count) for count in range((most - statics[step]) // UNIT + 1)]
        return lax.switch(units, leaves, rest)

    pieces = {}
    outgoing = [first[0], first_rest]
    wide_now = first[1:]
    keys_now = [[(at, 0), (at, last)] for at in moving]
    static_part = from_behind(outgoing[0], "narrow", order[0])
    wide_got = [from_behind(value, "wide", at - 1) for value, at in zip(wide_now, moving)]
    table_then = table
    for phase, step in enumerate(order):
        static = statics[step]
        operands, loads, merges, blocks, stores, named = [], [], [], [], [], []
        used = 0
        if phase + 1 < len(order):
            coming = order[phase + 1]
            if coming == last:
                operands += [pieces[at, last][0] for at in moving] + [local_rows]
                for index, at in enumerate(moving):
                    loads.append((index, here(pieces[at, last][1]), piece, most + at * piece))
                loads.append((len(moving), here(piece), piece, most + piece))
                for at in range(WIN):
                    merges.append(
                        (most + at * piece, groups_of(last, at), entry(2, last, at))
                    )
                used = most + WIN * piece
            else:
                operands.append(raw_groups[coming])
                loads.append((0, None, most, 0))
                used = most
            blocks += group_blocks(0, coming)
            stores += [(here(0), statics[coming]), (here(statics[coming]), most - statics[coming])]
        extra = []
        if phase == 0:
            extra.append(((1, 0), (local_rows, 0)))
        if phase == 1:
            extra += [((at, 0), pieces[at, 0]) for at in moving]
        if phase == 2:
            extra += [((at, order[0]), pieces[at, order[0]]) for at in range(WIN)]
        used = -(-used // block) * block
        for key, value in extra:
            operands.append(value[0])
            loads.append((len(operands) - 1, here(value[1]), piece, used))
            blocks.append((used, rows_of(key[1], key[0])))
            stores.append((here(used), piece))
            named.append(key)
            used += block
        if stores:
            results = integrate(table_then, operands, loads, merges, blocks, stores)
        else:
            results = []
        rest = outgoing[1]
        if phase == 0:
            static_part, results, rest, wide_got, units, starts = lax.optimization_barrier(
                (static_part, results, rest, wide_got, units, starts)
            )
        elif step != last:
            static_part, results, rest, wide_got = lax.optimization_barrier(
                (static_part, results, rest, wide_got)
            )
        else:
            static_part, results, rest = lax.optimization_barrier((static_part, results, rest))
        done = {key: (value, 0) for key, value in zip(named, results[len(results) - len(named):])}
        outgoing = results[:len(results) - len(named)]
        arrived = [static_part, step_over(step, units[phase], rest)]
        if step != last:
            arrived, outgoing = lax.optimization_barrier((arrived, outgoing))
            static_part = from_behind(outgoing[0], "narrow", order[phase + 1])
        if step != last:
            cut = pl.pallas_call(
                functools.partial(cut_kernel, static, tiles, piece, step),
                in_specs=[smem] + [hbm] * len(arrived),
                out_specs=[hbm] * WIN,
                out_shape=[rows_type(piece)] * WIN,
                scratch_shapes=[
                    room_type(most + piece),
                    pltpu.SemaphoreType.DMA((len(arrived),)),
                    pltpu.SemaphoreType.DMA((2, WIN)),
                ],
                compiler_params=params,
                name="cut_pieces",
            )(table, *arrived)
            cut, table_then = lax.optimization_barrier((cut, table))
        for keys, value in zip(keys_now, wide_got):
            pieces.update({key: (value, part * piece) for part, key in enumerate(keys)})
        pieces.update(done)
        if step != last:
            pieces[1, step] = (cut[1], 0)
            keys_now = [[(at, step)] for at in moving]
            wide_got = [from_behind(cut[at], "wide", at - 1) for at in moving]

    held = [pieces[at, step] for step in range(last) for at in range(WIN)]
    buffers = [value for value, _ in held] + arrived
    updated = pl.pallas_call(
        functools.partial(
            finish_kernel,
            (species, levels, columns, tiles, static, piece, wide_count, narrow_count,
             [begin for _, begin in held]),
        ),
        in_specs=[smem, smem] + [hbm] * len(buffers),
        out_specs=hbm,
        out_shape=jax.ShapeDtypeStruct((species, levels, columns), jnp.float32),
        scratch_shapes=[
            pltpu.VMEM((pair_total - WIN, piece * 8 * tiles, LANES), jnp.float32),
            room_type(most + piece),
            room_type(columns // 8 + 1),
            pltpu.VMEM((species, levels, columns), jnp.float32),
            pltpu.SemaphoreType.DMA((2, pair_total)),
            pltpu.SemaphoreType.DMA((columns // LANES,)),
        ],
        compiler_params=params,
        name="place_columns",
    )(table, starts, *buffers)
    return updated.transpose(1, 0, 2)


def solution(mesh):
    placed = (
        P(None, None, ("wide", "narrow")),
        P(("wide", "narrow")),
        P(),
        P(),
        P(("wide", "narrow")),
        P(("wide", "narrow")),
    )
    return jax.shard_map(
        local,
        mesh=mesh,
        in_specs=placed,
        out_specs=P(None, None, ("wide", "narrow")),
        check_vma=False,
    )
```

```python
import functools

import jax
import jax.numpy as jnp
from jax import lax
from jax.experimental import pallas as pl
from jax.experimental.pallas import tpu as pltpu
from jax.sharding import PartitionSpec as P

WIN = 4
MAXIT = 12
LANES = 128
SORT_COLUMNS = 256
INT_ROWS = 256
UNIT = 8
VMEM = 60 * 1024 * 1024


def from_behind(value, axis, steps):
    count = lax.axis_size(axis)
    pairs = [(source, (source + steps) % count) for source in range(count)]
    return lax.ppermute(value, axis, pairs)


def log2(value):
    bits = value.bit_length() - 1
    assert 1 << bits == value
    return bits


def span_of(group, groups, tiles):
    return pl.ds(pl.multiple_of(group * 8 * tiles, 8), groups * 8 * tiles)


def sort_kernel(sizes, cuts, targets, early, *refs):
    species, levels, columns, tiles, wide_count, narrow_count, pair_total = sizes
    turn_ref, wide_ref, sorted_ref = refs[-4:-1]
    sem_ref = refs[-1]
    if early:
        phys_ref, rate_ref, count_ref, tracers_ref, table_ref, pos_ref = refs[:6]
        cut_refs = refs[6:6 + targets]
        at_ref, table_smem, place_sem = refs[6 + targets:9 + targets]
    else:
        phys_ref, rate_ref, count_ref, tracers_ref, table_smem, at_ref = refs[:6]
        cut_refs = refs[6:6 + targets]
    step = pl.program_id(0)
    lanes = tiles * LANES
    real = species * levels

    def find_places():
        phys = phys_ref[...]
        target = lax.shift_right_logical(phys, log2(columns))
        slot = phys & (columns - 1)
        wide_step = lax.shift_right_logical(target, log2(narrow_count)) - lax.axis_index("wide")
        wide_step = (wide_step + 1) & (wide_count - 1)
        narrow_step = ((target & (narrow_count - 1)) - lax.axis_index("narrow")) & (narrow_count - 1)
        pair = narrow_step * WIN + wide_step
        member = pair == lax.broadcasted_iota(jnp.int32, (pair_total, columns), 0)
        counts = jnp.sum(jnp.where(member, 1.0, 0.0), axis=1, keepdims=True)
        slot_f = slot.astype(jnp.float32)
        starts = jnp.min(jnp.where(member, slot_f, float(columns)), axis=1, keepdims=True)
        groups = lax.shift_right_logical(counts.astype(jnp.int32) + 7, 3).astype(jnp.float32)
        lane = lax.broadcasted_iota(jnp.int32, (pair_total, LANES), 1)
        row = lax.broadcasted_iota(jnp.int32, (pair_total, LANES), 0)

        def across(value):
            return jnp.sum(jnp.where(lane == row, value, 0.0), axis=0, keepdims=True)

        groups_t = across(groups)
        base = jnp.sum(jnp.where(lane < row, groups_t, 0.0), axis=1, keepdims=True)
        section = row & -WIN
        inner = base - jnp.sum(jnp.where(lane < section, groups_t, 0.0), axis=1, keepdims=True)
        same = (lane & -WIN) == section
        in_step = jnp.sum(jnp.where(same, groups_t, 0.0), axis=1, keepdims=True)
        pos = slot_f + jnp.sum(jnp.where(member, base * 8.0 - starts, 0.0), axis=0, keepdims=True)
        pos_ref[...] = pos.astype(jnp.int32)
        pltpu.make_async_copy(pos_ref, at_ref, place_sem.at[0]).start()
        table_ref[...] = jnp.zeros_like(table_ref)
        for at, value in enumerate((counts, base, inner, in_step)):
            table_ref[at:at + 1, :] = across(value).astype(jnp.int32)
        pltpu.make_async_copy(table_ref, table_smem, place_sem.at[1]).start()

    if early:
        pl.when(step == 0)(find_places)
    block = tracers_ref.shape[2]
    begin = step * block
    in_group = lax.broadcasted_iota(jnp.int32, (8, LANES), 0)
    for half in range(block // LANES):
        span = slice(half * LANES, (half + 1) * LANES)
        at = pl.ds(pl.multiple_of(begin + half * LANES, LANES), LANES)
        turn_ref[lanes - 16:lanes, :] = jnp.zeros((16, LANES), jnp.float32)
        turn_ref[0:real, :] = tracers_ref[:, :, span].reshape(real, LANES)
        extra = jnp.where(in_group == 5, (phys_ref[:, at] & (columns - 1)).astype(jnp.float32), 0.0)
        extra = jnp.where(in_group == 6, rate_ref[:, at], extra)
        extra = jnp.where(in_group == 7, count_ref[:, at].astype(jnp.float32), extra)
        turn_ref[lanes - 8:lanes, :] = extra
        for tile in range(tiles):
            wide_ref[pl.ds(tile, LANES, stride=8), :] = turn_ref[
                tile * LANES:(tile + 1) * LANES, :
            ].T

        if early and half == 0:
            @pl.when(step == 0)
            def _():
                pltpu.make_async_copy(pos_ref, at_ref, place_sem.at[0]).wait()
                pltpu.make_async_copy(table_ref, table_smem, place_sem.at[1]).wait()

        def move(part, carry):
            for extra_row in range(16):
                column = part * 16 + extra_row
                to = at_ref[0, begin + half * LANES + column] * tiles
                record = wide_ref[pl.ds(pl.multiple_of(column * 8, 8), 8), :]
                sorted_ref[pl.ds(to, tiles), :] = record[:tiles]
            return carry

        lax.fori_loop(0, LANES // 16, move, 0)

    @pl.when(step == pl.num_programs(0) - 1)
    def _():
        copies = []
        for index, (target, to, begin, size, valid) in enumerate(cuts):
            begin = begin(table_smem)
            valid = jnp.clip(valid(table_smem), 0, size)
            copy = pltpu.make_async_copy(
                sorted_ref.at[span_of(begin, size, tiles)],
                cut_refs[target].at[span_of(to, size, tiles)], sem_ref.at[index],
            )
            pl.when(valid > 0)(copy.start)
            copies.append((valid > 0, copy))
        wait_all(copies)


def start_arrival(refs, sems, room_ref, in_step, static, tiles):
    waits = []
    for index, wanted in enumerate((None, in_step > static)):
        copy = pltpu.make_async_copy(
            refs[index], room_ref.at[pl.ds(index * static * 8 * tiles, refs[index].shape[0])],
            sems(index),
        )
        if wanted is None:
            copy.start()
        else:
            pl.when(wanted)(copy.start)
        waits.append((wanted, copy))
    return waits


def wait_all(waits):
    for wanted, copy in waits:
        if wanted is None:
            copy.wait()
        else:
            pl.when(wanted)(copy.wait)


def integrate_block(sizes, room_ref, first, valid, loss_ref, coupling_ref,
                    turn_ref, y_ref, inverse_ref):
    levels, pad, tiles = sizes
    halves = INT_ROWS // LANES
    lanes = tiles * LANES
    first = pl.multiple_of(first * 8 * tiles, 8)
    for half in range(halves):
        begin = first + half * LANES * tiles
        for tile in range(tiles):
            block = room_ref[pl.ds(begin + tile, LANES, stride=tiles), :]
            turn_ref[half, tile * LANES:(tile + 1) * LANES, :] = block.T
        for level in range(levels):
            y_ref[level, :, half * LANES:(half + 1) * LANES] = turn_ref[
                half, pl.ds(level, pad, stride=levels), :
            ]
    rate = jnp.concatenate(
        [turn_ref[half, lanes - 2:lanes - 1, :] for half in range(halves)], axis=1
    )
    count = jnp.concatenate(
        [turn_ref[half, lanes - 1:lanes, :] for half in range(halves)], axis=1
    )
    lane = lax.broadcasted_iota(jnp.int32, (1, INT_ROWS), 1)
    count = jnp.where((lane < valid) & (count <= MAXIT), count, 0.0)
    step_len = rate / jnp.maximum(count, 1.0)
    inverse_ref[...] = 1.0 / (1.0 + step_len * loss_ref[...])
    last = jnp.max(count).astype(jnp.int32)

    def advance(k, carry):
        active = k.astype(jnp.float32) < count

        def one_level(level, inner):
            y = y_ref[level]
            squashed = jnp.tanh(y).astype(jnp.bfloat16)
            produced = jnp.dot(coupling_ref[...], squashed, preferred_element_type=jnp.float32)
            y_ref[level] = jnp.where(active, (y + step_len * produced) * inverse_ref[...], y)
            return inner

        for level in range(levels):
            one_level(level, 0)
        return carry

    lax.fori_loop(0, last, advance, 0)
    for half in range(halves):
        begin = first + half * LANES * tiles
        for level in range(levels):
            turn_ref[half, pl.ds(level, pad, stride=levels), :] = y_ref[
                level, :, half * LANES:(half + 1) * LANES
            ]
        for tile in range(tiles):
            block = turn_ref[half, tile * LANES:(tile + 1) * LANES, :]
            room_ref[pl.ds(begin + tile, LANES, stride=tiles), :] = block.T


def integrate_kernel(sizes, plan, table_ref, loss_ref, coupling_ref, *refs):
    loads, merges, blocks, stores, operands = plan
    tiles = sizes[2]
    sources = refs[:operands]
    results = refs[operands:operands + len(stores)]
    room_ref, turn_ref, y_ref, inverse_ref, rows_ref, sem_ref, out_sem = refs[
        operands + len(stores):
    ]
    copies = []
    for index, (source, begin, groups, to) in enumerate(loads):
        ref = sources[source]
        if begin is not None:
            ref = ref.at[span_of(begin(table_ref), groups, tiles)]
        copies.append(pltpu.make_async_copy(
            ref, room_ref.at[span_of(to, groups, tiles)], sem_ref.at[index]
        ))
    for copy in copies:
        copy.start()
    for copy in copies:
        copy.wait()
    for begin, groups, to in merges:
        to = to(table_ref)

        def move(group, carry):
            room_ref[span_of(to + group, 1, tiles), :] = room_ref[
                span_of(begin + group, 1, tiles), :
            ]
            return carry

        lax.fori_loop(0, groups(table_ref), move, 0)
    for index, (begin, rows) in enumerate(blocks):
        rows_ref[0, index] = jnp.int32(begin)
        rows_ref[1, index] = rows(table_ref)

    def one_block(index, carry):
        valid = rows_ref[1, index]

        @pl.when(valid > 0)
        def _():
            integrate_block(sizes, room_ref, rows_ref[0, index], valid, loss_ref, coupling_ref,
                            turn_ref, y_ref, inverse_ref)

        return carry

    lax.fori_loop(0, len(blocks), one_block, 0)
    copies = []
    for index, (begin, groups) in enumerate(stores):
        copies.append(pltpu.make_async_copy(
            room_ref.at[span_of(begin(table_ref), groups, tiles)], results[index],
            out_sem.at[index],
        ))
    for copy in copies:
        copy.start()
    for copy in copies:
        copy.wait()


def cut_kernel(static, tiles, piece, step, table_ref, *refs):
    pieces = refs[2:2 + WIN]
    room_ref, sem_ref, out_sem = refs[2 + WIN:]
    wait_all(start_arrival(refs[:2], lambda at: sem_ref.at[at], room_ref,
                           table_ref[3, step * WIN], static, tiles))
    copies = []
    half = piece // 2
    for at in range(WIN):
        begin = table_ref[2, step * WIN + at]
        for part in range(2):
            wanted = table_ref[0, step * WIN + at] > part * half * 8
            copy = pltpu.make_async_copy(
                room_ref.at[span_of(begin + part * half, half, tiles)],
                pieces[at].at[span_of(part * half, half, tiles)], out_sem.at[part, at],
            )
            pl.when(wanted)(copy.start)
            copies.append((wanted, copy))
    wait_all(copies)


def finish_kernel(sizes, table_ref, *refs):
    species, levels, columns, tiles, static, piece, narrow_count, begins = sizes
    pair_total = narrow_count * WIN
    whole_pieces = pair_total - WIN
    out_ref, piece_ref, room_ref, placed_ref, whole_ref, sem_ref, out_sem = refs[-7:]
    copies = []
    half = piece // 2
    for pair in range(whole_pieces):
        both = []
        for part in range(2):
            copy = pltpu.make_async_copy(
                refs[pair].at[span_of(begins[pair] + part * half, half, tiles)],
                piece_ref.at[pair, span_of(part * half, half, tiles)], sem_ref.at[part, pair],
            )
            wanted = table_ref[0, pair] > part * half * 8
            pl.when(wanted)(copy.start)
            both.append((wanted, copy))
        copies.append(both)
    waits = start_arrival(refs[whole_pieces:whole_pieces + 2],
                          lambda at: sem_ref.at[at, whole_pieces], room_ref,
                          table_ref[3, whole_pieces], static, tiles)
    lane = lax.broadcasted_iota(jnp.int32, (1, LANES), 1)
    in_group = lax.broadcasted_iota(jnp.int32, (8, LANES), 0)
    for pair in range(pair_total):
        if pair < whole_pieces:
            wait_all(copies[pair])
            held = piece_ref.at[pair]
            begin = 0
        else:
            if pair == whole_pieces:
                wait_all(waits)
            held = room_ref
            begin = pl.multiple_of(table_ref[2, pair] * 8 * tiles, 8)
        count = table_ref[0, pair]
        first = held[pl.ds(begin + tiles - 1, 1), :]
        start = jnp.max(jnp.where(lane == LANES - 3, first, 0.0)).astype(jnp.int32)
        start = jnp.clip(start, 0, columns - 1) * tiles
        full = lax.shift_right_logical(count, 3)

        def move(group, carry):
            for row in range(0, 8 * tiles, 8):
                at = group * 8 * tiles + row
                placed_ref[pl.ds(start + at, 8), :] = held[pl.ds(pl.multiple_of(begin + at, 8), 8), :]
            return carry

        lax.fori_loop(0, full, move, 0)

        @pl.when((count & 7) > 0)
        def _():
            for row in range(0, 8 * tiles, 8):
                at = full * 8 * tiles + row
                to = pl.ds(start + at, 8)
                placed_ref[to, :] = jnp.where(
                    in_group + row < (count & 7) * tiles,
                    held[pl.ds(pl.multiple_of(begin + at, 8), 8), :], placed_ref[to, :],
                )

    per_tile = LANES // levels
    for part in range(columns // LANES):
        at = slice(part * LANES, (part + 1) * LANES)
        for tile in range(tiles):
            block = placed_ref[pl.ds(part * LANES * tiles + tile, LANES, stride=tiles), :]
            block = block.T.reshape(per_tile, levels, LANES)
            keep = min(per_tile, species - tile * per_tile)
            whole_ref[tile * per_tile:tile * per_tile + keep, :, at] = block[:keep]
        pltpu.make_async_copy(whole_ref.at[:, :, at], out_ref.at[:, :, at], out_sem.at[part]).start()
    for part in range(columns // LANES):
        at = slice(part * LANES, (part + 1) * LANES)
        pltpu.make_async_copy(whole_ref.at[:, :, at], out_ref.at[:, :, at], out_sem.at[part]).wait()


def local(tracers, column_rate, loss_rate, coupling, phys_index, iter_count):
    levels, species, columns = tracers.shape
    wide_count = lax.axis_size("wide")
    narrow_count = lax.axis_size("narrow")
    pair_total = WIN * narrow_count
    room = 2 * columns // pair_total
    piece = room // 8
    pad = -(-species // 8) * 8
    while levels * pad % LANES or levels * (pad - species) < 8:
        pad += 8
    tiles = levels * pad // LANES
    mean = columns // narrow_count // 8
    full = pl.BlockSpec(memory_space=pltpu.VMEM)
    smem = pl.BlockSpec(memory_space=pltpu.SMEM)
    hbm = pl.BlockSpec(memory_space=pltpu.HBM)
    last = narrow_count - 1
    moving = [at for at in range(WIN) if at != 1]
    order = [narrow_count // 2]
    order += [step for step in range(1, last) if step not in order] + [last]
    statics = {step: mean if step == order[0] else mean + mean // 8 for step in order}
    most = WIN * piece

    params = pltpu.CompilerParams(vmem_limit_bytes=VMEM)

    def rows_type(groups):
        return jax.ShapeDtypeStruct((groups * 8 * tiles, LANES), jnp.float32)

    def room_type(groups):
        return pltpu.VMEM((groups * 8 * tiles, LANES), jnp.float32)

    def entry(row, step, at=0):
        return lambda table: table[row, step * WIN + at]

    def over(step):
        return lambda table: entry(1, step)(table) + statics[step]

    def groups_of(step, at):
        return lambda table: lax.shift_right_logical(table[0, step * WIN + at] + 7, 3)

    def groups_over(step):
        return lambda table: table[3, step * WIN] - statics[step]

    def pair_cuts(target, at):
        return [
            (target, part * piece + half,
             lambda table, step=step, half=half: entry(1, step, at)(table) + half, piece // 2,
             lambda table, step=step, half=half: groups_of(step, at)(table) - half)
            for part, step in enumerate((0, last)) for half in range(0, piece, piece // 2)
        ]

    def sort(cuts, target_sizes, early, known):
        known_types = [
            jax.ShapeDtypeStruct((8, LANES), jnp.int32),
            jax.ShapeDtypeStruct((1, columns), jnp.int32),
        ]
        groups = columns // 8 + pair_total + most
        return pl.pallas_call(
            functools.partial(
                sort_kernel,
                (species, levels, columns, tiles, wide_count, narrow_count, pair_total),
                cuts, len(target_sizes), early,
            ),
            grid=(columns // SORT_COLUMNS,),
            in_specs=[full, full, full,
                      pl.BlockSpec((species, levels, SORT_COLUMNS), lambda at: (0, 0, at))]
            + [smem] * len(known),
            out_specs=([full, full] if early else []) + [hbm] * len(target_sizes),
            out_shape=(known_types if early else []) + [rows_type(size) for size in target_sizes],
            scratch_shapes=([
                pltpu.SMEM((1, columns), jnp.int32), pltpu.SMEM((8, LANES), jnp.int32),
                pltpu.SemaphoreType.DMA((2,)),
            ] if early else []) + [
                pltpu.VMEM((tiles * LANES, LANES), jnp.float32),
                pltpu.VMEM((LANES * 8, LANES), jnp.float32),
                room_type(groups),
                pltpu.SemaphoreType.DMA((len(cuts),)),
            ],
            compiler_params=params,
            name="sort_columns" if early else "sort_later_columns",
        )(
            phys_index.reshape(1, columns),
            column_rate.reshape(1, columns),
            iter_count.reshape(1, columns),
            tracers.transpose(1, 0, 2),
            *known,
        )

    cuts = [(0, 0, entry(1, order[0]), mean, entry(3, order[0]))]
    for index, at in enumerate(moving):
        cuts += pair_cuts(1 + index, at)
    table, places, *first = sort(cuts, [mean] + [2 * piece] * len(moving), True, ())
    cuts = [(0, 0, over(order[0]), most - mean, groups_over(order[0]))] + pair_cuts(1, 1)
    for index, step in enumerate(order[1:-1]):
        rest = most - statics[step]
        cuts.append((2 + index, 0, entry(1, step), statics[step], entry(3, step)))
        cuts.append((2 + index, statics[step], over(step), rest, groups_over(step)))
    first_rest, local_rows, *raw = sort(
        cuts, [most - mean, 2 * piece] + [most] * (len(order) - 2), False, (table, places)
    )
    raw_groups = dict(zip(order[1:-1], raw))
    units = [
        (jnp.maximum(table[3, step * WIN] - statics[step], 0) + UNIT - 1) // UNIT
        for step in order
    ]
    loss_pad = jnp.pad(loss_rate, (0, pad - species)).reshape(pad, 1)
    coupling_pad = jnp.pad(coupling, ((0, pad - species), (0, pad - species)))
    block = INT_ROWS // 8

    def integrate(table, operands, loads, merges, blocks, stores):
        groups = max([to + size for _, _, size, to in loads] + [begin + block for begin, _ in blocks])
        groups += piece
        flops = 2 * levels * pad * pad * 6 * INT_ROWS * len(blocks)
        return pl.pallas_call(
            functools.partial(
                integrate_kernel, (levels, pad, tiles),
                (loads, merges, blocks, stores, len(operands)),
            ),
            in_specs=[smem, full, full] + [hbm] * len(operands),
            out_specs=[hbm] * len(stores),
            out_shape=[rows_type(size) for _, size in stores],
            scratch_shapes=[
                room_type(groups),
                pltpu.VMEM((INT_ROWS // LANES, tiles * LANES, LANES), jnp.float32),
                pltpu.VMEM((levels, pad, INT_ROWS), jnp.float32),
                pltpu.VMEM((pad, INT_ROWS), jnp.float32),
                pltpu.SMEM((2, LANES), jnp.int32),
                pltpu.SemaphoreType.DMA((len(loads),)),
                pltpu.SemaphoreType.DMA((len(stores),)),
            ],
            compiler_params=params,
            cost_estimate=pl.CostEstimate(
                flops=flops, bytes_accessed=8 * groups * 8 * tiles * LANES,
                transcendentals=flops // (2 * pad),
            ),
            name="integrate_columns",
        )(table, loss_pad, coupling_pad, *operands)

    def rows_of(step, at=0):
        return entry(0, step, at)

    def group_blocks(begin, step):
        return [
            (begin + part * block,
             lambda table, part=part: table[3, step * WIN] * 8 - part * INT_ROWS)
            for part in range(most // block)
        ]

    def here(begin):
        return lambda table: jnp.int32(begin)

    def step_over(step, units, rest):
        def leaf(units, rest):
            if units == 0:
                return jnp.zeros_like(rest)
            got = from_behind(rest[:units * UNIT * 8 * tiles], "narrow", step)
            return jnp.pad(got, ((0, rest.shape[0] - got.shape[0]), (0, 0)))

        leaves = [functools.partial(leaf, count) for count in range((most - statics[step]) // UNIT + 1)]
        return lax.switch(units, leaves, rest)

    pieces = {}
    outgoing = [first[0], first_rest]
    wide_now = first[1:]
    keys_now = [[(at, 0), (at, last)] for at in moving]
    static_part = from_behind(outgoing[0], "narrow", order[0])
    wide_got = [from_behind(value, "wide", at - 1) for value, at in zip(wide_now, moving)]
    table_then = table
    for phase, step in enumerate(order):
        static = statics[step]
        operands, loads, merges, blocks, stores, named = [], [], [], [], [], []
        used = 0
        if phase + 1 < len(order):
            coming = order[phase + 1]
            if coming == last:
                operands += [pieces[at, last][0] for at in moving] + [local_rows]
                for index, at in enumerate(moving):
                    loads.append((index, here(pieces[at, last][1]), piece, most + at * piece))
                loads.append((len(moving), here(piece), piece, most + piece))
                for at in range(WIN):
                    merges.append(
                        (most + at * piece, groups_of(last, at), entry(2, last, at))
                    )
                used = most + WIN * piece
            else:
                operands.append(raw_groups[coming])
                loads.append((0, None, most, 0))
                used = most
            blocks += group_blocks(0, coming)
            stores += [(here(0), statics[coming]), (here(statics[coming]), most - statics[coming])]
        extra = []
        if phase == 0:
            extra.append(((1, 0), (local_rows, 0)))
        if phase == 1:
            extra += [((at, 0), pieces[at, 0]) for at in moving]
        if phase == 2:
            extra += [((at, order[0]), pieces[at, order[0]]) for at in range(WIN)]
        used = -(-used // block) * block
        for key, value in extra:
            operands.append(value[0])
            loads.append((len(operands) - 1, here(value[1]), piece, used))
            blocks.append((used, rows_of(key[1], key[0])))
            stores.append((here(used), piece))
            named.append(key)
            used += block
        if stores:
            results = integrate(table_then, operands, loads, merges, blocks, stores)
        else:
            results = []
        rest = outgoing[1]
        if phase == 0:
            static_part, results, rest, wide_got, units = lax.optimization_barrier(
                (static_part, results, rest, wide_got, units)
            )
        elif step != last:
            static_part, results, rest, wide_got = lax.optimization_barrier(
                (static_part, results, rest, wide_got)
            )
        else:
            static_part, results, rest = lax.optimization_barrier((static_part, results, rest))
        done = {key: (value, 0) for key, value in zip(named, results[len(results) - len(named):])}
        outgoing = results[:len(results) - len(named)]
        arrived = [static_part, step_over(step, units[phase], rest)]
        if step != last:
            arrived, outgoing = lax.optimization_barrier((arrived, outgoing))
            static_part = from_behind(outgoing[0], "narrow", order[phase + 1])
        if step != last:
            cut = pl.pallas_call(
                functools.partial(cut_kernel, static, tiles, piece, step),
                in_specs=[smem] + [hbm] * len(arrived),
                out_specs=[hbm] * WIN,
                out_shape=[rows_type(piece)] * WIN,
                scratch_shapes=[
                    room_type(most + piece),
                    pltpu.SemaphoreType.DMA((len(arrived),)),
                    pltpu.SemaphoreType.DMA((2, WIN)),
                ],
                compiler_params=params,
                name="cut_pieces",
            )(table, *arrived)
            cut, table_then = lax.optimization_barrier((cut, table))
        for keys, value in zip(keys_now, wide_got):
            pieces.update({key: (value, part * piece) for part, key in enumerate(keys)})
        pieces.update(done)
        if step != last:
            pieces[1, step] = (cut[1], 0)
            keys_now = [[(at, step)] for at in moving]
            wide_got = [from_behind(cut[at], "wide", at - 1) for at in moving]

    held = [pieces[at, step] for step in range(last) for at in range(WIN)]
    buffers = [value for value, _ in held] + arrived
    updated = pl.pallas_call(
        functools.partial(
            finish_kernel,
            (species, levels, columns, tiles, static, piece, narrow_count,
             [begin for _, begin in held]),
        ),
        in_specs=[smem] + [hbm] * len(buffers),
        out_specs=hbm,
        out_shape=jax.ShapeDtypeStruct((species, levels, columns), jnp.float32),
        scratch_shapes=[
            pltpu.VMEM((pair_total - WIN, piece * 8 * tiles, LANES), jnp.float32),
            room_type(most + piece),
            room_type(columns // 8 + 1),
            pltpu.VMEM((species, levels, columns), jnp.float32),
            pltpu.SemaphoreType.DMA((2, pair_total)),
            pltpu.SemaphoreType.DMA((columns // LANES,)),
        ],
        compiler_params=params,
        name="place_columns",
    )(table, *buffers)
    return updated.transpose(1, 0, 2)


def solution(mesh):
    placed = (
        P(None, None, ("wide", "narrow")),
        P(("wide", "narrow")),
        P(),
        P(),
        P(("wide", "narrow")),
        P(("wide", "narrow")),
    )
    return jax.shard_map(
        local,
        mesh=mesh,
        in_specs=placed,
        out_specs=P(None, None, ("wide", "narrow")),
        check_vma=False,
    )
```

```python
import functools

import jax
import jax.numpy as jnp
from jax import lax
from jax.experimental import pallas as pl
from jax.experimental.pallas import tpu as pltpu
from jax.sharding import PartitionSpec as P

WIN = 4
MAXIT = 12
LANES = 128
SORT_COLUMNS = 256
INT_ROWS = 256
UNIT = 8
VMEM = 62 * 1024 * 1024


def from_behind(value, axis, steps):
    count = lax.axis_size(axis)
    pairs = [(source, (source + steps) % count) for source in range(count)]
    return lax.ppermute(value, axis, pairs)


def log2(value):
    bits = value.bit_length() - 1
    assert 1 << bits == value
    return bits


def span_of(group, groups, tiles):
    return pl.ds(pl.multiple_of(group * 8 * tiles, 8), groups * 8 * tiles)


def sort_kernel(sizes, cuts, targets, early, *refs):
    species, levels, columns, tiles, wide_count, narrow_count, pair_total = sizes
    turn_ref, wide_ref, sorted_ref = refs[-4:-1]
    sem_ref = refs[-1]
    if early:
        phys_ref, rate_ref, count_ref, tracers_ref, table_ref, pos_ref = refs[:6]
        cut_refs = refs[6:6 + targets]
        at_ref, table_smem, place_sem = refs[6 + targets:9 + targets]
    else:
        phys_ref, rate_ref, count_ref, tracers_ref, table_smem, at_ref = refs[:6]
        cut_refs = refs[6:6 + targets]
    step = pl.program_id(0)
    lanes = tiles * LANES
    real = species * levels

    def find_places():
        phys = phys_ref[...]
        target = lax.shift_right_logical(phys, log2(columns))
        slot = phys & (columns - 1)
        wide_step = lax.shift_right_logical(target, log2(narrow_count)) - lax.axis_index("wide")
        wide_step = (wide_step + 1) & (wide_count - 1)
        narrow_step = ((target & (narrow_count - 1)) - lax.axis_index("narrow")) & (narrow_count - 1)
        pair = narrow_step * WIN + wide_step
        member = pair == lax.broadcasted_iota(jnp.int32, (pair_total, columns), 0)
        counts = jnp.sum(jnp.where(member, 1.0, 0.0), axis=1, keepdims=True)
        slot_f = slot.astype(jnp.float32)
        starts = jnp.min(jnp.where(member, slot_f, float(columns)), axis=1, keepdims=True)
        groups = lax.shift_right_logical(counts.astype(jnp.int32) + 7, 3).astype(jnp.float32)
        lane = lax.broadcasted_iota(jnp.int32, (pair_total, LANES), 1)
        row = lax.broadcasted_iota(jnp.int32, (pair_total, LANES), 0)

        def across(value):
            return jnp.sum(jnp.where(lane == row, value, 0.0), axis=0, keepdims=True)

        groups_t = across(groups)
        base = jnp.sum(jnp.where(lane < row, groups_t, 0.0), axis=1, keepdims=True)
        section = row & -WIN
        inner = base - jnp.sum(jnp.where(lane < section, groups_t, 0.0), axis=1, keepdims=True)
        same = (lane & -WIN) == section
        in_step = jnp.sum(jnp.where(same, groups_t, 0.0), axis=1, keepdims=True)
        pos = slot_f + jnp.sum(jnp.where(member, base * 8.0 - starts, 0.0), axis=0, keepdims=True)
        pos_ref[...] = pos.astype(jnp.int32)
        pltpu.make_async_copy(pos_ref, at_ref, place_sem.at[0]).start()
        table_ref[...] = jnp.zeros_like(table_ref)
        for at, value in enumerate((counts, base, inner, in_step)):
            table_ref[at:at + 1, :] = across(value).astype(jnp.int32)
        pltpu.make_async_copy(table_ref, table_smem, place_sem.at[1]).start()

    if early:
        pl.when(step == 0)(find_places)
    block = tracers_ref.shape[2]
    begin = step * block
    in_group = lax.broadcasted_iota(jnp.int32, (8, LANES), 0)
    for half in range(block // LANES):
        span = slice(half * LANES, (half + 1) * LANES)
        at = pl.ds(pl.multiple_of(begin + half * LANES, LANES), LANES)
        turn_ref[lanes - 16:lanes, :] = jnp.zeros((16, LANES), jnp.float32)
        turn_ref[0:real, :] = tracers_ref[:, :, span].reshape(real, LANES)
        extra = jnp.where(in_group == 5, (phys_ref[:, at] & (columns - 1)).astype(jnp.float32), 0.0)
        extra = jnp.where(in_group == 6, rate_ref[:, at], extra)
        extra = jnp.where(in_group == 7, count_ref[:, at].astype(jnp.float32), extra)
        turn_ref[lanes - 8:lanes, :] = extra
        for tile in range(tiles):
            wide_ref[half, pl.ds(tile, LANES, stride=8), :] = turn_ref[
                tile * LANES:(tile + 1) * LANES, :
            ].T

        if early and half == 0:
            @pl.when(step == 0)
            def _():
                pltpu.make_async_copy(pos_ref, at_ref, place_sem.at[0]).wait()
                pltpu.make_async_copy(table_ref, table_smem, place_sem.at[1]).wait()

        for column in range(LANES):
            to = at_ref[0, begin + half * LANES + column] * tiles
            sorted_ref[pl.ds(to, tiles), :] = wide_ref[half, column * 8:column * 8 + tiles, :]

    @pl.when(step == pl.num_programs(0) - 1)
    def _():
        copies = []
        for index, (target, to, begin, size, valid) in enumerate(cuts):
            begin = begin(table_smem)
            valid = jnp.clip(valid(table_smem), 0, size)
            copy = pltpu.make_async_copy(
                sorted_ref.at[span_of(begin, size, tiles)],
                cut_refs[target].at[span_of(to, size, tiles)], sem_ref.at[index],
            )
            pl.when(valid > 0)(copy.start)
            copies.append((valid > 0, copy))
        wait_all(copies)


def start_arrival(refs, sems, room_ref, in_step, static, tiles):
    waits = []
    for index, wanted in enumerate((None, in_step > static)):
        copy = pltpu.make_async_copy(
            refs[index], room_ref.at[pl.ds(index * static * 8 * tiles, refs[index].shape[0])],
            sems(index),
        )
        if wanted is None:
            copy.start()
        else:
            pl.when(wanted)(copy.start)
        waits.append((wanted, copy))
    return waits


def wait_all(waits):
    for wanted, copy in waits:
        if wanted is None:
            copy.wait()
        else:
            pl.when(wanted)(copy.wait)


def integrate_block(sizes, room_ref, first, valid, loss_ref, coupling_ref,
                    turn_ref, y_ref, inverse_ref):
    levels, pad, tiles = sizes
    halves = INT_ROWS // LANES
    lanes = tiles * LANES
    first = pl.multiple_of(first * 8 * tiles, 8)
    for half in range(halves):
        begin = first + half * LANES * tiles
        for tile in range(tiles):
            block = room_ref[pl.ds(begin + tile, LANES, stride=tiles), :]
            turn_ref[half, tile * LANES:(tile + 1) * LANES, :] = block.T
        for level in range(levels):
            y_ref[level, :, half * LANES:(half + 1) * LANES] = turn_ref[
                half, pl.ds(level, pad, stride=levels), :
            ]
    rate = jnp.concatenate(
        [turn_ref[half, lanes - 2:lanes - 1, :] for half in range(halves)], axis=1
    )
    count = jnp.concatenate(
        [turn_ref[half, lanes - 1:lanes, :] for half in range(halves)], axis=1
    )
    lane = lax.broadcasted_iota(jnp.int32, (1, INT_ROWS), 1)
    count = jnp.where((lane < valid) & (count <= MAXIT), count, 0.0)
    step_len = rate / jnp.maximum(count, 1.0)
    inverse_ref[...] = 1.0 / (1.0 + step_len * loss_ref[...])
    last = jnp.max(count).astype(jnp.int32)

    def advance(k, carry):
        active = k.astype(jnp.float32) < count

        def one_level(level, inner):
            y = y_ref[level]
            squashed = jnp.tanh(y).astype(jnp.bfloat16)
            produced = jnp.dot(coupling_ref[...], squashed, preferred_element_type=jnp.float32)
            y_ref[level] = jnp.where(active, (y + step_len * produced) * inverse_ref[...], y)
            return inner

        for level in range(levels):
            one_level(level, 0)
        return carry

    lax.fori_loop(0, last, advance, 0)
    for half in range(halves):
        begin = first + half * LANES * tiles
        for level in range(levels):
            turn_ref[half, pl.ds(level, pad, stride=levels), :] = y_ref[
                level, :, half * LANES:(half + 1) * LANES
            ]
        for tile in range(tiles):
            block = turn_ref[half, tile * LANES:(tile + 1) * LANES, :]
            room_ref[pl.ds(begin + tile, LANES, stride=tiles), :] = block.T


def integrate_kernel(sizes, plan, table_ref, loss_ref, coupling_ref, *refs):
    loads, merges, blocks, stores, operands = plan
    tiles = sizes[2]
    sources = refs[:operands]
    results = refs[operands:operands + len(stores)]
    room_ref, turn_ref, y_ref, inverse_ref, rows_ref, sem_ref, out_sem = refs[
        operands + len(stores):
    ]
    copies = []
    for index, (source, begin, groups, to) in enumerate(loads):
        ref = sources[source]
        if begin is not None:
            ref = ref.at[span_of(begin(table_ref), groups, tiles)]
        copies.append(pltpu.make_async_copy(
            ref, room_ref.at[span_of(to, groups, tiles)], sem_ref.at[index]
        ))
    for copy in copies:
        copy.start()
    for copy in copies:
        copy.wait()
    for begin, groups, to in merges:
        to = to(table_ref)

        def move(group, carry):
            room_ref[span_of(to + group, 1, tiles), :] = room_ref[
                span_of(begin + group, 1, tiles), :
            ]
            return carry

        lax.fori_loop(0, groups(table_ref), move, 0)
    for index, (begin, rows) in enumerate(blocks):
        rows_ref[0, index] = jnp.int32(begin)
        rows_ref[1, index] = rows(table_ref)

    def one_block(index, carry):
        valid = rows_ref[1, index]

        @pl.when(valid > 0)
        def _():
            integrate_block(sizes, room_ref, rows_ref[0, index], valid, loss_ref, coupling_ref,
                            turn_ref, y_ref, inverse_ref)

        return carry

    lax.fori_loop(0, len(blocks), one_block, 0)
    copies = []
    for index, (begin, groups) in enumerate(stores):
        copies.append(pltpu.make_async_copy(
            room_ref.at[span_of(begin(table_ref), groups, tiles)], results[index],
            out_sem.at[index],
        ))
    for copy in copies:
        copy.start()
    for copy in copies:
        copy.wait()


def cut_kernel(static, tiles, piece, step, table_ref, *refs):
    pieces = refs[2:2 + WIN]
    room_ref, sem_ref, out_sem = refs[2 + WIN:]
    wait_all(start_arrival(refs[:2], lambda at: sem_ref.at[at], room_ref,
                           table_ref[3, step * WIN], static, tiles))
    copies = []
    half = piece // 2
    for at in range(WIN):
        begin = table_ref[2, step * WIN + at]
        for part in range(2):
            wanted = table_ref[0, step * WIN + at] > part * half * 8
            copy = pltpu.make_async_copy(
                room_ref.at[span_of(begin + part * half, half, tiles)],
                pieces[at].at[span_of(part * half, half, tiles)], out_sem.at[part, at],
            )
            pl.when(wanted)(copy.start)
            copies.append((wanted, copy))
    wait_all(copies)


def finish_kernel(sizes, table_ref, *refs):
    species, levels, columns, tiles, static, piece, narrow_count, begins = sizes
    pair_total = narrow_count * WIN
    whole_pieces = pair_total - WIN
    out_ref, piece_ref, room_ref, placed_ref, whole_ref, sem_ref, out_sem = refs[-7:]
    copies = []
    half = piece // 2
    for pair in range(whole_pieces):
        both = []
        for part in range(2):
            copy = pltpu.make_async_copy(
                refs[pair].at[span_of(begins[pair] + part * half, half, tiles)],
                piece_ref.at[pair, span_of(part * half, half, tiles)], sem_ref.at[part, pair],
            )
            wanted = table_ref[0, pair] > part * half * 8
            pl.when(wanted)(copy.start)
            both.append((wanted, copy))
        copies.append(both)
    waits = start_arrival(refs[whole_pieces:whole_pieces + 2],
                          lambda at: sem_ref.at[at, whole_pieces], room_ref,
                          table_ref[3, whole_pieces], static, tiles)
    lane = lax.broadcasted_iota(jnp.int32, (1, LANES), 1)
    in_group = lax.broadcasted_iota(jnp.int32, (8, LANES), 0)
    for pair in range(pair_total):
        if pair < whole_pieces:
            wait_all(copies[pair])
            held = piece_ref.at[pair]
            begin = 0
        else:
            if pair == whole_pieces:
                wait_all(waits)
            held = room_ref
            begin = pl.multiple_of(table_ref[2, pair] * 8 * tiles, 8)
        count = table_ref[0, pair]
        first = held[pl.ds(begin + tiles - 1, 1), :]
        start = jnp.max(jnp.where(lane == LANES - 3, first, 0.0)).astype(jnp.int32)
        start = jnp.clip(start, 0, columns - 1) * tiles
        full = lax.shift_right_logical(count, 3)

        def move(group, carry):
            for row in range(0, 8 * tiles, 8):
                at = group * 8 * tiles + row
                placed_ref[pl.ds(start + at, 8), :] = held[pl.ds(pl.multiple_of(begin + at, 8), 8), :]
            return carry

        lax.fori_loop(0, full, move, 0)

        @pl.when((count & 7) > 0)
        def _():
            for row in range(0, 8 * tiles, 8):
                at = full * 8 * tiles + row
                to = pl.ds(start + at, 8)
                placed_ref[to, :] = jnp.where(
                    in_group + row < (count & 7) * tiles,
                    held[pl.ds(pl.multiple_of(begin + at, 8), 8), :], placed_ref[to, :],
                )

    per_tile = LANES // levels
    for part in range(columns // LANES):
        at = slice(part * LANES, (part + 1) * LANES)
        for tile in range(tiles):
            block = placed_ref[pl.ds(part * LANES * tiles + tile, LANES, stride=tiles), :]
            block = block.T.reshape(per_tile, levels, LANES)
            keep = min(per_tile, species - tile * per_tile)
            whole_ref[tile * per_tile:tile * per_tile + keep, :, at] = block[:keep]
        pltpu.make_async_copy(whole_ref.at[:, :, at], out_ref.at[:, :, at], out_sem.at[part]).start()
    for part in range(columns // LANES):
        at = slice(part * LANES, (part + 1) * LANES)
        pltpu.make_async_copy(whole_ref.at[:, :, at], out_ref.at[:, :, at], out_sem.at[part]).wait()


def local(tracers, column_rate, loss_rate, coupling, phys_index, iter_count):
    levels, species, columns = tracers.shape
    wide_count = lax.axis_size("wide")
    narrow_count = lax.axis_size("narrow")
    pair_total = WIN * narrow_count
    room = 2 * columns // pair_total
    piece = room // 8
    pad = -(-species // 8) * 8
    while levels * pad % LANES or levels * (pad - species) < 8:
        pad += 8
    tiles = levels * pad // LANES
    mean = columns // narrow_count // 8
    full = pl.BlockSpec(memory_space=pltpu.VMEM)
    smem = pl.BlockSpec(memory_space=pltpu.SMEM)
    hbm = pl.BlockSpec(memory_space=pltpu.HBM)
    last = narrow_count - 1
    moving = [at for at in range(WIN) if at != 1]
    order = [narrow_count // 2]
    order += [step for step in range(1, last) if step not in order] + [last]
    statics = {step: mean for step in order}
    most = WIN * piece

    params = pltpu.CompilerParams(vmem_limit_bytes=VMEM)

    def rows_type(groups):
        return jax.ShapeDtypeStruct((groups * 8 * tiles, LANES), jnp.float32)

    def room_type(groups):
        return pltpu.VMEM((groups * 8 * tiles, LANES), jnp.float32)

    def entry(row, step, at=0):
        return lambda table: table[row, step * WIN + at]

    def over(step):
        return lambda table: entry(1, step)(table) + statics[step]

    def groups_of(step, at):
        return lambda table: lax.shift_right_logical(table[0, step * WIN + at] + 7, 3)

    def groups_over(step):
        return lambda table: table[3, step * WIN] - statics[step]

    def pair_cuts(target, at):
        return [
            (target, part * piece + half,
             lambda table, step=step, half=half: entry(1, step, at)(table) + half, piece // 2,
             lambda table, step=step, half=half: groups_of(step, at)(table) - half)
            for part, step in enumerate((0, last)) for half in range(0, piece, piece // 2)
        ]

    def sort(cuts, target_sizes, early, known):
        known_types = [
            jax.ShapeDtypeStruct((8, LANES), jnp.int32),
            jax.ShapeDtypeStruct((1, columns), jnp.int32),
        ]
        groups = columns // 8 + pair_total + most
        return pl.pallas_call(
            functools.partial(
                sort_kernel,
                (species, levels, columns, tiles, wide_count, narrow_count, pair_total),
                cuts, len(target_sizes), early,
            ),
            grid=(columns // SORT_COLUMNS,),
            in_specs=[full, full, full,
                      pl.BlockSpec((species, levels, SORT_COLUMNS), lambda at: (0, 0, at))]
            + [smem] * len(known),
            out_specs=([full, full] if early else []) + [hbm] * len(target_sizes),
            out_shape=(known_types if early else []) + [rows_type(size) for size in target_sizes],
            scratch_shapes=([
                pltpu.SMEM((1, columns), jnp.int32), pltpu.SMEM((8, LANES), jnp.int32),
                pltpu.SemaphoreType.DMA((2,)),
            ] if early else []) + [
                pltpu.VMEM((tiles * LANES, LANES), jnp.float32),
                pltpu.VMEM((SORT_COLUMNS // LANES, LANES * 8, LANES), jnp.float32),
                room_type(groups),
                pltpu.SemaphoreType.DMA((len(cuts),)),
            ],
            compiler_params=params,
            name="sort_columns" if early else "sort_later_columns",
        )(
            phys_index.reshape(1, columns),
            column_rate.reshape(1, columns),
            iter_count.reshape(1, columns),
            tracers.transpose(1, 0, 2),
            *known,
        )

    cuts = [(0, 0, entry(1, order[0]), mean, entry(3, order[0]))]
    for index, at in enumerate(moving):
        cuts += pair_cuts(1 + index, at)
    table, places, *first = sort(cuts, [mean] + [2 * piece] * len(moving), True, ())
    cuts = [(0, 0, over(order[0]), most - mean, groups_over(order[0]))] + pair_cuts(1, 1)
    for index, step in enumerate(order[1:-1]):
        rest = most - statics[step]
        cuts.append((2 + index, 0, entry(1, step), statics[step], entry(3, step)))
        cuts.append((2 + index, statics[step], over(step), rest, groups_over(step)))
    first_rest, local_rows, *raw = sort(
        cuts, [most - mean, 2 * piece] + [most] * (len(order) - 2), False, (table, places)
    )
    raw_groups = dict(zip(order[1:-1], raw))
    units = [
        (jnp.maximum(table[3, step * WIN] - statics[step], 0) + UNIT - 1) // UNIT
        for step in order
    ]
    loss_pad = jnp.pad(loss_rate, (0, pad - species)).reshape(pad, 1)
    coupling_pad = jnp.pad(coupling, ((0, pad - species), (0, pad - species)))
    block = INT_ROWS // 8

    def integrate(table, operands, loads, merges, blocks, stores):
        groups = max([to + size for _, _, size, to in loads] + [begin + block for begin, _ in blocks])
        groups += piece
        flops = 2 * levels * pad * pad * 6 * INT_ROWS * len(blocks)
        return pl.pallas_call(
            functools.partial(
                integrate_kernel, (levels, pad, tiles),
                (loads, merges, blocks, stores, len(operands)),
            ),
            in_specs=[smem, full, full] + [hbm] * len(operands),
            out_specs=[hbm] * len(stores),
            out_shape=[rows_type(size) for _, size in stores],
            scratch_shapes=[
                room_type(groups),
                pltpu.VMEM((INT_ROWS // LANES, tiles * LANES, LANES), jnp.float32),
                pltpu.VMEM((levels, pad, INT_ROWS), jnp.float32),
                pltpu.VMEM((pad, INT_ROWS), jnp.float32),
                pltpu.SMEM((2, LANES), jnp.int32),
                pltpu.SemaphoreType.DMA((len(loads),)),
                pltpu.SemaphoreType.DMA((len(stores),)),
            ],
            compiler_params=params,
            cost_estimate=pl.CostEstimate(
                flops=flops, bytes_accessed=8 * groups * 8 * tiles * LANES,
                transcendentals=flops // (2 * pad),
            ),
            name="integrate_columns",
        )(table, loss_pad, coupling_pad, *operands)

    def rows_of(step, at=0):
        return entry(0, step, at)

    def group_blocks(begin, step):
        return [
            (begin + part * block,
             lambda table, part=part: table[3, step * WIN] * 8 - part * INT_ROWS)
            for part in range(most // block)
        ]

    def here(begin):
        return lambda table: jnp.int32(begin)

    def step_over(step, units, rest):
        def leaf(units, rest):
            if units == 0:
                return jnp.zeros_like(rest)
            got = from_behind(rest[:units * UNIT * 8 * tiles], "narrow", step)
            return jnp.pad(got, ((0, rest.shape[0] - got.shape[0]), (0, 0)))

        leaves = [functools.partial(leaf, count) for count in range((most - statics[step]) // UNIT + 1)]
        return lax.switch(units, leaves, rest)

    pieces = {}
    outgoing = [first[0], first_rest]
    wide_now = first[1:]
    keys_now = [[(at, 0), (at, last)] for at in moving]
    static_part = from_behind(outgoing[0], "narrow", order[0])
    wide_got = [from_behind(value, "wide", at - 1) for value, at in zip(wide_now, moving)]
    table_then = table
    for phase, step in enumerate(order):
        static = statics[step]
        operands, loads, merges, blocks, stores, named = [], [], [], [], [], []
        used = 0
        if phase + 1 < len(order):
            coming = order[phase + 1]
            if coming == last:
                operands += [pieces[at, last][0] for at in moving] + [local_rows]
                for index, at in enumerate(moving):
                    loads.append((index, here(pieces[at, last][1]), piece, most + at * piece))
                loads.append((len(moving), here(piece), piece, most + piece))
                for at in range(WIN):
                    merges.append(
                        (most + at * piece, groups_of(last, at), entry(2, last, at))
                    )
                used = most + WIN * piece
            else:
                operands.append(raw_groups[coming])
                loads.append((0, None, most, 0))
                used = most
            blocks += group_blocks(0, coming)
            stores += [(here(0), statics[coming]), (here(statics[coming]), most - statics[coming])]
        extra = []
        if phase == 0:
            extra.append(((1, 0), (local_rows, 0)))
        if phase == 1:
            extra += [((at, 0), pieces[at, 0]) for at in moving]
        if phase == 2:
            extra += [((at, order[0]), pieces[at, order[0]]) for at in range(WIN)]
        used = -(-used // block) * block
        for key, value in extra:
            operands.append(value[0])
            loads.append((len(operands) - 1, here(value[1]), piece, used))
            blocks.append((used, rows_of(key[1], key[0])))
            stores.append((here(used), piece))
            named.append(key)
            used += block
        if stores:
            results = integrate(table_then, operands, loads, merges, blocks, stores)
        else:
            results = []
        rest = outgoing[1]
        if phase == 0:
            static_part, results, rest, wide_got, units = lax.optimization_barrier(
                (static_part, results, rest, wide_got, units)
            )
        elif step != last:
            static_part, results, rest, wide_got = lax.optimization_barrier(
                (static_part, results, rest, wide_got)
            )
        else:
            static_part, results, rest = lax.optimization_barrier((static_part, results, rest))
        done = {key: (value, 0) for key, value in zip(named, results[len(results) - len(named):])}
        outgoing = results[:len(results) - len(named)]
        arrived = [static_part, step_over(step, units[phase], rest)]
        if step != last:
            arrived, outgoing = lax.optimization_barrier((arrived, outgoing))
            static_part = from_behind(outgoing[0], "narrow", order[phase + 1])
        if step != last:
            cut = pl.pallas_call(
                functools.partial(cut_kernel, static, tiles, piece, step),
                in_specs=[smem] + [hbm] * len(arrived),
                out_specs=[hbm] * WIN,
                out_shape=[rows_type(piece)] * WIN,
                scratch_shapes=[
                    room_type(most + piece),
                    pltpu.SemaphoreType.DMA((len(arrived),)),
                    pltpu.SemaphoreType.DMA((2, WIN)),
                ],
                compiler_params=params,
                name="cut_pieces",
            )(table, *arrived)
            cut, table_then = lax.optimization_barrier((cut, table))
        for keys, value in zip(keys_now, wide_got):
            pieces.update({key: (value, part * piece) for part, key in enumerate(keys)})
        pieces.update(done)
        if step != last:
            pieces[1, step] = (cut[1], 0)
            keys_now = [[(at, step)] for at in moving]
            wide_got = [from_behind(cut[at], "wide", at - 1) for at in moving]

    held = [pieces[at, step] for step in range(last) for at in range(WIN)]
    buffers = [value for value, _ in held] + arrived
    updated = pl.pallas_call(
        functools.partial(
            finish_kernel,
            (species, levels, columns, tiles, static, piece, narrow_count,
             [begin for _, begin in held]),
        ),
        in_specs=[smem] + [hbm] * len(buffers),
        out_specs=hbm,
        out_shape=jax.ShapeDtypeStruct((species, levels, columns), jnp.float32),
        scratch_shapes=[
            pltpu.VMEM((pair_total - WIN, piece * 8 * tiles, LANES), jnp.float32),
            room_type(most + piece),
            room_type(columns // 8 + 1),
            pltpu.VMEM((species, levels, columns), jnp.float32),
            pltpu.SemaphoreType.DMA((2, pair_total)),
            pltpu.SemaphoreType.DMA((columns // LANES,)),
        ],
        compiler_params=params,
        name="place_columns",
    )(table, *buffers)
    return updated.transpose(1, 0, 2)


def solution(mesh):
    placed = (
        P(None, None, ("wide", "narrow")),
        P(("wide", "narrow")),
        P(),
        P(),
        P(("wide", "narrow")),
        P(("wide", "narrow")),
    )
    return jax.shard_map(
        local,
        mesh=mesh,
        in_specs=placed,
        out_specs=P(None, None, ("wide", "narrow")),
        check_vma=False,
    )
```

```python
import functools

import jax
import jax.numpy as jnp
from jax import lax
from jax.experimental import pallas as pl
from jax.experimental.pallas import tpu as pltpu
from jax.sharding import PartitionSpec as P

WIN = 4
MAXIT = 12
LANES = 128
SORT_COLUMNS = 256
INT_ROWS = 256
UNIT = 8
VMEM = 64 * 1024 * 1024 - 256 * 1024


def from_behind(value, axis, steps):
    count = lax.axis_size(axis)
    pairs = [(source, (source + steps) % count) for source in range(count)]
    return lax.ppermute(value, axis, pairs)


def log2(value):
    bits = value.bit_length() - 1
    assert 1 << bits == value
    return bits


def span_of(group, groups, tiles):
    return pl.ds(pl.multiple_of(group * 8 * tiles, 8), groups * 8 * tiles)


def sort_kernel(sizes, cuts, targets, early, *refs):
    species, levels, columns, tiles, wide_count, narrow_count, pair_total = sizes
    turn_ref, wide_ref, sorted_ref = refs[-4:-1]
    sem_ref = refs[-1]
    if early:
        phys_ref, rate_ref, count_ref, tracers_ref, table_ref, pos_ref = refs[:6]
        cut_refs = refs[6:6 + targets]
        at_ref, table_smem, place_sem = refs[6 + targets:9 + targets]
    else:
        phys_ref, rate_ref, count_ref, tracers_ref, table_smem, at_ref = refs[:6]
        cut_refs = refs[6:6 + targets]
    step = pl.program_id(0)
    lanes = tiles * LANES
    real = species * levels

    def find_places():
        phys = phys_ref[...]
        target = lax.shift_right_logical(phys, log2(columns))
        slot = phys & (columns - 1)
        wide_step = lax.shift_right_logical(target, log2(narrow_count)) - lax.axis_index("wide")
        wide_step = (wide_step + 1) & (wide_count - 1)
        narrow_step = ((target & (narrow_count - 1)) - lax.axis_index("narrow")) & (narrow_count - 1)
        pair = narrow_step * WIN + wide_step
        member = pair == lax.broadcasted_iota(jnp.int32, (pair_total, columns), 0)
        counts = jnp.sum(jnp.where(member, 1.0, 0.0), axis=1, keepdims=True)
        slot_f = slot.astype(jnp.float32)
        starts = jnp.min(jnp.where(member, slot_f, float(columns)), axis=1, keepdims=True)
        groups = lax.shift_right_logical(counts.astype(jnp.int32) + 7, 3).astype(jnp.float32)
        lane = lax.broadcasted_iota(jnp.int32, (pair_total, LANES), 1)
        row = lax.broadcasted_iota(jnp.int32, (pair_total, LANES), 0)

        def across(value):
            return jnp.sum(jnp.where(lane == row, value, 0.0), axis=0, keepdims=True)

        groups_t = across(groups)
        base = jnp.sum(jnp.where(lane < row, groups_t, 0.0), axis=1, keepdims=True)
        section = row & -WIN
        inner = base - jnp.sum(jnp.where(lane < section, groups_t, 0.0), axis=1, keepdims=True)
        same = (lane & -WIN) == section
        in_step = jnp.sum(jnp.where(same, groups_t, 0.0), axis=1, keepdims=True)
        pos = slot_f + jnp.sum(jnp.where(member, base * 8.0 - starts, 0.0), axis=0, keepdims=True)
        pos_ref[...] = pos.astype(jnp.int32)
        pltpu.make_async_copy(pos_ref, at_ref, place_sem.at[0]).start()
        table_ref[...] = jnp.zeros_like(table_ref)
        for at, value in enumerate((counts, base, inner, in_step)):
            table_ref[at:at + 1, :] = across(value).astype(jnp.int32)
        pltpu.make_async_copy(table_ref, table_smem, place_sem.at[1]).start()

    if early:
        pl.when(step == 0)(find_places)
    block = tracers_ref.shape[2]
    begin = step * block
    in_group = lax.broadcasted_iota(jnp.int32, (8, LANES), 0)
    for half in range(block // LANES):
        span = slice(half * LANES, (half + 1) * LANES)
        at = pl.ds(pl.multiple_of(begin + half * LANES, LANES), LANES)
        turn_ref[lanes - 16:lanes, :] = jnp.zeros((16, LANES), jnp.float32)
        turn_ref[0:real, :] = tracers_ref[:, :, span].reshape(real, LANES)
        extra = jnp.where(in_group == 5, (phys_ref[:, at] & (columns - 1)).astype(jnp.float32), 0.0)
        extra = jnp.where(in_group == 6, rate_ref[:, at], extra)
        extra = jnp.where(in_group == 7, count_ref[:, at].astype(jnp.float32), extra)
        turn_ref[lanes - 8:lanes, :] = extra
        for tile in range(tiles):
            wide_ref[half, pl.ds(tile, LANES, stride=8), :] = turn_ref[
                tile * LANES:(tile + 1) * LANES, :
            ].T

        if early and half == 0:
            @pl.when(step == 0)
            def _():
                pltpu.make_async_copy(pos_ref, at_ref, place_sem.at[0]).wait()
                pltpu.make_async_copy(table_ref, table_smem, place_sem.at[1]).wait()

        for column in range(LANES):
            to = at_ref[0, begin + half * LANES + column] * tiles
            sorted_ref[pl.ds(to, tiles), :] = wide_ref[half, column * 8:column * 8 + tiles, :]

    @pl.when(step == pl.num_programs(0) - 1)
    def _():
        copies = []
        for index, (target, to, begin, size, valid) in enumerate(cuts):
            begin = begin(table_smem)
            valid = jnp.clip(valid(table_smem), 0, size)
            copy = pltpu.make_async_copy(
                sorted_ref.at[span_of(begin, size, tiles)],
                cut_refs[target].at[span_of(to, size, tiles)], sem_ref.at[index],
            )
            pl.when(valid > 0)(copy.start)
            copies.append((valid > 0, copy))
        wait_all(copies)


def start_arrival(refs, sems, room_ref, in_step, static, tiles):
    waits = []
    for index, wanted in enumerate((None, in_step > static)):
        copy = pltpu.make_async_copy(
            refs[index], room_ref.at[pl.ds(index * static * 8 * tiles, refs[index].shape[0])],
            sems(index),
        )
        if wanted is None:
            copy.start()
        else:
            pl.when(wanted)(copy.start)
        waits.append((wanted, copy))
    return waits


def wait_all(waits):
    for wanted, copy in waits:
        if wanted is None:
            copy.wait()
        else:
            pl.when(wanted)(copy.wait)


def integrate_block(sizes, room_ref, first, valid, loss_ref, coupling_ref,
                    turn_ref, y_ref, inverse_ref):
    levels, pad, tiles = sizes
    halves = INT_ROWS // LANES
    lanes = tiles * LANES
    first = pl.multiple_of(first * 8 * tiles, 8)
    for half in range(halves):
        begin = first + half * LANES * tiles
        for tile in range(tiles):
            block = room_ref[pl.ds(begin + tile, LANES, stride=tiles), :]
            turn_ref[half, tile * LANES:(tile + 1) * LANES, :] = block.T
        for level in range(levels):
            y_ref[level, :, half * LANES:(half + 1) * LANES] = turn_ref[
                half, pl.ds(level, pad, stride=levels), :
            ]
    rate = jnp.concatenate(
        [turn_ref[half, lanes - 2:lanes - 1, :] for half in range(halves)], axis=1
    )
    count = jnp.concatenate(
        [turn_ref[half, lanes - 1:lanes, :] for half in range(halves)], axis=1
    )
    lane = lax.broadcasted_iota(jnp.int32, (1, INT_ROWS), 1)
    count = jnp.where((lane < valid) & (count <= MAXIT), count, 0.0)
    step_len = rate / jnp.maximum(count, 1.0)
    inverse_ref[...] = 1.0 / (1.0 + step_len * loss_ref[...])
    last = jnp.max(count).astype(jnp.int32)

    def advance(k, carry):
        active = k.astype(jnp.float32) < count

        def one_level(level, inner):
            y = y_ref[level]
            squashed = jnp.tanh(y).astype(jnp.bfloat16)
            produced = jnp.dot(coupling_ref[...], squashed, preferred_element_type=jnp.float32)
            y_ref[level] = jnp.where(active, (y + step_len * produced) * inverse_ref[...], y)
            return inner

        for level in range(levels):
            one_level(level, 0)
        return carry

    lax.fori_loop(0, last, advance, 0)
    for half in range(halves):
        begin = first + half * LANES * tiles
        for level in range(levels):
            turn_ref[half, pl.ds(level, pad, stride=levels), :] = y_ref[
                level, :, half * LANES:(half + 1) * LANES
            ]
        for tile in range(tiles):
            block = turn_ref[half, tile * LANES:(tile + 1) * LANES, :]
            room_ref[pl.ds(begin + tile, LANES, stride=tiles), :] = block.T


def integrate_kernel(sizes, plan, table_ref, loss_ref, coupling_ref, *refs):
    loads, merges, blocks, stores, operands = plan
    tiles = sizes[2]
    sources = refs[:operands]
    results = refs[operands:operands + len(stores)]
    room_ref, turn_ref, y_ref, inverse_ref, rows_ref, sem_ref, out_sem = refs[
        operands + len(stores):
    ]
    copies = []
    for index, (source, begin, groups, to) in enumerate(loads):
        ref = sources[source]
        if begin is not None:
            ref = ref.at[span_of(begin(table_ref), groups, tiles)]
        copies.append(pltpu.make_async_copy(
            ref, room_ref.at[span_of(to, groups, tiles)], sem_ref.at[index]
        ))
    for copy in copies:
        copy.start()
    for copy in copies:
        copy.wait()
    for begin, groups, to in merges:
        to = to(table_ref)

        def move(group, carry):
            room_ref[span_of(to + group, 1, tiles), :] = room_ref[
                span_of(begin + group, 1, tiles), :
            ]
            return carry

        lax.fori_loop(0, groups(table_ref), move, 0)
    for index, (begin, rows) in enumerate(blocks):
        rows_ref[0, index] = jnp.int32(begin)
        rows_ref[1, index] = rows(table_ref)

    def one_block(index, carry):
        valid = rows_ref[1, index]

        @pl.when(valid > 0)
        def _():
            integrate_block(sizes, room_ref, rows_ref[0, index], valid, loss_ref, coupling_ref,
                            turn_ref, y_ref, inverse_ref)

        return carry

    lax.fori_loop(0, len(blocks), one_block, 0)
    copies = []
    for index, (begin, groups) in enumerate(stores):
        copies.append(pltpu.make_async_copy(
            room_ref.at[span_of(begin(table_ref), groups, tiles)], results[index],
            out_sem.at[index],
        ))
    for copy in copies:
        copy.start()
    for copy in copies:
        copy.wait()


def cut_kernel(static, tiles, piece, step, table_ref, *refs):
    pieces = refs[2:2 + WIN]
    room_ref, sem_ref, out_sem = refs[2 + WIN:]
    wait_all(start_arrival(refs[:2], lambda at: sem_ref.at[at], room_ref,
                           table_ref[3, step * WIN], static, tiles))
    copies = []
    half = piece // 2
    for at in range(WIN):
        begin = table_ref[2, step * WIN + at]
        for part in range(2):
            wanted = table_ref[0, step * WIN + at] > part * half * 8
            copy = pltpu.make_async_copy(
                room_ref.at[span_of(begin + part * half, half, tiles)],
                pieces[at].at[span_of(part * half, half, tiles)], out_sem.at[part, at],
            )
            pl.when(wanted)(copy.start)
            copies.append((wanted, copy))
    wait_all(copies)


def finish_kernel(sizes, table_ref, *refs):
    species, levels, columns, tiles, static, piece, narrow_count, begins = sizes
    pair_total = narrow_count * WIN
    whole_pieces = pair_total - WIN
    out_ref, piece_ref, room_ref, placed_ref, whole_ref, sem_ref, out_sem = refs[-7:]
    copies = []
    half = piece // 2
    for pair in range(whole_pieces):
        both = []
        for part in range(2):
            copy = pltpu.make_async_copy(
                refs[pair].at[span_of(begins[pair] + part * half, half, tiles)],
                piece_ref.at[pair, span_of(part * half, half, tiles)], sem_ref.at[part, pair],
            )
            wanted = table_ref[0, pair] > part * half * 8
            pl.when(wanted)(copy.start)
            both.append((wanted, copy))
        copies.append(both)
    waits = start_arrival(refs[whole_pieces:whole_pieces + 2],
                          lambda at: sem_ref.at[at, whole_pieces], room_ref,
                          table_ref[3, whole_pieces], static, tiles)
    lane = lax.broadcasted_iota(jnp.int32, (1, LANES), 1)
    in_group = lax.broadcasted_iota(jnp.int32, (8, LANES), 0)
    for pair in range(pair_total):
        if pair < whole_pieces:
            wait_all(copies[pair])
            held = piece_ref.at[pair]
            begin = 0
        else:
            if pair == whole_pieces:
                wait_all(waits)
            held = room_ref
            begin = pl.multiple_of(table_ref[2, pair] * 8 * tiles, 8)
        count = table_ref[0, pair]
        first = held[pl.ds(begin + tiles - 1, 1), :]
        start = jnp.max(jnp.where(lane == LANES - 3, first, 0.0)).astype(jnp.int32)
        start = jnp.clip(start, 0, columns - 1) * tiles
        full = lax.shift_right_logical(count, 3)

        def move(group, carry):
            for row in range(0, 8 * tiles, 8):
                at = group * 8 * tiles + row
                placed_ref[pl.ds(start + at, 8), :] = held[pl.ds(pl.multiple_of(begin + at, 8), 8), :]
            return carry

        lax.fori_loop(0, full, move, 0)

        @pl.when((count & 7) > 0)
        def _():
            for row in range(0, 8 * tiles, 8):
                at = full * 8 * tiles + row
                to = pl.ds(start + at, 8)
                placed_ref[to, :] = jnp.where(
                    in_group + row < (count & 7) * tiles,
                    held[pl.ds(pl.multiple_of(begin + at, 8), 8), :], placed_ref[to, :],
                )

    per_tile = LANES // levels
    for part in range(columns // LANES):
        at = slice(part * LANES, (part + 1) * LANES)
        for tile in range(tiles):
            block = placed_ref[pl.ds(part * LANES * tiles + tile, LANES, stride=tiles), :]
            block = block.T.reshape(per_tile, levels, LANES)
            keep = min(per_tile, species - tile * per_tile)
            whole_ref[tile * per_tile:tile * per_tile + keep, :, at] = block[:keep]
        pltpu.make_async_copy(whole_ref.at[:, :, at], out_ref.at[:, :, at], out_sem.at[part]).start()
    for part in range(columns // LANES):
        at = slice(part * LANES, (part + 1) * LANES)
        pltpu.make_async_copy(whole_ref.at[:, :, at], out_ref.at[:, :, at], out_sem.at[part]).wait()


def local(tracers, column_rate, loss_rate, coupling, phys_index, iter_count):
    levels, species, columns = tracers.shape
    wide_count = lax.axis_size("wide")
    narrow_count = lax.axis_size("narrow")
    pair_total = WIN * narrow_count
    room = 2 * columns // pair_total
    piece = room // 8
    pad = -(-species // 8) * 8
    while levels * pad % LANES or levels * (pad - species) < 8:
        pad += 8
    tiles = levels * pad // LANES
    mean = columns // narrow_count // 8
    full = pl.BlockSpec(memory_space=pltpu.VMEM)
    smem = pl.BlockSpec(memory_space=pltpu.SMEM)
    hbm = pl.BlockSpec(memory_space=pltpu.HBM)
    last = narrow_count - 1
    moving = [at for at in range(WIN) if at != 1]
    order = [narrow_count // 2]
    order += [step for step in range(1, last) if step not in order] + [last]
    statics = {step: mean - mean // 4 for step in order}
    most = WIN * piece

    params = pltpu.CompilerParams(vmem_limit_bytes=VMEM)

    def rows_type(groups):
        return jax.ShapeDtypeStruct((groups * 8 * tiles, LANES), jnp.float32)

    def room_type(groups):
        return pltpu.VMEM((groups * 8 * tiles, LANES), jnp.float32)

    def entry(row, step, at=0):
        return lambda table: table[row, step * WIN + at]

    def over(step):
        return lambda table: entry(1, step)(table) + statics[step]

    def groups_of(step, at):
        return lambda table: lax.shift_right_logical(table[0, step * WIN + at] + 7, 3)

    def groups_over(step):
        return lambda table: table[3, step * WIN] - statics[step]

    def pair_cuts(target, at):
        return [
            (target, part * piece + half,
             lambda table, step=step, half=half: entry(1, step, at)(table) + half, piece // 2,
             lambda table, step=step, half=half: groups_of(step, at)(table) - half)
            for part, step in enumerate((0, last)) for half in range(0, piece, piece // 2)
        ]

    def sort(cuts, target_sizes, early, known):
        known_types = [
            jax.ShapeDtypeStruct((8, LANES), jnp.int32),
            jax.ShapeDtypeStruct((1, columns), jnp.int32),
        ]
        groups = columns // 8 + pair_total + most
        return pl.pallas_call(
            functools.partial(
                sort_kernel,
                (species, levels, columns, tiles, wide_count, narrow_count, pair_total),
                cuts, len(target_sizes), early,
            ),
            grid=(columns // SORT_COLUMNS,),
            in_specs=[full, full, full,
                      pl.BlockSpec((species, levels, SORT_COLUMNS), lambda at: (0, 0, at))]
            + [smem] * len(known),
            out_specs=([full, full] if early else []) + [hbm] * len(target_sizes),
            out_shape=(known_types if early else []) + [rows_type(size) for size in target_sizes],
            scratch_shapes=([
                pltpu.SMEM((1, columns), jnp.int32), pltpu.SMEM((8, LANES), jnp.int32),
                pltpu.SemaphoreType.DMA((2,)),
            ] if early else []) + [
                pltpu.VMEM((tiles * LANES, LANES), jnp.float32),
                pltpu.VMEM((SORT_COLUMNS // LANES, LANES * 8, LANES), jnp.float32),
                room_type(groups),
                pltpu.SemaphoreType.DMA((len(cuts),)),
            ],
            compiler_params=params,
            name="sort_columns" if early else "sort_later_columns",
        )(
            phys_index.reshape(1, columns),
            column_rate.reshape(1, columns),
            iter_count.reshape(1, columns),
            tracers.transpose(1, 0, 2),
            *known,
        )

    first_static = statics[order[0]]
    cuts = [(0, 0, entry(1, order[0]), first_static, entry(3, order[0]))]
    for index, at in enumerate(moving):
        cuts += pair_cuts(1 + index, at)
    table, places, *first = sort(
        cuts, [first_static] + [2 * piece] * len(moving), True, ()
    )
    cuts = [(0, 0, over(order[0]), most - first_static, groups_over(order[0]))]
    cuts += pair_cuts(1, 1)
    for index, step in enumerate(order[1:-1]):
        rest = most - statics[step]
        cuts.append((2 + index, 0, entry(1, step), statics[step], entry(3, step)))
        cuts.append((2 + index, statics[step], over(step), rest, groups_over(step)))
    first_rest, local_rows, *raw = sort(
        cuts, [most - first_static, 2 * piece] + [most] * (len(order) - 2), False, (table, places)
    )
    raw_groups = dict(zip(order[1:-1], raw))
    units = [
        (jnp.maximum(table[3, step * WIN] - statics[step], 0) + UNIT - 1) // UNIT
        for step in order
    ]
    loss_pad = jnp.pad(loss_rate, (0, pad - species)).reshape(pad, 1)
    coupling_pad = jnp.pad(coupling, ((0, pad - species), (0, pad - species)))
    block = INT_ROWS // 8

    def integrate(table, operands, loads, merges, blocks, stores):
        groups = max([to + size for _, _, size, to in loads] + [begin + block for begin, _ in blocks])
        groups += piece
        return pl.pallas_call(
            functools.partial(
                integrate_kernel, (levels, pad, tiles),
                (loads, merges, blocks, stores, len(operands)),
            ),
            in_specs=[smem, full, full] + [hbm] * len(operands),
            out_specs=[hbm] * len(stores),
            out_shape=[rows_type(size) for _, size in stores],
            scratch_shapes=[
                room_type(groups),
                pltpu.VMEM((INT_ROWS // LANES, tiles * LANES, LANES), jnp.float32),
                pltpu.VMEM((levels, pad, INT_ROWS), jnp.float32),
                pltpu.VMEM((pad, INT_ROWS), jnp.float32),
                pltpu.SMEM((2, LANES), jnp.int32),
                pltpu.SemaphoreType.DMA((len(loads),)),
                pltpu.SemaphoreType.DMA((len(stores),)),
            ],
            compiler_params=params,
            name="integrate_columns",
        )(table, loss_pad, coupling_pad, *operands)

    def rows_of(step, at=0):
        return entry(0, step, at)

    def group_blocks(begin, step):
        return [
            (begin + part * block,
             lambda table, part=part: table[3, step * WIN] * 8 - part * INT_ROWS)
            for part in range(most // block)
        ]

    def here(begin):
        return lambda table: jnp.int32(begin)

    def step_over(step, units, rest):
        def leaf(units, rest):
            if units == 0:
                return jnp.zeros_like(rest)
            got = from_behind(rest[:units * UNIT * 8 * tiles], "narrow", step)
            return jnp.pad(got, ((0, rest.shape[0] - got.shape[0]), (0, 0)))

        leaves = [functools.partial(leaf, count) for count in range((most - statics[step]) // UNIT + 1)]
        return lax.switch(units, leaves, rest)

    pieces = {}
    outgoing = [first[0], first_rest]
    wide_now = first[1:]
    keys_now = [[(at, 0), (at, last)] for at in moving]
    static_part = from_behind(outgoing[0], "narrow", order[0])
    wide_got = [from_behind(value, "wide", at - 1) for value, at in zip(wide_now, moving)]
    table_then = table
    for phase, step in enumerate(order):
        static = statics[step]
        operands, loads, merges, blocks, stores, named = [], [], [], [], [], []
        used = 0
        if phase + 1 < len(order):
            coming = order[phase + 1]
            if coming == last:
                operands += [pieces[at, last][0] for at in moving] + [local_rows]
                for index, at in enumerate(moving):
                    loads.append((index, here(pieces[at, last][1]), piece, most + at * piece))
                loads.append((len(moving), here(piece), piece, most + piece))
                for at in range(WIN):
                    merges.append(
                        (most + at * piece, groups_of(last, at), entry(2, last, at))
                    )
                used = most + WIN * piece
            else:
                operands.append(raw_groups[coming])
                loads.append((0, None, most, 0))
                used = most
            blocks += group_blocks(0, coming)
            stores += [(here(0), statics[coming]), (here(statics[coming]), most - statics[coming])]
        extra = []
        if phase == 0:
            extra.append(((1, 0), (local_rows, 0)))
        if phase == 1:
            extra += [((at, 0), pieces[at, 0]) for at in moving]
        if phase == 2:
            extra += [((at, order[0]), pieces[at, order[0]]) for at in range(WIN)]
        used = -(-used // block) * block
        for key, value in extra:
            operands.append(value[0])
            loads.append((len(operands) - 1, here(value[1]), piece, used))
            blocks.append((used, rows_of(key[1], key[0])))
            stores.append((here(used), piece))
            named.append(key)
            used += block
        if stores:
            results = integrate(table_then, operands, loads, merges, blocks, stores)
        else:
            results = []
        rest = outgoing[1]
        if phase == 0:
            static_part, results, rest, units = lax.optimization_barrier(
                (static_part, results, rest, units)
            )
        else:
            static_part, results, rest = lax.optimization_barrier((static_part, results, rest))
        done = {key: (value, 0) for key, value in zip(named, results[len(results) - len(named):])}
        outgoing = results[:len(results) - len(named)]
        arrived = [static_part, step_over(step, units[phase], rest)]
        if step != last:
            arrived, outgoing = lax.optimization_barrier((arrived, outgoing))
            static_part = from_behind(outgoing[0], "narrow", order[phase + 1])
        if step != last:
            cut = pl.pallas_call(
                functools.partial(cut_kernel, static, tiles, piece, step),
                in_specs=[smem] + [hbm] * len(arrived),
                out_specs=[hbm] * WIN,
                out_shape=[rows_type(piece)] * WIN,
                scratch_shapes=[
                    room_type(most + piece),
                    pltpu.SemaphoreType.DMA((len(arrived),)),
                    pltpu.SemaphoreType.DMA((2, WIN)),
                ],
                compiler_params=params,
                name="cut_pieces",
            )(table, *arrived)
            cut, wide_got, table_then = lax.optimization_barrier((cut, wide_got, table))
        for keys, value in zip(keys_now, wide_got):
            pieces.update({key: (value, part * piece) for part, key in enumerate(keys)})
        pieces.update(done)
        if step != last:
            pieces[1, step] = (cut[1], 0)
            keys_now = [[(at, step)] for at in moving]
            wide_got = [from_behind(cut[at], "wide", at - 1) for at in moving]

    held = [pieces[at, step] for step in range(last) for at in range(WIN)]
    buffers = [value for value, _ in held] + arrived
    updated = pl.pallas_call(
        functools.partial(
            finish_kernel,
            (species, levels, columns, tiles, static, piece, narrow_count,
             [begin for _, begin in held]),
        ),
        in_specs=[smem] + [hbm] * len(buffers),
        out_specs=hbm,
        out_shape=jax.ShapeDtypeStruct((species, levels, columns), jnp.float32),
        scratch_shapes=[
            pltpu.VMEM((pair_total - WIN, piece * 8 * tiles, LANES), jnp.float32),
            room_type(most + piece),
            room_type(columns // 8 + 1),
            pltpu.VMEM((species, levels, columns), jnp.float32),
            pltpu.SemaphoreType.DMA((2, pair_total)),
            pltpu.SemaphoreType.DMA((columns // LANES,)),
        ],
        compiler_params=params,
        name="place_columns",
    )(table, *buffers)
    return updated.transpose(1, 0, 2)


def solution(mesh):
    placed = (
        P(None, None, ("wide", "narrow")),
        P(("wide", "narrow")),
        P(),
        P(),
        P(("wide", "narrow")),
        P(("wide", "narrow")),
    )
    return jax.shard_map(
        local,
        mesh=mesh,
        in_specs=placed,
        out_specs=P(None, None, ("wide", "narrow")),
        check_vma=False,
    )
```

```python
import functools

import jax
import jax.numpy as jnp
from jax import lax
from jax.experimental import pallas as pl
from jax.experimental.pallas import tpu as pltpu
from jax.sharding import PartitionSpec as P

WIN = 4
MAXIT = 12
LANES = 128
SORT_COLUMNS = 256
INT_ROWS = 256
UNIT = 8
VMEM = 64 * 1024 * 1024 - 256 * 1024


def from_behind(value, axis, steps):
    count = lax.axis_size(axis)
    pairs = [(source, (source + steps) % count) for source in range(count)]
    return lax.ppermute(value, axis, pairs)


def log2(value):
    bits = value.bit_length() - 1
    assert 1 << bits == value
    return bits


def span_of(group, groups, tiles):
    return pl.ds(pl.multiple_of(group * 8 * tiles, 8), groups * 8 * tiles)


def sort_kernel(sizes, cuts, targets, early, *refs):
    species, levels, columns, tiles, wide_count, narrow_count, pair_total = sizes
    turn_ref, wide_ref, sorted_ref = refs[-4:-1]
    sem_ref = refs[-1]
    if early:
        phys_ref, rate_ref, count_ref, tracers_ref, table_ref, pos_ref = refs[:6]
        cut_refs = refs[6:6 + targets]
        at_ref, table_smem, place_sem = refs[6 + targets:9 + targets]
    else:
        phys_ref, rate_ref, count_ref, tracers_ref, table_smem, at_ref = refs[:6]
        cut_refs = refs[6:6 + targets]
    step = pl.program_id(0)
    lanes = tiles * LANES
    real = species * levels

    def find_places():
        phys = phys_ref[...]
        target = lax.shift_right_logical(phys, log2(columns))
        slot = phys & (columns - 1)
        wide_step = lax.shift_right_logical(target, log2(narrow_count)) - lax.axis_index("wide")
        wide_step = (wide_step + 1) & (wide_count - 1)
        narrow_step = ((target & (narrow_count - 1)) - lax.axis_index("narrow")) & (narrow_count - 1)
        pair = narrow_step * WIN + wide_step
        member = pair == lax.broadcasted_iota(jnp.int32, (pair_total, columns), 0)
        counts = jnp.sum(jnp.where(member, 1.0, 0.0), axis=1, keepdims=True)
        slot_f = slot.astype(jnp.float32)
        starts = jnp.min(jnp.where(member, slot_f, float(columns)), axis=1, keepdims=True)
        groups = lax.shift_right_logical(counts.astype(jnp.int32) + 7, 3).astype(jnp.float32)
        lane = lax.broadcasted_iota(jnp.int32, (pair_total, LANES), 1)
        row = lax.broadcasted_iota(jnp.int32, (pair_total, LANES), 0)

        def across(value):
            return jnp.sum(jnp.where(lane == row, value, 0.0), axis=0, keepdims=True)

        groups_t = across(groups)
        base = jnp.sum(jnp.where(lane < row, groups_t, 0.0), axis=1, keepdims=True)
        section = row & -WIN
        inner = base - jnp.sum(jnp.where(lane < section, groups_t, 0.0), axis=1, keepdims=True)
        same = (lane & -WIN) == section
        in_step = jnp.sum(jnp.where(same, groups_t, 0.0), axis=1, keepdims=True)
        pos = slot_f + jnp.sum(jnp.where(member, base * 8.0 - starts, 0.0), axis=0, keepdims=True)
        pos_ref[...] = pos.astype(jnp.int32)
        pltpu.make_async_copy(pos_ref, at_ref, place_sem.at[0]).start()
        table_ref[...] = jnp.zeros_like(table_ref)
        for at, value in enumerate((counts, base, inner, in_step)):
            table_ref[at:at + 1, :] = across(value).astype(jnp.int32)
        pltpu.make_async_copy(table_ref, table_smem, place_sem.at[1]).start()

    if early:
        pl.when(step == 0)(find_places)
    block = tracers_ref.shape[2]
    begin = step * block
    in_group = lax.broadcasted_iota(jnp.int32, (8, LANES), 0)
    for half in range(block // LANES):
        span = slice(half * LANES, (half + 1) * LANES)
        at = pl.ds(pl.multiple_of(begin + half * LANES, LANES), LANES)
        turn_ref[lanes - 16:lanes, :] = jnp.zeros((16, LANES), jnp.float32)
        turn_ref[0:real, :] = tracers_ref[:, :, span].reshape(real, LANES)
        extra = jnp.where(in_group == 5, (phys_ref[:, at] & (columns - 1)).astype(jnp.float32), 0.0)
        extra = jnp.where(in_group == 6, rate_ref[:, at], extra)
        extra = jnp.where(in_group == 7, count_ref[:, at].astype(jnp.float32), extra)
        turn_ref[lanes - 8:lanes, :] = extra
        for tile in range(tiles):
            wide_ref[half, pl.ds(tile, LANES, stride=8), :] = turn_ref[
                tile * LANES:(tile + 1) * LANES, :
            ].T

        if early and half == 0:
            @pl.when(step == 0)
            def _():
                pltpu.make_async_copy(pos_ref, at_ref, place_sem.at[0]).wait()
                pltpu.make_async_copy(table_ref, table_smem, place_sem.at[1]).wait()

        for column in range(LANES):
            to = at_ref[0, begin + half * LANES + column] * tiles
            sorted_ref[pl.ds(to, tiles), :] = wide_ref[half, column * 8:column * 8 + tiles, :]

    @pl.when(step == pl.num_programs(0) - 1)
    def _():
        copies = []
        for index, (target, to, begin, size, valid) in enumerate(cuts):
            begin = begin(table_smem)
            valid = jnp.clip(valid(table_smem), 0, size)
            copy = pltpu.make_async_copy(
                sorted_ref.at[span_of(begin, size, tiles)],
                cut_refs[target].at[span_of(to, size, tiles)], sem_ref.at[index],
            )
            pl.when(valid > 0)(copy.start)
            copies.append((valid > 0, copy))
        wait_all(copies)


def start_arrival(refs, sems, room_ref, in_step, static, tiles):
    waits = []
    for index, wanted in enumerate((None, in_step > static)):
        copy = pltpu.make_async_copy(
            refs[index], room_ref.at[pl.ds(index * static * 8 * tiles, refs[index].shape[0])],
            sems(index),
        )
        if wanted is None:
            copy.start()
        else:
            pl.when(wanted)(copy.start)
        waits.append((wanted, copy))
    return waits


def wait_all(waits):
    for wanted, copy in waits:
        if wanted is None:
            copy.wait()
        else:
            pl.when(wanted)(copy.wait)


def integrate_block(sizes, room_ref, first, valid, loss_ref, coupling_ref,
                    turn_ref, y_ref, inverse_ref):
    levels, pad, tiles = sizes
    halves = INT_ROWS // LANES
    lanes = tiles * LANES
    first = pl.multiple_of(first * 8 * tiles, 8)
    for half in range(halves):
        begin = first + half * LANES * tiles
        for tile in range(tiles):
            block = room_ref[pl.ds(begin + tile, LANES, stride=tiles), :]
            turn_ref[half, tile * LANES:(tile + 1) * LANES, :] = block.T
        for level in range(levels):
            y_ref[level, :, half * LANES:(half + 1) * LANES] = turn_ref[
                half, pl.ds(level, pad, stride=levels), :
            ]
    rate = jnp.concatenate(
        [turn_ref[half, lanes - 2:lanes - 1, :] for half in range(halves)], axis=1
    )
    count = jnp.concatenate(
        [turn_ref[half, lanes - 1:lanes, :] for half in range(halves)], axis=1
    )
    lane = lax.broadcasted_iota(jnp.int32, (1, INT_ROWS), 1)
    count = jnp.where((lane < valid) & (count <= MAXIT), count, 0.0)
    step_len = rate / jnp.maximum(count, 1.0)
    inverse_ref[...] = 1.0 / (1.0 + step_len * loss_ref[...])
    last = jnp.max(count).astype(jnp.int32)

    def advance(k, carry):
        active = k.astype(jnp.float32) < count

        def one_level(level, inner):
            y = y_ref[level]
            squashed = jnp.tanh(y).astype(jnp.bfloat16)
            produced = jnp.dot(coupling_ref[...], squashed, preferred_element_type=jnp.float32)
            y_ref[level] = jnp.where(active, (y + step_len * produced) * inverse_ref[...], y)
            return inner

        for level in range(levels):
            one_level(level, 0)
        return carry

    lax.fori_loop(0, last, advance, 0)
    for half in range(halves):
        begin = first + half * LANES * tiles
        for level in range(levels):
            turn_ref[half, pl.ds(level, pad, stride=levels), :] = y_ref[
                level, :, half * LANES:(half + 1) * LANES
            ]
        for tile in range(tiles):
            block = turn_ref[half, tile * LANES:(tile + 1) * LANES, :]
            room_ref[pl.ds(begin + tile, LANES, stride=tiles), :] = block.T


def integrate_kernel(sizes, plan, table_ref, loss_ref, coupling_ref, *refs):
    loads, merges, blocks, stores, operands = plan
    tiles = sizes[2]
    sources = refs[:operands]
    results = refs[operands:operands + len(stores)]
    room_ref, turn_ref, y_ref, inverse_ref, rows_ref, sem_ref, out_sem = refs[
        operands + len(stores):
    ]
    copies = []
    for index, (source, begin, groups, to) in enumerate(loads):
        ref = sources[source]
        if begin is not None:
            ref = ref.at[span_of(begin(table_ref), groups, tiles)]
        copies.append(pltpu.make_async_copy(
            ref, room_ref.at[span_of(to, groups, tiles)], sem_ref.at[index]
        ))
    for copy in copies:
        copy.start()
    for copy in copies:
        copy.wait()
    for begin, groups, to in merges:
        to = to(table_ref)

        def move(group, carry):
            room_ref[span_of(to + group, 1, tiles), :] = room_ref[
                span_of(begin + group, 1, tiles), :
            ]
            return carry

        lax.fori_loop(0, groups(table_ref), move, 0)
    for index, (begin, rows) in enumerate(blocks):
        rows_ref[0, index] = jnp.int32(begin)
        rows_ref[1, index] = rows(table_ref)

    def one_block(index, carry):
        valid = rows_ref[1, index]

        @pl.when(valid > 0)
        def _():
            integrate_block(sizes, room_ref, rows_ref[0, index], valid, loss_ref, coupling_ref,
                            turn_ref, y_ref, inverse_ref)

        return carry

    lax.fori_loop(0, len(blocks), one_block, 0)
    copies = []
    for index, (begin, groups) in enumerate(stores):
        copies.append(pltpu.make_async_copy(
            room_ref.at[span_of(begin(table_ref), groups, tiles)], results[index],
            out_sem.at[index],
        ))
    for copy in copies:
        copy.start()
    for copy in copies:
        copy.wait()


def cut_kernel(static, tiles, piece, step, table_ref, *refs):
    pieces = refs[2:2 + WIN]
    room_ref, sem_ref, out_sem = refs[2 + WIN:]
    wait_all(start_arrival(refs[:2], lambda at: sem_ref.at[at], room_ref,
                           table_ref[3, step * WIN], static, tiles))
    copies = []
    half = piece // 2
    for at in range(WIN):
        begin = table_ref[2, step * WIN + at]
        for part in range(2):
            wanted = table_ref[0, step * WIN + at] > part * half * 8
            copy = pltpu.make_async_copy(
                room_ref.at[span_of(begin + part * half, half, tiles)],
                pieces[at].at[span_of(part * half, half, tiles)], out_sem.at[part, at],
            )
            pl.when(wanted)(copy.start)
            copies.append((wanted, copy))
    wait_all(copies)


def finish_kernel(sizes, table_ref, *refs):
    species, levels, columns, tiles, static, piece, narrow_count, begins = sizes
    pair_total = narrow_count * WIN
    whole_pieces = pair_total - WIN
    out_ref, piece_ref, room_ref, placed_ref, whole_ref, sem_ref, out_sem = refs[-7:]
    copies = []
    half = piece // 2
    for pair in range(whole_pieces):
        both = []
        for part in range(2):
            copy = pltpu.make_async_copy(
                refs[pair].at[span_of(begins[pair] + part * half, half, tiles)],
                piece_ref.at[pair, span_of(part * half, half, tiles)], sem_ref.at[part, pair],
            )
            wanted = table_ref[0, pair] > part * half * 8
            pl.when(wanted)(copy.start)
            both.append((wanted, copy))
        copies.append(both)
    waits = start_arrival(refs[whole_pieces:whole_pieces + 2],
                          lambda at: sem_ref.at[at, whole_pieces], room_ref,
                          table_ref[3, whole_pieces], static, tiles)
    lane = lax.broadcasted_iota(jnp.int32, (1, LANES), 1)
    in_group = lax.broadcasted_iota(jnp.int32, (8, LANES), 0)
    for pair in range(pair_total):
        if pair < whole_pieces:
            wait_all(copies[pair])
            held = piece_ref.at[pair]
            begin = 0
        else:
            if pair == whole_pieces:
                wait_all(waits)
            held = room_ref
            begin = pl.multiple_of(table_ref[2, pair] * 8 * tiles, 8)
        count = table_ref[0, pair]
        first = held[pl.ds(begin + tiles - 1, 1), :]
        start = jnp.max(jnp.where(lane == LANES - 3, first, 0.0)).astype(jnp.int32)
        start = jnp.clip(start, 0, columns - 1) * tiles
        full = lax.shift_right_logical(count, 3)

        def move(group, carry):
            for row in range(0, 8 * tiles, 8):
                at = group * 8 * tiles + row
                placed_ref[pl.ds(start + at, 8), :] = held[pl.ds(pl.multiple_of(begin + at, 8), 8), :]
            return carry

        lax.fori_loop(0, full, move, 0)

        @pl.when((count & 7) > 0)
        def _():
            for row in range(0, 8 * tiles, 8):
                at = full * 8 * tiles + row
                to = pl.ds(start + at, 8)
                placed_ref[to, :] = jnp.where(
                    in_group + row < (count & 7) * tiles,
                    held[pl.ds(pl.multiple_of(begin + at, 8), 8), :], placed_ref[to, :],
                )

    per_tile = LANES // levels
    for part in range(columns // LANES):
        at = slice(part * LANES, (part + 1) * LANES)
        for tile in range(tiles):
            block = placed_ref[pl.ds(part * LANES * tiles + tile, LANES, stride=tiles), :]
            block = block.T.reshape(per_tile, levels, LANES)
            keep = min(per_tile, species - tile * per_tile)
            whole_ref[tile * per_tile:tile * per_tile + keep, :, at] = block[:keep]
        pltpu.make_async_copy(whole_ref.at[:, :, at], out_ref.at[:, :, at], out_sem.at[part]).start()
    for part in range(columns // LANES):
        at = slice(part * LANES, (part + 1) * LANES)
        pltpu.make_async_copy(whole_ref.at[:, :, at], out_ref.at[:, :, at], out_sem.at[part]).wait()


def local(tracers, column_rate, loss_rate, coupling, phys_index, iter_count):
    levels, species, columns = tracers.shape
    wide_count = lax.axis_size("wide")
    narrow_count = lax.axis_size("narrow")
    pair_total = WIN * narrow_count
    room = 2 * columns // pair_total
    piece = room // 8
    pad = -(-species // 8) * 8
    while levels * pad % LANES or levels * (pad - species) < 8:
        pad += 8
    tiles = levels * pad // LANES
    mean = columns // narrow_count // 8
    full = pl.BlockSpec(memory_space=pltpu.VMEM)
    smem = pl.BlockSpec(memory_space=pltpu.SMEM)
    hbm = pl.BlockSpec(memory_space=pltpu.HBM)
    last = narrow_count - 1
    moving = [at for at in range(WIN) if at != 1]
    order = [narrow_count // 2]
    order += [step for step in range(1, last) if step not in order] + [last]
    statics = {step: mean for step in order}
    most = WIN * piece

    params = pltpu.CompilerParams(vmem_limit_bytes=VMEM)

    def rows_type(groups):
        return jax.ShapeDtypeStruct((groups * 8 * tiles, LANES), jnp.float32)

    def room_type(groups):
        return pltpu.VMEM((groups * 8 * tiles, LANES), jnp.float32)

    def entry(row, step, at=0):
        return lambda table: table[row, step * WIN + at]

    def over(step):
        return lambda table: entry(1, step)(table) + statics[step]

    def groups_of(step, at):
        return lambda table: lax.shift_right_logical(table[0, step * WIN + at] + 7, 3)

    def groups_over(step):
        return lambda table: table[3, step * WIN] - statics[step]

    def pair_cuts(target, at):
        return [
            (target, part * piece + half,
             lambda table, step=step, half=half: entry(1, step, at)(table) + half, piece // 2,
             lambda table, step=step, half=half: groups_of(step, at)(table) - half)
            for part, step in enumerate((0, last)) for half in range(0, piece, piece // 2)
        ]

    def sort(cuts, target_sizes, early, known):
        known_types = [
            jax.ShapeDtypeStruct((8, LANES), jnp.int32),
            jax.ShapeDtypeStruct((1, columns), jnp.int32),
        ]
        groups = columns // 8 + pair_total + most
        return pl.pallas_call(
            functools.partial(
                sort_kernel,
                (species, levels, columns, tiles, wide_count, narrow_count, pair_total),
                cuts, len(target_sizes), early,
            ),
            grid=(columns // SORT_COLUMNS,),
            in_specs=[full, full, full,
                      pl.BlockSpec((species, levels, SORT_COLUMNS), lambda at: (0, 0, at))]
            + [smem] * len(known),
            out_specs=([full, full] if early else []) + [hbm] * len(target_sizes),
            out_shape=(known_types if early else []) + [rows_type(size) for size in target_sizes],
            scratch_shapes=([
                pltpu.SMEM((1, columns), jnp.int32), pltpu.SMEM((8, LANES), jnp.int32),
                pltpu.SemaphoreType.DMA((2,)),
            ] if early else []) + [
                pltpu.VMEM((tiles * LANES, LANES), jnp.float32),
                pltpu.VMEM((SORT_COLUMNS // LANES, LANES * 8, LANES), jnp.float32),
                room_type(groups),
                pltpu.SemaphoreType.DMA((len(cuts),)),
            ],
            compiler_params=params,
            name="sort_columns" if early else "sort_later_columns",
        )(
            phys_index.reshape(1, columns),
            column_rate.reshape(1, columns),
            iter_count.reshape(1, columns),
            tracers.transpose(1, 0, 2),
            *known,
        )

    first_static = statics[order[0]]
    cuts = [(0, 0, entry(1, order[0]), first_static, entry(3, order[0]))]
    for index, at in enumerate(moving):
        cuts += pair_cuts(1 + index, at)
    table, places, *first = sort(
        cuts, [first_static] + [2 * piece] * len(moving), True, ()
    )
    cuts = [(0, 0, over(order[0]), most - first_static, groups_over(order[0]))]
    cuts += pair_cuts(1, 1)
    for index, step in enumerate(order[1:-1]):
        rest = most - statics[step]
        cuts.append((2 + index, 0, entry(1, step), statics[step], entry(3, step)))
        cuts.append((2 + index, statics[step], over(step), rest, groups_over(step)))
    first_rest, local_rows, *raw = sort(
        cuts, [most - first_static, 2 * piece] + [most] * (len(order) - 2), False, (table, places)
    )
    raw_groups = dict(zip(order[1:-1], raw))
    units = [
        (jnp.maximum(table[3, step * WIN] - statics[step], 0) + UNIT - 1) // UNIT
        for step in order
    ]
    loss_pad = jnp.pad(loss_rate, (0, pad - species)).reshape(pad, 1)
    coupling_pad = jnp.pad(coupling, ((0, pad - species), (0, pad - species)))
    block = INT_ROWS // 8

    def integrate(table, operands, loads, merges, blocks, stores):
        groups = max([to + size for _, _, size, to in loads] + [begin + block for begin, _ in blocks])
        groups += piece
        return pl.pallas_call(
            functools.partial(
                integrate_kernel, (levels, pad, tiles),
                (loads, merges, blocks, stores, len(operands)),
            ),
            in_specs=[smem, full, full] + [hbm] * len(operands),
            out_specs=[hbm] * len(stores),
            out_shape=[rows_type(size) for _, size in stores],
            scratch_shapes=[
                room_type(groups),
                pltpu.VMEM((INT_ROWS // LANES, tiles * LANES, LANES), jnp.float32),
                pltpu.VMEM((levels, pad, INT_ROWS), jnp.float32),
                pltpu.VMEM((pad, INT_ROWS), jnp.float32),
                pltpu.SMEM((2, LANES), jnp.int32),
                pltpu.SemaphoreType.DMA((len(loads),)),
                pltpu.SemaphoreType.DMA((len(stores),)),
            ],
            compiler_params=params,
            name="integrate_columns",
        )(table, loss_pad, coupling_pad, *operands)

    def rows_of(step, at=0):
        return entry(0, step, at)

    def group_blocks(begin, step):
        return [
            (begin + part * block,
             lambda table, part=part: table[3, step * WIN] * 8 - part * INT_ROWS)
            for part in range(most // block)
        ]

    def here(begin):
        return lambda table: jnp.int32(begin)

    def step_over(step, units, rest):
        def leaf(units, rest):
            if units == 0:
                return jnp.zeros_like(rest)
            got = from_behind(rest[:units * UNIT * 8 * tiles], "narrow", step)
            return jnp.pad(got, ((0, rest.shape[0] - got.shape[0]), (0, 0)))

        leaves = [functools.partial(leaf, count) for count in range((most - statics[step]) // UNIT + 1)]
        return lax.switch(units, leaves, rest)

    pieces = {}
    outgoing = [first[0], first_rest]
    wide_now = first[1:]
    keys_now = [[(at, 0), (at, last)] for at in moving]
    static_part = from_behind(outgoing[0], "narrow", order[0])
    wide_got = [from_behind(value, "wide", at - 1) for value, at in zip(wide_now, moving)]
    table_then = table
    for phase, step in enumerate(order):
        static = statics[step]
        operands, loads, merges, blocks, stores, named = [], [], [], [], [], []
        used = 0
        if phase + 1 < len(order):
            coming = order[phase + 1]
            if coming == last:
                operands += [pieces[at, last][0] for at in moving] + [local_rows]
                for index, at in enumerate(moving):
                    loads.append((index, here(pieces[at, last][1]), piece, most + at * piece))
                loads.append((len(moving), here(piece), piece, most + piece))
                for at in range(WIN):
                    merges.append(
                        (most + at * piece, groups_of(last, at), entry(2, last, at))
                    )
                used = most + WIN * piece
            else:
                operands.append(raw_groups[coming])
                loads.append((0, None, most, 0))
                used = most
            blocks += group_blocks(0, coming)
            stores += [(here(0), statics[coming]), (here(statics[coming]), most - statics[coming])]
        extra = []
        if phase == 0:
            extra.append(((1, 0), (local_rows, 0)))
        if phase == 1:
            extra += [((at, 0), pieces[at, 0]) for at in moving]
        if phase == 2:
            extra += [((at, order[0]), pieces[at, order[0]]) for at in range(WIN)]
        used = -(-used // block) * block
        for key, value in extra:
            operands.append(value[0])
            loads.append((len(operands) - 1, here(value[1]), piece, used))
            blocks.append((used, rows_of(key[1], key[0])))
            stores.append((here(used), piece))
            named.append(key)
            used += block
        if stores:
            results = integrate(table_then, operands, loads, merges, blocks, stores)
        else:
            results = []
        rest = outgoing[1]
        if phase == 0:
            static_part, results, rest, units = lax.optimization_barrier(
                (static_part, results, rest, units)
            )
        else:
            static_part, results, rest = lax.optimization_barrier((static_part, results, rest))
        done = {key: (value, 0) for key, value in zip(named, results[len(results) - len(named):])}
        outgoing = results[:len(results) - len(named)]
        arrived = [static_part, step_over(step, units[phase], rest)]
        if step != last:
            arrived, outgoing = lax.optimization_barrier((arrived, outgoing))
            static_part = from_behind(outgoing[0], "narrow", order[phase + 1])
        if step != last:
            cut = pl.pallas_call(
                functools.partial(cut_kernel, static, tiles, piece, step),
                in_specs=[smem] + [hbm] * len(arrived),
                out_specs=[hbm] * WIN,
                out_shape=[rows_type(piece)] * WIN,
                scratch_shapes=[
                    room_type(most + piece),
                    pltpu.SemaphoreType.DMA((len(arrived),)),
                    pltpu.SemaphoreType.DMA((2, WIN)),
                ],
                compiler_params=params,
                name="cut_pieces",
            )(table, *arrived)
            cut, wide_got, table_then = lax.optimization_barrier((cut, wide_got, table))
        for keys, value in zip(keys_now, wide_got):
            pieces.update({key: (value, part * piece) for part, key in enumerate(keys)})
        pieces.update(done)
        if step != last:
            pieces[1, step] = (cut[1], 0)
            keys_now = [[(at, step)] for at in moving]
            wide_got = [from_behind(cut[at], "wide", at - 1) for at in moving]

    held = [pieces[at, step] for step in range(last) for at in range(WIN)]
    buffers = [value for value, _ in held] + arrived
    updated = pl.pallas_call(
        functools.partial(
            finish_kernel,
            (species, levels, columns, tiles, static, piece, narrow_count,
             [begin for _, begin in held]),
        ),
        in_specs=[smem] + [hbm] * len(buffers),
        out_specs=hbm,
        out_shape=jax.ShapeDtypeStruct((species, levels, columns), jnp.float32),
        scratch_shapes=[
            pltpu.VMEM((pair_total - WIN, piece * 8 * tiles, LANES), jnp.float32),
            room_type(most + piece),
            room_type(columns // 8 + 1),
            pltpu.VMEM((species, levels, columns), jnp.float32),
            pltpu.SemaphoreType.DMA((2, pair_total)),
            pltpu.SemaphoreType.DMA((columns // LANES,)),
        ],
        compiler_params=params,
        name="place_columns",
    )(table, *buffers)
    return updated.transpose(1, 0, 2)


def solution(mesh):
    placed = (
        P(None, None, ("wide", "narrow")),
        P(("wide", "narrow")),
        P(),
        P(),
        P(("wide", "narrow")),
        P(("wide", "narrow")),
    )
    return jax.shard_map(
        local,
        mesh=mesh,
        in_specs=placed,
        out_specs=P(None, None, ("wide", "narrow")),
        check_vma=False,
    )
```

```python
import functools

import jax
import jax.numpy as jnp
from jax import lax
from jax.experimental import pallas as pl
from jax.experimental.pallas import tpu as pltpu
from jax.sharding import PartitionSpec as P

WIN = 4
MAXIT = 12
LANES = 128
SORT_COLUMNS = 256
INT_ROWS = 256
UNIT = 8
VMEM = 64 * 1024 * 1024 - 256 * 1024


def from_behind(value, axis, steps):
    count = lax.axis_size(axis)
    pairs = [(source, (source + steps) % count) for source in range(count)]
    return lax.ppermute(value, axis, pairs)


def log2(value):
    bits = value.bit_length() - 1
    assert 1 << bits == value
    return bits


def span_of(group, groups, tiles):
    return pl.ds(pl.multiple_of(group * 8 * tiles, 8), groups * 8 * tiles)


def sort_kernel(sizes, cuts, targets, early, *refs):
    species, levels, columns, tiles, wide_count, narrow_count, pair_total = sizes
    turn_ref, wide_ref, sorted_ref = refs[-4:-1]
    sem_ref = refs[-1]
    if early:
        phys_ref, rate_ref, count_ref, tracers_ref, table_ref, pos_ref = refs[:6]
        cut_refs = refs[6:6 + targets]
        at_ref, table_smem, place_sem = refs[6 + targets:9 + targets]
    else:
        phys_ref, rate_ref, count_ref, tracers_ref, table_smem, at_ref = refs[:6]
        cut_refs = refs[6:6 + targets]
    step = pl.program_id(0)
    lanes = tiles * LANES
    real = species * levels

    def find_places():
        phys = phys_ref[...]
        target = lax.shift_right_logical(phys, log2(columns))
        slot = phys & (columns - 1)
        wide_step = lax.shift_right_logical(target, log2(narrow_count)) - lax.axis_index("wide")
        wide_step = (wide_step + 1) & (wide_count - 1)
        narrow_step = ((target & (narrow_count - 1)) - lax.axis_index("narrow")) & (narrow_count - 1)
        pair = narrow_step * WIN + wide_step
        member = pair == lax.broadcasted_iota(jnp.int32, (pair_total, columns), 0)
        counts = jnp.sum(jnp.where(member, 1.0, 0.0), axis=1, keepdims=True)
        slot_f = slot.astype(jnp.float32)
        starts = jnp.min(jnp.where(member, slot_f, float(columns)), axis=1, keepdims=True)
        groups = lax.shift_right_logical(counts.astype(jnp.int32) + 7, 3).astype(jnp.float32)
        lane = lax.broadcasted_iota(jnp.int32, (pair_total, LANES), 1)
        row = lax.broadcasted_iota(jnp.int32, (pair_total, LANES), 0)

        def across(value):
            return jnp.sum(jnp.where(lane == row, value, 0.0), axis=0, keepdims=True)

        groups_t = across(groups)
        base = jnp.sum(jnp.where(lane < row, groups_t, 0.0), axis=1, keepdims=True)
        section = row & -WIN
        inner = base - jnp.sum(jnp.where(lane < section, groups_t, 0.0), axis=1, keepdims=True)
        same = (lane & -WIN) == section
        in_step = jnp.sum(jnp.where(same, groups_t, 0.0), axis=1, keepdims=True)
        pos = slot_f + jnp.sum(jnp.where(member, base * 8.0 - starts, 0.0), axis=0, keepdims=True)
        pos_ref[...] = pos.astype(jnp.int32)
        pltpu.make_async_copy(pos_ref, at_ref, place_sem.at[0]).start()
        table_ref[...] = jnp.zeros_like(table_ref)
        for at, value in enumerate((counts, base, inner, in_step)):
            table_ref[at:at + 1, :] = across(value).astype(jnp.int32)
        pltpu.make_async_copy(table_ref, table_smem, place_sem.at[1]).start()

    if early:
        pl.when(step == 0)(find_places)
    block = tracers_ref.shape[2]
    begin = step * block
    in_group = lax.broadcasted_iota(jnp.int32, (8, LANES), 0)
    for half in range(block // LANES):
        span = slice(half * LANES, (half + 1) * LANES)
        at = pl.ds(pl.multiple_of(begin + half * LANES, LANES), LANES)
        turn_ref[lanes - 16:lanes, :] = jnp.zeros((16, LANES), jnp.float32)
        turn_ref[0:real, :] = tracers_ref[:, :, span].reshape(real, LANES)
        extra = jnp.where(in_group == 5, (phys_ref[:, at] & (columns - 1)).astype(jnp.float32), 0.0)
        extra = jnp.where(in_group == 6, rate_ref[:, at], extra)
        extra = jnp.where(in_group == 7, count_ref[:, at].astype(jnp.float32), extra)
        turn_ref[lanes - 8:lanes, :] = extra
        for tile in range(tiles):
            wide_ref[half, pl.ds(tile, LANES, stride=8), :] = turn_ref[
                tile * LANES:(tile + 1) * LANES, :
            ].T

        if early and half == 0:
            @pl.when(step == 0)
            def _():
                pltpu.make_async_copy(pos_ref, at_ref, place_sem.at[0]).wait()
                pltpu.make_async_copy(table_ref, table_smem, place_sem.at[1]).wait()

        for column in range(LANES):
            to = at_ref[0, begin + half * LANES + column] * tiles
            sorted_ref[pl.ds(to, tiles), :] = wide_ref[half, column * 8:column * 8 + tiles, :]

    @pl.when(step == pl.num_programs(0) - 1)
    def _():
        copies = []
        for index, (target, to, begin, size, valid) in enumerate(cuts):
            begin = begin(table_smem)
            valid = jnp.clip(valid(table_smem), 0, size)
            copy = pltpu.make_async_copy(
                sorted_ref.at[span_of(begin, size, tiles)],
                cut_refs[target].at[span_of(to, size, tiles)], sem_ref.at[index],
            )
            pl.when(valid > 0)(copy.start)
            copies.append((valid > 0, copy))
        wait_all(copies)


def start_arrival(refs, sem_ref, room_ref, in_step, static, tiles):
    waits = []
    quarter = static // 4
    for part in range(4):
        span = span_of(part * quarter, quarter, tiles)
        copy = pltpu.make_async_copy(refs[0].at[span], room_ref.at[span], sem_ref.at[part])
        copy.start()
        waits.append((None, copy))
    copy = pltpu.make_async_copy(
        refs[1], room_ref.at[pl.ds(static * 8 * tiles, refs[1].shape[0])], sem_ref.at[4]
    )
    pl.when(in_step > static)(copy.start)
    waits.append((in_step > static, copy))
    return waits


def wait_all(waits):
    for wanted, copy in waits:
        if wanted is None:
            copy.wait()
        else:
            pl.when(wanted)(copy.wait)


def integrate_block(sizes, room_ref, first, valid, loss_ref, coupling_ref,
                    turn_ref, y_ref, inverse_ref):
    levels, pad, tiles = sizes
    halves = INT_ROWS // LANES
    lanes = tiles * LANES
    first = pl.multiple_of(first * 8 * tiles, 8)
    for half in range(halves):
        begin = first + half * LANES * tiles
        for tile in range(tiles):
            block = room_ref[pl.ds(begin + tile, LANES, stride=tiles), :]
            turn_ref[half, tile * LANES:(tile + 1) * LANES, :] = block.T
        for level in range(levels):
            y_ref[level, :, half * LANES:(half + 1) * LANES] = turn_ref[
                half, pl.ds(level, pad, stride=levels), :
            ]
    rate = jnp.concatenate(
        [turn_ref[half, lanes - 2:lanes - 1, :] for half in range(halves)], axis=1
    )
    count = jnp.concatenate(
        [turn_ref[half, lanes - 1:lanes, :] for half in range(halves)], axis=1
    )
    lane = lax.broadcasted_iota(jnp.int32, (1, INT_ROWS), 1)
    count = jnp.where((lane < valid) & (count <= MAXIT), count, 0.0)
    step_len = rate / jnp.maximum(count, 1.0)
    inverse_ref[...] = 1.0 / (1.0 + step_len * loss_ref[...])
    last = jnp.max(count).astype(jnp.int32)

    def advance(k, carry):
        active = k.astype(jnp.float32) < count

        def one_level(level, inner):
            y = y_ref[level]
            squashed = jnp.tanh(y).astype(jnp.bfloat16)
            produced = jnp.dot(coupling_ref[...], squashed, preferred_element_type=jnp.float32)
            y_ref[level] = jnp.where(active, (y + step_len * produced) * inverse_ref[...], y)
            return inner

        for level in range(levels):
            one_level(level, 0)
        return carry

    lax.fori_loop(0, last, advance, 0)
    for half in range(halves):
        begin = first + half * LANES * tiles
        for level in range(levels):
            turn_ref[half, pl.ds(level, pad, stride=levels), :] = y_ref[
                level, :, half * LANES:(half + 1) * LANES
            ]
        for tile in range(tiles):
            block = turn_ref[half, tile * LANES:(tile + 1) * LANES, :]
            room_ref[pl.ds(begin + tile, LANES, stride=tiles), :] = block.T


def integrate_kernel(sizes, plan, table_ref, loss_ref, coupling_ref, *refs):
    loads, merges, blocks, stores, operands = plan
    tiles = sizes[2]
    sources = refs[:operands]
    results = refs[operands:operands + len(stores)]
    room_ref, turn_ref, y_ref, inverse_ref, rows_ref, sem_ref, out_sem = refs[
        operands + len(stores):
    ]
    copies = []
    for index, (source, begin, groups, to) in enumerate(loads):
        ref = sources[source]
        if begin is not None:
            ref = ref.at[span_of(begin(table_ref), groups, tiles)]
        copies.append(pltpu.make_async_copy(
            ref, room_ref.at[span_of(to, groups, tiles)], sem_ref.at[index]
        ))
    for copy in copies:
        copy.start()
    for copy in copies:
        copy.wait()
    for begin, groups, to in merges:
        to = to(table_ref)

        def move(group, carry):
            room_ref[span_of(to + group, 1, tiles), :] = room_ref[
                span_of(begin + group, 1, tiles), :
            ]
            return carry

        lax.fori_loop(0, groups(table_ref), move, 0)
    for index, (begin, rows) in enumerate(blocks):
        rows_ref[0, index] = jnp.int32(begin)
        rows_ref[1, index] = rows(table_ref)

    def one_block(index, carry):
        valid = rows_ref[1, index]

        @pl.when(valid > 0)
        def _():
            integrate_block(sizes, room_ref, rows_ref[0, index], valid, loss_ref, coupling_ref,
                            turn_ref, y_ref, inverse_ref)

        return carry

    lax.fori_loop(0, len(blocks), one_block, 0)
    copies = []
    for index, (begin, groups) in enumerate(stores):
        copies.append(pltpu.make_async_copy(
            room_ref.at[span_of(begin(table_ref), groups, tiles)], results[index],
            out_sem.at[index],
        ))
    for copy in copies:
        copy.start()
    for copy in copies:
        copy.wait()


def cut_kernel(static, tiles, piece, step, table_ref, *refs):
    pieces = refs[2:2 + WIN]
    room_ref, sem_ref, out_sem = refs[2 + WIN:]
    wait_all(start_arrival(refs[:2], sem_ref, room_ref, table_ref[3, step * WIN], static, tiles))
    copies = []
    quarter = piece // 4
    for at in range(WIN):
        begin = table_ref[2, step * WIN + at]
        for part in range(4):
            wanted = table_ref[0, step * WIN + at] > part * quarter * 8
            copy = pltpu.make_async_copy(
                room_ref.at[span_of(begin + part * quarter, quarter, tiles)],
                pieces[at].at[span_of(part * quarter, quarter, tiles)], out_sem.at[part, at],
            )
            pl.when(wanted)(copy.start)
            copies.append((wanted, copy))
    wait_all(copies)


def finish_kernel(sizes, table_ref, *refs):
    species, levels, columns, tiles, static, piece, narrow_count, begins = sizes
    pair_total = narrow_count * WIN
    whole_pieces = pair_total - WIN
    (out_ref, piece_ref, room_ref, placed_ref, whole_ref, sem_ref, room_sem,
     out_sem) = refs[-8:]
    copies = []
    quarter = piece // 4
    for pair in range(whole_pieces):
        parts = []
        for part in range(4):
            copy = pltpu.make_async_copy(
                refs[pair].at[span_of(begins[pair] + part * quarter, quarter, tiles)],
                piece_ref.at[pair, span_of(part * quarter, quarter, tiles)],
                sem_ref.at[part, pair],
            )
            wanted = table_ref[0, pair] > part * quarter * 8
            pl.when(wanted)(copy.start)
            parts.append((wanted, copy))
        copies.append(parts)
    waits = start_arrival(refs[whole_pieces:whole_pieces + 2], room_sem, room_ref,
                          table_ref[3, whole_pieces], static, tiles)
    lane = lax.broadcasted_iota(jnp.int32, (1, LANES), 1)
    in_group = lax.broadcasted_iota(jnp.int32, (8, LANES), 0)
    for pair in range(pair_total):
        if pair < whole_pieces:
            wait_all(copies[pair])
            held = piece_ref.at[pair]
            begin = 0
        else:
            if pair == whole_pieces:
                wait_all(waits)
            held = room_ref
            begin = pl.multiple_of(table_ref[2, pair] * 8 * tiles, 8)
        count = table_ref[0, pair]
        first = held[pl.ds(begin + tiles - 1, 1), :]
        start = jnp.max(jnp.where(lane == LANES - 3, first, 0.0)).astype(jnp.int32)
        start = jnp.clip(start, 0, columns - 1) * tiles
        full = lax.shift_right_logical(count, 3)

        def move(group, carry):
            for row in range(0, 8 * tiles, 8):
                at = group * 8 * tiles + row
                placed_ref[pl.ds(start + at, 8), :] = held[pl.ds(pl.multiple_of(begin + at, 8), 8), :]
            return carry

        lax.fori_loop(0, full, move, 0)

        @pl.when((count & 7) > 0)
        def _():
            for row in range(0, 8 * tiles, 8):
                at = full * 8 * tiles + row
                to = pl.ds(start + at, 8)
                placed_ref[to, :] = jnp.where(
                    in_group + row < (count & 7) * tiles,
                    held[pl.ds(pl.multiple_of(begin + at, 8), 8), :], placed_ref[to, :],
                )

    per_tile = LANES // levels
    for part in range(columns // LANES):
        at = slice(part * LANES, (part + 1) * LANES)
        for tile in range(tiles):
            block = placed_ref[pl.ds(part * LANES * tiles + tile, LANES, stride=tiles), :]
            block = block.T.reshape(per_tile, levels, LANES)
            keep = min(per_tile, species - tile * per_tile)
            whole_ref[tile * per_tile:tile * per_tile + keep, :, at] = block[:keep]
        pltpu.make_async_copy(whole_ref.at[:, :, at], out_ref.at[:, :, at], out_sem.at[part]).start()
    for part in range(columns // LANES):
        at = slice(part * LANES, (part + 1) * LANES)
        pltpu.make_async_copy(whole_ref.at[:, :, at], out_ref.at[:, :, at], out_sem.at[part]).wait()


def local(tracers, column_rate, loss_rate, coupling, phys_index, iter_count):
    levels, species, columns = tracers.shape
    wide_count = lax.axis_size("wide")
    narrow_count = lax.axis_size("narrow")
    pair_total = WIN * narrow_count
    room = 2 * columns // pair_total
    piece = room // 8
    pad = -(-species // 8) * 8
    while levels * pad % LANES or levels * (pad - species) < 8:
        pad += 8
    tiles = levels * pad // LANES
    mean = columns // narrow_count // 8
    full = pl.BlockSpec(memory_space=pltpu.VMEM)
    smem = pl.BlockSpec(memory_space=pltpu.SMEM)
    hbm = pl.BlockSpec(memory_space=pltpu.HBM)
    last = narrow_count - 1
    moving = [at for at in range(WIN) if at != 1]
    order = [narrow_count // 2]
    order += [step for step in range(1, last) if step not in order] + [last]
    statics = {step: mean - UNIT if step == order[0] else mean for step in order}
    most = WIN * piece

    params = pltpu.CompilerParams(vmem_limit_bytes=VMEM)

    def rows_type(groups):
        return jax.ShapeDtypeStruct((groups * 8 * tiles, LANES), jnp.float32)

    def room_type(groups):
        return pltpu.VMEM((groups * 8 * tiles, LANES), jnp.float32)

    def entry(row, step, at=0):
        return lambda table: table[row, step * WIN + at]

    def over(step):
        return lambda table: entry(1, step)(table) + statics[step]

    def groups_of(step, at):
        return lambda table: lax.shift_right_logical(table[0, step * WIN + at] + 7, 3)

    def groups_over(step):
        return lambda table: table[3, step * WIN] - statics[step]

    def pair_cuts(target, at):
        return [
            (target, part * piece + half,
             lambda table, step=step, half=half: entry(1, step, at)(table) + half, piece // 2,
             lambda table, step=step, half=half: groups_of(step, at)(table) - half)
            for part, step in enumerate((0, last)) for half in range(0, piece, piece // 2)
        ]

    def sort(cuts, target_sizes, early, known):
        known_types = [
            jax.ShapeDtypeStruct((8, LANES), jnp.int32),
            jax.ShapeDtypeStruct((1, columns), jnp.int32),
        ]
        groups = columns // 8 + pair_total + most
        return pl.pallas_call(
            functools.partial(
                sort_kernel,
                (species, levels, columns, tiles, wide_count, narrow_count, pair_total),
                cuts, len(target_sizes), early,
            ),
            grid=(columns // SORT_COLUMNS,),
            in_specs=[full, full, full,
                      pl.BlockSpec((species, levels, SORT_COLUMNS), lambda at: (0, 0, at))]
            + [smem] * len(known),
            out_specs=([full, full] if early else []) + [hbm] * len(target_sizes),
            out_shape=(known_types if early else []) + [rows_type(size) for size in target_sizes],
            scratch_shapes=([
                pltpu.SMEM((1, columns), jnp.int32), pltpu.SMEM((8, LANES), jnp.int32),
                pltpu.SemaphoreType.DMA((2,)),
            ] if early else []) + [
                pltpu.VMEM((tiles * LANES, LANES), jnp.float32),
                pltpu.VMEM((SORT_COLUMNS // LANES, LANES * 8, LANES), jnp.float32),
                room_type(groups),
                pltpu.SemaphoreType.DMA((len(cuts),)),
            ],
            compiler_params=params,
            name="sort_columns" if early else "sort_later_columns",
        )(
            phys_index.reshape(1, columns),
            column_rate.reshape(1, columns),
            iter_count.reshape(1, columns),
            tracers.transpose(1, 0, 2),
            *known,
        )

    first_static = statics[order[0]]
    cuts = [(0, 0, entry(1, order[0]), first_static, entry(3, order[0]))]
    for index, at in enumerate(moving):
        cuts += pair_cuts(1 + index, at)
    table, places, *first = sort(
        cuts, [first_static] + [2 * piece] * len(moving), True, ()
    )
    cuts = [(0, 0, over(order[0]), most - first_static, groups_over(order[0]))]
    cuts += pair_cuts(1, 1)
    for index, step in enumerate(order[1:-1]):
        rest = most - statics[step]
        cuts.append((2 + index, 0, entry(1, step), statics[step], entry(3, step)))
        cuts.append((2 + index, statics[step], over(step), rest, groups_over(step)))
    first_rest, local_rows, *raw = sort(
        cuts, [most - first_static, 2 * piece] + [most] * (len(order) - 2), False, (table, places)
    )
    raw_groups = dict(zip(order[1:-1], raw))
    units = [
        (jnp.maximum(table[3, step * WIN] - statics[step], 0) + UNIT - 1) // UNIT
        for step in order
    ]
    loss_pad = jnp.pad(loss_rate, (0, pad - species)).reshape(pad, 1)
    coupling_pad = jnp.pad(coupling, ((0, pad - species), (0, pad - species)))
    block = INT_ROWS // 8

    def integrate(table, operands, loads, merges, blocks, stores):
        groups = max([to + size for _, _, size, to in loads] + [begin + block for begin, _ in blocks])
        groups += piece
        return pl.pallas_call(
            functools.partial(
                integrate_kernel, (levels, pad, tiles),
                (loads, merges, blocks, stores, len(operands)),
            ),
            in_specs=[smem, full, full] + [hbm] * len(operands),
            out_specs=[hbm] * len(stores),
            out_shape=[rows_type(size) for _, size in stores],
            scratch_shapes=[
                room_type(groups),
                pltpu.VMEM((INT_ROWS // LANES, tiles * LANES, LANES), jnp.float32),
                pltpu.VMEM((levels, pad, INT_ROWS), jnp.float32),
                pltpu.VMEM((pad, INT_ROWS), jnp.float32),
                pltpu.SMEM((2, LANES), jnp.int32),
                pltpu.SemaphoreType.DMA((len(loads),)),
                pltpu.SemaphoreType.DMA((len(stores),)),
            ],
            compiler_params=params,
            name="integrate_columns",
        )(table, loss_pad, coupling_pad, *operands)

    def rows_of(step, at=0):
        return entry(0, step, at)

    def group_blocks(begin, step):
        return [
            (begin + part * block,
             lambda table, part=part: table[3, step * WIN] * 8 - part * INT_ROWS)
            for part in range(most // block)
        ]

    def here(begin):
        return lambda table: jnp.int32(begin)

    def step_over(step, units, rest):
        def leaf(units, rest):
            if units == 0:
                return rest
            got = from_behind(rest[:units * UNIT * 8 * tiles], "narrow", step)
            return lax.dynamic_update_slice(rest, got, (0, 0))

        leaves = [functools.partial(leaf, count) for count in range((most - statics[step]) // UNIT + 1)]
        return lax.switch(units, leaves, rest)

    pieces = {}
    outgoing = [first[0], first_rest]
    wide_now = first[1:]
    keys_now = [[(at, 0), (at, last)] for at in moving]
    static_part = from_behind(outgoing[0], "narrow", order[0])
    wide_got = [from_behind(value, "wide", at - 1) for value, at in zip(wide_now, moving)]
    table_then = table
    for phase, step in enumerate(order):
        static = statics[step]
        operands, loads, merges, blocks, stores, named = [], [], [], [], [], []
        used = 0
        if phase + 1 < len(order):
            coming = order[phase + 1]
            if coming == last:
                operands += [pieces[at, last][0] for at in moving] + [local_rows]
                for index, at in enumerate(moving):
                    loads.append((index, here(pieces[at, last][1]), piece, most + at * piece))
                loads.append((len(moving), here(piece), piece, most + piece))
                for at in range(WIN):
                    merges.append(
                        (most + at * piece, groups_of(last, at), entry(2, last, at))
                    )
                used = most + WIN * piece
            else:
                operands.append(raw_groups[coming])
                loads.append((0, None, most, 0))
                used = most
            blocks += group_blocks(0, coming)
            stores += [(here(0), statics[coming]), (here(statics[coming]), most - statics[coming])]
        extra = []
        if phase == 0:
            extra.append(((1, 0), (local_rows, 0)))
        if phase == 1:
            extra += [((at, 0), pieces[at, 0]) for at in moving]
        if phase == 2:
            extra += [((at, order[0]), pieces[at, order[0]]) for at in range(WIN)]
        used = -(-used // block) * block
        for key, value in extra:
            operands.append(value[0])
            loads.append((len(operands) - 1, here(value[1]), piece, used))
            blocks.append((used, rows_of(key[1], key[0])))
            stores.append((here(used), piece))
            named.append(key)
            used += block
        if stores:
            results = integrate(table_then, operands, loads, merges, blocks, stores)
        else:
            results = []
        rest = outgoing[1]
        if phase == 0:
            static_part, results, rest, units = lax.optimization_barrier(
                (static_part, results, rest, units)
            )
        else:
            static_part, results, rest = lax.optimization_barrier((static_part, results, rest))
        done = {key: (value, 0) for key, value in zip(named, results[len(results) - len(named):])}
        outgoing = results[:len(results) - len(named)]
        arrived = [static_part, step_over(step, units[phase], rest)]
        if step != last:
            arrived, outgoing = lax.optimization_barrier((arrived, outgoing))
            static_part = from_behind(outgoing[0], "narrow", order[phase + 1])
        if step != last:
            cut = pl.pallas_call(
                functools.partial(cut_kernel, static, tiles, piece, step),
                in_specs=[smem] + [hbm] * len(arrived),
                out_specs=[hbm] * WIN,
                out_shape=[rows_type(piece)] * WIN,
                scratch_shapes=[
                    room_type(most + piece),
                    pltpu.SemaphoreType.DMA((5,)),
                    pltpu.SemaphoreType.DMA((4, WIN)),
                ],
                compiler_params=params,
                name="cut_pieces",
            )(table, *arrived)
            cut, wide_got, table_then = lax.optimization_barrier((cut, wide_got, table))
        for keys, value in zip(keys_now, wide_got):
            pieces.update({key: (value, part * piece) for part, key in enumerate(keys)})
        pieces.update(done)
        if step != last:
            pieces[1, step] = (cut[1], 0)
            keys_now = [[(at, step)] for at in moving]
            wide_got = [from_behind(cut[at], "wide", at - 1) for at in moving]

    held = [pieces[at, step] for step in range(last) for at in range(WIN)]
    buffers = [value for value, _ in held] + arrived
    updated = pl.pallas_call(
        functools.partial(
            finish_kernel,
            (species, levels, columns, tiles, static, piece, narrow_count,
             [begin for _, begin in held]),
        ),
        in_specs=[smem] + [hbm] * len(buffers),
        out_specs=hbm,
        out_shape=jax.ShapeDtypeStruct((species, levels, columns), jnp.float32),
        scratch_shapes=[
            pltpu.VMEM((pair_total - WIN, piece * 8 * tiles, LANES), jnp.float32),
            room_type(most + piece),
            room_type(columns // 8 + 1),
            pltpu.VMEM((species, levels, columns), jnp.float32),
            pltpu.SemaphoreType.DMA((4, pair_total)),
            pltpu.SemaphoreType.DMA((5,)),
            pltpu.SemaphoreType.DMA((columns // LANES,)),
        ],
        compiler_params=params,
        name="place_columns",
    )(table, *buffers)
    return updated.transpose(1, 0, 2)


def solution(mesh):
    placed = (
        P(None, None, ("wide", "narrow")),
        P(("wide", "narrow")),
        P(),
        P(),
        P(("wide", "narrow")),
        P(("wide", "narrow")),
    )
    return jax.shard_map(
        local,
        mesh=mesh,
        in_specs=placed,
        out_specs=P(None, None, ("wide", "narrow")),
        check_vma=False,
    )
```

```python
import functools

import jax
import jax.numpy as jnp
from jax import lax
from jax.experimental import pallas as pl
from jax.experimental.pallas import tpu as pltpu
from jax.sharding import PartitionSpec as P

WIN = 4
MAXIT = 12
LANES = 128
SORT_COLUMNS = 256
INT_ROWS = 256
UNIT = 8
VMEM = 64 * 1024 * 1024 - 256 * 1024


def from_behind(value, axis, steps):
    count = lax.axis_size(axis)
    pairs = [(source, (source + steps) % count) for source in range(count)]
    return lax.ppermute(value, axis, pairs)


def log2(value):
    bits = value.bit_length() - 1
    assert 1 << bits == value
    return bits


def span_of(group, groups, tiles):
    return pl.ds(pl.multiple_of(group * 8 * tiles, 8), groups * 8 * tiles)


def sort_kernel(sizes, cuts, targets, early, *refs):
    species, levels, columns, tiles, wide_count, narrow_count, pair_total = sizes
    turn_ref, wide_ref, sorted_ref = refs[-4:-1]
    sem_ref = refs[-1]
    if early:
        phys_ref, rate_ref, count_ref, tracers_ref, table_ref, pos_ref = refs[:6]
        cut_refs = refs[6:6 + targets]
        at_ref, table_smem, place_sem = refs[6 + targets:9 + targets]
    else:
        phys_ref, rate_ref, count_ref, tracers_ref, table_smem, at_ref = refs[:6]
        cut_refs = refs[6:6 + targets]
    step = pl.program_id(0)
    lanes = tiles * LANES
    real = species * levels

    def find_places():
        phys = phys_ref[...]
        target = lax.shift_right_logical(phys, log2(columns))
        slot = phys & (columns - 1)
        wide_step = lax.shift_right_logical(target, log2(narrow_count)) - lax.axis_index("wide")
        wide_step = (wide_step + 1) & (wide_count - 1)
        narrow_step = ((target & (narrow_count - 1)) - lax.axis_index("narrow")) & (narrow_count - 1)
        pair = narrow_step * WIN + wide_step
        member = pair == lax.broadcasted_iota(jnp.int32, (pair_total, columns), 0)
        counts = jnp.sum(jnp.where(member, 1.0, 0.0), axis=1, keepdims=True)
        slot_f = slot.astype(jnp.float32)
        starts = jnp.min(jnp.where(member, slot_f, float(columns)), axis=1, keepdims=True)
        groups = lax.shift_right_logical(counts.astype(jnp.int32) + 7, 3).astype(jnp.float32)
        lane = lax.broadcasted_iota(jnp.int32, (pair_total, LANES), 1)
        row = lax.broadcasted_iota(jnp.int32, (pair_total, LANES), 0)

        def across(value):
            return jnp.sum(jnp.where(lane == row, value, 0.0), axis=0, keepdims=True)

        groups_t = across(groups)
        base = jnp.sum(jnp.where(lane < row, groups_t, 0.0), axis=1, keepdims=True)
        section = row & -WIN
        inner = base - jnp.sum(jnp.where(lane < section, groups_t, 0.0), axis=1, keepdims=True)
        same = (lane & -WIN) == section
        in_step = jnp.sum(jnp.where(same, groups_t, 0.0), axis=1, keepdims=True)
        pos = slot_f + jnp.sum(jnp.where(member, base * 8.0 - starts, 0.0), axis=0, keepdims=True)
        pos_ref[...] = pos.astype(jnp.int32)
        pltpu.make_async_copy(pos_ref, at_ref, place_sem.at[0]).start()
        table_ref[...] = jnp.zeros_like(table_ref)
        for at, value in enumerate((counts, base, inner, in_step)):
            table_ref[at:at + 1, :] = across(value).astype(jnp.int32)
        pltpu.make_async_copy(table_ref, table_smem, place_sem.at[1]).start()

    if early:
        pl.when(step == 0)(find_places)
    block = tracers_ref.shape[2]
    begin = step * block
    in_group = lax.broadcasted_iota(jnp.int32, (8, LANES), 0)
    for half in range(block // LANES):
        span = slice(half * LANES, (half + 1) * LANES)
        at = pl.ds(pl.multiple_of(begin + half * LANES, LANES), LANES)
        turn_ref[lanes - 16:lanes, :] = jnp.zeros((16, LANES), jnp.float32)
        turn_ref[0:real, :] = tracers_ref[:, :, span].reshape(real, LANES)
        extra = jnp.where(in_group == 5, (phys_ref[:, at] & (columns - 1)).astype(jnp.float32), 0.0)
        extra = jnp.where(in_group == 6, rate_ref[:, at], extra)
        extra = jnp.where(in_group == 7, count_ref[:, at].astype(jnp.float32), extra)
        turn_ref[lanes - 8:lanes, :] = extra
        for tile in range(tiles):
            wide_ref[half, pl.ds(tile, LANES, stride=8), :] = turn_ref[
                tile * LANES:(tile + 1) * LANES, :
            ].T

        if early and half == 0:
            @pl.when(step == 0)
            def _():
                pltpu.make_async_copy(pos_ref, at_ref, place_sem.at[0]).wait()
                pltpu.make_async_copy(table_ref, table_smem, place_sem.at[1]).wait()

        for column in range(LANES):
            to = at_ref[0, begin + half * LANES + column] * tiles
            sorted_ref[pl.ds(to, tiles), :] = wide_ref[half, column * 8:column * 8 + tiles, :]

    @pl.when(step == pl.num_programs(0) - 1)
    def _():
        copies = []
        for index, (target, to, begin, size, valid) in enumerate(cuts):
            begin = begin(table_smem)
            valid = jnp.clip(valid(table_smem), 0, size)
            copy = pltpu.make_async_copy(
                sorted_ref.at[span_of(begin, size, tiles)],
                cut_refs[target].at[span_of(to, size, tiles)], sem_ref.at[index],
            )
            pl.when(valid > 0)(copy.start)
            copies.append((valid > 0, copy))
        wait_all(copies)


def start_arrival(refs, sem_ref, room_ref, in_step, static, tiles):
    waits = []
    quarter = static // 4
    for part in range(4):
        copy = pltpu.make_async_copy(
            refs[part // 2].at[span_of(part % 2 * quarter, quarter, tiles)],
            room_ref.at[span_of(part * quarter, quarter, tiles)], sem_ref.at[part],
        )
        copy.start()
        waits.append((None, copy))
    copy = pltpu.make_async_copy(
        refs[2], room_ref.at[pl.ds(static * 8 * tiles, refs[2].shape[0])], sem_ref.at[4]
    )
    pl.when(in_step > static)(copy.start)
    waits.append((in_step > static, copy))
    return waits


def wait_all(waits):
    for wanted, copy in waits:
        if wanted is None:
            copy.wait()
        else:
            pl.when(wanted)(copy.wait)


def integrate_block(sizes, room_ref, first, valid, loss_ref, coupling_ref,
                    turn_ref, y_ref, inverse_ref):
    levels, pad, tiles = sizes
    halves = INT_ROWS // LANES
    lanes = tiles * LANES
    first = pl.multiple_of(first * 8 * tiles, 8)
    for half in range(halves):
        begin = first + half * LANES * tiles
        for tile in range(tiles):
            block = room_ref[pl.ds(begin + tile, LANES, stride=tiles), :]
            turn_ref[half, tile * LANES:(tile + 1) * LANES, :] = block.T
        for level in range(levels):
            y_ref[level, :, half * LANES:(half + 1) * LANES] = turn_ref[
                half, pl.ds(level, pad, stride=levels), :
            ]
    rate = jnp.concatenate(
        [turn_ref[half, lanes - 2:lanes - 1, :] for half in range(halves)], axis=1
    )
    count = jnp.concatenate(
        [turn_ref[half, lanes - 1:lanes, :] for half in range(halves)], axis=1
    )
    lane = lax.broadcasted_iota(jnp.int32, (1, INT_ROWS), 1)
    count = jnp.where((lane < valid) & (count <= MAXIT), count, 0.0)
    step_len = rate / jnp.maximum(count, 1.0)
    inverse_ref[...] = 1.0 / (1.0 + step_len * loss_ref[...])
    last = jnp.max(count).astype(jnp.int32)

    def advance(k, carry):
        active = k.astype(jnp.float32) < count

        def one_level(level, inner):
            y = y_ref[level]
            squashed = jnp.tanh(y).astype(jnp.bfloat16)
            produced = jnp.dot(coupling_ref[...], squashed, preferred_element_type=jnp.float32)
            y_ref[level] = jnp.where(active, (y + step_len * produced) * inverse_ref[...], y)
            return inner

        for level in range(levels):
            one_level(level, 0)
        return carry

    lax.fori_loop(0, last, advance, 0)
    for half in range(halves):
        begin = first + half * LANES * tiles
        for level in range(levels):
            turn_ref[half, pl.ds(level, pad, stride=levels), :] = y_ref[
                level, :, half * LANES:(half + 1) * LANES
            ]
        for tile in range(tiles):
            block = turn_ref[half, tile * LANES:(tile + 1) * LANES, :]
            room_ref[pl.ds(begin + tile, LANES, stride=tiles), :] = block.T


def integrate_kernel(sizes, plan, table_ref, loss_ref, coupling_ref, *refs):
    loads, merges, blocks, stores, operands = plan
    tiles = sizes[2]
    sources = refs[:operands]
    results = refs[operands:operands + len(stores)]
    room_ref, turn_ref, y_ref, inverse_ref, rows_ref, sem_ref, out_sem = refs[
        operands + len(stores):
    ]
    copies = []
    for index, (source, begin, groups, to) in enumerate(loads):
        ref = sources[source]
        if begin is not None:
            ref = ref.at[span_of(begin(table_ref), groups, tiles)]
        copies.append(pltpu.make_async_copy(
            ref, room_ref.at[span_of(to, groups, tiles)], sem_ref.at[index]
        ))
    for copy in copies:
        copy.start()
    for copy in copies:
        copy.wait()
    for begin, groups, to in merges:
        to = to(table_ref)

        def move(group, carry):
            room_ref[span_of(to + group, 1, tiles), :] = room_ref[
                span_of(begin + group, 1, tiles), :
            ]
            return carry

        lax.fori_loop(0, groups(table_ref), move, 0)
    for index, (begin, rows) in enumerate(blocks):
        rows_ref[0, index] = jnp.int32(begin)
        rows_ref[1, index] = rows(table_ref)

    def one_block(index, carry):
        valid = rows_ref[1, index]

        @pl.when(valid > 0)
        def _():
            integrate_block(sizes, room_ref, rows_ref[0, index], valid, loss_ref, coupling_ref,
                            turn_ref, y_ref, inverse_ref)

        return carry

    lax.fori_loop(0, len(blocks), one_block, 0)
    copies = []
    for index, (begin, groups) in enumerate(stores):
        copies.append(pltpu.make_async_copy(
            room_ref.at[span_of(begin(table_ref), groups, tiles)], results[index],
            out_sem.at[index],
        ))
    for copy in copies:
        copy.start()
    for copy in copies:
        copy.wait()


def cut_kernel(static, tiles, piece, step, table_ref, *refs):
    pieces = refs[3:3 + WIN]
    room_ref, sem_ref, out_sem = refs[3 + WIN:]
    wait_all(start_arrival(refs[:3], sem_ref, room_ref, table_ref[3, step * WIN], static, tiles))
    copies = []
    quarter = piece // 4
    for at in range(WIN):
        begin = table_ref[2, step * WIN + at]
        for part in range(4):
            wanted = table_ref[0, step * WIN + at] > part * quarter * 8
            copy = pltpu.make_async_copy(
                room_ref.at[span_of(begin + part * quarter, quarter, tiles)],
                pieces[at].at[span_of(part * quarter, quarter, tiles)], out_sem.at[part, at],
            )
            pl.when(wanted)(copy.start)
            copies.append((wanted, copy))
    wait_all(copies)


def finish_kernel(sizes, table_ref, *refs):
    species, levels, columns, tiles, static, piece, narrow_count, begins = sizes
    pair_total = narrow_count * WIN
    whole_pieces = pair_total - WIN
    (out_ref, piece_ref, room_ref, placed_ref, whole_ref, sem_ref, room_sem,
     out_sem) = refs[-8:]
    copies = []
    quarter = piece // 4
    for pair in range(whole_pieces):
        parts = []
        for part in range(4):
            copy = pltpu.make_async_copy(
                refs[pair].at[span_of(begins[pair] + part * quarter, quarter, tiles)],
                piece_ref.at[pair, span_of(part * quarter, quarter, tiles)],
                sem_ref.at[part, pair],
            )
            wanted = table_ref[0, pair] > part * quarter * 8
            pl.when(wanted)(copy.start)
            parts.append((wanted, copy))
        copies.append(parts)
    waits = start_arrival(refs[whole_pieces:whole_pieces + 3], room_sem, room_ref,
                          table_ref[3, whole_pieces], static, tiles)
    lane = lax.broadcasted_iota(jnp.int32, (1, LANES), 1)
    in_group = lax.broadcasted_iota(jnp.int32, (8, LANES), 0)
    for pair in range(pair_total):
        if pair < whole_pieces:
            wait_all(copies[pair])
            held = piece_ref.at[pair]
            begin = 0
        else:
            if pair == whole_pieces:
                wait_all(waits)
            held = room_ref
            begin = pl.multiple_of(table_ref[2, pair] * 8 * tiles, 8)
        count = table_ref[0, pair]
        first = held[pl.ds(begin + tiles - 1, 1), :]
        start = jnp.max(jnp.where(lane == LANES - 3, first, 0.0)).astype(jnp.int32)
        start = jnp.clip(start, 0, columns - 1) * tiles
        full = lax.shift_right_logical(count, 3)

        def move(group, carry):
            for row in range(0, 8 * tiles, 8):
                at = group * 8 * tiles + row
                placed_ref[pl.ds(start + at, 8), :] = held[pl.ds(pl.multiple_of(begin + at, 8), 8), :]
            return carry

        lax.fori_loop(0, full, move, 0)

        @pl.when((count & 7) > 0)
        def _():
            for row in range(0, 8 * tiles, 8):
                at = full * 8 * tiles + row
                to = pl.ds(start + at, 8)
                placed_ref[to, :] = jnp.where(
                    in_group + row < (count & 7) * tiles,
                    held[pl.ds(pl.multiple_of(begin + at, 8), 8), :], placed_ref[to, :],
                )

    per_tile = LANES // levels
    for part in range(columns // LANES):
        at = slice(part * LANES, (part + 1) * LANES)
        for tile in range(tiles):
            block = placed_ref[pl.ds(part * LANES * tiles + tile, LANES, stride=tiles), :]
            block = block.T.reshape(per_tile, levels, LANES)
            keep = min(per_tile, species - tile * per_tile)
            whole_ref[tile * per_tile:tile * per_tile + keep, :, at] = block[:keep]
        pltpu.make_async_copy(whole_ref.at[:, :, at], out_ref.at[:, :, at], out_sem.at[part]).start()
    for part in range(columns // LANES):
        at = slice(part * LANES, (part + 1) * LANES)
        pltpu.make_async_copy(whole_ref.at[:, :, at], out_ref.at[:, :, at], out_sem.at[part]).wait()


def local(tracers, column_rate, loss_rate, coupling, phys_index, iter_count):
    levels, species, columns = tracers.shape
    wide_count = lax.axis_size("wide")
    narrow_count = lax.axis_size("narrow")
    pair_total = WIN * narrow_count
    room = 2 * columns // pair_total
    piece = room // 8
    pad = -(-species // 8) * 8
    while levels * pad % LANES or levels * (pad - species) < 8:
        pad += 8
    tiles = levels * pad // LANES
    mean = columns // narrow_count // 8
    full = pl.BlockSpec(memory_space=pltpu.VMEM)
    smem = pl.BlockSpec(memory_space=pltpu.SMEM)
    hbm = pl.BlockSpec(memory_space=pltpu.HBM)
    last = narrow_count - 1
    moving = [at for at in range(WIN) if at != 1]
    order = [narrow_count // 2]
    order += [step for step in range(1, last) if step not in order] + [last]
    statics = {step: mean - UNIT if step == order[0] else mean for step in order}
    most = WIN * piece

    params = pltpu.CompilerParams(vmem_limit_bytes=VMEM)

    def rows_type(groups):
        return jax.ShapeDtypeStruct((groups * 8 * tiles, LANES), jnp.float32)

    def room_type(groups):
        return pltpu.VMEM((groups * 8 * tiles, LANES), jnp.float32)

    def entry(row, step, at=0):
        return lambda table: table[row, step * WIN + at]

    def over(step):
        return lambda table: entry(1, step)(table) + statics[step]

    def groups_of(step, at):
        return lambda table: lax.shift_right_logical(table[0, step * WIN + at] + 7, 3)

    def groups_over(step):
        return lambda table: table[3, step * WIN] - statics[step]

    def pair_cuts(target, at):
        return [
            (target, part * piece + half,
             lambda table, step=step, half=half: entry(1, step, at)(table) + half, piece // 2,
             lambda table, step=step, half=half: groups_of(step, at)(table) - half)
            for part, step in enumerate((0, last)) for half in range(0, piece, piece // 2)
        ]

    def sort(cuts, target_sizes, early, known):
        known_types = [
            jax.ShapeDtypeStruct((8, LANES), jnp.int32),
            jax.ShapeDtypeStruct((1, columns), jnp.int32),
        ]
        groups = columns // 8 + pair_total + most
        return pl.pallas_call(
            functools.partial(
                sort_kernel,
                (species, levels, columns, tiles, wide_count, narrow_count, pair_total),
                cuts, len(target_sizes), early,
            ),
            grid=(columns // SORT_COLUMNS,),
            in_specs=[full, full, full,
                      pl.BlockSpec((species, levels, SORT_COLUMNS), lambda at: (0, 0, at))]
            + [smem] * len(known),
            out_specs=([full, full] if early else []) + [hbm] * len(target_sizes),
            out_shape=(known_types if early else []) + [rows_type(size) for size in target_sizes],
            scratch_shapes=([
                pltpu.SMEM((1, columns), jnp.int32), pltpu.SMEM((8, LANES), jnp.int32),
                pltpu.SemaphoreType.DMA((2,)),
            ] if early else []) + [
                pltpu.VMEM((tiles * LANES, LANES), jnp.float32),
                pltpu.VMEM((SORT_COLUMNS // LANES, LANES * 8, LANES), jnp.float32),
                room_type(groups),
                pltpu.SemaphoreType.DMA((len(cuts),)),
            ],
            compiler_params=params,
            name="sort_columns" if early else "sort_later_columns",
        )(
            phys_index.reshape(1, columns),
            column_rate.reshape(1, columns),
            iter_count.reshape(1, columns),
            tracers.transpose(1, 0, 2),
            *known,
        )

    first_static = statics[order[0]]
    half = first_static // 2
    cuts = [
        (0, 0, entry(1, order[0]), half, entry(3, order[0])),
        (1, 0, lambda table: entry(1, order[0])(table) + half, half,
         lambda table: entry(3, order[0])(table) - half),
    ]
    for index, at in enumerate(moving):
        cuts += pair_cuts(2 + index, at)
    table, places, *first = sort(
        cuts, [half, half] + [2 * piece] * len(moving), True, ()
    )
    cuts = [(0, 0, over(order[0]), most - first_static, groups_over(order[0]))]
    cuts += pair_cuts(1, 1)
    for index, step in enumerate(order[1:-1]):
        rest = most - statics[step]
        cuts.append((2 + index, 0, entry(1, step), statics[step], entry(3, step)))
        cuts.append((2 + index, statics[step], over(step), rest, groups_over(step)))
    first_rest, local_rows, *raw = sort(
        cuts, [most - first_static, 2 * piece] + [most] * (len(order) - 2), False, (table, places)
    )
    raw_groups = dict(zip(order[1:-1], raw))
    units = [
        (jnp.maximum(table[3, step * WIN] - statics[step], 0) + UNIT - 1) // UNIT
        for step in order
    ]
    loss_pad = jnp.pad(loss_rate, (0, pad - species)).reshape(pad, 1)
    coupling_pad = jnp.pad(coupling, ((0, pad - species), (0, pad - species)))
    block = INT_ROWS // 8

    def integrate(table, operands, loads, merges, blocks, stores):
        groups = max([to + size for _, _, size, to in loads] + [begin + block for begin, _ in blocks])
        groups += piece
        return pl.pallas_call(
            functools.partial(
                integrate_kernel, (levels, pad, tiles),
                (loads, merges, blocks, stores, len(operands)),
            ),
            in_specs=[smem, full, full] + [hbm] * len(operands),
            out_specs=[hbm] * len(stores),
            out_shape=[rows_type(size) for _, size in stores],
            scratch_shapes=[
                room_type(groups),
                pltpu.VMEM((INT_ROWS // LANES, tiles * LANES, LANES), jnp.float32),
                pltpu.VMEM((levels, pad, INT_ROWS), jnp.float32),
                pltpu.VMEM((pad, INT_ROWS), jnp.float32),
                pltpu.SMEM((2, LANES), jnp.int32),
                pltpu.SemaphoreType.DMA((len(loads),)),
                pltpu.SemaphoreType.DMA((len(stores),)),
            ],
            compiler_params=params,
            name="integrate_columns",
        )(table, loss_pad, coupling_pad, *operands)

    def rows_of(step, at=0):
        return entry(0, step, at)

    def group_blocks(begin, step):
        return [
            (begin + part * block,
             lambda table, part=part: table[3, step * WIN] * 8 - part * INT_ROWS)
            for part in range(most // block)
        ]

    def here(begin):
        return lambda table: jnp.int32(begin)

    def step_over(step, units, rest):
        def leaf(units, rest):
            if units == 0:
                return rest
            half = units * UNIT * 4 * tiles
            both = [
                from_behind(rest[part * half:(part + 1) * half], "narrow", step)
                for part in range(2)
            ]
            for part in range(2):
                rest = lax.dynamic_update_slice(rest, both[part], (part * half, 0))
            return rest

        leaves = [functools.partial(leaf, count) for count in range((most - statics[step]) // UNIT + 1)]
        return lax.switch(units, leaves, rest)

    pieces = {}
    outgoing = [first[0], first[1], first_rest]
    wide_now = first[2:]
    keys_now = [[(at, 0), (at, last)] for at in moving]
    static_part = [from_behind(value, "narrow", order[0]) for value in outgoing[:2]]
    wide_got = [from_behind(value, "wide", at - 1) for value, at in zip(wide_now, moving)]
    table_then = table
    for phase, step in enumerate(order):
        static = statics[step]
        operands, loads, merges, blocks, stores, named = [], [], [], [], [], []
        used = 0
        if phase + 1 < len(order):
            coming = order[phase + 1]
            if coming == last:
                operands += [pieces[at, last][0] for at in moving] + [local_rows]
                for index, at in enumerate(moving):
                    loads.append((index, here(pieces[at, last][1]), piece, most + at * piece))
                loads.append((len(moving), here(piece), piece, most + piece))
                for at in range(WIN):
                    merges.append(
                        (most + at * piece, groups_of(last, at), entry(2, last, at))
                    )
                used = most + WIN * piece
            else:
                operands.append(raw_groups[coming])
                loads.append((0, None, most, 0))
                used = most
            blocks += group_blocks(0, coming)
            half = statics[coming] // 2
            stores += [(here(0), half), (here(half), half)]
            stores += [(here(statics[coming]), most - statics[coming])]
        extra = []
        if phase == 0:
            extra.append(((1, 0), (local_rows, 0)))
        if phase == 1:
            extra += [((at, 0), pieces[at, 0]) for at in moving]
        if phase == 2:
            extra += [((at, order[0]), pieces[at, order[0]]) for at in range(WIN)]
        used = -(-used // block) * block
        for key, value in extra:
            operands.append(value[0])
            loads.append((len(operands) - 1, here(value[1]), piece, used))
            blocks.append((used, rows_of(key[1], key[0])))
            stores.append((here(used), piece))
            named.append(key)
            used += block
        if stores:
            results = integrate(table_then, operands, loads, merges, blocks, stores)
        else:
            results = []
        rest = outgoing[2]
        if phase == 0:
            static_part, results, rest, units = lax.optimization_barrier(
                (static_part, results, rest, units)
            )
        else:
            static_part, results, rest = lax.optimization_barrier((static_part, results, rest))
        done = {key: (value, 0) for key, value in zip(named, results[len(results) - len(named):])}
        outgoing = results[:len(results) - len(named)]
        arrived = list(static_part) + [step_over(step, units[phase], rest)]
        if step != last:
            arrived, outgoing = lax.optimization_barrier((arrived, outgoing))
            static_part = [
                from_behind(value, "narrow", order[phase + 1]) for value in outgoing[:2]
            ]
        if step != last:
            cut = pl.pallas_call(
                functools.partial(cut_kernel, static, tiles, piece, step),
                in_specs=[smem] + [hbm] * len(arrived),
                out_specs=[hbm] * WIN,
                out_shape=[rows_type(piece)] * WIN,
                scratch_shapes=[
                    room_type(most + piece),
                    pltpu.SemaphoreType.DMA((5,)),
                    pltpu.SemaphoreType.DMA((4, WIN)),
                ],
                compiler_params=params,
                name="cut_pieces",
            )(table, *arrived)
            cut, wide_got, table_then = lax.optimization_barrier((cut, wide_got, table))
        for keys, value in zip(keys_now, wide_got):
            pieces.update({key: (value, part * piece) for part, key in enumerate(keys)})
        pieces.update(done)
        if step != last:
            pieces[1, step] = (cut[1], 0)
            keys_now = [[(at, step)] for at in moving]
            wide_got = [from_behind(cut[at], "wide", at - 1) for at in moving]

    held = [pieces[at, step] for step in range(last) for at in range(WIN)]
    buffers = [value for value, _ in held] + arrived
    updated = pl.pallas_call(
        functools.partial(
            finish_kernel,
            (species, levels, columns, tiles, static, piece, narrow_count,
             [begin for _, begin in held]),
        ),
        in_specs=[smem] + [hbm] * len(buffers),
        out_specs=hbm,
        out_shape=jax.ShapeDtypeStruct((species, levels, columns), jnp.float32),
        scratch_shapes=[
            pltpu.VMEM((pair_total - WIN, piece * 8 * tiles, LANES), jnp.float32),
            room_type(most + piece),
            room_type(columns // 8 + 1),
            pltpu.VMEM((species, levels, columns), jnp.float32),
            pltpu.SemaphoreType.DMA((4, pair_total)),
            pltpu.SemaphoreType.DMA((5,)),
            pltpu.SemaphoreType.DMA((columns // LANES,)),
        ],
        compiler_params=params,
        name="place_columns",
    )(table, *buffers)
    return updated.transpose(1, 0, 2)


def solution(mesh):
    placed = (
        P(None, None, ("wide", "narrow")),
        P(("wide", "narrow")),
        P(),
        P(),
        P(("wide", "narrow")),
        P(("wide", "narrow")),
    )
    return jax.shard_map(
        local,
        mesh=mesh,
        in_specs=placed,
        out_specs=P(None, None, ("wide", "narrow")),
        check_vma=False,
    )
```

```python
import functools

import jax
import jax.numpy as jnp
from jax import lax
from jax.experimental import pallas as pl
from jax.experimental.pallas import tpu as pltpu
from jax.sharding import PartitionSpec as P

WIN = 4
MAXIT = 12
LANES = 128
SORT_COLUMNS = 512
INT_ROWS = 256
UNIT = 8
VMEM = 64 * 1024 * 1024 - 256 * 1024


def from_behind(value, axis, steps):
    count = lax.axis_size(axis)
    pairs = [(source, (source + steps) % count) for source in range(count)]
    return lax.ppermute(value, axis, pairs)


def log2(value):
    bits = value.bit_length() - 1
    assert 1 << bits == value
    return bits


def span_of(group, groups, tiles):
    return pl.ds(pl.multiple_of(group * 8 * tiles, 8), groups * 8 * tiles)


def sort_kernel(sizes, cuts, targets, early, *refs):
    species, levels, columns, tiles, wide_count, narrow_count, pair_total = sizes
    turn_ref, wide_ref, sorted_ref = refs[-4:-1]
    sem_ref = refs[-1]
    if early:
        phys_ref, rate_ref, count_ref, tracers_ref, table_ref, pos_ref = refs[:6]
        cut_refs = refs[6:6 + targets]
        at_ref, table_smem, place_sem = refs[6 + targets:9 + targets]
    else:
        phys_ref, rate_ref, count_ref, tracers_ref, table_smem, at_ref = refs[:6]
        cut_refs = refs[6:6 + targets]
    step = pl.program_id(0)
    lanes = tiles * LANES
    real = species * levels

    def find_places():
        phys = phys_ref[...]
        target = lax.shift_right_logical(phys, log2(columns))
        slot = phys & (columns - 1)
        wide_step = lax.shift_right_logical(target, log2(narrow_count)) - lax.axis_index("wide")
        wide_step = (wide_step + 1) & (wide_count - 1)
        narrow_step = ((target & (narrow_count - 1)) - lax.axis_index("narrow")) & (narrow_count - 1)
        pair = narrow_step * WIN + wide_step
        member = pair == lax.broadcasted_iota(jnp.int32, (pair_total, columns), 0)
        counts = jnp.sum(jnp.where(member, 1.0, 0.0), axis=1, keepdims=True)
        slot_f = slot.astype(jnp.float32)
        starts = jnp.min(jnp.where(member, slot_f, float(columns)), axis=1, keepdims=True)
        groups = lax.shift_right_logical(counts.astype(jnp.int32) + 7, 3).astype(jnp.float32)
        lane = lax.broadcasted_iota(jnp.int32, (pair_total, LANES), 1)
        row = lax.broadcasted_iota(jnp.int32, (pair_total, LANES), 0)

        def across(value):
            return jnp.sum(jnp.where(lane == row, value, 0.0), axis=0, keepdims=True)

        groups_t = across(groups)
        base = jnp.sum(jnp.where(lane < row, groups_t, 0.0), axis=1, keepdims=True)
        section = row & -WIN
        inner = base - jnp.sum(jnp.where(lane < section, groups_t, 0.0), axis=1, keepdims=True)
        same = (lane & -WIN) == section
        in_step = jnp.sum(jnp.where(same, groups_t, 0.0), axis=1, keepdims=True)
        pos = slot_f + jnp.sum(jnp.where(member, base * 8.0 - starts, 0.0), axis=0, keepdims=True)
        pos_ref[...] = pos.astype(jnp.int32)
        pltpu.make_async_copy(pos_ref, at_ref, place_sem.at[0]).start()
        table_ref[...] = jnp.zeros_like(table_ref)
        for at, value in enumerate((counts, base, inner, in_step)):
            table_ref[at:at + 1, :] = across(value).astype(jnp.int32)
        pltpu.make_async_copy(table_ref, table_smem, place_sem.at[1]).start()

    if early:
        pl.when(step == 0)(find_places)
    block = tracers_ref.shape[2]
    begin = step * block
    in_group = lax.broadcasted_iota(jnp.int32, (8, LANES), 0)
    for half in range(block // LANES):
        span = slice(half * LANES, (half + 1) * LANES)
        at = pl.ds(pl.multiple_of(begin + half * LANES, LANES), LANES)
        turn_ref[lanes - 16:lanes, :] = jnp.zeros((16, LANES), jnp.float32)
        turn_ref[0:real, :] = tracers_ref[:, :, span].reshape(real, LANES)
        extra = jnp.where(in_group == 5, (phys_ref[:, at] & (columns - 1)).astype(jnp.float32), 0.0)
        extra = jnp.where(in_group == 6, rate_ref[:, at], extra)
        extra = jnp.where(in_group == 7, count_ref[:, at].astype(jnp.float32), extra)
        turn_ref[lanes - 8:lanes, :] = extra
        for tile in range(tiles):
            wide_ref[half, pl.ds(tile, LANES, stride=8), :] = turn_ref[
                tile * LANES:(tile + 1) * LANES, :
            ].T

        if early and half == 0:
            @pl.when(step == 0)
            def _():
                pltpu.make_async_copy(pos_ref, at_ref, place_sem.at[0]).wait()
                pltpu.make_async_copy(table_ref, table_smem, place_sem.at[1]).wait()

        for column in range(LANES):
            to = at_ref[0, begin + half * LANES + column] * tiles
            sorted_ref[pl.ds(to, tiles), :] = wide_ref[half, column * 8:column * 8 + tiles, :]

    @pl.when(step == pl.num_programs(0) - 1)
    def _():
        copies = []
        for index, (target, to, begin, size, valid) in enumerate(cuts):
            begin = begin(table_smem)
            valid = jnp.clip(valid(table_smem), 0, size)
            copy = pltpu.make_async_copy(
                sorted_ref.at[span_of(begin, size, tiles)],
                cut_refs[target].at[span_of(to, size, tiles)], sem_ref.at[index],
            )
            pl.when(valid > 0)(copy.start)
            copies.append((valid > 0, copy))
        wait_all(copies)


def start_arrival(refs, sem_ref, room_ref, in_step, static, tiles):
    waits = []
    quarter = static // 4
    for part in range(4):
        span = span_of(part * quarter, quarter, tiles)
        copy = pltpu.make_async_copy(refs[0].at[span], room_ref.at[span], sem_ref.at[part])
        copy.start()
        waits.append((None, copy))
    copy = pltpu.make_async_copy(
        refs[1], room_ref.at[pl.ds(static * 8 * tiles, refs[1].shape[0])], sem_ref.at[4]
    )
    pl.when(in_step > static)(copy.start)
    waits.append((in_step > static, copy))
    return waits


def wait_all(waits):
    for wanted, copy in waits:
        if wanted is None:
            copy.wait()
        else:
            pl.when(wanted)(copy.wait)


def integrate_block(sizes, room_ref, first, valid, loss_ref, coupling_ref,
                    turn_ref, y_ref, inverse_ref):
    levels, pad, tiles = sizes
    halves = INT_ROWS // LANES
    lanes = tiles * LANES
    first = pl.multiple_of(first * 8 * tiles, 8)
    for half in range(halves):
        begin = first + half * LANES * tiles
        for tile in range(tiles):
            block = room_ref[pl.ds(begin + tile, LANES, stride=tiles), :]
            turn_ref[half, tile * LANES:(tile + 1) * LANES, :] = block.T
        for level in range(levels):
            y_ref[level, :, half * LANES:(half + 1) * LANES] = turn_ref[
                half, pl.ds(level, pad, stride=levels), :
            ]
    rate = jnp.concatenate(
        [turn_ref[half, lanes - 2:lanes - 1, :] for half in range(halves)], axis=1
    )
    count = jnp.concatenate(
        [turn_ref[half, lanes - 1:lanes, :] for half in range(halves)], axis=1
    )
    lane = lax.broadcasted_iota(jnp.int32, (1, INT_ROWS), 1)
    count = jnp.where((lane < valid) & (count <= MAXIT), count, 0.0)
    step_len = rate / jnp.maximum(count, 1.0)
    inverse_ref[...] = 1.0 / (1.0 + step_len * loss_ref[...])
    last = jnp.max(count).astype(jnp.int32)

    def advance(k, carry):
        active = k.astype(jnp.float32) < count

        def one_level(level, inner):
            y = y_ref[level]
            squashed = jnp.tanh(y).astype(jnp.bfloat16)
            produced = jnp.dot(coupling_ref[...], squashed, preferred_element_type=jnp.float32)
            y_ref[level] = jnp.where(active, (y + step_len * produced) * inverse_ref[...], y)
            return inner

        for level in range(levels):
            one_level(level, 0)
        return carry

    lax.fori_loop(0, last, advance, 0)
    for half in range(halves):
        begin = first + half * LANES * tiles
        for level in range(levels):
            turn_ref[half, pl.ds(level, pad, stride=levels), :] = y_ref[
                level, :, half * LANES:(half + 1) * LANES
            ]
        for tile in range(tiles):
            block = turn_ref[half, tile * LANES:(tile + 1) * LANES, :]
            room_ref[pl.ds(begin + tile, LANES, stride=tiles), :] = block.T


def integrate_kernel(sizes, plan, table_ref, loss_ref, coupling_ref, *refs):
    loads, merges, blocks, stores, operands = plan
    tiles = sizes[2]
    sources = refs[:operands]
    results = refs[operands:operands + len(stores)]
    room_ref, turn_ref, y_ref, inverse_ref, rows_ref, sem_ref, out_sem = refs[
        operands + len(stores):
    ]
    copies = []
    for index, (source, begin, groups, to) in enumerate(loads):
        ref = sources[source]
        if begin is not None:
            ref = ref.at[span_of(begin(table_ref), groups, tiles)]
        copies.append(pltpu.make_async_copy(
            ref, room_ref.at[span_of(to, groups, tiles)], sem_ref.at[index]
        ))
    for copy in copies:
        copy.start()
    for copy in copies:
        copy.wait()
    for begin, groups, to in merges:
        to = to(table_ref)

        def move(group, carry):
            room_ref[span_of(to + group, 1, tiles), :] = room_ref[
                span_of(begin + group, 1, tiles), :
            ]
            return carry

        lax.fori_loop(0, groups(table_ref), move, 0)
    for index, (begin, rows) in enumerate(blocks):
        rows_ref[0, index] = jnp.int32(begin)
        rows_ref[1, index] = rows(table_ref)

    def one_block(index, carry):
        valid = rows_ref[1, index]

        @pl.when(valid > 0)
        def _():
            integrate_block(sizes, room_ref, rows_ref[0, index], valid, loss_ref, coupling_ref,
                            turn_ref, y_ref, inverse_ref)

        return carry

    lax.fori_loop(0, len(blocks), one_block, 0)
    copies = []
    for index, (begin, groups) in enumerate(stores):
        copies.append(pltpu.make_async_copy(
            room_ref.at[span_of(begin(table_ref), groups, tiles)], results[index],
            out_sem.at[index],
        ))
    for copy in copies:
        copy.start()
    for copy in copies:
        copy.wait()


def cut_kernel(static, tiles, piece, step, table_ref, *refs):
    pieces = refs[2:2 + WIN]
    room_ref, sem_ref, out_sem = refs[2 + WIN:]
    wait_all(start_arrival(refs[:2], sem_ref, room_ref, table_ref[3, step * WIN], static, tiles))
    copies = []
    quarter = piece // 4
    for at in range(WIN):
        begin = table_ref[2, step * WIN + at]
        for part in range(4):
            wanted = table_ref[0, step * WIN + at] > part * quarter * 8
            copy = pltpu.make_async_copy(
                room_ref.at[span_of(begin + part * quarter, quarter, tiles)],
                pieces[at].at[span_of(part * quarter, quarter, tiles)], out_sem.at[part, at],
            )
            pl.when(wanted)(copy.start)
            copies.append((wanted, copy))
    wait_all(copies)


def finish_kernel(sizes, table_ref, *refs):
    species, levels, columns, tiles, static, piece, narrow_count, begins = sizes
    pair_total = narrow_count * WIN
    whole_pieces = pair_total - WIN
    (out_ref, piece_ref, room_ref, placed_ref, whole_ref, sem_ref, room_sem,
     out_sem) = refs[-8:]
    copies = []
    quarter = piece // 4
    for pair in range(whole_pieces):
        parts = []
        for part in range(4):
            copy = pltpu.make_async_copy(
                refs[pair].at[span_of(begins[pair] + part * quarter, quarter, tiles)],
                piece_ref.at[pair, span_of(part * quarter, quarter, tiles)],
                sem_ref.at[part, pair],
            )
            wanted = table_ref[0, pair] > part * quarter * 8
            pl.when(wanted)(copy.start)
            parts.append((wanted, copy))
        copies.append(parts)
    waits = start_arrival(refs[whole_pieces:whole_pieces + 2], room_sem, room_ref,
                          table_ref[3, whole_pieces], static, tiles)
    lane = lax.broadcasted_iota(jnp.int32, (1, LANES), 1)
    in_group = lax.broadcasted_iota(jnp.int32, (8, LANES), 0)
    for pair in range(pair_total):
        if pair < whole_pieces:
            wait_all(copies[pair])
            held = piece_ref.at[pair]
            begin = 0
        else:
            if pair == whole_pieces:
                wait_all(waits)
            held = room_ref
            begin = pl.multiple_of(table_ref[2, pair] * 8 * tiles, 8)
        count = table_ref[0, pair]
        first = held[pl.ds(begin + tiles - 1, 1), :]
        start = jnp.max(jnp.where(lane == LANES - 3, first, 0.0)).astype(jnp.int32)
        start = jnp.clip(start, 0, columns - 1) * tiles
        full = lax.shift_right_logical(count, 3)

        def move(groups, part, carry):
            for row in range(0, groups * 8 * tiles, 8):
                at = part * groups * 8 * tiles + row
                placed_ref[pl.ds(start + at, 8), :] = held[pl.ds(pl.multiple_of(begin + at, 8), 8), :]
            return carry

        many = lax.shift_right_logical(full, 2)
        lax.fori_loop(0, many, functools.partial(move, 4), 0)
        lax.fori_loop(many * 4, full, functools.partial(move, 1), 0)

        @pl.when((count & 7) > 0)
        def _():
            for row in range(0, 8 * tiles, 8):
                at = full * 8 * tiles + row
                to = pl.ds(start + at, 8)
                placed_ref[to, :] = jnp.where(
                    in_group + row < (count & 7) * tiles,
                    held[pl.ds(pl.multiple_of(begin + at, 8), 8), :], placed_ref[to, :],
                )

    per_tile = LANES // levels
    for part in range(columns // LANES):
        at = slice(part * LANES, (part + 1) * LANES)
        for tile in range(tiles):
            block = placed_ref[pl.ds(part * LANES * tiles + tile, LANES, stride=tiles), :]
            block = block.T.reshape(per_tile, levels, LANES)
            keep = min(per_tile, species - tile * per_tile)
            whole_ref[tile * per_tile:tile * per_tile + keep, :, at] = block[:keep]
        pltpu.make_async_copy(whole_ref.at[:, :, at], out_ref.at[:, :, at], out_sem.at[part]).start()
    for part in range(columns // LANES):
        at = slice(part * LANES, (part + 1) * LANES)
        pltpu.make_async_copy(whole_ref.at[:, :, at], out_ref.at[:, :, at], out_sem.at[part]).wait()


def local(tracers, column_rate, loss_rate, coupling, phys_index, iter_count):
    levels, species, columns = tracers.shape
    wide_count = lax.axis_size("wide")
    narrow_count = lax.axis_size("narrow")
    pair_total = WIN * narrow_count
    room = 2 * columns // pair_total
    piece = room // 8
    pad = -(-species // 8) * 8
    while levels * pad % LANES or levels * (pad - species) < 8:
        pad += 8
    tiles = levels * pad // LANES
    mean = columns // narrow_count // 8
    full = pl.BlockSpec(memory_space=pltpu.VMEM)
    smem = pl.BlockSpec(memory_space=pltpu.SMEM)
    hbm = pl.BlockSpec(memory_space=pltpu.HBM)
    last = narrow_count - 1
    moving = [at for at in range(WIN) if at != 1]
    order = [narrow_count // 2]
    order += [step for step in range(1, last) if step not in order] + [last]
    statics = {step: mean - UNIT if step == order[0] else mean for step in order}
    most = WIN * piece

    params = pltpu.CompilerParams(vmem_limit_bytes=VMEM)

    def rows_type(groups):
        return jax.ShapeDtypeStruct((groups * 8 * tiles, LANES), jnp.float32)

    def room_type(groups):
        return pltpu.VMEM((groups * 8 * tiles, LANES), jnp.float32)

    def entry(row, step, at=0):
        return lambda table: table[row, step * WIN + at]

    def over(step):
        return lambda table: entry(1, step)(table) + statics[step]

    def groups_of(step, at):
        return lambda table: lax.shift_right_logical(table[0, step * WIN + at] + 7, 3)

    def groups_over(step):
        return lambda table: table[3, step * WIN] - statics[step]

    def pair_cuts(target, at):
        return [
            (target, part * piece + half,
             lambda table, step=step, half=half: entry(1, step, at)(table) + half, piece // 2,
             lambda table, step=step, half=half: groups_of(step, at)(table) - half)
            for part, step in enumerate((0, last)) for half in range(0, piece, piece // 2)
        ]

    def sort(cuts, target_sizes, early, known):
        known_types = [
            jax.ShapeDtypeStruct((8, LANES), jnp.int32),
            jax.ShapeDtypeStruct((1, columns), jnp.int32),
        ]
        groups = columns // 8 + pair_total + most
        return pl.pallas_call(
            functools.partial(
                sort_kernel,
                (species, levels, columns, tiles, wide_count, narrow_count, pair_total),
                cuts, len(target_sizes), early,
            ),
            grid=(columns // SORT_COLUMNS,),
            in_specs=[full, full, full,
                      pl.BlockSpec((species, levels, SORT_COLUMNS), lambda at: (0, 0, at))]
            + [smem] * len(known),
            out_specs=([full, full] if early else []) + [hbm] * len(target_sizes),
            out_shape=(known_types if early else []) + [rows_type(size) for size in target_sizes],
            scratch_shapes=([
                pltpu.SMEM((1, columns), jnp.int32), pltpu.SMEM((8, LANES), jnp.int32),
                pltpu.SemaphoreType.DMA((2,)),
            ] if early else []) + [
                pltpu.VMEM((tiles * LANES, LANES), jnp.float32),
                pltpu.VMEM((SORT_COLUMNS // LANES, LANES * 8, LANES), jnp.float32),
                room_type(groups),
                pltpu.SemaphoreType.DMA((len(cuts),)),
            ],
            compiler_params=params,
            name="sort_columns" if early else "sort_later_columns",
        )(
            phys_index.reshape(1, columns),
            column_rate.reshape(1, columns),
            iter_count.reshape(1, columns),
            tracers.transpose(1, 0, 2),
            *known,
        )

    first_static = statics[order[0]]
    cuts = [(0, 0, entry(1, order[0]), first_static, entry(3, order[0]))]
    for index, at in enumerate(moving):
        cuts += pair_cuts(1 + index, at)
    table, places, *first = sort(
        cuts, [first_static] + [2 * piece] * len(moving), True, ()
    )
    cuts = [(0, 0, over(order[0]), most - first_static, groups_over(order[0]))]
    cuts += pair_cuts(1, 1)
    for index, step in enumerate(order[1:-1]):
        rest = most - statics[step]
        cuts.append((2 + index, 0, entry(1, step), statics[step], entry(3, step)))
        cuts.append((2 + index, statics[step], over(step), rest, groups_over(step)))
    first_rest, local_rows, *raw = sort(
        cuts, [most - first_static, 2 * piece] + [most] * (len(order) - 2), False, (table, places)
    )
    raw_groups = dict(zip(order[1:-1], raw))
    units = [
        (jnp.maximum(table[3, step * WIN] - statics[step], 0) + UNIT - 1) // UNIT
        for step in order
    ]
    loss_pad = jnp.pad(loss_rate, (0, pad - species)).reshape(pad, 1)
    coupling_pad = jnp.pad(coupling, ((0, pad - species), (0, pad - species)))
    block = INT_ROWS // 8

    def integrate(table, operands, loads, merges, blocks, stores):
        groups = max([to + size for _, _, size, to in loads] + [begin + block for begin, _ in blocks])
        groups += piece
        return pl.pallas_call(
            functools.partial(
                integrate_kernel, (levels, pad, tiles),
                (loads, merges, blocks, stores, len(operands)),
            ),
            in_specs=[smem, full, full] + [hbm] * len(operands),
            out_specs=[hbm] * len(stores),
            out_shape=[rows_type(size) for _, size in stores],
            scratch_shapes=[
                room_type(groups),
                pltpu.VMEM((INT_ROWS // LANES, tiles * LANES, LANES), jnp.float32),
                pltpu.VMEM((levels, pad, INT_ROWS), jnp.float32),
                pltpu.VMEM((pad, INT_ROWS), jnp.float32),
                pltpu.SMEM((2, LANES), jnp.int32),
                pltpu.SemaphoreType.DMA((len(loads),)),
                pltpu.SemaphoreType.DMA((len(stores),)),
            ],
            compiler_params=params,
            name="integrate_columns",
        )(table, loss_pad, coupling_pad, *operands)

    def rows_of(step, at=0):
        return entry(0, step, at)

    def group_blocks(begin, step):
        return [
            (begin + part * block,
             lambda table, part=part: table[3, step * WIN] * 8 - part * INT_ROWS)
            for part in range(most // block)
        ]

    def here(begin):
        return lambda table: jnp.int32(begin)

    def step_over(step, units, rest):
        def leaf(units, rest):
            if units == 0:
                return rest
            got = from_behind(rest[:units * UNIT * 8 * tiles], "narrow", step)
            return lax.dynamic_update_slice(rest, got, (0, 0))

        leaves = [functools.partial(leaf, count) for count in range((most - statics[step]) // UNIT + 1)]
        return lax.switch(units, leaves, rest)

    pieces = {}
    outgoing = [first[0], first_rest]
    wide_now = first[1:]
    keys_now = [[(at, 0), (at, last)] for at in moving]
    static_part = from_behind(outgoing[0], "narrow", order[0])
    wide_got = [from_behind(value, "wide", at - 1) for value, at in zip(wide_now, moving)]
    table_then = table
    for phase, step in enumerate(order):
        static = statics[step]
        operands, loads, merges, blocks, stores, named = [], [], [], [], [], []
        used = 0
        if phase + 1 < len(order):
            coming = order[phase + 1]
            if coming == last:
                operands += [pieces[at, last][0] for at in moving] + [local_rows]
                for index, at in enumerate(moving):
                    loads.append((index, here(pieces[at, last][1]), piece, most + at * piece))
                loads.append((len(moving), here(piece), piece, most + piece))
                for at in range(WIN):
                    merges.append(
                        (most + at * piece, groups_of(last, at), entry(2, last, at))
                    )
                used = most + WIN * piece
            else:
                operands.append(raw_groups[coming])
                loads.append((0, None, most, 0))
                used = most
            blocks += group_blocks(0, coming)
            stores += [(here(0), statics[coming]), (here(statics[coming]), most - statics[coming])]
        extra = []
        if phase == 0:
            extra.append(((1, 0), (local_rows, 0)))
        if phase == 1:
            extra += [((at, 0), pieces[at, 0]) for at in moving]
        if phase == 2:
            extra += [((at, order[0]), pieces[at, order[0]]) for at in range(WIN)]
        used = -(-used // block) * block
        for key, value in extra:
            operands.append(value[0])
            loads.append((len(operands) - 1, here(value[1]), piece, used))
            blocks.append((used, rows_of(key[1], key[0])))
            stores.append((here(used), piece))
            named.append(key)
            used += block
        if stores:
            results = integrate(table_then, operands, loads, merges, blocks, stores)
        else:
            results = []
        rest = outgoing[1]
        if phase == 0:
            static_part, results, rest, units = lax.optimization_barrier(
                (static_part, results, rest, units)
            )
        else:
            static_part, results, rest = lax.optimization_barrier((static_part, results, rest))
        done = {key: (value, 0) for key, value in zip(named, results[len(results) - len(named):])}
        outgoing = results[:len(results) - len(named)]
        arrived = [static_part, step_over(step, units[phase], rest)]
        if step != last:
            arrived, outgoing = lax.optimization_barrier((arrived, outgoing))
            static_part = from_behind(outgoing[0], "narrow", order[phase + 1])
        if step != last:
            cut = pl.pallas_call(
                functools.partial(cut_kernel, static, tiles, piece, step),
                in_specs=[smem] + [hbm] * len(arrived),
                out_specs=[hbm] * WIN,
                out_shape=[rows_type(piece)] * WIN,
                scratch_shapes=[
                    room_type(most + piece),
                    pltpu.SemaphoreType.DMA((5,)),
                    pltpu.SemaphoreType.DMA((4, WIN)),
                ],
                compiler_params=params,
                name="cut_pieces",
            )(table, *arrived)
            cut, wide_got, table_then = lax.optimization_barrier((cut, wide_got, table))
        for keys, value in zip(keys_now, wide_got):
            pieces.update({key: (value, part * piece) for part, key in enumerate(keys)})
        pieces.update(done)
        if step != last:
            pieces[1, step] = (cut[1], 0)
            keys_now = [[(at, step)] for at in moving]
            wide_got = [from_behind(cut[at], "wide", at - 1) for at in moving]

    held = [pieces[at, step] for step in range(last) for at in range(WIN)]
    buffers = [value for value, _ in held] + arrived
    updated = pl.pallas_call(
        functools.partial(
            finish_kernel,
            (species, levels, columns, tiles, static, piece, narrow_count,
             [begin for _, begin in held]),
        ),
        in_specs=[smem] + [hbm] * len(buffers),
        out_specs=hbm,
        out_shape=jax.ShapeDtypeStruct((species, levels, columns), jnp.float32),
        scratch_shapes=[
            pltpu.VMEM((pair_total - WIN, piece * 8 * tiles, LANES), jnp.float32),
            room_type(most + piece),
            room_type(columns // 8 + 1),
            pltpu.VMEM((species, levels, columns), jnp.float32),
            pltpu.SemaphoreType.DMA((4, pair_total)),
            pltpu.SemaphoreType.DMA((5,)),
            pltpu.SemaphoreType.DMA((columns // LANES,)),
        ],
        compiler_params=params,
        name="place_columns",
    )(table, *buffers)
    return updated.transpose(1, 0, 2)


def solution(mesh):
    placed = (
        P(None, None, ("wide", "narrow")),
        P(("wide", "narrow")),
        P(),
        P(),
        P(("wide", "narrow")),
        P(("wide", "narrow")),
    )
    return jax.shard_map(
        local,
        mesh=mesh,
        in_specs=placed,
        out_specs=P(None, None, ("wide", "narrow")),
        check_vma=False,
    )
```

```python
import functools

import jax
import jax.numpy as jnp
from jax import lax
from jax.experimental import pallas as pl
from jax.experimental.pallas import tpu as pltpu
from jax.sharding import PartitionSpec as P

WIN = 4
MAXIT = 12
LANES = 128
SORT_COLUMNS = 512
INT_ROWS = 256
UNIT = 8
VMEM = 64 * 1024 * 1024 - 256 * 1024


def from_behind(value, axis, steps):
    count = lax.axis_size(axis)
    pairs = [(source, (source + steps) % count) for source in range(count)]
    return lax.ppermute(value, axis, pairs)


def log2(value):
    bits = value.bit_length() - 1
    assert 1 << bits == value
    return bits


def span_of(group, groups, tiles):
    return pl.ds(pl.multiple_of(group * 8 * tiles, 8), groups * 8 * tiles)


def sort_kernel(sizes, cuts, targets, early, *refs):
    species, levels, columns, tiles, wide_count, narrow_count, pair_total = sizes
    turn_ref, wide_ref, sorted_ref = refs[-4:-1]
    sem_ref = refs[-1]
    if early:
        phys_ref, rate_ref, count_ref, tracers_ref, table_ref, pos_ref = refs[:6]
        cut_refs = refs[6:6 + targets]
        at_ref, table_smem, place_sem = refs[6 + targets:9 + targets]
    else:
        phys_ref, rate_ref, count_ref, tracers_ref, table_smem, at_ref = refs[:6]
        cut_refs = refs[6:6 + targets]
    step = pl.program_id(0)
    lanes = tiles * LANES
    real = species * levels

    def find_places():
        phys = phys_ref[...]
        target = lax.shift_right_logical(phys, log2(columns))
        slot = phys & (columns - 1)
        wide_step = lax.shift_right_logical(target, log2(narrow_count)) - lax.axis_index("wide")
        wide_step = (wide_step + 1) & (wide_count - 1)
        narrow_step = ((target & (narrow_count - 1)) - lax.axis_index("narrow")) & (narrow_count - 1)
        pair = narrow_step * WIN + wide_step
        member = pair == lax.broadcasted_iota(jnp.int32, (pair_total, columns), 0)
        counts = jnp.sum(jnp.where(member, 1.0, 0.0), axis=1, keepdims=True)
        slot_f = slot.astype(jnp.float32)
        starts = jnp.min(jnp.where(member, slot_f, float(columns)), axis=1, keepdims=True)
        groups = lax.shift_right_logical(counts.astype(jnp.int32) + 7, 3).astype(jnp.float32)
        lane = lax.broadcasted_iota(jnp.int32, (pair_total, LANES), 1)
        row = lax.broadcasted_iota(jnp.int32, (pair_total, LANES), 0)

        def across(value):
            return jnp.sum(jnp.where(lane == row, value, 0.0), axis=0, keepdims=True)

        groups_t = across(groups)
        base = jnp.sum(jnp.where(lane < row, groups_t, 0.0), axis=1, keepdims=True)
        section = row & -WIN
        inner = base - jnp.sum(jnp.where(lane < section, groups_t, 0.0), axis=1, keepdims=True)
        same = (lane & -WIN) == section
        in_step = jnp.sum(jnp.where(same, groups_t, 0.0), axis=1, keepdims=True)
        pos = slot_f + jnp.sum(jnp.where(member, base * 8.0 - starts, 0.0), axis=0, keepdims=True)
        pos_ref[...] = pos.astype(jnp.int32)
        pltpu.make_async_copy(pos_ref, at_ref, place_sem.at[0]).start()
        table_ref[...] = jnp.zeros_like(table_ref)
        for at, value in enumerate((counts, base, inner, in_step)):
            table_ref[at:at + 1, :] = across(value).astype(jnp.int32)
        pltpu.make_async_copy(table_ref, table_smem, place_sem.at[1]).start()

    if early:
        pl.when(step == 0)(find_places)
    block = tracers_ref.shape[2]
    begin = step * block
    in_group = lax.broadcasted_iota(jnp.int32, (8, LANES), 0)
    for half in range(block // LANES):
        span = slice(half * LANES, (half + 1) * LANES)
        at = pl.ds(pl.multiple_of(begin + half * LANES, LANES), LANES)
        turn_ref[lanes - 16:lanes, :] = jnp.zeros((16, LANES), jnp.float32)
        turn_ref[0:real, :] = tracers_ref[:, :, span].reshape(real, LANES)
        extra = jnp.where(in_group == 5, (phys_ref[:, at] & (columns - 1)).astype(jnp.float32), 0.0)
        extra = jnp.where(in_group == 6, rate_ref[:, at], extra)
        extra = jnp.where(in_group == 7, count_ref[:, at].astype(jnp.float32), extra)
        turn_ref[lanes - 8:lanes, :] = extra
        for tile in range(tiles):
            wide_ref[half, pl.ds(tile, LANES, stride=8), :] = turn_ref[
                tile * LANES:(tile + 1) * LANES, :
            ].T

        if early and half == 0:
            @pl.when(step == 0)
            def _():
                pltpu.make_async_copy(pos_ref, at_ref, place_sem.at[0]).wait()
                pltpu.make_async_copy(table_ref, table_smem, place_sem.at[1]).wait()

        for column in range(LANES):
            to = at_ref[0, begin + half * LANES + column] * tiles
            sorted_ref[pl.ds(to, tiles), :] = wide_ref[half, column * 8:column * 8 + tiles, :]

    @pl.when(step == pl.num_programs(0) - 1)
    def _():
        copies = []
        for index, (target, to, begin, size, valid) in enumerate(cuts):
            begin = begin(table_smem)
            valid = jnp.clip(valid(table_smem), 0, size)
            copy = pltpu.make_async_copy(
                sorted_ref.at[span_of(begin, size, tiles)],
                cut_refs[target].at[span_of(to, size, tiles)], sem_ref.at[index],
            )
            pl.when(valid > 0)(copy.start)
            copies.append((valid > 0, copy))
        wait_all(copies)


def start_arrival(refs, sem_ref, room_ref, in_step, static, tiles):
    waits = []
    quarter = static // 4
    for part in range(4):
        span = span_of(part * quarter, quarter, tiles)
        copy = pltpu.make_async_copy(refs[0].at[span], room_ref.at[span], sem_ref.at[part])
        copy.start()
        waits.append((None, copy))
    copy = pltpu.make_async_copy(
        refs[1], room_ref.at[pl.ds(static * 8 * tiles, refs[1].shape[0])], sem_ref.at[4]
    )
    pl.when(in_step > static)(copy.start)
    waits.append((in_step > static, copy))
    return waits


def wait_all(waits):
    for wanted, copy in waits:
        if wanted is None:
            copy.wait()
        else:
            pl.when(wanted)(copy.wait)


def integrate_block(sizes, room_ref, first, valid, loss_ref, coupling_ref,
                    turn_ref, y_ref, inverse_ref):
    levels, pad, tiles = sizes
    halves = INT_ROWS // LANES
    lanes = tiles * LANES
    first = pl.multiple_of(first * 8 * tiles, 8)
    for half in range(halves):
        begin = first + half * LANES * tiles
        for tile in range(tiles):
            block = room_ref[pl.ds(begin + tile, LANES, stride=tiles), :]
            turn_ref[half, tile * LANES:(tile + 1) * LANES, :] = block.T
        for level in range(levels):
            y_ref[level, :, half * LANES:(half + 1) * LANES] = turn_ref[
                half, pl.ds(level, pad, stride=levels), :
            ]
    rate = jnp.concatenate(
        [turn_ref[half, lanes - 2:lanes - 1, :] for half in range(halves)], axis=1
    )
    count = jnp.concatenate(
        [turn_ref[half, lanes - 1:lanes, :] for half in range(halves)], axis=1
    )
    lane = lax.broadcasted_iota(jnp.int32, (1, INT_ROWS), 1)
    count = jnp.where((lane < valid) & (count <= MAXIT), count, 0.0)
    step_len = rate / jnp.maximum(count, 1.0)
    inverse_ref[...] = 1.0 / (1.0 + step_len * loss_ref[...])
    last = jnp.max(count).astype(jnp.int32)

    def advance(k, carry):
        active = k.astype(jnp.float32) < count

        def one_level(level, inner):
            y = y_ref[level]
            squashed = jnp.tanh(y).astype(jnp.bfloat16)
            produced = jnp.dot(coupling_ref[...], squashed, preferred_element_type=jnp.float32)
            y_ref[level] = jnp.where(active, (y + step_len * produced) * inverse_ref[...], y)
            return inner

        for level in range(levels):
            one_level(level, 0)
        return carry

    lax.fori_loop(0, last, advance, 0)
    for half in range(halves):
        begin = first + half * LANES * tiles
        for level in range(levels):
            turn_ref[half, pl.ds(level, pad, stride=levels), :] = y_ref[
                level, :, half * LANES:(half + 1) * LANES
            ]
        for tile in range(tiles):
            block = turn_ref[half, tile * LANES:(tile + 1) * LANES, :]
            room_ref[pl.ds(begin + tile, LANES, stride=tiles), :] = block.T


def integrate_kernel(sizes, plan, table_ref, loss_ref, coupling_ref, *refs):
    loads, merges, blocks, stores, operands = plan
    tiles = sizes[2]
    sources = refs[:operands]
    results = refs[operands:operands + len(stores)]
    room_ref, turn_ref, y_ref, inverse_ref, rows_ref, sem_ref, out_sem = refs[
        operands + len(stores):
    ]
    copies = []
    for index, (source, begin, groups, to) in enumerate(loads):
        ref = sources[source]
        if begin is not None:
            ref = ref.at[span_of(begin(table_ref), groups, tiles)]
        copies.append(pltpu.make_async_copy(
            ref, room_ref.at[span_of(to, groups, tiles)], sem_ref.at[index]
        ))
    for copy in copies:
        copy.start()
    for copy in copies:
        copy.wait()
    for begin, groups, to in merges:
        to = to(table_ref)

        def move(group, carry):
            room_ref[span_of(to + group, 1, tiles), :] = room_ref[
                span_of(begin + group, 1, tiles), :
            ]
            return carry

        lax.fori_loop(0, groups(table_ref), move, 0)
    for index, (begin, rows) in enumerate(blocks):
        rows_ref[0, index] = jnp.int32(begin)
        rows_ref[1, index] = rows(table_ref)

    def one_block(index, carry):
        valid = rows_ref[1, index]

        @pl.when(valid > 0)
        def _():
            integrate_block(sizes, room_ref, rows_ref[0, index], valid, loss_ref, coupling_ref,
                            turn_ref, y_ref, inverse_ref)

        return carry

    lax.fori_loop(0, len(blocks), one_block, 0)
    copies = []
    for index, (begin, groups) in enumerate(stores):
        copies.append(pltpu.make_async_copy(
            room_ref.at[span_of(begin(table_ref), groups, tiles)], results[index],
            out_sem.at[index],
        ))
    for copy in copies:
        copy.start()
    for copy in copies:
        copy.wait()


def cut_kernel(static, tiles, piece, step, table_ref, *refs):
    pieces = refs[2:2 + WIN]
    room_ref, sem_ref, out_sem = refs[2 + WIN:]
    wait_all(start_arrival(refs[:2], sem_ref, room_ref, table_ref[3, step * WIN], static, tiles))
    copies = []
    quarter = piece // 4
    for at in range(WIN):
        begin = table_ref[2, step * WIN + at]
        for part in range(4):
            wanted = table_ref[0, step * WIN + at] > part * quarter * 8
            copy = pltpu.make_async_copy(
                room_ref.at[span_of(begin + part * quarter, quarter, tiles)],
                pieces[at].at[span_of(part * quarter, quarter, tiles)], out_sem.at[part, at],
            )
            pl.when(wanted)(copy.start)
            copies.append((wanted, copy))
    wait_all(copies)


def finish_kernel(sizes, table_ref, *refs):
    species, levels, columns, tiles, static, piece, narrow_count, begins = sizes
    pair_total = narrow_count * WIN
    whole_pieces = pair_total - WIN
    (out_ref, piece_ref, room_ref, placed_ref, whole_ref, sem_ref, room_sem,
     out_sem) = refs[-8:]
    copies = []
    quarter = piece // 4
    for pair in range(whole_pieces):
        parts = []
        for part in range(4):
            copy = pltpu.make_async_copy(
                refs[pair].at[span_of(begins[pair] + part * quarter, quarter, tiles)],
                piece_ref.at[pair, span_of(part * quarter, quarter, tiles)],
                sem_ref.at[part, pair],
            )
            wanted = table_ref[0, pair] > part * quarter * 8
            pl.when(wanted)(copy.start)
            parts.append((wanted, copy))
        copies.append(parts)
    waits = start_arrival(refs[whole_pieces:whole_pieces + 2], room_sem, room_ref,
                          table_ref[3, whole_pieces], static, tiles)
    lane = lax.broadcasted_iota(jnp.int32, (1, LANES), 1)
    in_group = lax.broadcasted_iota(jnp.int32, (8, LANES), 0)
    for pair in range(pair_total):
        if pair < whole_pieces:
            wait_all(copies[pair])
            held = piece_ref.at[pair]
            begin = 0
        else:
            if pair == whole_pieces:
                wait_all(waits)
            held = room_ref
            begin = pl.multiple_of(table_ref[2, pair] * 8 * tiles, 8)
        count = table_ref[0, pair]
        first = held[pl.ds(begin + tiles - 1, 1), :]
        start = jnp.max(jnp.where(lane == LANES - 3, first, 0.0)).astype(jnp.int32)
        start = jnp.clip(start, 0, columns - 1) * tiles
        full = lax.shift_right_logical(count, 3)

        def move(groups, part, carry):
            for row in range(0, groups * 8 * tiles, 8):
                at = part * groups * 8 * tiles + row
                placed_ref[pl.ds(start + at, 8), :] = held[pl.ds(pl.multiple_of(begin + at, 8), 8), :]
            return carry

        many = lax.shift_right_logical(full, 2)
        lax.fori_loop(0, many, functools.partial(move, 4), 0)
        lax.fori_loop(many * 4, full, functools.partial(move, 1), 0)

        @pl.when((count & 7) > 0)
        def _():
            for row in range(0, 8 * tiles, 8):
                at = full * 8 * tiles + row
                to = pl.ds(start + at, 8)
                placed_ref[to, :] = jnp.where(
                    in_group + row < (count & 7) * tiles,
                    held[pl.ds(pl.multiple_of(begin + at, 8), 8), :], placed_ref[to, :],
                )

    per_tile = LANES // levels
    for part in range(columns // LANES):
        at = slice(part * LANES, (part + 1) * LANES)
        for tile in range(tiles):
            block = placed_ref[pl.ds(part * LANES * tiles + tile, LANES, stride=tiles), :]
            block = block.T.reshape(per_tile, levels, LANES)
            keep = min(per_tile, species - tile * per_tile)
            whole_ref[tile * per_tile:tile * per_tile + keep, :, at] = block[:keep]
        pltpu.make_async_copy(whole_ref.at[:, :, at], out_ref.at[:, :, at], out_sem.at[part]).start()
    for part in range(columns // LANES):
        at = slice(part * LANES, (part + 1) * LANES)
        pltpu.make_async_copy(whole_ref.at[:, :, at], out_ref.at[:, :, at], out_sem.at[part]).wait()


def local(tracers, column_rate, loss_rate, coupling, phys_index, iter_count):
    levels, species, columns = tracers.shape
    wide_count = lax.axis_size("wide")
    narrow_count = lax.axis_size("narrow")
    pair_total = WIN * narrow_count
    room = 2 * columns // pair_total
    piece = room // 8
    pad = -(-species // 8) * 8
    while levels * pad % LANES or levels * (pad - species) < 8:
        pad += 8
    tiles = levels * pad // LANES
    mean = columns // narrow_count // 8
    full = pl.BlockSpec(memory_space=pltpu.VMEM)
    smem = pl.BlockSpec(memory_space=pltpu.SMEM)
    hbm = pl.BlockSpec(memory_space=pltpu.HBM)
    last = narrow_count - 1
    moving = [at for at in range(WIN) if at != 1]
    order = [narrow_count // 2]
    order += [step for step in range(1, last) if step not in order] + [last]
    statics = {step: mean - UNIT if step == order[0] else mean for step in order}
    most = WIN * piece

    params = pltpu.CompilerParams(vmem_limit_bytes=VMEM)

    def rows_type(groups):
        return jax.ShapeDtypeStruct((groups * 8 * tiles, LANES), jnp.float32)

    def room_type(groups):
        return pltpu.VMEM((groups * 8 * tiles, LANES), jnp.float32)

    def entry(row, step, at=0):
        return lambda table: table[row, step * WIN + at]

    def over(step):
        return lambda table: entry(1, step)(table) + statics[step]

    def groups_of(step, at):
        return lambda table: lax.shift_right_logical(table[0, step * WIN + at] + 7, 3)

    def groups_over(step):
        return lambda table: table[3, step * WIN] - statics[step]

    def pair_cuts(target, at):
        return [
            (target, part * piece + half,
             lambda table, step=step, half=half: entry(1, step, at)(table) + half, piece // 2,
             lambda table, step=step, half=half: groups_of(step, at)(table) - half)
            for part, step in enumerate((0, last)) for half in range(0, piece, piece // 2)
        ]

    def sort(cuts, target_sizes, early, known):
        known_types = [
            jax.ShapeDtypeStruct((8, LANES), jnp.int32),
            jax.ShapeDtypeStruct((1, columns), jnp.int32),
        ]
        groups = columns // 8 + pair_total + most
        return pl.pallas_call(
            functools.partial(
                sort_kernel,
                (species, levels, columns, tiles, wide_count, narrow_count, pair_total),
                cuts, len(target_sizes), early,
            ),
            grid=(columns // SORT_COLUMNS,),
            in_specs=[full, full, full,
                      pl.BlockSpec((species, levels, SORT_COLUMNS), lambda at: (0, 0, at))]
            + [smem] * len(known),
            out_specs=([full, full] if early else []) + [hbm] * len(target_sizes),
            out_shape=(known_types if early else []) + [rows_type(size) for size in target_sizes],
            scratch_shapes=([
                pltpu.SMEM((1, columns), jnp.int32), pltpu.SMEM((8, LANES), jnp.int32),
                pltpu.SemaphoreType.DMA((2,)),
            ] if early else []) + [
                pltpu.VMEM((tiles * LANES, LANES), jnp.float32),
                pltpu.VMEM((SORT_COLUMNS // LANES, LANES * 8, LANES), jnp.float32),
                room_type(groups),
                pltpu.SemaphoreType.DMA((len(cuts),)),
            ],
            compiler_params=params,
            name="sort_columns" if early else "sort_later_columns",
        )(
            phys_index.reshape(1, columns),
            column_rate.reshape(1, columns),
            iter_count.reshape(1, columns),
            tracers.transpose(1, 0, 2),
            *known,
        )

    first_static = statics[order[0]]
    cuts = [(0, 0, entry(1, order[0]), first_static, entry(3, order[0]))]
    for index, at in enumerate(moving):
        cuts += pair_cuts(1 + index, at)
    table, places, *first = sort(
        cuts, [first_static] + [2 * piece] * len(moving), True, ()
    )
    cuts = [(0, 0, over(order[0]), most - first_static, groups_over(order[0]))]
    cuts += pair_cuts(1, 1)
    for index, step in enumerate(order[1:-1]):
        rest = most - statics[step]
        cuts.append((2 + index, 0, entry(1, step), statics[step], entry(3, step)))
        cuts.append((2 + index, statics[step], over(step), rest, groups_over(step)))
    first_rest, local_rows, *raw = sort(
        cuts, [most - first_static, 2 * piece] + [most] * (len(order) - 2), False, (table, places)
    )
    raw_groups = dict(zip(order[1:-1], raw))
    units = [
        (jnp.maximum(table[3, step * WIN] - statics[step], 0) + UNIT - 1) // UNIT
        for step in order
    ]
    loss_pad = jnp.pad(loss_rate, (0, pad - species)).reshape(pad, 1)
    coupling_pad = jnp.pad(coupling, ((0, pad - species), (0, pad - species)))
    block = INT_ROWS // 8

    def integrate(table, operands, loads, merges, blocks, stores):
        groups = max([to + size for _, _, size, to in loads] + [begin + block for begin, _ in blocks])
        groups += piece
        return pl.pallas_call(
            functools.partial(
                integrate_kernel, (levels, pad, tiles),
                (loads, merges, blocks, stores, len(operands)),
            ),
            in_specs=[smem, full, full] + [hbm] * len(operands),
            out_specs=[hbm] * len(stores),
            out_shape=[rows_type(size) for _, size in stores],
            scratch_shapes=[
                room_type(groups),
                pltpu.VMEM((INT_ROWS // LANES, tiles * LANES, LANES), jnp.float32),
                pltpu.VMEM((levels, pad, INT_ROWS), jnp.float32),
                pltpu.VMEM((pad, INT_ROWS), jnp.float32),
                pltpu.SMEM((2, LANES), jnp.int32),
                pltpu.SemaphoreType.DMA((len(loads),)),
                pltpu.SemaphoreType.DMA((len(stores),)),
            ],
            compiler_params=params,
            name="integrate_columns",
        )(table, loss_pad, coupling_pad, *operands)

    def rows_of(step, at=0):
        return entry(0, step, at)

    def group_blocks(begin, step):
        return [
            (begin + part * block,
             lambda table, part=part: table[3, step * WIN] * 8 - part * INT_ROWS)
            for part in range(most // block)
        ]

    def here(begin):
        return lambda table: jnp.int32(begin)

    def step_over(step, units, rest):
        def leaf(units, rest):
            if units == 0:
                return rest
            got = from_behind(rest[:units * UNIT * 8 * tiles], "narrow", step)
            return lax.dynamic_update_slice(rest, got, (0, 0))

        leaves = [functools.partial(leaf, count) for count in range((most - statics[step]) // UNIT + 1)]
        return lax.switch(units, leaves, rest)

    pieces = {}
    outgoing = [first[0], first_rest]
    wide_now = first[1:]
    keys_now = [[(at, 0), (at, last)] for at in moving]
    static_part = from_behind(outgoing[0], "narrow", order[0])
    wide_got = [from_behind(value, "wide", at - 1) for value, at in zip(wide_now, moving)]
    table_then = table
    for phase, step in enumerate(order):
        static = statics[step]
        operands, loads, merges, blocks, stores, named = [], [], [], [], [], []
        used = 0
        if phase + 1 < len(order):
            coming = order[phase + 1]
            if coming == last:
                operands += [pieces[at, last][0] for at in moving] + [local_rows]
                for index, at in enumerate(moving):
                    loads.append((index, here(pieces[at, last][1]), piece, most + at * piece))
                loads.append((len(moving), here(piece), piece, most + piece))
                for at in range(WIN):
                    merges.append(
                        (most + at * piece, groups_of(last, at), entry(2, last, at))
                    )
                used = most + WIN * piece
            else:
                operands.append(raw_groups[coming])
                loads.append((0, None, most, 0))
                used = most
            blocks += group_blocks(0, coming)
            stores += [(here(0), statics[coming]), (here(statics[coming]), most - statics[coming])]
        extra = []
        if phase == 0:
            extra.append(((1, 0), (local_rows, 0)))
        if phase == 1:
            extra += [((at, 0), pieces[at, 0]) for at in moving[1:]]
        if phase == 2:
            extra += [((at, order[0]), pieces[at, order[0]]) for at in range(WIN)]
            extra.append(((moving[0], 0), pieces[moving[0], 0]))
        used = -(-used // block) * block
        for key, value in extra:
            operands.append(value[0])
            loads.append((len(operands) - 1, here(value[1]), piece, used))
            blocks.append((used, rows_of(key[1], key[0])))
            stores.append((here(used), piece))
            named.append(key)
            used += block
        if stores:
            results = integrate(table_then, operands, loads, merges, blocks, stores)
        else:
            results = []
        rest = outgoing[1]
        if phase == 0:
            static_part, results, rest, units = lax.optimization_barrier(
                (static_part, results, rest, units)
            )
        else:
            static_part, results, rest = lax.optimization_barrier((static_part, results, rest))
        done = {key: (value, 0) for key, value in zip(named, results[len(results) - len(named):])}
        outgoing = results[:len(results) - len(named)]
        arrived = [static_part, step_over(step, units[phase], rest)]
        if step != last:
            arrived, outgoing = lax.optimization_barrier((arrived, outgoing))
            static_part = from_behind(outgoing[0], "narrow", order[phase + 1])
        if step != last:
            cut = pl.pallas_call(
                functools.partial(cut_kernel, static, tiles, piece, step),
                in_specs=[smem] + [hbm] * len(arrived),
                out_specs=[hbm] * WIN,
                out_shape=[rows_type(piece)] * WIN,
                scratch_shapes=[
                    room_type(most + piece),
                    pltpu.SemaphoreType.DMA((5,)),
                    pltpu.SemaphoreType.DMA((4, WIN)),
                ],
                compiler_params=params,
                name="cut_pieces",
            )(table, *arrived)
            cut, wide_got, table_then = lax.optimization_barrier((cut, wide_got, table))
        for keys, value in zip(keys_now, wide_got):
            pieces.update({key: (value, part * piece) for part, key in enumerate(keys)})
        pieces.update(done)
        if step != last:
            pieces[1, step] = (cut[1], 0)
            keys_now = [[(at, step)] for at in moving]
            wide_got = [from_behind(cut[at], "wide", at - 1) for at in moving]

    held = [pieces[at, step] for step in range(last) for at in range(WIN)]
    buffers = [value for value, _ in held] + arrived
    updated = pl.pallas_call(
        functools.partial(
            finish_kernel,
            (species, levels, columns, tiles, static, piece, narrow_count,
             [begin for _, begin in held]),
        ),
        in_specs=[smem] + [hbm] * len(buffers),
        out_specs=hbm,
        out_shape=jax.ShapeDtypeStruct((species, levels, columns), jnp.float32),
        scratch_shapes=[
            pltpu.VMEM((pair_total - WIN, piece * 8 * tiles, LANES), jnp.float32),
            room_type(most + piece),
            room_type(columns // 8 + 1),
            pltpu.VMEM((species, levels, columns), jnp.float32),
            pltpu.SemaphoreType.DMA((4, pair_total)),
            pltpu.SemaphoreType.DMA((5,)),
            pltpu.SemaphoreType.DMA((columns // LANES,)),
        ],
        compiler_params=params,
        name="place_columns",
    )(table, *buffers)
    return updated.transpose(1, 0, 2)


def solution(mesh):
    placed = (
        P(None, None, ("wide", "narrow")),
        P(("wide", "narrow")),
        P(),
        P(),
        P(("wide", "narrow")),
        P(("wide", "narrow")),
    )
    return jax.shard_map(
        local,
        mesh=mesh,
        in_specs=placed,
        out_specs=P(None, None, ("wide", "narrow")),
        check_vma=False,
    )
```

```python
import functools

import jax
import jax.numpy as jnp
from jax import lax
from jax.experimental import pallas as pl
from jax.experimental.pallas import tpu as pltpu
from jax.sharding import PartitionSpec as P

WIN = 4
MAXIT = 12
LANES = 128
SORT_COLUMNS = 512
INT_ROWS = 256
UNIT = 8
VMEM = 64 * 1024 * 1024 - 256 * 1024


def from_behind(value, axis, steps):
    count = lax.axis_size(axis)
    pairs = [(source, (source + steps) % count) for source in range(count)]
    return lax.ppermute(value, axis, pairs)


def log2(value):
    bits = value.bit_length() - 1
    assert 1 << bits == value
    return bits


def span_of(group, groups, tiles):
    return pl.ds(pl.multiple_of(group * 8 * tiles, 8), groups * 8 * tiles)


def sort_kernel(sizes, cuts, targets, early, *refs):
    species, levels, columns, tiles, wide_count, narrow_count, pair_total = sizes
    turn_ref, wide_ref, sorted_ref = refs[-4:-1]
    sem_ref = refs[-1]
    if early:
        phys_ref, rate_ref, count_ref, tracers_ref, table_ref, pos_ref = refs[:6]
        cut_refs = refs[6:6 + targets]
        at_ref, table_smem, place_sem = refs[6 + targets:9 + targets]
    else:
        phys_ref, rate_ref, count_ref, tracers_ref, table_smem, at_ref = refs[:6]
        cut_refs = refs[6:6 + targets]
    step = pl.program_id(0)
    lanes = tiles * LANES
    real = species * levels

    def find_places():
        phys = phys_ref[...]
        target = lax.shift_right_logical(phys, log2(columns))
        slot = phys & (columns - 1)
        wide_step = lax.shift_right_logical(target, log2(narrow_count)) - lax.axis_index("wide")
        wide_step = (wide_step + 1) & (wide_count - 1)
        narrow_step = ((target & (narrow_count - 1)) - lax.axis_index("narrow")) & (narrow_count - 1)
        pair = narrow_step * WIN + wide_step
        member = pair == lax.broadcasted_iota(jnp.int32, (pair_total, columns), 0)
        counts = jnp.sum(jnp.where(member, 1.0, 0.0), axis=1, keepdims=True)
        slot_f = slot.astype(jnp.float32)
        starts = jnp.min(jnp.where(member, slot_f, float(columns)), axis=1, keepdims=True)
        groups = lax.shift_right_logical(counts.astype(jnp.int32) + 7, 3).astype(jnp.float32)
        lane = lax.broadcasted_iota(jnp.int32, (pair_total, LANES), 1)
        row = lax.broadcasted_iota(jnp.int32, (pair_total, LANES), 0)

        def across(value):
            return jnp.sum(jnp.where(lane == row, value, 0.0), axis=0, keepdims=True)

        groups_t = across(groups)
        base = jnp.sum(jnp.where(lane < row, groups_t, 0.0), axis=1, keepdims=True)
        section = row & -WIN
        inner = base - jnp.sum(jnp.where(lane < section, groups_t, 0.0), axis=1, keepdims=True)
        same = (lane & -WIN) == section
        in_step = jnp.sum(jnp.where(same, groups_t, 0.0), axis=1, keepdims=True)
        pos = slot_f + jnp.sum(jnp.where(member, base * 8.0 - starts, 0.0), axis=0, keepdims=True)
        pos_ref[...] = pos.astype(jnp.int32)
        pltpu.make_async_copy(pos_ref, at_ref, place_sem.at[0]).start()
        table_ref[...] = jnp.zeros_like(table_ref)
        for at, value in enumerate((counts, base, inner, in_step)):
            table_ref[at:at + 1, :] = across(value).astype(jnp.int32)
        pltpu.make_async_copy(table_ref, table_smem, place_sem.at[1]).start()

    if early:
        pl.when(step == 0)(find_places)
    block = tracers_ref.shape[2]
    begin = step * block
    in_group = lax.broadcasted_iota(jnp.int32, (8, LANES), 0)
    for half in range(block // LANES):
        span = slice(half * LANES, (half + 1) * LANES)
        at = pl.ds(pl.multiple_of(begin + half * LANES, LANES), LANES)
        turn_ref[lanes - 16:lanes, :] = jnp.zeros((16, LANES), jnp.float32)
        turn_ref[0:real, :] = tracers_ref[:, :, span].reshape(real, LANES)
        extra = jnp.where(in_group == 5, (phys_ref[:, at] & (columns - 1)).astype(jnp.float32), 0.0)
        extra = jnp.where(in_group == 6, rate_ref[:, at], extra)
        extra = jnp.where(in_group == 7, count_ref[:, at].astype(jnp.float32), extra)
        turn_ref[lanes - 8:lanes, :] = extra
        for tile in range(tiles):
            wide_ref[half, pl.ds(tile, LANES, stride=8), :] = turn_ref[
                tile * LANES:(tile + 1) * LANES, :
            ].T

        if early and half == 0:
            @pl.when(step == 0)
            def _():
                pltpu.make_async_copy(pos_ref, at_ref, place_sem.at[0]).wait()
                pltpu.make_async_copy(table_ref, table_smem, place_sem.at[1]).wait()

        for column in range(LANES):
            to = at_ref[0, begin + half * LANES + column] * tiles
            sorted_ref[pl.ds(to, tiles), :] = wide_ref[half, column * 8:column * 8 + tiles, :]

    @pl.when(step == pl.num_programs(0) - 1)
    def _():
        copies = []
        for index, (target, to, begin, size, valid) in enumerate(cuts):
            begin = begin(table_smem)
            valid = jnp.clip(valid(table_smem), 0, size)
            copy = pltpu.make_async_copy(
                sorted_ref.at[span_of(begin, size, tiles)],
                cut_refs[target].at[span_of(to, size, tiles)], sem_ref.at[index],
            )
            pl.when(valid > 0)(copy.start)
            copies.append((valid > 0, copy))
        wait_all(copies)


def start_arrival(refs, sem_ref, room_ref, in_step, static, tiles):
    waits = []
    quarter = static // 4
    for part in range(4):
        span = span_of(part * quarter, quarter, tiles)
        copy = pltpu.make_async_copy(refs[0].at[span], room_ref.at[span], sem_ref.at[part])
        copy.start()
        waits.append((None, copy))
    copy = pltpu.make_async_copy(
        refs[1], room_ref.at[pl.ds(static * 8 * tiles, refs[1].shape[0])], sem_ref.at[4]
    )
    pl.when(in_step > static)(copy.start)
    waits.append((in_step > static, copy))
    return waits


def wait_all(waits):
    for wanted, copy in waits:
        if wanted is None:
            copy.wait()
        else:
            pl.when(wanted)(copy.wait)


def integrate_block(sizes, room_ref, first, valid, loss_ref, coupling_ref,
                    turn_ref, y_ref, inverse_ref):
    levels, pad, tiles = sizes
    halves = INT_ROWS // LANES
    lanes = tiles * LANES
    first = pl.multiple_of(first * 8 * tiles, 8)
    for half in range(halves):
        begin = first + half * LANES * tiles
        for tile in range(tiles):
            block = room_ref[pl.ds(begin + tile, LANES, stride=tiles), :]
            turn_ref[half, tile * LANES:(tile + 1) * LANES, :] = block.T
        for level in range(levels):
            y_ref[level, :, half * LANES:(half + 1) * LANES] = turn_ref[
                half, pl.ds(level, pad, stride=levels), :
            ]
    rate = jnp.concatenate(
        [turn_ref[half, lanes - 2:lanes - 1, :] for half in range(halves)], axis=1
    )
    count = jnp.concatenate(
        [turn_ref[half, lanes - 1:lanes, :] for half in range(halves)], axis=1
    )
    lane = lax.broadcasted_iota(jnp.int32, (1, INT_ROWS), 1)
    count = jnp.where((lane < valid) & (count <= MAXIT), count, 0.0)
    step_len = rate / jnp.maximum(count, 1.0)
    inverse_ref[...] = 1.0 / (1.0 + step_len * loss_ref[...])
    last = jnp.max(count).astype(jnp.int32)

    def advance(k, carry):
        active = k.astype(jnp.float32) < count

        def one_level(level, inner):
            y = y_ref[level]
            squashed = jnp.tanh(y).astype(jnp.bfloat16)
            produced = jnp.dot(coupling_ref[...], squashed, preferred_element_type=jnp.float32)
            y_ref[level] = jnp.where(active, (y + step_len * produced) * inverse_ref[...], y)
            return inner

        for level in range(levels):
            one_level(level, 0)
        return carry

    lax.fori_loop(0, last, advance, 0)
    for half in range(halves):
        begin = first + half * LANES * tiles
        for level in range(levels):
            turn_ref[half, pl.ds(level, pad, stride=levels), :] = y_ref[
                level, :, half * LANES:(half + 1) * LANES
            ]
        for tile in range(tiles):
            block = turn_ref[half, tile * LANES:(tile + 1) * LANES, :]
            room_ref[pl.ds(begin + tile, LANES, stride=tiles), :] = block.T


def integrate_kernel(sizes, plan, table_ref, loss_ref, coupling_ref, *refs):
    loads, merges, blocks, stores, operands = plan
    tiles = sizes[2]
    sources = refs[:operands]
    results = refs[operands:operands + len(stores)]
    room_ref, turn_ref, y_ref, inverse_ref, rows_ref, sem_ref, out_sem = refs[
        operands + len(stores):
    ]
    copies = []
    for index, (source, begin, groups, to) in enumerate(loads):
        ref = sources[source]
        if begin is not None:
            ref = ref.at[span_of(begin(table_ref), groups, tiles)]
        copies.append(pltpu.make_async_copy(
            ref, room_ref.at[span_of(to, groups, tiles)], sem_ref.at[index]
        ))
    for copy in copies:
        copy.start()
    for copy in copies:
        copy.wait()
    for begin, groups, to in merges:
        to = to(table_ref)

        def move(group, carry):
            room_ref[span_of(to + group, 1, tiles), :] = room_ref[
                span_of(begin + group, 1, tiles), :
            ]
            return carry

        lax.fori_loop(0, groups(table_ref), move, 0)
    for index, (begin, rows) in enumerate(blocks):
        rows_ref[0, index] = jnp.int32(begin)
        rows_ref[1, index] = rows(table_ref)

    def one_block(index, carry):
        valid = rows_ref[1, index]

        @pl.when(valid > 0)
        def _():
            integrate_block(sizes, room_ref, rows_ref[0, index], valid, loss_ref, coupling_ref,
                            turn_ref, y_ref, inverse_ref)

        return carry

    lax.fori_loop(0, len(blocks), one_block, 0)
    copies = []
    for index, (begin, groups) in enumerate(stores):
        copies.append(pltpu.make_async_copy(
            room_ref.at[span_of(begin(table_ref), groups, tiles)], results[index],
            out_sem.at[index],
        ))
    for copy in copies:
        copy.start()
    for copy in copies:
        copy.wait()


def cut_kernel(static, tiles, piece, step, table_ref, *refs):
    pieces = refs[2:2 + WIN]
    room_ref, sem_ref, out_sem = refs[2 + WIN:]
    wait_all(start_arrival(refs[:2], sem_ref, room_ref, table_ref[3, step * WIN], static, tiles))
    copies = []
    quarter = piece // 4
    for at in range(WIN):
        begin = table_ref[2, step * WIN + at]
        for part in range(4):
            wanted = table_ref[0, step * WIN + at] > part * quarter * 8
            copy = pltpu.make_async_copy(
                room_ref.at[span_of(begin + part * quarter, quarter, tiles)],
                pieces[at].at[span_of(part * quarter, quarter, tiles)], out_sem.at[part, at],
            )
            pl.when(wanted)(copy.start)
            copies.append((wanted, copy))
    wait_all(copies)


def finish_kernel(sizes, table_ref, *refs):
    species, levels, columns, tiles, static, piece, narrow_count, begins = sizes
    pair_total = narrow_count * WIN
    whole_pieces = pair_total - WIN
    (out_ref, piece_ref, room_ref, placed_ref, whole_ref, sem_ref, room_sem,
     out_sem) = refs[-8:]
    copies = []
    quarter = piece // 4
    for pair in range(whole_pieces):
        parts = []
        for part in range(4):
            copy = pltpu.make_async_copy(
                refs[pair].at[span_of(begins[pair] + part * quarter, quarter, tiles)],
                piece_ref.at[pair, span_of(part * quarter, quarter, tiles)],
                sem_ref.at[part, pair],
            )
            wanted = table_ref[0, pair] > part * quarter * 8
            pl.when(wanted)(copy.start)
            parts.append((wanted, copy))
        copies.append(parts)
    waits = start_arrival(refs[whole_pieces:whole_pieces + 2], room_sem, room_ref,
                          table_ref[3, whole_pieces], static, tiles)
    lane = lax.broadcasted_iota(jnp.int32, (1, LANES), 1)
    in_group = lax.broadcasted_iota(jnp.int32, (8, LANES), 0)
    for pair in range(pair_total):
        if pair < whole_pieces:
            wait_all(copies[pair])
            held = piece_ref.at[pair]
            begin = 0
        else:
            if pair == whole_pieces:
                wait_all(waits)
            held = room_ref
            begin = pl.multiple_of(table_ref[2, pair] * 8 * tiles, 8)
        count = table_ref[0, pair]
        first = held[pl.ds(begin + tiles - 1, 1), :]
        start = jnp.max(jnp.where(lane == LANES - 3, first, 0.0)).astype(jnp.int32)
        start = jnp.clip(start, 0, columns - 1) * tiles
        full = lax.shift_right_logical(count, 3)

        def move(groups, part, carry):
            for row in range(0, groups * 8 * tiles, 8):
                at = part * groups * 8 * tiles + row
                placed_ref[pl.ds(start + at, 8), :] = held[pl.ds(pl.multiple_of(begin + at, 8), 8), :]
            return carry

        many = lax.shift_right_logical(full, 2)
        lax.fori_loop(0, many, functools.partial(move, 4), 0)
        lax.fori_loop(many * 4, full, functools.partial(move, 1), 0)

        @pl.when((count & 7) > 0)
        def _():
            for row in range(0, 8 * tiles, 8):
                at = full * 8 * tiles + row
                to = pl.ds(start + at, 8)
                placed_ref[to, :] = jnp.where(
                    in_group + row < (count & 7) * tiles,
                    held[pl.ds(pl.multiple_of(begin + at, 8), 8), :], placed_ref[to, :],
                )

    per_tile = LANES // levels
    for part in range(columns // LANES):
        at = slice(part * LANES, (part + 1) * LANES)
        for tile in range(tiles):
            block = placed_ref[pl.ds(part * LANES * tiles + tile, LANES, stride=tiles), :]
            block = block.T.reshape(per_tile, levels, LANES)
            keep = min(per_tile, species - tile * per_tile)
            whole_ref[tile * per_tile:tile * per_tile + keep, :, at] = block[:keep]
        pltpu.make_async_copy(whole_ref.at[:, :, at], out_ref.at[:, :, at], out_sem.at[part]).start()
    for part in range(columns // LANES):
        at = slice(part * LANES, (part + 1) * LANES)
        pltpu.make_async_copy(whole_ref.at[:, :, at], out_ref.at[:, :, at], out_sem.at[part]).wait()


def local(tracers, column_rate, loss_rate, coupling, phys_index, iter_count):
    levels, species, columns = tracers.shape
    wide_count = lax.axis_size("wide")
    narrow_count = lax.axis_size("narrow")
    pair_total = WIN * narrow_count
    room = 2 * columns // pair_total
    piece = room // 8
    pad = -(-species // 8) * 8
    while levels * pad % LANES or levels * (pad - species) < 8:
        pad += 8
    tiles = levels * pad // LANES
    mean = columns // narrow_count // 8
    full = pl.BlockSpec(memory_space=pltpu.VMEM)
    smem = pl.BlockSpec(memory_space=pltpu.SMEM)
    hbm = pl.BlockSpec(memory_space=pltpu.HBM)
    last = narrow_count - 1
    moving = [at for at in range(WIN) if at != 1]
    order = [narrow_count // 2]
    order += [step for step in range(1, last) if step not in order] + [last]
    statics = {step: mean - UNIT if step == order[0] else mean for step in order}
    most = WIN * piece

    params = pltpu.CompilerParams(vmem_limit_bytes=VMEM)

    def rows_type(groups):
        return jax.ShapeDtypeStruct((groups * 8 * tiles, LANES), jnp.float32)

    def room_type(groups):
        return pltpu.VMEM((groups * 8 * tiles, LANES), jnp.float32)

    def entry(row, step, at=0):
        return lambda table: table[row, step * WIN + at]

    def over(step):
        return lambda table: entry(1, step)(table) + statics[step]

    def groups_of(step, at):
        return lambda table: lax.shift_right_logical(table[0, step * WIN + at] + 7, 3)

    def groups_over(step):
        return lambda table: table[3, step * WIN] - statics[step]

    def pair_cuts(target, at):
        return [
            (target, part * piece + half,
             lambda table, step=step, half=half: entry(1, step, at)(table) + half, piece // 2,
             lambda table, step=step, half=half: groups_of(step, at)(table) - half)
            for part, step in enumerate((0, last)) for half in range(0, piece, piece // 2)
        ]

    def sort(cuts, target_sizes, early, known):
        known_types = [
            jax.ShapeDtypeStruct((8, LANES), jnp.int32),
            jax.ShapeDtypeStruct((1, columns), jnp.int32),
        ]
        groups = columns // 8 + pair_total + most
        return pl.pallas_call(
            functools.partial(
                sort_kernel,
                (species, levels, columns, tiles, wide_count, narrow_count, pair_total),
                cuts, len(target_sizes), early,
            ),
            grid=(columns // SORT_COLUMNS,),
            in_specs=[full, full, full,
                      pl.BlockSpec((species, levels, SORT_COLUMNS), lambda at: (0, 0, at))]
            + [smem] * len(known),
            out_specs=([full, full] if early else []) + [hbm] * len(target_sizes),
            out_shape=(known_types if early else []) + [rows_type(size) for size in target_sizes],
            scratch_shapes=([
                pltpu.SMEM((1, columns), jnp.int32), pltpu.SMEM((8, LANES), jnp.int32),
                pltpu.SemaphoreType.DMA((2,)),
            ] if early else []) + [
                pltpu.VMEM((tiles * LANES, LANES), jnp.float32),
                pltpu.VMEM((SORT_COLUMNS // LANES, LANES * 8, LANES), jnp.float32),
                room_type(groups),
                pltpu.SemaphoreType.DMA((len(cuts),)),
            ],
            compiler_params=params,
            name="sort_columns" if early else "sort_later_columns",
        )(
            phys_index.reshape(1, columns),
            column_rate.reshape(1, columns),
            iter_count.reshape(1, columns),
            tracers.transpose(1, 0, 2),
            *known,
        )

    first_static = statics[order[0]]
    cuts = [(0, 0, entry(1, order[0]), first_static, entry(3, order[0]))]
    for index, at in enumerate(moving):
        cuts += pair_cuts(1 + index, at)
    table, places, *first = sort(
        cuts, [first_static] + [2 * piece] * len(moving), True, ()
    )
    cuts = [(0, 0, over(order[0]), most - first_static, groups_over(order[0]))]
    cuts += pair_cuts(1, 1)
    for index, step in enumerate(order[1:-1]):
        rest = most - statics[step]
        cuts.append((2 + index, 0, entry(1, step), statics[step], entry(3, step)))
        cuts.append((2 + index, statics[step], over(step), rest, groups_over(step)))
    first_rest, local_rows, *raw = sort(
        cuts, [most - first_static, 2 * piece] + [most] * (len(order) - 2), False, (table, places)
    )
    raw_groups = dict(zip(order[1:-1], raw))
    units = [
        (jnp.maximum(table[3, step * WIN] - statics[step], 0) + UNIT - 1) // UNIT
        for step in order
    ]
    loss_pad = jnp.pad(loss_rate, (0, pad - species)).reshape(pad, 1)
    coupling_pad = jnp.pad(coupling, ((0, pad - species), (0, pad - species)))
    block = INT_ROWS // 8

    def integrate(table, operands, loads, merges, blocks, stores):
        groups = max([to + size for _, _, size, to in loads] + [begin + block for begin, _ in blocks])
        groups += piece
        return pl.pallas_call(
            functools.partial(
                integrate_kernel, (levels, pad, tiles),
                (loads, merges, blocks, stores, len(operands)),
            ),
            in_specs=[smem, full, full] + [hbm] * len(operands),
            out_specs=[hbm] * len(stores),
            out_shape=[rows_type(size) for _, size in stores],
            scratch_shapes=[
                room_type(groups),
                pltpu.VMEM((INT_ROWS // LANES, tiles * LANES, LANES), jnp.float32),
                pltpu.VMEM((levels, pad, INT_ROWS), jnp.float32),
                pltpu.VMEM((pad, INT_ROWS), jnp.float32),
                pltpu.SMEM((2, LANES), jnp.int32),
                pltpu.SemaphoreType.DMA((len(loads),)),
                pltpu.SemaphoreType.DMA((len(stores),)),
            ],
            compiler_params=params,
            cost_estimate=pl.CostEstimate(
                flops=10**10, bytes_accessed=2**26, transcendentals=0
            ),
            name="integrate_columns",
        )(table, loss_pad, coupling_pad, *operands)

    def rows_of(step, at=0):
        return entry(0, step, at)

    def group_blocks(begin, step):
        return [
            (begin + part * block,
             lambda table, part=part: table[3, step * WIN] * 8 - part * INT_ROWS)
            for part in range(most // block)
        ]

    def here(begin):
        return lambda table: jnp.int32(begin)

    def step_over(step, units, rest):
        def leaf(units, rest):
            if units == 0:
                return rest
            got = from_behind(rest[:units * UNIT * 8 * tiles], "narrow", step)
            return lax.dynamic_update_slice(rest, got, (0, 0))

        leaves = [functools.partial(leaf, count) for count in range((most - statics[step]) // UNIT + 1)]
        return lax.switch(units, leaves, rest)

    pieces = {}
    outgoing = [first[0], first_rest]
    wide_now = first[1:]
    keys_now = [[(at, 0), (at, last)] for at in moving]
    static_part = from_behind(outgoing[0], "narrow", order[0])
    wide_got = [from_behind(value, "wide", at - 1) for value, at in zip(wide_now, moving)]
    table_then = table
    for phase, step in enumerate(order):
        static = statics[step]
        operands, loads, merges, blocks, stores, named = [], [], [], [], [], []
        used = 0
        if phase + 1 < len(order):
            coming = order[phase + 1]
            if coming == last:
                operands += [pieces[at, last][0] for at in moving] + [local_rows]
                for index, at in enumerate(moving):
                    loads.append((index, here(pieces[at, last][1]), piece, most + at * piece))
                loads.append((len(moving), here(piece), piece, most + piece))
                for at in range(WIN):
                    merges.append(
                        (most + at * piece, groups_of(last, at), entry(2, last, at))
                    )
                used = most + WIN * piece
            else:
                operands.append(raw_groups[coming])
                loads.append((0, None, most, 0))
                used = most
            blocks += group_blocks(0, coming)
            stores += [(here(0), statics[coming]), (here(statics[coming]), most - statics[coming])]
        extra = []
        if phase == 0:
            extra.append(((1, 0), (local_rows, 0)))
        if phase == 1:
            extra += [((at, 0), pieces[at, 0]) for at in moving if at != moving[0]]
        if phase == 2:
            extra += [((at, order[0]), pieces[at, order[0]]) for at in range(WIN)]
            extra.append(((moving[0], 0), pieces[moving[0], 0]))
        used = -(-used // block) * block
        for key, value in extra:
            operands.append(value[0])
            loads.append((len(operands) - 1, here(value[1]), piece, used))
            blocks.append((used, rows_of(key[1], key[0])))
            stores.append((here(used), piece))
            named.append(key)
            used += block
        if stores:
            results = integrate(table_then, operands, loads, merges, blocks, stores)
        else:
            results = []
        rest = outgoing[1]
        if phase == 0:
            static_part, results, rest, units = lax.optimization_barrier(
                (static_part, results, rest, units)
            )
        else:
            static_part, results, rest = lax.optimization_barrier((static_part, results, rest))
        done = {key: (value, 0) for key, value in zip(named, results[len(results) - len(named):])}
        outgoing = results[:len(results) - len(named)]
        arrived = [static_part, step_over(step, units[phase], rest)]
        if step != last:
            arrived, outgoing = lax.optimization_barrier((arrived, outgoing))
            static_part = from_behind(outgoing[0], "narrow", order[phase + 1])
        if step != last:
            cut = pl.pallas_call(
                functools.partial(cut_kernel, static, tiles, piece, step),
                in_specs=[smem] + [hbm] * len(arrived),
                out_specs=[hbm] * WIN,
                out_shape=[rows_type(piece)] * WIN,
                scratch_shapes=[
                    room_type(most + piece),
                    pltpu.SemaphoreType.DMA((5,)),
                    pltpu.SemaphoreType.DMA((4, WIN)),
                ],
                compiler_params=params,
                name="cut_pieces",
            )(table, *arrived)
            cut, wide_got, table_then = lax.optimization_barrier((cut, wide_got, table))
        for keys, value in zip(keys_now, wide_got):
            pieces.update({key: (value, part * piece) for part, key in enumerate(keys)})
        pieces.update(done)
        if step != last:
            pieces[1, step] = (cut[1], 0)
            keys_now = [[(at, step)] for at in moving]
            wide_got = [from_behind(cut[at], "wide", at - 1) for at in moving]

    held = [pieces[at, step] for step in range(last) for at in range(WIN)]
    buffers = [value for value, _ in held] + arrived
    updated = pl.pallas_call(
        functools.partial(
            finish_kernel,
            (species, levels, columns, tiles, static, piece, narrow_count,
             [begin for _, begin in held]),
        ),
        in_specs=[smem] + [hbm] * len(buffers),
        out_specs=hbm,
        out_shape=jax.ShapeDtypeStruct((species, levels, columns), jnp.float32),
        scratch_shapes=[
            pltpu.VMEM((pair_total - WIN, piece * 8 * tiles, LANES), jnp.float32),
            room_type(most + piece),
            room_type(columns // 8 + 1),
            pltpu.VMEM((species, levels, columns), jnp.float32),
            pltpu.SemaphoreType.DMA((4, pair_total)),
            pltpu.SemaphoreType.DMA((5,)),
            pltpu.SemaphoreType.DMA((columns // LANES,)),
        ],
        compiler_params=params,
        name="place_columns",
    )(table, *buffers)
    return updated.transpose(1, 0, 2)


def solution(mesh):
    placed = (
        P(None, None, ("wide", "narrow")),
        P(("wide", "narrow")),
        P(),
        P(),
        P(("wide", "narrow")),
        P(("wide", "narrow")),
    )
    return jax.shard_map(
        local,
        mesh=mesh,
        in_specs=placed,
        out_specs=P(None, None, ("wide", "narrow")),
        check_vma=False,
    )
```
